32 devices in a mesh: dp: 4 (over y, x), fsdp: 8 (over z, core).
Axes of the slice: x: 2, y: 2, z: 4, core: 2. Of those that a mesh axis runs over, the one named last changes fastest.
Arguments:
- token_ids: int32 [2, 32, 128], P(None, ('dp', 'fsdp')), may hold values from 0 to 50303
- loss_mask: int32 [2, 32, 128], P(None, ('dp', 'fsdp')), may hold values 0 or 1
- lengths: int32 [2, 32], P(None, ('dp', 'fsdp')), may hold values from 64 to 128, as said below
- buffer_ids: int32 [2, 32, 128], P(None, ('dp', 'fsdp')), may hold values from 0 to 2, never falling along the last dimension, each value on 1 to 64 neighbouring positions
- embed_table: float32 [50304, 512], P('fsdp'), may hold values from -6 to 6
- embed_moment: float32 [50304, 512], P(('fsdp', 'dp')), may hold values from -1.66893e-06 to 1.66893e-06
- embed_average: float32 [50304, 512], P(('fsdp', 'dp')), may hold values from -6 to 6
- head_table: float32 [50304, 512], P('fsdp'), may hold values from -0.25 to 0.25
- head_moment: float32 [50304, 512], P(('fsdp', 'dp')), may hold values from -1.66893e-06 to 1.66893e-06
- head_average: float32 [50304, 512], P(('fsdp', 'dp')), may hold values from -0.25 to 0.25
- in_weights: float32 [512, 3584], P('fsdp'), may hold values from -0.25 to 0.25
- in_moment: float32 [512, 3584], P('fsdp'), may hold values from -1.66893e-06 to 1.66893e-06
- in_average: float32 [512, 3584], P('fsdp'), may hold values from -0.25 to 0.25
- out_weights: float32 [2560, 512], P('fsdp')
- out_moment: float32 [2560, 512], P('fsdp'), may hold values from -1.66893e-06 to 1.66893e-06
- out_average: float32 [2560, 512], P('fsdp'), may hold values from -0.25 to 0.25
- vectors: float32 [7680], P('fsdp')
- vector_moment: float32 [7680], P('fsdp'), may hold values from -1.66893e-06 to 1.66893e-06
- vector_average: float32 [7680], P('fsdp')
Outputs:
- new_embed: float32 [50304, 512], P('fsdp')
- new_embed_moment: float32 [50304, 512], P(('fsdp', 'dp'))
- new_embed_average: float32 [50304, 512], P(('fsdp', 'dp'))
- new_head: float32 [50304, 512], P('fsdp')
- new_head_moment: float32 [50304, 512], P(('fsdp', 'dp'))
- new_head_average: float32 [50304, 512], P(('fsdp', 'dp'))
- new_in: float32 [512, 3584], P('fsdp')
- new_in_moment: float32 [512, 3584], P('fsdp')
- new_in_average: float32 [512, 3584], P('fsdp')
- new_out: float32 [2560, 512], P('fsdp')
- new_out_moment: float32 [2560, 512], P('fsdp')
- new_out_average: float32 [2560, 512], P('fsdp')
- new_vectors: float32 [7680], P('fsdp')
- new_vector_moment: float32 [7680], P('fsdp')
- new_vector_average: float32 [7680], P('fsdp')
- loss: float32 [], replicated
- grad_norm: float32 [], replicated
The draws below stay inside these ranges and needn't reach their ends.
Inputs may be any that keep to these rules, and one draw needn't show every extreme that they name: `lengths`: each slot has 64 or 128 live positions. `buffer_ids`: along a slot the buffer numbers never fall; a buffer covers 1 to 64 positions.
All inputs are finite; a program needn't handle non-finite values. No bound on the sum of `loss_mask` on one device may be relied on, other than what follows from the above.
Results may differ from the reference program's by a relative error of at most 0.002.
The reference program's roundings to bfloat16 on the way count: a program that leaves them out, or rounds other values in their place, can miss the bound.
Values may be sent and summed in bfloat16 or wider, within the bound.
A program may use at most 320 MiB of HBM per device.

```python
import functools
import math
import jax
import jax.numpy as jnp
import numpy as np
from jax import lax

D = 512
HEADS = 8
FF = 2048
V = 50304
VECS = 7680
NPARAM = 54664704
SEQ = 128
NSEG = 3
MB = 2
SEQS = 32


def draw_lengths(key, part):
    pick = jax.random.randint(jax.random.fold_in(key, 11), (MB, SEQS), 0, 2)
    values = SEQ // 2 * (1 + pick)
    return values.at[0, 0].set(SEQ).astype(jnp.int32)


def draw_out_weights(key, part):
    inner = jax.random.fold_in(key, 13)
    places = jnp.arange(D + FF)[:, None]
    spread = jnp.where(places < D, (D / 32.0) ** (-0.5), 1.5 / FF ** 0.5).astype(jnp.float32)
    base = jax.random.normal(inner, (D + FF, D), jnp.float32)
    return base * spread


def vector_values(key):
    places = jnp.arange(VECS)
    gain_zone = (places < 6 * D) & (places // D % 2 == 0)
    noise = jax.random.uniform(key, (VECS,), jnp.float32, -1.0, 1.0)
    return jnp.where(gain_zone, 1.0 + 0.5 * noise, 0.3 * noise).astype(jnp.float32)


def draw_vectors(key, part):
    return vector_values(jax.random.fold_in(key, 17))


def draw_vector_average(key, part):
    return vector_values(jax.random.fold_in(key, 19))


def plant(drawn, key, least, largest):
    longest = drawn.shape.index(max(drawn.shape))
    spots = []
    for shift in (0, 1):
        where = [jax.random.randint(jax.random.fold_in(key, axis), (), 0, length) for axis, length in enumerate(drawn.shape)]
        where[longest] = (where[longest] + shift) % drawn.shape[longest]
        spots.append(tuple(where))
    return drawn.at[spots[0]].set(least).at[spots[1]].set(largest)


def shard_levels(key, extent, pieces, low, high):
    factor_of = 1.0
    for dim, blocks in pieces:
        draws = jax.random.uniform(jax.random.fold_in(jax.random.fold_in(key, 6), dim), (blocks,), jnp.float32, low / len(pieces), high / len(pieces))
        factor_of = factor_of * jnp.repeat(jnp.exp(draws), extent[dim] // blocks).reshape((-1,) + (1,) * (len(extent) - 1 - dim))
    return factor_of


def rank_bounds(count, skew):
    portions = [(1 << 20) // math.isqrt(standing ** skew) + 1 for standing in range(1, count + 1)]
    scale = 1 + sum(portions) // (1 << 30)
    return np.cumsum(np.array([max(1, weight // scale) for weight in portions]))


def skewed_ids(own_key, extent, count, lean):
    grid = rank_bounds(count, lean)
    lot = jax.random.randint(jax.random.fold_in(own_key, 1), extent, 0, int(grid[count - 1]))
    rank = jnp.searchsorted(jnp.asarray(grid, jnp.int32), lot, side="right")
    return jax.random.permutation(jax.random.fold_in(own_key, 2), count)[rank].astype(jnp.int32)


def length_profile(count, total, reach, skew):
    loads = [(1 << 20) // math.isqrt(rank ** skew) + 1 for rank in range(2, count + 1)]
    surplus, given = total - reach - (count - 1), [1] * (count - 1)
    while surplus > 0:
        free = [i for i in range(count - 1) if given[i] < reach]
        mass, left = sum([loads[i] for i in free]), surplus
        for i in free:
            addition = min(reach - given[i], max(1, left * loads[i] // mass), surplus)
            given[i] = given[i] + addition
            surplus = surplus - addition
    return np.array([reach] + given)


def uneven(key, number_of, total, reach, slope):
    if number_of == 2:
        one = jax.random.randint(key, (), max(1, total - reach), min(reach, total - 1) + 1)
        return jnp.stack([one, total - one])
    sizes = jnp.asarray(length_profile(number_of, total, reach, slope), jnp.int32)
    pairs = (number_of - 1) // 2
    source_of, taker = sizes[1:1 + 2 * pairs:2], sizes[2:2 + 2 * pairs:2]
    room = jnp.minimum(source_of - 1, reach - taker)
    moved = jax.random.randint(jax.random.fold_in(key, 1), (pairs,), 0, 1 << 20) % (room + 1)
    sizes = sizes.at[1:1 + 2 * pairs:2].set(source_of - moved).at[2:2 + 2 * pairs:2].set(taker + moved)
    return sizes[jax.random.permutation(jax.random.fold_in(key, 2), number_of)]


def gaussian(stream_key, dims, scale, bound, pieces=(), kind=jnp.bfloat16):
    values = jax.random.normal(stream_key, dims, jnp.float32) * scale
    if len(pieces) > 0:
        values = shard_levels(stream_key, dims, pieces, -0.22, 0.18) * values
    return jnp.clip(values, min=-bound, max=bound).astype(kind)


def setup_inputs(seed: int = 0) -> dict:
    arg_keys = jax.random.split(jax.random.key(seed), 20)
    return {
        "token_ids": plant(skewed_ids(arg_keys[0], (MB, SEQS, SEQ), V, 2), jax.random.fold_in(arg_keys[0], 3), 0, V - 1).astype(jnp.int32),
        "loss_mask": plant((jax.random.randint(arg_keys[1], (MB, SEQS, SEQ), 0, 8) < 7).astype(jnp.int32), jax.random.fold_in(arg_keys[1], 1), 0, 1),
        "lengths": draw_lengths(jax.random.fold_in(arg_keys[19], 71), 0),
        "buffer_ids": jax.vmap(lambda own: jnp.searchsorted(jnp.cumsum(uneven(own, NSEG, SEQ, SEQ // 2, 0)), jnp.arange(SEQ), side="right"))(jax.random.split(arg_keys[3], MB * SEQS)).reshape((MB, SEQS, SEQ)).astype(jnp.int32),
        "embed_table": gaussian(arg_keys[4], (V, D), 1.0, 6.0, ((0, 8),), jnp.float32),
        "embed_moment": gaussian(arg_keys[5], (V, D), (0.002 / NPARAM ** 0.5), 1.6689300537109375e-06, ((0, 32),), jnp.float32),
        "embed_average": gaussian(arg_keys[6], (V, D), 1.0, 6.0, ((0, 32),), jnp.float32),
        "head_table": gaussian(arg_keys[7], (V, D), D ** -0.5, 0.25, ((0, 8),), jnp.float32),
        "head_moment": gaussian(arg_keys[8], (V, D), (0.002 / NPARAM ** 0.5), 1.6689300537109375e-06, ((0, 32),), jnp.float32),
        "head_average": gaussian(arg_keys[9], (V, D), D ** -0.5, 0.25, ((0, 32),), jnp.float32),
        "in_weights": gaussian(arg_keys[10], (D, 3 * D + FF), D ** -0.5, 0.25, ((0, 8),), jnp.float32),
        "in_moment": gaussian(arg_keys[11], (D, 3 * D + FF), (0.002 / NPARAM ** 0.5), 1.6689300537109375e-06, ((0, 8),), jnp.float32),
        "in_average": gaussian(arg_keys[12], (D, 3 * D + FF), D ** -0.5, 0.25, ((0, 8),), jnp.float32),
        "out_weights": draw_out_weights(jax.random.fold_in(arg_keys[19], 71), 0),
        "out_moment": gaussian(arg_keys[14], (D + FF, D), (0.002 / NPARAM ** 0.5), 1.6689300537109375e-06, ((0, 8),), jnp.float32),
        "out_average": gaussian(arg_keys[15], (D + FF, D), D ** -0.5, 0.25, ((0, 8),), jnp.float32),
        "vectors": draw_vectors(jax.random.fold_in(arg_keys[19], 71), 0),
        "vector_moment": gaussian(arg_keys[17], (VECS,), (0.002 / NPARAM ** 0.5), 1.6689300537109375e-06, ((0, 8),), jnp.float32),
        "vector_average": draw_vector_average(jax.random.fold_in(arg_keys[19], 71), 0),
    }


EPSILON = 1e-05
CLIP_LEVEL = 0.002
MOMENTUM = 0.5
DECAY = 0.5
HIGHEST = lax.Precision.HIGHEST

@jax.custom_vjp
def low(v):
    return lax.optimization_barrier(v.astype(jnp.bfloat16)).astype(jnp.float32)

@jax.custom_vjp
def low_back(v):
    return v

def low_keep(v):
    return (low(v), None)

def low_pass(kept, grad):
    return (grad,)

def back_keep(v):
    return (v, None)

def back_low(kept, grad):
    return (low(grad),)
low.defvjp(low_keep, low_pass)
low_back.defvjp(back_keep, back_low)

def slot_info(tokens, marks, length, buffers, buffer_count):
    seq = tokens.shape[0]
    places = jnp.arange(seq, dtype=jnp.int32)
    same_buffer = jnp.concatenate([buffers[1:] == buffers[:-1], jnp.zeros((1,), dtype=bool)])
    valid = jnp.where((marks == 1) & (places + 1 < length) & same_buffer, 1.0, 0.0).astype(jnp.float32)
    member = buffers[None, :] == jnp.arange(buffer_count, dtype=jnp.int32)[:, None]
    weights = jnp.where(member, 1.0, 0.0).astype(jnp.float32)
    tally = lax.optimization_barrier(jnp.sum(weights * valid[None, :], axis=1))
    share = valid * lax.optimization_barrier(jnp.sum(weights / jnp.maximum(tally, 1.0)[:, None], axis=0))
    counted = jnp.sum(jnp.where(tally > 0.5, 1.0, 0.0).astype(jnp.float32))
    first = lax.optimization_barrier(jnp.min(jnp.where(member, places[None, :], seq), axis=1))
    offset = places - lax.optimization_barrier(jnp.sum(jnp.where(member, first[:, None], 0), axis=0))
    successor = jnp.concatenate([tokens[1:], jnp.zeros((1,), dtype=jnp.int32)])
    return (share, successor, offset.astype(jnp.int32), counted)

def vector_parts(vectors, width, hidden):
    amounts = [width] * 6 + [3 * width, width, hidden, width]
    parts = []
    begin = 0
    for amount in amounts:
        parts.append(vectors[begin:begin + amount])
        begin = begin + amount
    return parts

def rotary_tables(offset, rot):
    half = rot // 2
    freqs = jnp.power(10000.0, -2.0 * jnp.arange(half, dtype=jnp.float32) / rot)
    angles = offset.astype(jnp.float32)[:, None] * freqs[None, :]
    return (jnp.cos(angles)[:, None, :], jnp.sin(angles)[:, None, :])

def rotate(values, cosine, sine, rot):
    half = rot // 2
    first = values[..., :half]
    second = values[..., half:rot]
    return jnp.concatenate([first * cosine - second * sine, second * cosine + first * sine, values[..., rot:]], axis=-1)

def layer_norm(values, gain, bias):
    mean = lax.optimization_barrier(jnp.mean(values, axis=-1, keepdims=True))
    centred = values - mean
    return centred * lax.rsqrt(lax.optimization_barrier(jnp.mean(centred * centred, axis=-1, keepdims=True)) + EPSILON) * gain + bias

def product(left, right):
    return jnp.dot(left, right, precision=HIGHEST, preferred_element_type=jnp.float32)

def slot_loss(params, tokens, share, successor, offset, buffers):
    embed_low, head_low, in_low, out_low, vector_low = params
    width = embed_low.shape[1]
    hidden = in_low.shape[1] - 3 * width
    head_size = width // HEADS
    rot = head_size // 4
    factor = 1.0 / math.sqrt(head_size)
    seq = tokens.shape[0]
    parts = vector_parts(vector_low, width, hidden)
    resid = low_back(jnp.take(embed_low, tokens, axis=0))
    input_one = low(layer_norm(resid, parts[0], parts[1]))
    input_two = low(layer_norm(resid, parts[2], parts[3]))
    triple = (low_back(product(input_one, in_low[:, :3 * width])) + parts[6]).reshape(seq, 3, HEADS, head_size)
    cosine, sine = rotary_tables(offset, rot)
    queries = low(rotate(triple[:, 0], cosine, sine, rot))
    keys = low(rotate(triple[:, 1], cosine, sine, rot))
    values = low(triple[:, 2])
    places = jnp.arange(seq, dtype=jnp.int32)
    allowed = (buffers[:, None] == buffers[None, :]) & (places[None, :] <= places[:, None])
    scores = low_back(jnp.einsum('qhd,khd->hqk', queries, keys, precision=HIGHEST)) * factor
    scores = jnp.where(allowed[None, :, :], scores, -1e+30)
    probs = jax.nn.softmax(scores, axis=-1)
    mixed = low(low_back(jnp.einsum('hqk,khd->qhd', low(probs), values, precision=HIGHEST))).reshape(seq, width)
    activated = low(jax.nn.gelu(low_back(product(input_two, in_low[:, 3 * width:])) + parts[8], approximate=False))
    joined = jnp.concatenate([mixed, activated], axis=1)
    resid = resid + low_back(product(joined, out_low)) + parts[7] + parts[9]
    final = low(layer_norm(resid, parts[4], parts[5]))
    logits = low_back(lax.dot_general(final, head_low, (((1,), (1,)), ((), ())), precision=HIGHEST, preferred_element_type=jnp.float32))
    logsum = jax.nn.logsumexp(logits, axis=-1)
    target = jnp.take_along_axis(logits, successor[:, None], axis=1)[:, 0]
    return jnp.sum(share * (logsum - target))

def reference(token_ids, loss_mask, lengths, buffer_ids, embed_table, embed_moment, embed_average, head_table, head_moment, head_average, in_weights, in_moment, in_average, out_weights, out_moment, out_average, vectors, vector_moment, vector_average):
    slots = token_ids.shape[0] * token_ids.shape[1]
    seq = token_ids.shape[2]
    tokens = token_ids.reshape(slots, seq)
    marks = loss_mask.reshape(slots, seq)
    buffers = buffer_ids.reshape(slots, seq)
    live = lengths.reshape(slots)
    share, successor, offset, counted = jax.vmap(functools.partial(slot_info, buffer_count=NSEG))(tokens, marks, live, buffers)
    count = jnp.maximum(jnp.sum(counted), 1.0)
    checked = jax.checkpoint(slot_loss)

    def total_loss(params):
        rounded = tuple((low(item) for item in params))

        def step(carry, items):
            return (carry + checked(rounded, *items), None)
        total, unused = lax.scan(step, jnp.zeros((), jnp.float32), (tokens, share, successor, offset, buffers))
        return total / count
    weights = (embed_table, head_table, in_weights, out_weights, vectors)
    loss, pullback = jax.vjp(total_loss, weights)
    grads = pullback(jnp.ones((), jnp.float32))[0]
    square = jnp.zeros((), jnp.float32)
    for grad in grads:
        square = square + jnp.sum(grad * grad)
    grad_norm = jnp.sqrt(square)
    factor = CLIP_LEVEL / jnp.maximum(grad_norm, CLIP_LEVEL)
    base = math.sqrt(NPARAM) / CLIP_LEVEL
    width = embed_table.shape[1]
    rates = (base, base / math.sqrt(width), base / math.sqrt(width), base / math.sqrt(width), 0.3 * base)
    moments = (embed_moment, head_moment, in_moment, out_moment, vector_moment)
    averages = (embed_average, head_average, in_average, out_average, vector_average)
    results = []
    for weight, grad, moment, average, rate in zip(weights, grads, moments, averages, rates):
        clipped = factor * grad
        new_moment = MOMENTUM * moment + clipped
        new_weight = weight - rate * (clipped + MOMENTUM * new_moment)
        new_average = DECAY * average + (1.0 - DECAY) * new_weight
        results.append((new_weight, new_moment, new_average))
    return (results[0][0], results[0][1], results[0][2], results[1][0], results[1][1], results[1][2], results[2][0], results[2][1], results[2][2], results[3][0], results[3][1], results[3][2], results[4][0], results[4][1], results[4][2], loss, grad_norm)
```

```python
import functools
import math

import jax
import jax.numpy as jnp
from jax import lax
from jax.experimental import pallas as pl
from jax.experimental.pallas import tpu as pltpu
from jax.sharding import PartitionSpec as P

HEADS = 8
NPARAM = 54664704
NSEG = 3


EPSILON = 1e-05
CLIP_LEVEL = 0.002
MOMENTUM = 0.5
DECAY = 0.5
NARROW = jnp.bfloat16
FLOAT = jnp.float32
ROWS_CONTRACT = (((0,), (0,)), ((), ()))
LAST_CONTRACT = (((1,), (1,)), ((), ()))


VMEM_LIMIT = 60 * 2**20


def slot_info(tokens, marks, length, buffers, buffer_count):
    seq = tokens.shape[0]
    places = jnp.arange(seq, dtype=jnp.int32)
    same_buffer = jnp.concatenate([buffers[1:] == buffers[:-1], jnp.zeros((1,), dtype=bool)])
    valid = jnp.where((marks == 1) & (places + 1 < length) & same_buffer, 1.0, 0.0).astype(FLOAT)
    member = buffers[None, :] == jnp.arange(buffer_count, dtype=jnp.int32)[:, None]
    weights = jnp.where(member, 1.0, 0.0).astype(FLOAT)
    tally = jnp.sum(weights * valid[None, :], axis=1)
    divisor = valid * jnp.sum(weights * tally[:, None], axis=0)
    counted = jnp.sum(jnp.where(tally > 0.5, 1.0, 0.0).astype(FLOAT))
    first = jnp.min(jnp.where(member, places[None, :], seq), axis=1)
    offset = places - jnp.sum(jnp.where(member, first[:, None], 0), axis=0)
    return (divisor.astype(jnp.int32), offset, counted.astype(jnp.int32))


def vector_parts(vectors, width, hidden):
    amounts = [width] * 6 + [3 * width, width, hidden, width]
    parts = []
    begin = 0
    for amount in amounts:
        parts.append(vectors[begin : begin + amount])
        begin = begin + amount
    return parts


def rotary_tables(offset, rot):
    half = rot // 2
    freqs = jnp.power(10000.0, -2.0 * jnp.arange(half, dtype=FLOAT) / rot)
    angles = offset.astype(FLOAT)[:, None] * freqs[None, :]
    return (jnp.cos(angles)[:, None, :], jnp.sin(angles)[:, None, :])


def rotate(values, cosine, sine, rot):
    half = rot // 2
    first = values[..., :half]
    second = values[..., half:rot]
    return jnp.concatenate(
        [first * cosine - second * sine, second * cosine + first * sine, values[..., rot:]], axis=-1
    )


def rotate_back(grads, cosine, sine, rot):
    half = rot // 2
    first = grads[..., :half]
    second = grads[..., half:rot]
    return jnp.concatenate(
        [first * cosine + second * sine, second * cosine - first * sine, grads[..., rot:]], axis=-1
    )


def norm_unit(values):
    mean = jnp.mean(values, axis=-1, keepdims=True)
    centred = values - mean
    scale = lax.rsqrt(jnp.mean(centred * centred, axis=-1, keepdims=True) + EPSILON)
    return (centred * scale, scale)


def norm_back(scaled, unit, scale):
    return scale * (
        scaled
        - jnp.mean(scaled, axis=-1, keepdims=True)
        - unit * jnp.mean(scaled * unit, axis=-1, keepdims=True)
    )


def gelu_slope(values):
    return (
        0.5 * (1.0 + lax.erf(values * 0.7071067811865476))
        + values * jnp.exp(-0.5 * values * values) * 0.3989422804014327
    )


def attention_scores(queries, keys, allowed, factor):
    scores = jnp.einsum("bqhd,bkhd->bhqk", queries, keys, preferred_element_type=FLOAT) * factor
    return jnp.where(allowed[:, None, :, :], scores, -1e30)


def layer_forward(resid, in_full, out_full, parts, allowed, cosine, sine, factor):
    rows, width = resid.shape
    batches = allowed.shape[0]
    seq = rows // batches
    head_size = width // HEADS
    rot = head_size // 4
    unit, scale = norm_unit(resid)
    input_one = (unit * parts[0] + parts[1]).astype(NARROW)
    input_two = (unit * parts[2] + parts[3]).astype(NARROW)
    triple = (
        jnp.dot(input_one, in_full[:, : 3 * width], preferred_element_type=FLOAT) + parts[6]
    ).reshape(rows, 3, HEADS, head_size)
    shape = (batches, seq, HEADS, head_size)
    queries = rotate(triple[:, 0], cosine, sine, rot).astype(NARROW).reshape(shape)
    keys = rotate(triple[:, 1], cosine, sine, rot).astype(NARROW).reshape(shape)
    values = triple[:, 2].astype(NARROW).reshape(shape)
    scores = attention_scores(queries, keys, allowed, factor)
    top = jnp.max(scores, axis=-1, keepdims=True)
    logsum = top + jnp.log(jnp.sum(jnp.exp(scores - top), axis=-1, keepdims=True))
    probs = jnp.exp(scores - logsum).astype(NARROW)
    mixed = (
        jnp.einsum("bhqk,bkhd->bqhd", probs, values, preferred_element_type=FLOAT)
        .astype(NARROW)
        .reshape(rows, width)
    )
    pre_act = jnp.dot(input_two, in_full[:, 3 * width :], preferred_element_type=FLOAT) + parts[8]
    activated = jax.nn.gelu(pre_act, approximate=False).astype(NARROW)
    joined = jnp.concatenate([mixed, activated], axis=1)
    result = resid + jnp.dot(joined, out_full, preferred_element_type=FLOAT) + parts[7] + parts[9]
    kept = (input_one, input_two, unit, scale, queries, keys, values, logsum, pre_act, joined)
    return (result, kept)


def layer_backward(grad_out, in_full, out_full, parts, kept, allowed, cosine, sine, factor):
    input_one, input_two, unit, scale, queries, keys, values, logsum, pre_act, joined = kept
    rows, width = grad_out.shape
    batches = allowed.shape[0]
    head_size = width // HEADS
    rot = head_size // 4
    grad_low = grad_out.astype(NARROW)
    out_grad = lax.dot_general(joined, grad_low, ROWS_CONTRACT, preferred_element_type=FLOAT)
    joined_grad = lax.dot_general(grad_low, out_full, LAST_CONTRACT, preferred_element_type=FLOAT)
    mixed_grad = joined_grad[:, :width].astype(NARROW).reshape(batches, -1, HEADS, head_size)
    pre_grad = joined_grad[:, width:] * gelu_slope(pre_act)
    pre_low = pre_grad.astype(NARROW)
    probs = jnp.exp(attention_scores(queries, keys, allowed, factor) - logsum)
    prob_grad = jnp.einsum("bqhd,bkhd->bhqk", mixed_grad, values, preferred_element_type=FLOAT)
    value_grad = jnp.einsum(
        "bhqk,bqhd->bkhd", probs.astype(NARROW), mixed_grad, preferred_element_type=FLOAT
    )
    score_grad = (
        probs * (prob_grad - jnp.sum(probs * prob_grad, axis=-1, keepdims=True)) * factor
    ).astype(NARROW)
    flat = (rows, HEADS, head_size)
    query_grad = rotate_back(
        jnp.einsum("bhqk,bkhd->bqhd", score_grad, keys, preferred_element_type=FLOAT).reshape(flat),
        cosine,
        sine,
        rot,
    )
    key_grad = rotate_back(
        jnp.einsum("bhqk,bqhd->bkhd", score_grad, queries, preferred_element_type=FLOAT).reshape(
            flat
        ),
        cosine,
        sine,
        rot,
    )
    qkv_grad = jnp.stack([query_grad, key_grad, value_grad.reshape(flat)], axis=1).reshape(
        rows, 3 * width
    )
    qkv_low = qkv_grad.astype(NARROW)
    in_grad = jnp.concatenate(
        [
            lax.dot_general(input_one, qkv_low, ROWS_CONTRACT, preferred_element_type=FLOAT),
            lax.dot_general(input_two, pre_low, ROWS_CONTRACT, preferred_element_type=FLOAT),
        ],
        axis=1,
    )
    back_one = lax.dot_general(
        qkv_low, in_full[:, : 3 * width], LAST_CONTRACT, preferred_element_type=FLOAT
    )
    back_two = lax.dot_general(
        pre_low, in_full[:, 3 * width :], LAST_CONTRACT, preferred_element_type=FLOAT
    )
    resid_grad = grad_out + norm_back(back_one * parts[0] + back_two * parts[2], unit, scale)
    residual_bias = jnp.sum(grad_out, axis=0)
    small = (
        jnp.sum(back_one * unit, axis=0),
        jnp.sum(back_one, axis=0),
        jnp.sum(back_two * unit, axis=0),
        jnp.sum(back_two, axis=0),
        jnp.sum(qkv_grad, axis=0),
        residual_bias,
        jnp.sum(pre_grad, axis=0),
        residual_bias,
    )
    return (resid_grad, in_grad, out_grad, small)


def block_rows(rows, cap):
    best = rows
    for size in range(8, cap + 1, 8):
        if rows % size == 0:
            best = size
    return best


def head_forward(table, hidden, target):
    vocab, width = table.shape
    rows = hidden.shape[0]
    tile = 512
    block = block_rows(vocab, 1100)
    blocks = vocab // block
    lines = -(-(2 * blocks + 1) // 8) * 8

    def kernel(table_ref, hidden_ref, target_ref, exps_ref, stats_ref):
        here = hidden_ref[...]
        places = lax.broadcasted_iota(jnp.int32, (block, tile), 0)
        hit = jnp.zeros((1, tile), FLOAT)
        for b in range(blocks):
            part = slice(b * block, (b + 1) * block)
            logits = lax.dot_general(
                table_ref[part, :], here, LAST_CONTRACT, preferred_element_type=FLOAT
            )
            top = jnp.max(logits, axis=0, keepdims=True)
            exps = jnp.exp(logits - top)
            stats_ref[0, b : b + 1, :] = top
            stats_ref[0, blocks + b : blocks + b + 1, :] = jnp.sum(exps, axis=0, keepdims=True)
            hit = hit + jnp.sum(
                jnp.where(places == target_ref[0] - b * block, logits, 0.0), axis=0, keepdims=True
            )
            exps_ref[part, :] = exps.astype(NARROW)
        stats_ref[0, 2 * blocks : 2 * blocks + 1, :] = hit

    whole = pl.BlockSpec(memory_space=pltpu.VMEM)
    tiles = rows // tile
    exps, stats = pl.pallas_call(
        kernel,
        grid=(tiles,),
        in_specs=[
            whole,
            pl.BlockSpec((tile, width), lambda i: (i, 0)),
            pl.BlockSpec((1, 1, tile), lambda i: (i, 0, 0)),
        ],
        out_specs=[
            pl.BlockSpec((vocab, tile), lambda i: (0, i)),
            pl.BlockSpec((1, lines, tile), lambda i: (i, 0, 0)),
        ],
        out_shape=[
            jax.ShapeDtypeStruct((vocab, rows), NARROW),
            jax.ShapeDtypeStruct((tiles, lines, tile), FLOAT),
        ],
        compiler_params=pltpu.CompilerParams(vmem_limit_bytes=VMEM_LIMIT),
        cost_estimate=pl.CostEstimate(
            flops=2 * vocab * rows * width,
            bytes_accessed=vocab * (rows + width) * 2,
            transcendentals=vocab * rows,
        ),
    )(table, hidden, target.reshape(tiles, 1, tile))
    tops = stats[:, :blocks].transpose(1, 0, 2).reshape(blocks, rows)
    totals = stats[:, blocks : 2 * blocks].transpose(1, 0, 2).reshape(blocks, rows)
    hits = stats[:, 2 * blocks].reshape(rows)
    return exps, tops, totals, hits


def head_back(table, exps, scales, weights, target):
    vocab, width = table.shape
    rows = exps.shape[1]
    tile = 256
    blocks = scales.shape[0]
    block = vocab // blocks

    def kernel(table_ref, exps_ref, scale_ref, weight_ref, target_ref, back_ref):
        places = lax.broadcasted_iota(jnp.int32, (block, tile), 0)
        total = jnp.zeros((tile, width), FLOAT)
        for b in range(blocks):
            part = slice(b * block, (b + 1) * block)
            grads = exps_ref[part, :].astype(FLOAT) * scale_ref[0, b : b + 1, :]
            grads = jnp.where(
                places == target_ref[0] - b * block, grads - weight_ref[0], grads
            ).astype(NARROW)
            total = total + lax.dot_general(
                grads, table_ref[part, :], ROWS_CONTRACT, preferred_element_type=FLOAT
            )
        back_ref[...] = total

    tiles = rows // tile
    line = pl.BlockSpec((1, 1, tile), lambda i: (i, 0, 0))
    return pl.pallas_call(
        kernel,
        grid=(tiles,),
        in_specs=[
            pl.BlockSpec(memory_space=pltpu.VMEM),
            pl.BlockSpec((vocab, tile), lambda i: (0, i)),
            pl.BlockSpec((1, blocks, tile), lambda i: (i, 0, 0)),
            line,
            line,
        ],
        out_specs=pl.BlockSpec((tile, width), lambda i: (i, 0)),
        out_shape=jax.ShapeDtypeStruct((rows, width), FLOAT),
        compiler_params=pltpu.CompilerParams(vmem_limit_bytes=VMEM_LIMIT),
        cost_estimate=pl.CostEstimate(
            flops=2 * vocab * rows * width,
            bytes_accessed=vocab * (rows + width) * 2,
            transcendentals=0,
        ),
    )(
        table,
        exps,
        scales.reshape(blocks, tiles, tile).transpose(1, 0, 2),
        weights.reshape(tiles, 1, tile),
        target.reshape(tiles, 1, tile),
    )


MESH = pl.DeviceIdType.MESH


def meet(peers):
    barrier = pltpu.get_barrier_semaphore()
    for peer in peers:
        pl.semaphore_signal(barrier, inc=1, device_id=peer, device_id_type=MESH)
    pl.semaphore_wait(barrier, len(peers))


class Place:
    def __init__(self, groups, replicas):
        self.groups = groups
        self.replicas = replicas
        self.chips = groups // 2
        self.replica = lax.axis_index("dp")
        self.member = lax.axis_index("fsdp")
        self.chip = self.member // 2
        self.core = self.member % 2
        self.sibling_member = self.chip * 2 + 1 - self.core

    def lane_chip(self, step):
        return lax.rem(self.chip + step, self.chips)

    def at(self, replica, member):
        return {"dp": replica, "fsdp": member}

    def lane(self, step):
        return self.at(self.replica, self.lane_chip(step) * 2 + self.core)

    def plane_replica(self, step):
        return lax.rem(self.replica + step, self.replicas)

    def plane(self, step):
        return self.at(self.plane_replica(step), self.member)

    def sibling(self):
        return self.at(self.replica, self.sibling_member)

    def lanes(self):
        return [self.lane(step) for step in range(1, self.chips)]

    def planes(self):
        return [self.plane(step) for step in range(1, self.replicas)]


def remote(source, target, send, recv, device):
    return pltpu.make_async_remote_copy(
        src_ref=source,
        dst_ref=target,
        send_sem=send,
        recv_sem=recv,
        device_id=device,
        device_id_type=MESH,
    )


def head_table_grad(table, hidden, logsum, weights, target, token_grad, groups, replicas):
    vocab, width = table.shape
    rows = hidden.shape[0]
    own = token_grad.shape[0]
    tile = math.gcd(rows, 2048)
    block = block_rows(vocab, 1100)
    tiles = rows // tile
    steps = vocab // block
    chips = groups // 2
    last = steps - 1
    when_plane, when_core = min(1, last), min(3, last)

    def kernel(
        table_ref,
        hidden_ref,
        logsum_ref,
        weight_ref,
        target_ref,
        own_ref,
        grad_ref,
        square_ref,
        all_ref,
        local_sem,
        lane_send,
        lane_recv,
        plane_send,
        plane_recv,
        core_send,
        core_recv,
    ):
        step = pl.program_id(0)
        place = Place(groups, replicas)
        me = place.replica * groups + place.member

        def slot(replica, member):
            return all_ref.at[replica * groups + member]

        def lane_copy(k):
            here = all_ref.at[me]
            return remote(own_ref, here, lane_send.at[k], lane_recv.at[k], place.lane(k))

        def lane_wait(k):
            back = lax.rem(place.chip + chips - k, chips) * 2 + place.core
            there = slot(place.replica, back)
            remote(there, there, lane_send.at[k], lane_recv.at[k], place.lane(k)).wait_recv()

        def plane_copy(k, c):
            here = slot(place.replica, c * 2 + place.core)
            return remote(here, here, plane_send.at[k, c], plane_recv.at[k, c], place.plane(k))

        def plane_wait(k, c):
            back = lax.rem(place.replica + replicas - k, replicas)
            there = slot(back, c * 2 + place.core)
            remote(
                there, there, plane_send.at[k, c], plane_recv.at[k, c], place.plane(k)
            ).wait_recv()

        def core_copy(r, c):
            here = slot(r, c * 2 + place.core)
            return remote(here, here, core_send.at[r, c], core_recv.at[r, c], place.sibling())

        def core_wait(r, c):
            there = slot(r, c * 2 + 1 - place.core)
            remote(
                there, there, core_send.at[r, c], core_recv.at[r, c], place.sibling()
            ).wait_recv()

        local = pltpu.make_async_copy(own_ref, all_ref.at[me], local_sem)

        @pl.when(step == 0)
        def _():
            meet(place.lanes() + place.planes() + [place.sibling()])
            local.start()
            for k in range(1, chips):
                lane_copy(k).start()

        @pl.when(step == when_plane)
        def _():
            local.wait()
            for k in range(1, chips):
                lane_wait(k)
            for c in range(chips):
                for k in range(1, replicas):
                    plane_copy(k, c).start()
                core_copy(place.replica, c).start()

        @pl.when(step == when_core)
        def _():
            for k in range(1, replicas):
                for c in range(chips):
                    plane_wait(k, c)
            for k in range(1, replicas):
                for c in range(chips):
                    core_copy(place.plane_replica(k), c).start()

        start = step * block
        part = table_ref[...].astype(NARROW)
        places = lax.broadcasted_iota(jnp.int32, (block, tile), 0)

        def lap(k, carry):
            here = hidden_ref[pl.ds(pl.multiple_of(k * tile, tile), tile), :]
            logits = lax.dot_general(part, here, LAST_CONTRACT, preferred_element_type=FLOAT)
            probs = jnp.exp(logits - logsum_ref[k])
            grads = jnp.where(
                places == target_ref[k] - start, probs - weight_ref[k], probs
            ).astype(NARROW)
            piece = jnp.dot(grads, here, preferred_element_type=FLOAT)

            @pl.when(k == 0)
            def _():
                grad_ref[...] = piece

            @pl.when(k > 0)
            def _():
                grad_ref[...] += piece

            return carry

        lax.fori_loop(0, tiles, lap, 0)
        squares = jnp.sum(jnp.square(grad_ref[...]), axis=0, keepdims=True)

        @pl.when(step == 0)
        def _():
            square_ref[...] = squares

        @pl.when(step > 0)
        def _():
            square_ref[...] += squares

        @pl.when(step == last)
        def _():
            for r in range(replicas):
                for c in range(chips):
                    core_wait(r, c)
            for k in range(1, chips):
                lane_copy(k).wait_send()
            for c in range(chips):
                for k in range(1, replicas):
                    plane_copy(k, c).wait_send()
                for r in range(replicas):
                    core_copy(r, c).wait_send()

    whole = pl.BlockSpec(memory_space=pltpu.VMEM)
    anywhere = pl.BlockSpec(memory_space=pl.ANY)
    shape = (tiles, 1, tile)
    dma = pltpu.SemaphoreType.DMA
    return pl.pallas_call(
        kernel,
        grid=(steps,),
        in_specs=[pl.BlockSpec((block, width), lambda i: (i, 0))] + [whole] * 4 + [anywhere],
        out_specs=[
            pl.BlockSpec((block, width), lambda i: (i, 0)),
            pl.BlockSpec((1, width), lambda i: (0, 0)),
            anywhere,
        ],
        out_shape=[
            jax.ShapeDtypeStruct((vocab, width), FLOAT),
            jax.ShapeDtypeStruct((1, width), FLOAT),
            jax.ShapeDtypeStruct((groups * replicas, own, width), NARROW),
        ],
        scratch_shapes=[
            dma,
            dma((chips,)),
            dma((chips,)),
            dma((replicas, chips)),
            dma((replicas, chips)),
            dma((replicas, chips)),
            dma((replicas, chips)),
        ],
        compiler_params=pltpu.CompilerParams(
            vmem_limit_bytes=VMEM_LIMIT, collective_id=1, has_side_effects=True
        ),
        cost_estimate=pl.CostEstimate(
            flops=4 * vocab * rows * width,
            bytes_accessed=vocab * width * 8 + rows * width * 4,
            transcendentals=vocab * rows,
        ),
    )(
        table,
        hidden,
        logsum.reshape(shape),
        weights.reshape(shape),
        target.reshape(shape),
        token_grad,
    )


def exchange_scalars(line, groups, replicas):
    amount = groups * replicas

    def kernel(own_ref, all_ref, local_sem, send_sem, recv_sem):
        place = Place(groups, replicas)
        me = place.replica * groups + place.member

        def device(index):
            return place.at(index // groups, lax.rem(index, groups))

        barrier = pltpu.get_barrier_semaphore()

        def greet(k, carry):
            pl.semaphore_signal(
                barrier, inc=1, device_id=device(lax.rem(me + k, amount)), device_id_type=MESH
            )
            return carry

        def copy(k):
            return remote(
                own_ref,
                all_ref.at[me],
                send_sem.at[k],
                recv_sem.at[k],
                device(lax.rem(me + k, amount)),
            )

        def begin(k, carry):
            copy(k).start()
            return carry

        def finish(k, carry):
            there = all_ref.at[lax.rem(me + amount - k, amount)]
            remote(there, there, send_sem.at[k], recv_sem.at[k], device(me)).wait_recv()
            copy(k).wait_send()
            return carry

        lax.fori_loop(1, amount, greet, 0)
        local = pltpu.make_async_copy(own_ref, all_ref.at[me], local_sem)
        local.start()
        pl.semaphore_wait(barrier, amount - 1)
        lax.fori_loop(1, amount, begin, 0)
        local.wait()
        lax.fori_loop(1, amount, finish, 0)

    whole = pl.BlockSpec(memory_space=pltpu.VMEM)
    dma = pltpu.SemaphoreType.DMA
    return pl.pallas_call(
        kernel,
        in_specs=[whole],
        out_specs=whole,
        out_shape=jax.ShapeDtypeStruct((amount,) + line.shape, line.dtype),
        scratch_shapes=[dma, dma((amount,)), dma((amount,))],
        compiler_params=pltpu.CompilerParams(collective_id=2, has_side_effects=True),
    )(line)


def chunk_lists(local, inside, chunk):
    chunks = local.shape[0] // chunk
    flags = inside.reshape(chunks, chunk)
    spots = jnp.arange(chunk, dtype=jnp.int32)
    ahead = (spots[:, None] < spots[None, :]).astype(NARROW)
    order = jnp.dot(flags.astype(NARROW), ahead, preferred_element_type=FLOAT).astype(jnp.int32)
    chosen = (order[:, None, :] == spots[None, :, None]) & flags[:, None, :]
    places = jnp.sum(jnp.where(chosen, spots[None, None, :], 0), axis=2)
    rows = jnp.sum(jnp.where(chosen, local.reshape(chunks, 1, chunk), 0), axis=2)
    return places, rows, jnp.sum(flags.astype(jnp.int32), axis=1)


def embed_table_grad(token_grads, places, rows, counts, vocab):
    chunks, chunk = places.shape
    width = token_grads.shape[-1]
    padded = vocab + 8
    unroll = 4

    def kernel(
        count_ref, place_ref, row_ref, tokens_ref, grad_ref, square_ref, wide_ref, total_ref, sem
    ):
        step = pl.program_id(0)

        @pl.when(step == 0)
        def _():
            total_ref[...] = jnp.zeros_like(total_ref)

        wide_ref[...] = tokens_ref[...].astype(FLOAT)
        amount = count_ref[step]

        def lap(j, carry):
            for u in range(unroll):
                spot = j * unroll + u
                row = jnp.where(spot < amount, row_ref[0, 0, spot], vocab)
                place = place_ref[0, 0, spot]
                total_ref[pl.ds(row, 1), :] += wide_ref[pl.ds(place, 1), :]
            return carry

        lax.fori_loop(0, (amount + unroll - 1) // unroll, lap, 0)

        @pl.when(step == chunks - 1)
        def _():
            out = pltpu.make_async_copy(total_ref.at[pl.ds(0, vocab), :], grad_ref, sem)
            out.start()
            square_ref[...] = jnp.sum(
                jnp.square(total_ref[pl.ds(0, vocab), :]), axis=0, keepdims=True
            )
            out.wait()

    line = pl.BlockSpec((1, 1, chunk), lambda i, c: (i, 0, 0), memory_space=pltpu.SMEM)
    return pl.pallas_call(
        kernel,
        grid_spec=pltpu.PrefetchScalarGridSpec(
            num_scalar_prefetch=1,
            grid=(chunks,),
            in_specs=[line, line, pl.BlockSpec((chunk, width), lambda i, c: (i, 0))],
            out_specs=[
                pl.BlockSpec(memory_space=pl.ANY),
                pl.BlockSpec((1, width), lambda i, c: (0, 0)),
            ],
            scratch_shapes=[
                pltpu.VMEM((chunk, width), FLOAT),
                pltpu.VMEM((padded, width), FLOAT),
                pltpu.SemaphoreType.DMA,
            ],
        ),
        out_shape=[
            jax.ShapeDtypeStruct((vocab, width), FLOAT),
            jax.ShapeDtypeStruct((1, width), FLOAT),
        ],
        compiler_params=pltpu.CompilerParams(vmem_limit_bytes=VMEM_LIMIT),
    )(
        counts,
        places.reshape(chunks, 1, chunk),
        rows.reshape(chunks, 1, chunk),
        token_grads.reshape(chunks * chunk, width),
    )


def update_rule(weight, grad, moment, average, rate, clip_factor):
    clipped = clip_factor * grad
    new_moment = MOMENTUM * moment + clipped
    new_weight = weight - rate * (clipped + MOMENTUM * new_moment)
    new_average = DECAY * average + (1.0 - DECAY) * new_weight
    return (new_weight, new_moment, new_average)


def table_update(table, grad, moment_low, moment, average, rate, clip):
    vocab, width = table.shape
    sub = moment.shape[0]
    block = block_rows(vocab, 1100)

    def whole_kernel(clip_ref, table_ref, grad_ref, moment_ref, new_ref):
        new_ref[...], _, _ = update_rule(
            table_ref[...],
            grad_ref[...],
            moment_ref[...].astype(FLOAT),
            table_ref[...],
            rate,
            clip_ref[0],
        )

    spec = pl.BlockSpec((block, width), lambda i: (i, 0))
    scalar = pl.BlockSpec(memory_space=pltpu.SMEM)
    new_table = pl.pallas_call(
        whole_kernel,
        grid=(vocab // block,),
        in_specs=[scalar, spec, spec, spec],
        out_specs=spec,
        out_shape=jax.ShapeDtypeStruct((vocab, width), FLOAT),
        compiler_params=pltpu.CompilerParams(vmem_limit_bytes=VMEM_LIMIT),
    )(clip, table, grad, moment_low)

    window = max(-(-(sub + sub * r % 8) // 8) * 8 for r in range(vocab // sub))
    tile = 256

    def own_kernel(
        clip_ref, table_ref, grad_ref, moment_ref, average_ref, moment_out, average_out, *scratch
    ):
        table_win, grad_win, sems = scratch
        begin = lax.axis_index("dp") * sub
        low = pl.multiple_of(begin // 8 * 8, 8)
        shift = begin - low
        copies = [
            pltpu.make_async_copy(table_ref.at[pl.ds(low, window), :], table_win, sems.at[0]),
            pltpu.make_async_copy(grad_ref.at[pl.ds(low, window), :], grad_win, sems.at[1]),
        ]
        for copy in copies:
            copy.start()
        for copy in copies:
            copy.wait()
        for first in range(0, sub, tile):
            size = min(tile, sub - first)
            span = min(-(-size // 8) * 8 + 8, window - first)
            amount = jnp.where(shift == 0, 0, span - shift)
            own_table = pltpu.roll(table_win[first : first + span, :], amount, 0)[:size]
            own_grad = pltpu.roll(grad_win[first : first + span, :], amount, 0)[:size]
            _, new_moment, new_average = update_rule(
                own_table,
                own_grad,
                moment_ref[first : first + size, :],
                average_ref[first : first + size, :],
                rate,
                clip_ref[0],
            )
            moment_out[first : first + size, :] = new_moment
            average_out[first : first + size, :] = new_average

    anywhere = pl.BlockSpec(memory_space=pl.ANY)
    whole = pl.BlockSpec(memory_space=pltpu.VMEM)
    state = jax.ShapeDtypeStruct((sub, width), FLOAT)
    new_moment, new_average = pl.pallas_call(
        own_kernel,
        in_specs=[scalar, anywhere, anywhere, whole, whole],
        out_specs=[whole, whole],
        out_shape=[state, state],
        scratch_shapes=[
            pltpu.VMEM((window, width), FLOAT),
            pltpu.VMEM((window, width), FLOAT),
            pltpu.SemaphoreType.DMA((2,)),
        ],
        compiler_params=pltpu.CompilerParams(vmem_limit_bytes=VMEM_LIMIT),
    )(clip, table, grad, moment, average)
    return new_table, new_moment, new_average


def shards(
    token_ids,
    loss_mask,
    lengths,
    buffer_ids,
    embed_table,
    embed_moment,
    embed_average,
    head_table,
    head_moment,
    head_average,
    in_weights,
    in_moment,
    in_average,
    out_weights,
    out_moment,
    out_average,
    vectors,
    vector_moment,
    vector_average,
):
    groups = lax.axis_size("fsdp")
    replicas = lax.axis_size("dp")
    member = lax.axis_index("fsdp")
    replica = lax.axis_index("dp")
    batches, _, seq = token_ids.shape
    vocab_rows, width = embed_table.shape
    hidden = out_weights.shape[0] * groups - width
    head_size = width // HEADS
    rot = head_size // 4
    factor = 1.0 / math.sqrt(head_size)
    vocab_start = member * vocab_rows
    own_rows = batches * seq
    rows_all = groups * own_rows

    tokens, marks, buffers = token_ids[:, 0], loss_mask[:, 0], buffer_ids[:, 0]
    divisor, offset, counted = jax.vmap(functools.partial(slot_info, buffer_count=NSEG))(
        tokens, marks, lengths[:, 0], buffers
    )
    packed = jnp.concatenate(
        [tokens, divisor, jnp.broadcast_to(jnp.sum(counted), (1, seq))], axis=0
    )
    everyone = lax.all_gather(packed, ("dp", "fsdp"))
    in_full, out_full, vector_full = (
        lax.all_gather(in_weights.astype(NARROW), "fsdp", axis=0, tiled=True),
        lax.all_gather(out_weights.astype(NARROW), "fsdp", axis=0, tiled=True),
        lax.all_gather(vectors.astype(NARROW), "fsdp", axis=0, tiled=True),
    )
    embed_moment_low = lax.all_gather(embed_moment.astype(NARROW), "dp", axis=0, tiled=True)
    head_moment_low = lax.all_gather(head_moment.astype(NARROW), "dp", axis=0, tiled=True)
    tokens_all = everyone[:, :batches]
    count = jnp.maximum(jnp.sum(everyone[:, 2 * batches, 0]).astype(FLOAT), 1.0)
    divisor_all = everyone[:, batches : 2 * batches].astype(FLOAT)
    share_all = jnp.where(divisor_all > 0.5, 1.0 / jnp.maximum(divisor_all, 1.0), 0.0)
    weight_all = (share_all / count).reshape(-1)
    target_all = (
        jnp.concatenate([tokens_all[:, :, 1:], jnp.zeros_like(tokens_all[:, :, :1])], axis=2)
        .reshape(-1)
    ) - vocab_start
    tokens_flat = tokens_all.reshape(-1)
    local_all = tokens_flat - vocab_start
    inside_all = (local_all >= 0) & (local_all < vocab_rows)

    def group_part(values):
        return lax.dynamic_slice_in_dim(values, replica * rows_all, rows_all, 0)

    local_rows = group_part(local_all)
    inside = (local_rows >= 0) & (local_rows < vocab_rows)
    rows = jnp.take(embed_table, jnp.clip(local_rows, 0, vocab_rows - 1), axis=0)
    resid = lax.psum_scatter(
        jnp.where(inside[:, None], rows, 0.0).astype(NARROW),
        "fsdp",
        scatter_dimension=0,
        tiled=True,
    ).astype(FLOAT)
    parts = vector_parts(vector_full.astype(FLOAT), width, hidden)
    places = jnp.arange(seq, dtype=jnp.int32)
    allowed = (buffers[:, :, None] == buffers[:, None, :]) & (
        places[None, None, :] <= places[None, :, None]
    )
    cosine, sine = rotary_tables(offset.reshape(-1), rot)
    layer_out, kept = layer_forward(resid, in_full, out_full, parts, allowed, cosine, sine, factor)
    unit_last, scale_last = norm_unit(layer_out)
    final = (unit_last * parts[4] + parts[5]).astype(NARROW)
    group_hidden = lax.all_gather(final, "fsdp", axis=0, tiled=True)
    all_hidden = lax.all_gather(group_hidden, "dp", axis=0, tiled=True)

    head_low = head_table.astype(NARROW)
    target = group_part(target_all)
    weight = group_part(weight_all)
    exps, tops, totals, hits = head_forward(head_low, group_hidden, target)
    top = jnp.max(tops, axis=0)
    total = jnp.sum(totals * jnp.exp(tops - top), axis=0)
    stats = lax.all_gather(jnp.stack([top, total, hits]), "fsdp")
    top_all = jnp.max(stats[:, 0], axis=0)
    logsum = top_all + jnp.log(jnp.sum(stats[:, 1] * jnp.exp(stats[:, 0] - top_all), axis=0))
    logsum_all = lax.all_gather(logsum, "dp", axis=0, tiled=True)
    own = member * own_rows
    loss_part = jnp.sum(
        lax.dynamic_slice_in_dim(
            weight * (logsum - jnp.sum(stats[:, 2], axis=0)), own, own_rows
        )
    )
    scales = weight * jnp.exp(tops - logsum)
    back = head_back(head_low, exps, scales, weight, target)
    final_grad = lax.psum_scatter(back, "fsdp", scatter_dimension=0, tiled=True)

    less_weight = logsum_all - jnp.log(jnp.maximum(weight_all, 1e-30))
    shifted = jnp.where(weight_all > 0.0, less_weight, 1e30)
    chunk = min(512, rows_all)
    lists = chunk_lists(local_all, inside_all, chunk)

    layer_grad = norm_back(final_grad * parts[4], unit_last, scale_last)
    resid_grad, in_grad, out_grad, small = layer_backward(
        layer_grad, in_full, out_full, parts, kept, allowed, cosine, sine, factor
    )
    vector_grad = jnp.concatenate(
        [
            small[0],
            small[1],
            small[2],
            small[3],
            jnp.sum(final_grad * unit_last, axis=0),
            jnp.sum(final_grad, axis=0),
            small[4],
            small[5],
            small[6],
            small[7],
        ]
    )
    token_grad, in_grad, out_grad, vector_grad, embed_moment_low, head_moment_low, lists = (
        lax.optimization_barrier(
            (
                resid_grad.astype(NARROW),
                in_grad,
                out_grad,
                vector_grad,
                embed_moment_low,
                head_moment_low,
                lists,
            )
        )
    )
    layer_grads = [
        lax.psum(lax.psum_scatter(grad, "fsdp", scatter_dimension=0, tiled=True), "dp")
        for grad in (in_grad, out_grad, vector_grad)
    ]
    head_grad, head_square, token_grads = head_table_grad(
        head_table, all_hidden, shifted, weight_all, target_all, token_grad, groups, replicas
    )
    embed_grad, embed_square = embed_table_grad(token_grads, *lists, vocab_rows)
    square = jnp.sum(embed_square) + jnp.sum(head_square)
    for grad in layer_grads:
        square = square + jnp.sum(grad * grad)
    line = jnp.stack([loss_part, square / replicas])[:, None]
    line = jnp.pad(jnp.broadcast_to(line, (2, 128)), ((0, 6), (0, 0)))
    pair = jnp.sum(exchange_scalars(line, groups, replicas)[:, :2, 0], axis=0)
    loss = pair[0]
    grad_norm = jnp.sqrt(pair[1])
    clip_factor = CLIP_LEVEL / jnp.maximum(grad_norm, CLIP_LEVEL)
    clip = clip_factor.reshape(1)
    base = math.sqrt(NPARAM) / CLIP_LEVEL
    root = math.sqrt(width)
    embed = table_update(
        embed_table, embed_grad, embed_moment_low, embed_moment, embed_average, base, clip
    )
    head = table_update(
        head_table, head_grad, head_moment_low, head_moment, head_average, base / root, clip
    )
    inner = update_rule(
        in_weights, layer_grads[0], in_moment, in_average, base / root, clip_factor
    )
    outer = update_rule(
        out_weights, layer_grads[1], out_moment, out_average, base / root, clip_factor
    )
    vector = update_rule(
        vectors, layer_grads[2], vector_moment, vector_average, 0.3 * base, clip_factor
    )
    return (*embed, *head, *inner, *outer, *vector, loss, grad_norm)


def solution(mesh):
    placed = (
        P(None, ("dp", "fsdp"), None),
        P(None, ("dp", "fsdp"), None),
        P(None, ("dp", "fsdp")),
        P(None, ("dp", "fsdp"), None),
        P("fsdp", None),
        P(("fsdp", "dp"), None),
        P(("fsdp", "dp"), None),
        P("fsdp", None),
        P(("fsdp", "dp"), None),
        P(("fsdp", "dp"), None),
        P("fsdp", None),
        P("fsdp", None),
        P("fsdp", None),
        P("fsdp", None),
        P("fsdp", None),
        P("fsdp", None),
        P("fsdp"),
        P("fsdp"),
        P("fsdp"),
    )
    return jax.shard_map(
        shards,
        mesh=mesh,
        in_specs=placed,
        out_specs=(
            P("fsdp", None),
            P(("fsdp", "dp"), None),
            P(("fsdp", "dp"), None),
            P("fsdp", None),
            P(("fsdp", "dp"), None),
            P(("fsdp", "dp"), None),
            P("fsdp", None),
            P("fsdp", None),
            P("fsdp", None),
            P("fsdp", None),
            P("fsdp", None),
            P("fsdp", None),
            P("fsdp"),
            P("fsdp"),
            P("fsdp"),
            P(),
            P(),
        ),
        check_vma=False,
    )
```

```python
import functools
import math

import jax
import jax.numpy as jnp
from jax import lax
from jax.experimental import pallas as pl
from jax.experimental.pallas import tpu as pltpu
from jax.sharding import PartitionSpec as P

HEADS = 8
NPARAM = 54664704
NSEG = 3


EPSILON = 1e-05
CLIP_LEVEL = 0.002
MOMENTUM = 0.5
DECAY = 0.5
NARROW = jnp.bfloat16
FLOAT = jnp.float32
ROWS_CONTRACT = (((0,), (0,)), ((), ()))
LAST_CONTRACT = (((1,), (1,)), ((), ()))


VMEM_LIMIT = 60 * 2**20


def slot_info(tokens, marks, length, buffers, buffer_count):
    seq = tokens.shape[0]
    places = jnp.arange(seq, dtype=jnp.int32)
    same_buffer = jnp.concatenate([buffers[1:] == buffers[:-1], jnp.zeros((1,), dtype=bool)])
    valid = jnp.where((marks == 1) & (places + 1 < length) & same_buffer, 1.0, 0.0).astype(FLOAT)
    member = buffers[None, :] == jnp.arange(buffer_count, dtype=jnp.int32)[:, None]
    weights = jnp.where(member, 1.0, 0.0).astype(FLOAT)
    tally = jnp.sum(weights * valid[None, :], axis=1)
    divisor = valid * jnp.sum(weights * tally[:, None], axis=0)
    counted = jnp.sum(jnp.where(tally > 0.5, 1.0, 0.0).astype(FLOAT))
    first = jnp.min(jnp.where(member, places[None, :], seq), axis=1)
    offset = places - jnp.sum(jnp.where(member, first[:, None], 0), axis=0)
    return (divisor.astype(jnp.int32), offset, counted.astype(jnp.int32))


def vector_parts(vectors, width, hidden):
    amounts = [width] * 6 + [3 * width, width, hidden, width]
    parts = []
    begin = 0
    for amount in amounts:
        parts.append(vectors[begin : begin + amount])
        begin = begin + amount
    return parts


def rotary_tables(offset, rot):
    half = rot // 2
    freqs = jnp.power(10000.0, -2.0 * jnp.arange(half, dtype=FLOAT) / rot)
    angles = offset.astype(FLOAT)[:, None] * freqs[None, :]
    return (jnp.cos(angles)[:, None, :], jnp.sin(angles)[:, None, :])


def rotate(values, cosine, sine, rot):
    half = rot // 2
    first = values[..., :half]
    second = values[..., half:rot]
    return jnp.concatenate(
        [first * cosine - second * sine, second * cosine + first * sine, values[..., rot:]], axis=-1
    )


def rotate_back(grads, cosine, sine, rot):
    half = rot // 2
    first = grads[..., :half]
    second = grads[..., half:rot]
    return jnp.concatenate(
        [first * cosine + second * sine, second * cosine - first * sine, grads[..., rot:]], axis=-1
    )


def norm_unit(values):
    mean = jnp.mean(values, axis=-1, keepdims=True)
    centred = values - mean
    scale = lax.rsqrt(jnp.mean(centred * centred, axis=-1, keepdims=True) + EPSILON)
    return (centred * scale, scale)


def norm_back(scaled, unit, scale):
    return scale * (
        scaled
        - jnp.mean(scaled, axis=-1, keepdims=True)
        - unit * jnp.mean(scaled * unit, axis=-1, keepdims=True)
    )


def gelu_slope(values):
    return (
        0.5 * (1.0 + lax.erf(values * 0.7071067811865476))
        + values * jnp.exp(-0.5 * values * values) * 0.3989422804014327
    )


def attention_scores(queries, keys, allowed, factor):
    scores = jnp.einsum("bqhd,bkhd->bhqk", queries, keys, preferred_element_type=FLOAT) * factor
    return jnp.where(allowed[:, None, :, :], scores, -1e30)


def layer_forward(resid, in_full, out_full, parts, allowed, cosine, sine, factor):
    rows, width = resid.shape
    batches = allowed.shape[0]
    seq = rows // batches
    head_size = width // HEADS
    rot = head_size // 4
    unit, scale = norm_unit(resid)
    input_one = (unit * parts[0] + parts[1]).astype(NARROW)
    input_two = (unit * parts[2] + parts[3]).astype(NARROW)
    triple = (
        jnp.dot(input_one, in_full[:, : 3 * width], preferred_element_type=FLOAT) + parts[6]
    ).reshape(rows, 3, HEADS, head_size)
    shape = (batches, seq, HEADS, head_size)
    queries = rotate(triple[:, 0], cosine, sine, rot).astype(NARROW).reshape(shape)
    keys = rotate(triple[:, 1], cosine, sine, rot).astype(NARROW).reshape(shape)
    values = triple[:, 2].astype(NARROW).reshape(shape)
    scores = attention_scores(queries, keys, allowed, factor)
    top = jnp.max(scores, axis=-1, keepdims=True)
    logsum = top + jnp.log(jnp.sum(jnp.exp(scores - top), axis=-1, keepdims=True))
    probs = jnp.exp(scores - logsum).astype(NARROW)
    mixed = (
        jnp.einsum("bhqk,bkhd->bqhd", probs, values, preferred_element_type=FLOAT)
        .astype(NARROW)
        .reshape(rows, width)
    )
    pre_act = jnp.dot(input_two, in_full[:, 3 * width :], preferred_element_type=FLOAT) + parts[8]
    activated = jax.nn.gelu(pre_act, approximate=False).astype(NARROW)
    joined = jnp.concatenate([mixed, activated], axis=1)
    result = resid + jnp.dot(joined, out_full, preferred_element_type=FLOAT) + parts[7] + parts[9]
    kept = (input_one, input_two, unit, scale, queries, keys, values, logsum, pre_act, joined)
    return (result, kept)


def layer_backward(grad_out, in_full, out_full, parts, kept, allowed, cosine, sine, factor):
    input_one, input_two, unit, scale, queries, keys, values, logsum, pre_act, joined = kept
    rows, width = grad_out.shape
    batches = allowed.shape[0]
    head_size = width // HEADS
    rot = head_size // 4
    grad_low = grad_out.astype(NARROW)
    out_grad = lax.dot_general(joined, grad_low, ROWS_CONTRACT, preferred_element_type=FLOAT)
    joined_grad = lax.dot_general(grad_low, out_full, LAST_CONTRACT, preferred_element_type=FLOAT)
    mixed_grad = joined_grad[:, :width].astype(NARROW).reshape(batches, -1, HEADS, head_size)
    pre_grad = joined_grad[:, width:] * gelu_slope(pre_act)
    pre_low = pre_grad.astype(NARROW)
    probs = jnp.exp(attention_scores(queries, keys, allowed, factor) - logsum)
    prob_grad = jnp.einsum("bqhd,bkhd->bhqk", mixed_grad, values, preferred_element_type=FLOAT)
    value_grad = jnp.einsum(
        "bhqk,bqhd->bkhd", probs.astype(NARROW), mixed_grad, preferred_element_type=FLOAT
    )
    score_grad = (
        probs * (prob_grad - jnp.sum(probs * prob_grad, axis=-1, keepdims=True)) * factor
    ).astype(NARROW)
    flat = (rows, HEADS, head_size)
    query_grad = rotate_back(
        jnp.einsum("bhqk,bkhd->bqhd", score_grad, keys, preferred_element_type=FLOAT).reshape(flat),
        cosine,
        sine,
        rot,
    )
    key_grad = rotate_back(
        jnp.einsum("bhqk,bqhd->bkhd", score_grad, queries, preferred_element_type=FLOAT).reshape(
            flat
        ),
        cosine,
        sine,
        rot,
    )
    qkv_grad = jnp.stack([query_grad, key_grad, value_grad.reshape(flat)], axis=1).reshape(
        rows, 3 * width
    )
    qkv_low = qkv_grad.astype(NARROW)
    in_grad = jnp.concatenate(
        [
            lax.dot_general(input_one, qkv_low, ROWS_CONTRACT, preferred_element_type=FLOAT),
            lax.dot_general(input_two, pre_low, ROWS_CONTRACT, preferred_element_type=FLOAT),
        ],
        axis=1,
    )
    back_one = lax.dot_general(
        qkv_low, in_full[:, : 3 * width], LAST_CONTRACT, preferred_element_type=FLOAT
    )
    back_two = lax.dot_general(
        pre_low, in_full[:, 3 * width :], LAST_CONTRACT, preferred_element_type=FLOAT
    )
    resid_grad = grad_out + norm_back(back_one * parts[0] + back_two * parts[2], unit, scale)
    residual_bias = jnp.sum(grad_out, axis=0)
    small = (
        jnp.sum(back_one * unit, axis=0),
        jnp.sum(back_one, axis=0),
        jnp.sum(back_two * unit, axis=0),
        jnp.sum(back_two, axis=0),
        jnp.sum(qkv_grad, axis=0),
        residual_bias,
        jnp.sum(pre_grad, axis=0),
        residual_bias,
    )
    return (resid_grad, in_grad, out_grad, small)


def block_rows(rows, cap):
    best = rows
    for size in range(8, cap + 1, 8):
        if rows % size == 0:
            best = size
    return best


MESH = pl.DeviceIdType.MESH


def meet(peers):
    barrier = pltpu.get_barrier_semaphore()
    for peer in peers:
        pl.semaphore_signal(barrier, inc=1, device_id=peer, device_id_type=MESH)
    pl.semaphore_wait(barrier, len(peers))


class Place:
    def __init__(self, groups, replicas):
        self.groups = groups
        self.replicas = replicas
        self.chips = groups // 2
        self.replica = lax.axis_index("dp")
        self.member = lax.axis_index("fsdp")
        self.chip = self.member // 2
        self.core = self.member % 2
        self.sibling_member = self.chip * 2 + 1 - self.core

    def lane_chip(self, step):
        return lax.rem(self.chip + step, self.chips)

    def at(self, replica, member):
        return {"dp": replica, "fsdp": member}

    def lane(self, step):
        return self.at(self.replica, self.lane_chip(step) * 2 + self.core)

    def plane_replica(self, step):
        return lax.rem(self.replica + step, self.replicas)

    def plane(self, step):
        return self.at(self.plane_replica(step), self.member)

    def sibling(self):
        return self.at(self.replica, self.sibling_member)

    def lanes(self):
        return [self.lane(step) for step in range(1, self.chips)]

    def planes(self):
        return [self.plane(step) for step in range(1, self.replicas)]


def remote(source, target, send, recv, device):
    return pltpu.make_async_remote_copy(
        src_ref=source,
        dst_ref=target,
        send_sem=send,
        recv_sem=recv,
        device_id=device,
        device_id_type=MESH,
    )


def start_kernel(packed, line, in_shard, out_shard, table, batches, groups, replicas):
    vocab, width = table.shape
    seq = packed.shape[1]
    own = batches * seq
    chips = groups // 2
    amount = groups * replicas
    shards_in = (in_shard, out_shard)
    split = all(shard.shape[0] % (16 * replicas) == 0 for shard in shards_in)
    pieces = replicas if split else 1
    unroll = 8

    def kernel(
        packed_ref,
        line_ref,
        in_ref,
        out_ref,
        table_ref,
        every_ref,
        lines_ref,
        in_full,
        out_full,
        resid_ref,
        in_low,
        out_low,
        wide,
        looked,
        to_core,
        from_core,
        to_lane,
        from_lane,
        ids,
        table_sem,
        ids_sem,
        local_sem,
        meta_send,
        meta_recv,
        line_send,
        line_recv,
        lane_send,
        lane_recv,
        plane_send,
        plane_recv,
        core_send,
        core_recv,
        part_send,
        part_recv,
        sum_send,
        sum_recv,
    ):
        place = Place(groups, replicas)
        member = place.member
        core = place.core
        replica = place.replica
        me = replica * groups + member
        fulls = (in_full, out_full)
        lows = (in_low, out_low)

        def device(index):
            return place.at(index // groups, lax.rem(index, groups))

        def chip_at(j):
            return lax.rem(place.chip + j, chips)

        def chip_before(j):
            return lax.rem(place.chip + chips - j, chips)

        def replica_before(k):
            return lax.rem(replica + replicas - k, replicas)

        def lane_device(j):
            return place.at(replica, chip_at(j) * 2 + core)

        def plane_device(k):
            return place.at(lax.rem(replica + k, replicas), member)

        def meta_copy(k):
            return remote(
                packed_ref,
                every_ref.at[me],
                meta_send.at[k],
                meta_recv.at[k],
                device(lax.rem(me + k, amount)),
            )

        def line_copy(k):
            return remote(
                line_ref,
                lines_ref.at[member],
                line_send.at[k],
                line_recv.at[k],
                place.at(replica, lax.rem(member + k, groups)),
            )

        def piece(w, slot, from_replica):
            full = fulls[w]
            if not split:
                return full.at[slot]
            rows = full.shape[1] // pieces
            return full.at[slot, pl.ds(pl.multiple_of(from_replica * rows, 16), rows), :]

        def own_piece(w):
            low = lows[w]
            if not split:
                return low
            rows = low.shape[0] // pieces
            return low.at[pl.ds(pl.multiple_of(replica * rows, 16), rows), :]

        def lane_copy(w, j):
            return remote(
                own_piece(w),
                piece(w, member, replica),
                lane_send.at[w, j],
                lane_recv.at[w, j],
                lane_device(j),
            )

        def lane_wait(w, j):
            there = piece(w, chip_before(j) * 2 + core, replica)
            remote(
                there, there, lane_send.at[w, j], lane_recv.at[w, j], lane_device(j)
            ).wait_recv()

        def plane_copy(w, k, j):
            there = piece(w, chip_before(j) * 2 + core, replica)
            return remote(
                there, there, plane_send.at[w, k, j], plane_recv.at[w, k, j], plane_device(k)
            )

        def plane_wait(w, k, j):
            there = piece(w, chip_before(j) * 2 + core, replica_before(k))
            remote(
                there, there, plane_send.at[w, k, j], plane_recv.at[w, k, j], plane_device(k)
            ).wait_recv()

        def core_copy(w, j):
            here = fulls[w].at[chip_before(j) * 2 + core]
            return remote(here, here, core_send.at[w, j], core_recv.at[w, j], place.sibling())

        def own_core_copy(w):
            return remote(
                lows[w],
                fulls[w].at[member],
                core_send.at[w, 0],
                core_recv.at[w, 0],
                place.sibling(),
            )

        def core_wait(w, j):
            there = fulls[w].at[chip_before(j) * 2 + 1 - core]
            remote(
                there, there, core_send.at[w, j], core_recv.at[w, j], place.sibling()
            ).wait_recv()

        def part_copy(j):
            return remote(
                to_core.at[j], from_core.at[j], part_send.at[j], part_recv.at[j], place.sibling()
            )

        def sum_copy(j):
            return remote(
                to_lane.at[j], from_lane.at[j], sum_send.at[j], sum_recv.at[j], lane_device(j)
            )

        fetch = pltpu.make_async_copy(table_ref, wide, table_sem)
        fetch.start()
        barrier = pltpu.get_barrier_semaphore()

        def greet(k, carry):
            pl.semaphore_signal(
                barrier, inc=1, device_id=device(lax.rem(me + k, amount)), device_id_type=MESH
            )
            return carry

        lax.fori_loop(1, amount, greet, 0)
        in_low[...] = in_ref[...].astype(NARROW)
        out_low[...] = out_ref[...].astype(NARROW)
        every_ref[me] = packed_ref[...]
        lines_ref[member] = line_ref[...]
        pl.semaphore_wait(barrier, amount - 1)

        def tell(k, carry):
            meta_copy(k).start()
            return carry

        lax.fori_loop(1, amount, tell, 0)
        for k in range(1, groups):
            line_copy(k).start()
        for w in range(2):
            for j in range(1, chips):
                lane_copy(w, j).start()
            own_core_copy(w).start()
        kept = [
            pltpu.make_async_copy(lows[w], fulls[w].at[member], local_sem.at[w])
            for w in range(2)
        ]
        for copy in kept:
            copy.start()

        def hear(k, carry):
            there = every_ref.at[lax.rem(me + amount - k, amount)]
            remote(there, there, meta_send.at[k], meta_recv.at[k], device(me)).wait_recv()
            return carry

        lax.fori_loop(1, amount, hear, 0)
        load = pltpu.make_async_copy(
            every_ref.at[pl.ds(replica * groups, groups)], ids, ids_sem
        )
        load.start()
        load.wait()
        fetch.wait()
        start = member * vocab

        def look(slot):
            for b in range(batches):

                def lap(i, carry):
                    for u in range(unroll):
                        spot = i * unroll + u
                        row = ids[slot, b, spot] - start
                        inside = (row >= 0) & (row < vocab)
                        safe = jnp.where(inside, row, 0)
                        keep = jnp.where(inside, 1.0, 0.0)
                        looked[pl.ds(b * seq + spot, 1), :] = wide[pl.ds(safe, 1), :] * keep
                    return carry

                lax.fori_loop(0, seq // unroll, lap, 0)
            return looked[...].astype(NARROW)

        def lap(step, carry):
            j = lax.rem(step + 1, chips)
            there = chip_at(j) * 2
            to_core[j] = look(there + 1 - core)
            part_copy(j).start()
            mine = look(there + core).astype(FLOAT)
            part_copy(j).wait_recv()
            mine = mine + from_core[j].astype(FLOAT)

            @pl.when(j > 0)
            def _():
                to_lane[j] = mine.astype(NARROW)
                sum_copy(j).start()

            @pl.when(j == 0)
            def _():
                resid_ref[...] = mine

            return carry

        lax.fori_loop(0, chips, lap, 0)
        for w in range(2):
            for j in range(1, chips):
                lane_wait(w, j)
                if split:
                    for k in range(1, replicas):
                        plane_copy(w, k, j).start()
        for j in range(1, chips):
            sum_copy(j).wait_recv()
            resid_ref[...] += from_lane[j].astype(FLOAT)
        for w in range(2):
            for j in range(1, chips):
                if split:
                    for k in range(1, replicas):
                        plane_wait(w, k, j)
                core_copy(w, j).start()
        for w in range(2):
            kept[w].wait()
            for j in range(chips):
                core_wait(w, j)
                if j == 0:
                    own_core_copy(w).wait_send()
                else:
                    core_copy(w, j).wait_send()
                    lane_copy(w, j).wait_send()
                if split and j > 0:
                    for k in range(1, replicas):
                        plane_copy(w, k, j).wait_send()
        for k in range(1, groups):
            there = lines_ref.at[lax.rem(member + groups - k, groups)]
            remote(
                there, there, line_send.at[k], line_recv.at[k], place.at(replica, member)
            ).wait_recv()
            line_copy(k).wait_send()
        for j in range(chips):
            part_copy(j).wait_send()
            if j > 0:
                sum_copy(j).wait_send()

        def told(k, carry):
            meta_copy(k).wait_send()
            return carry

        lax.fori_loop(1, amount, told, 0)

    whole = pl.BlockSpec(memory_space=pltpu.VMEM)
    anywhere = pl.BlockSpec(memory_space=pl.ANY)
    dma = pltpu.SemaphoreType.DMA
    vmem = pltpu.VMEM
    every, lines, in_full, out_full, resid = pl.pallas_call(
        kernel,
        in_specs=[whole, whole, whole, whole, anywhere],
        out_specs=[whole, whole, anywhere, anywhere, whole],
        out_shape=[
            jax.ShapeDtypeStruct((amount,) + packed.shape, jnp.int32),
            jax.ShapeDtypeStruct((groups,) + line.shape, FLOAT),
            jax.ShapeDtypeStruct((groups,) + in_shard.shape, NARROW),
            jax.ShapeDtypeStruct((groups,) + out_shard.shape, NARROW),
            jax.ShapeDtypeStruct((own, width), FLOAT),
        ],
        scratch_shapes=[
            vmem(in_shard.shape, NARROW),
            vmem(out_shard.shape, NARROW),
            vmem((vocab, width), FLOAT),
            vmem((own, width), FLOAT),
            vmem((chips, own, width), NARROW),
            vmem((chips, own, width), NARROW),
            vmem((chips, own, width), NARROW),
            vmem((chips, own, width), NARROW),
            pltpu.SMEM((groups,) + packed.shape, jnp.int32),
            dma,
            dma,
            dma((2,)),
            dma((amount,)),
            dma((amount,)),
            dma((groups,)),
            dma((groups,)),
            dma((2, chips)),
            dma((2, chips)),
            dma((2, replicas, chips)),
            dma((2, replicas, chips)),
            dma((2, chips)),
            dma((2, chips)),
            dma((chips,)),
            dma((chips,)),
            dma((chips,)),
            dma((chips,)),
        ],
        compiler_params=pltpu.CompilerParams(
            vmem_limit_bytes=VMEM_LIMIT, collective_id=4, has_side_effects=True
        ),
        cost_estimate=pl.CostEstimate(
            flops=0, bytes_accessed=vocab * width * 4, transcendentals=0
        ),
    )(packed, line, in_shard, out_shard, table)
    return (
        every,
        lines,
        in_full.reshape(-1, in_shard.shape[1]),
        out_full.reshape(-1, out_shard.shape[1]),
        resid,
    )


def head_kernel(table, own_hidden, target, weight, groups, replicas):
    vocab, width = table.shape
    own = own_hidden.shape[0]
    block = block_rows(vocab, 1100)
    blocks = vocab // block
    chips = groups // 2
    lines = -(-blocks // 8) * 8

    def kernel(
        table_ref,
        own_ref,
        target_ref,
        weight_ref,
        grad_ref,
        logsum_ref,
        loss_ref,
        all_ref,
        wide,
        low,
        hid,
        exps,
        tops,
        totals,
        hits,
        shares,
        to_core,
        from_core,
        to_lane,
        from_lane,
        table_sem,
        local_sem,
        lane_send,
        lane_recv,
        core_send,
        core_recv,
        plane_send,
        plane_recv,
        pass_send,
        pass_recv,
        stat_send,
        stat_recv,
        line_send,
        line_recv,
        part_send,
        part_recv,
        sum_send,
        sum_recv,
    ):
        place = Place(groups, replicas)
        me = place.member
        core = place.core

        def table_copy(b):
            return pltpu.make_async_copy(
                table_ref.at[pl.ds(b * block, block), :], wide.at[b % 2], table_sem.at[b % 2]
            )

        def chip_at(j):
            return lax.rem(place.chip + j, chips)

        def chip_before(j):
            return lax.rem(place.chip + chips - j, chips)

        def lane_device(j):
            return place.at(place.replica, chip_at(j) * 2 + core)

        def plane_device(k):
            return place.at(lax.rem(place.replica + k, replicas), me)

        def replica_before(k):
            return lax.rem(place.replica + replicas - k, replicas)

        def lane_copy(j):
            return remote(own_ref, hid.at[me], lane_send.at[j], lane_recv.at[j], lane_device(j))

        def lane_slot(j):
            return chip_before(j) * 2 + core

        def lane_wait(j):
            there = hid.at[lane_slot(j)]
            remote(there, there, lane_send.at[j], lane_recv.at[j], lane_device(j)).wait_recv()

        def core_copy(j):
            here = hid.at[lane_slot(j)]
            return remote(here, here, core_send.at[j], core_recv.at[j], place.sibling())

        def core_wait(j):
            there = hid.at[chip_before(j) * 2 + 1 - core]
            remote(there, there, core_send.at[j], core_recv.at[j], place.sibling()).wait_recv()

        def plane_copy(k, j):
            slot = lane_slot(j)
            return remote(
                hid.at[slot],
                all_ref.at[place.replica * groups + slot],
                plane_send.at[k, j],
                plane_recv.at[k, j],
                plane_device(k),
            )

        def plane_wait(k, j):
            there = all_ref.at[replica_before(k) * groups + lane_slot(j)]
            remote(
                there, there, plane_send.at[k, j], plane_recv.at[k, j], plane_device(k)
            ).wait_recv()

        def pass_copy(k, j):
            here = all_ref.at[replica_before(k) * groups + lane_slot(j)]
            return remote(
                here, here, pass_send.at[k, j], pass_recv.at[k, j], place.sibling()
            )

        def pass_wait(k, j):
            there = all_ref.at[
                replica_before(k) * groups + chip_before(j) * 2 + 1 - core
            ]
            remote(
                there, there, pass_send.at[k, j], pass_recv.at[k, j], place.sibling()
            ).wait_recv()

        def member_at(k):
            return lax.rem(me + k, groups)

        def stat_copy(k):
            return remote(
                shares.at[me],
                shares.at[me],
                stat_send.at[k],
                stat_recv.at[k],
                place.at(place.replica, member_at(k)),
            )

        def stat_wait(k):
            there = shares.at[lax.rem(me + groups - k, groups)]
            remote(
                there, there, stat_send.at[k], stat_recv.at[k], place.at(place.replica, me)
            ).wait_recv()

        def line_copy(k):
            here = logsum_ref.at[place.replica]
            return remote(here, here, line_send.at[k], line_recv.at[k], plane_device(k))

        def line_wait(k):
            there = logsum_ref.at[replica_before(k)]
            remote(there, there, line_send.at[k], line_recv.at[k], plane_device(k)).wait_recv()

        def part_copy(j):
            return remote(
                to_core.at[j], from_core.at[j], part_send.at[j], part_recv.at[j], place.sibling()
            )

        def sum_copy(j):
            return remote(
                to_lane.at[j], from_lane.at[j], sum_send.at[j], sum_recv.at[j], lane_device(j)
            )

        table_copy(0).start()
        if blocks > 1:
            table_copy(1).start()
        meet(
            [place.at(place.replica, member_at(k)) for k in range(1, groups)] + place.planes()
        )
        own_core = remote(own_ref, hid.at[me], core_send.at[0], core_recv.at[0], place.sibling())
        own_core.start()
        for j in range(1, chips):
            lane_copy(j).start()
        hid[me] = own_ref[...]
        for k in range(1, replicas):
            plane_copy(k, 0).start()
        for b in range(blocks):
            table_copy(b).wait()
            low[b] = wide[b % 2].astype(NARROW)
            if b + 2 < blocks:
                table_copy(b + 2).start()

        spots = lax.broadcasted_iota(jnp.int32, (block, own), 0)

        def forward(step, carry):
            j = step // 2
            other = lax.rem(step, 2)

            @pl.when(step == 1)
            def _():
                there = hid.at[place.sibling_member]
                remote(
                    there, there, core_send.at[0], core_recv.at[0], place.sibling()
                ).wait_recv()

            @pl.when((step > 1) & (other == 0))
            def _():
                lane_wait(j)
                core_copy(j).start()

                def spread(k, carry):
                    plane_copy(k, j).start()
                    return carry

                lax.fori_loop(1, replicas, spread, 0)

            @pl.when((step > 1) & (other == 1))
            def _():
                core_wait(j)

            member = chip_before(j) * 2 + lax.rem(core + other, 2)
            here = hid[member]
            wanted = target_ref[member]
            hit = jnp.zeros((1, own), FLOAT)
            for b in range(blocks):
                logits = lax.dot_general(
                    low[b], here, LAST_CONTRACT, preferred_element_type=FLOAT
                )
                top = jnp.max(logits, axis=0, keepdims=True)
                values = jnp.exp(logits - top)
                tops[member, b : b + 1, :] = top
                totals[member, b : b + 1, :] = jnp.sum(values, axis=0, keepdims=True)
                hit = hit + jnp.sum(
                    jnp.where(spots == wanted - b * block, logits, 0.0), axis=0, keepdims=True
                )
                exps[b, member] = values.astype(NARROW)
            hits[pl.ds(member, 1), :] = hit
            block_tops = tops[member, :blocks, :]
            top = jnp.max(block_tops, axis=0, keepdims=True)
            total = jnp.sum(
                totals[member, :blocks, :] * jnp.exp(block_tops - top), axis=0, keepdims=True
            )
            shares[me, pl.ds(member, 1), :] = top + jnp.log(total)
            return carry

        lax.fori_loop(0, groups, forward, 0)
        local = pltpu.make_async_copy(
            hid, all_ref.at[pl.ds(place.replica * groups, groups)], local_sem
        )
        local.start()
        for k in range(1, groups):
            stat_copy(k).start()
        for k in range(1, groups):
            stat_wait(k)
        every = shares[...]
        top = jnp.max(every, axis=0)
        logsum_ref[place.replica] = top + jnp.log(jnp.sum(jnp.exp(every - top[None]), axis=0))
        for k in range(1, replicas):
            line_copy(k).start()

        def member_back(member):
            wanted = target_ref[member]
            weights = weight_ref[member]
            logsum = logsum_ref[place.replica, pl.ds(member, 1), :]
            total = jnp.zeros((own, width), FLOAT)
            for b in range(blocks):
                scale = weights * jnp.exp(tops[member, b : b + 1, :] - logsum)
                grads = exps[b, member].astype(FLOAT) * scale
                grads = jnp.where(spots == wanted - b * block, grads - weights, grads)
                total = total + lax.dot_general(
                    grads.astype(NARROW), low[b], ROWS_CONTRACT, preferred_element_type=FLOAT
                )
            return total

        def backward(step, carry):
            j = lax.rem(step + 1, chips)

            @pl.when(step == chips - 1)
            def _():
                for k in range(1, replicas):
                    for c in range(chips):
                        plane_wait(k, c)
                for k in range(1, replicas):
                    for c in range(chips):
                        pass_copy(k, c).start()

            there = chip_at(j) * 2
            to_core[j] = member_back(there + 1 - core)
            part_copy(j).start()
            mine = member_back(there + core)
            part_copy(j).wait_recv()
            mine = mine + from_core[j]

            @pl.when(j > 0)
            def _():
                to_lane[j] = mine
                sum_copy(j).start()

            @pl.when(j == 0)
            def _():
                grad_ref[...] = mine

            return carry

        lax.fori_loop(0, chips, backward, 0)
        held = lax.broadcasted_iota(jnp.int32, (groups, own), 0) == me
        amounts = jnp.concatenate([weight_ref[m] for m in range(groups)], axis=0)
        losses = amounts * (jnp.where(held, logsum_ref[place.replica], 0.0) - hits[...])
        loss_ref[...] = jnp.sum(losses, axis=0, keepdims=True)
        for j in range(1, chips):
            sum_copy(j).wait_recv()
            grad_ref[...] += from_lane[j]
        local.wait()
        own_core.wait_send()
        for k in range(1, groups):
            stat_copy(k).wait_send()
        for k in range(1, replicas):
            line_wait(k)
            line_copy(k).wait_send()
            for j in range(chips):
                pass_wait(k, j)
                plane_copy(k, j).wait_send()
                pass_copy(k, j).wait_send()
        for j in range(chips):
            part_copy(j).wait_send()
            if j > 0:
                lane_copy(j).wait_send()
                core_copy(j).wait_send()
                sum_copy(j).wait_send()

    whole = pl.BlockSpec(memory_space=pltpu.VMEM)
    anywhere = pl.BlockSpec(memory_space=pl.ANY)
    dma = pltpu.SemaphoreType.DMA
    vmem = pltpu.VMEM
    grad, logsum, loss, everyone = pl.pallas_call(
        kernel,
        in_specs=[anywhere, whole, whole, whole],
        out_specs=[whole, whole, whole, anywhere],
        out_shape=[
            jax.ShapeDtypeStruct((own, width), FLOAT),
            jax.ShapeDtypeStruct((replicas, groups, own), FLOAT),
            jax.ShapeDtypeStruct((1, own), FLOAT),
            jax.ShapeDtypeStruct((replicas * groups, own, width), NARROW),
        ],
        scratch_shapes=[
            vmem((2, block, width), FLOAT),
            vmem((blocks, block, width), NARROW),
            vmem((groups, own, width), NARROW),
            vmem((blocks, groups, block, own), NARROW),
            vmem((groups, lines, own), FLOAT),
            vmem((groups, lines, own), FLOAT),
            vmem((groups, own), FLOAT),
            vmem((groups, groups, own), FLOAT),
            vmem((chips, own, width), FLOAT),
            vmem((chips, own, width), FLOAT),
            vmem((chips, own, width), FLOAT),
            vmem((chips, own, width), FLOAT),
            dma((2,)),
            dma,
            dma((chips,)),
            dma((chips,)),
            dma((chips,)),
            dma((chips,)),
            dma((replicas, chips)),
            dma((replicas, chips)),
            dma((replicas, chips)),
            dma((replicas, chips)),
            dma((groups,)),
            dma((groups,)),
            dma((replicas,)),
            dma((replicas,)),
            dma((chips,)),
            dma((chips,)),
            dma((chips,)),
            dma((chips,)),
        ],
        compiler_params=pltpu.CompilerParams(
            vmem_limit_bytes=VMEM_LIMIT, collective_id=3, has_side_effects=True
        ),
        cost_estimate=pl.CostEstimate(
            flops=4 * vocab * groups * own * width,
            bytes_accessed=vocab * width * 4,
            transcendentals=vocab * groups * own,
        ),
    )(
        table,
        own_hidden,
        target.reshape(groups, 1, own),
        weight.reshape(groups, 1, own),
    )
    return grad, logsum.reshape(-1), jnp.sum(loss), everyone.reshape(-1, width)


def head_table_grad(
    table, hidden, logsum, weights, target, token_grad, slices, groups, replicas
):
    vocab, width = table.shape
    amount = groups * replicas
    rows = hidden.shape[0]
    own = token_grad.shape[0]
    tile = math.gcd(rows, 2048)
    block = block_rows(vocab, 1100)
    tiles = rows // tile
    steps = vocab // block
    chips = groups // 2
    last = steps - 1
    when_plane, when_core = min(1, last), min(3, last)

    def kernel(
        table_ref,
        hidden_ref,
        logsum_ref,
        weight_ref,
        target_ref,
        own_ref,
        slices_ref,
        grad_ref,
        square_ref,
        all_ref,
        summed_ref,
        gathered,
        local_sem,
        slice_send,
        slice_recv,
        lane_send,
        lane_recv,
        plane_send,
        plane_recv,
        core_send,
        core_recv,
    ):
        step = pl.program_id(0)
        place = Place(groups, replicas)
        me = place.replica * groups + place.member

        def slot(replica, member):
            return all_ref.at[replica * groups + member]

        def lane_copy(k):
            here = all_ref.at[me]
            return remote(own_ref, here, lane_send.at[k], lane_recv.at[k], place.lane(k))

        def lane_wait(k):
            back = lax.rem(place.chip + chips - k, chips) * 2 + place.core
            there = slot(place.replica, back)
            remote(there, there, lane_send.at[k], lane_recv.at[k], place.lane(k)).wait_recv()

        def plane_copy(k, c):
            here = slot(place.replica, c * 2 + place.core)
            return remote(here, here, plane_send.at[k, c], plane_recv.at[k, c], place.plane(k))

        def plane_wait(k, c):
            back = lax.rem(place.replica + replicas - k, replicas)
            there = slot(back, c * 2 + place.core)
            remote(
                there, there, plane_send.at[k, c], plane_recv.at[k, c], place.plane(k)
            ).wait_recv()

        def core_copy(r, c):
            here = slot(r, c * 2 + place.core)
            return remote(here, here, core_send.at[r, c], core_recv.at[r, c], place.sibling())

        def core_wait(r, c):
            there = slot(r, c * 2 + 1 - place.core)
            remote(
                there, there, core_send.at[r, c], core_recv.at[r, c], place.sibling()
            ).wait_recv()

        def device(index):
            return place.at(index // groups, lax.rem(index, groups))

        def slice_copy(k):
            there = lax.rem(me + k, amount)
            return remote(
                slices_ref.at[lax.rem(there, groups)],
                gathered.at[me],
                slice_send.at[k],
                slice_recv.at[k],
                device(there),
            )

        local = pltpu.make_async_copy(own_ref, all_ref.at[me], local_sem)

        @pl.when(step == 0)
        def _():
            barrier = pltpu.get_barrier_semaphore()

            def greet(k, carry):
                pl.semaphore_signal(
                    barrier,
                    inc=1,
                    device_id=device(lax.rem(me + k, amount)),
                    device_id_type=MESH,
                )
                return carry

            lax.fori_loop(1, amount, greet, 0)
            pl.semaphore_wait(barrier, amount - 1)
            local.start()
            for k in range(1, chips):
                lane_copy(k).start()

            def give(k, carry):
                slice_copy(k).start()
                return carry

            lax.fori_loop(1, amount, give, 0)
            gathered[me] = slices_ref[place.member]

        @pl.when(step == when_plane)
        def _():
            local.wait()
            for k in range(1, chips):
                lane_wait(k)
            for c in range(chips):
                for k in range(1, replicas):
                    plane_copy(k, c).start()
                core_copy(place.replica, c).start()

        @pl.when(step == when_core)
        def _():
            for k in range(1, replicas):
                for c in range(chips):
                    plane_wait(k, c)
            for k in range(1, replicas):
                for c in range(chips):
                    core_copy(place.plane_replica(k), c).start()

        start = step * block
        part = table_ref[...].astype(NARROW)
        places = lax.broadcasted_iota(jnp.int32, (block, tile), 0)

        def lap(k, carry):
            here = hidden_ref[pl.ds(pl.multiple_of(k * tile, tile), tile), :]
            logits = lax.dot_general(part, here, LAST_CONTRACT, preferred_element_type=FLOAT)
            probs = jnp.exp(logits - logsum_ref[k])
            grads = jnp.where(
                places == target_ref[k] - start, probs - weight_ref[k], probs
            ).astype(NARROW)
            piece = jnp.dot(grads, here, preferred_element_type=FLOAT)

            @pl.when(k == 0)
            def _():
                grad_ref[...] = piece

            @pl.when(k > 0)
            def _():
                grad_ref[...] += piece

            return carry

        lax.fori_loop(0, tiles, lap, 0)
        squares = jnp.sum(jnp.square(grad_ref[...]), axis=0, keepdims=True)

        @pl.when(step == 0)
        def _():
            square_ref[...] = squares

        @pl.when(step > 0)
        def _():
            square_ref[...] += squares

        @pl.when(step == last)
        def _():
            def take(k, carry):
                there = gathered.at[lax.rem(me + amount - k, amount)]
                remote(there, there, slice_send.at[k], slice_recv.at[k], device(me)).wait_recv()
                slice_copy(k).wait_send()
                return carry

            lax.fori_loop(1, amount, take, 0)
            summed_ref[...] = jnp.sum(gathered[...], axis=0)
            for r in range(replicas):
                for c in range(chips):
                    core_wait(r, c)
            for k in range(1, chips):
                lane_copy(k).wait_send()
            for c in range(chips):
                for k in range(1, replicas):
                    plane_copy(k, c).wait_send()
                for r in range(replicas):
                    core_copy(r, c).wait_send()

    whole = pl.BlockSpec(memory_space=pltpu.VMEM)
    anywhere = pl.BlockSpec(memory_space=pl.ANY)
    shape = (tiles, 1, tile)
    dma = pltpu.SemaphoreType.DMA
    return pl.pallas_call(
        kernel,
        grid=(steps,),
        in_specs=[pl.BlockSpec((block, width), lambda i: (i, 0))]
        + [whole] * 4
        + [anywhere, whole],
        out_specs=[
            pl.BlockSpec((block, width), lambda i: (i, 0)),
            pl.BlockSpec((1, width), lambda i: (0, 0)),
            anywhere,
            whole,
        ],
        out_shape=[
            jax.ShapeDtypeStruct((vocab, width), FLOAT),
            jax.ShapeDtypeStruct((1, width), FLOAT),
            jax.ShapeDtypeStruct((groups * replicas, own, width), NARROW),
            jax.ShapeDtypeStruct(slices.shape[1:], FLOAT),
        ],
        scratch_shapes=[
            pltpu.VMEM((amount,) + slices.shape[1:], FLOAT),
            dma,
            dma((amount,)),
            dma((amount,)),
            dma((chips,)),
            dma((chips,)),
            dma((replicas, chips)),
            dma((replicas, chips)),
            dma((replicas, chips)),
            dma((replicas, chips)),
        ],
        compiler_params=pltpu.CompilerParams(
            vmem_limit_bytes=VMEM_LIMIT, collective_id=1, has_side_effects=True
        ),
        cost_estimate=pl.CostEstimate(
            flops=4 * vocab * rows * width,
            bytes_accessed=vocab * width * 8 + rows * width * 4,
            transcendentals=vocab * rows,
        ),
    )(
        table,
        hidden,
        logsum.reshape(shape),
        weights.reshape(shape),
        target.reshape(shape),
        token_grad,
        slices,
    )


def exchange_scalars(line, groups, replicas):
    amount = groups * replicas

    def kernel(own_ref, all_ref, local_sem, send_sem, recv_sem):
        place = Place(groups, replicas)
        me = place.replica * groups + place.member

        def device(index):
            return place.at(index // groups, lax.rem(index, groups))

        barrier = pltpu.get_barrier_semaphore()

        def greet(k, carry):
            pl.semaphore_signal(
                barrier, inc=1, device_id=device(lax.rem(me + k, amount)), device_id_type=MESH
            )
            return carry

        def copy(k):
            return remote(
                own_ref,
                all_ref.at[me],
                send_sem.at[k],
                recv_sem.at[k],
                device(lax.rem(me + k, amount)),
            )

        def begin(k, carry):
            copy(k).start()
            return carry

        def finish(k, carry):
            there = all_ref.at[lax.rem(me + amount - k, amount)]
            remote(there, there, send_sem.at[k], recv_sem.at[k], device(me)).wait_recv()
            copy(k).wait_send()
            return carry

        lax.fori_loop(1, amount, greet, 0)
        local = pltpu.make_async_copy(own_ref, all_ref.at[me], local_sem)
        local.start()
        pl.semaphore_wait(barrier, amount - 1)
        lax.fori_loop(1, amount, begin, 0)
        local.wait()
        lax.fori_loop(1, amount, finish, 0)

    whole = pl.BlockSpec(memory_space=pltpu.VMEM)
    dma = pltpu.SemaphoreType.DMA
    return pl.pallas_call(
        kernel,
        in_specs=[whole],
        out_specs=whole,
        out_shape=jax.ShapeDtypeStruct((amount,) + line.shape, line.dtype),
        scratch_shapes=[dma, dma((amount,)), dma((amount,))],
        compiler_params=pltpu.CompilerParams(collective_id=2, has_side_effects=True),
    )(line)


def chunk_lists(local, inside, chunk):
    chunks = local.shape[0] // chunk
    flags = inside.reshape(chunks, chunk)
    spots = jnp.arange(chunk, dtype=jnp.int32)
    ahead = (spots[:, None] < spots[None, :]).astype(NARROW)
    order = jnp.dot(flags.astype(NARROW), ahead, preferred_element_type=FLOAT).astype(jnp.int32)
    chosen = (order[:, None, :] == spots[None, :, None]) & flags[:, None, :]
    places = jnp.sum(jnp.where(chosen, spots[None, None, :], 0), axis=2)
    rows = jnp.sum(jnp.where(chosen, local.reshape(chunks, 1, chunk), 0), axis=2)
    return places, rows, jnp.sum(flags.astype(jnp.int32), axis=1)


def embed_table_grad(token_grads, places, rows, counts, vocab):
    chunks, chunk = places.shape
    width = token_grads.shape[-1]
    padded = vocab + 8
    unroll = 4

    def kernel(
        count_ref, place_ref, row_ref, tokens_ref, grad_ref, square_ref, wide_ref, total_ref, sem
    ):
        step = pl.program_id(0)

        @pl.when(step == 0)
        def _():
            total_ref[...] = jnp.zeros_like(total_ref)

        wide_ref[...] = tokens_ref[...].astype(FLOAT)
        amount = count_ref[step]

        def lap(j, carry):
            for u in range(unroll):
                spot = j * unroll + u
                row = jnp.where(spot < amount, row_ref[0, 0, spot], vocab)
                place = place_ref[0, 0, spot]
                total_ref[pl.ds(row, 1), :] += wide_ref[pl.ds(place, 1), :]
            return carry

        lax.fori_loop(0, (amount + unroll - 1) // unroll, lap, 0)

        @pl.when(step == chunks - 1)
        def _():
            out = pltpu.make_async_copy(total_ref.at[pl.ds(0, vocab), :], grad_ref, sem)
            out.start()
            square_ref[...] = jnp.sum(
                jnp.square(total_ref[pl.ds(0, vocab), :]), axis=0, keepdims=True
            )
            out.wait()

    line = pl.BlockSpec((1, 1, chunk), lambda i, c: (i, 0, 0), memory_space=pltpu.SMEM)
    return pl.pallas_call(
        kernel,
        grid_spec=pltpu.PrefetchScalarGridSpec(
            num_scalar_prefetch=1,
            grid=(chunks,),
            in_specs=[line, line, pl.BlockSpec((chunk, width), lambda i, c: (i, 0))],
            out_specs=[
                pl.BlockSpec(memory_space=pl.ANY),
                pl.BlockSpec((1, width), lambda i, c: (0, 0)),
            ],
            scratch_shapes=[
                pltpu.VMEM((chunk, width), FLOAT),
                pltpu.VMEM((padded, width), FLOAT),
                pltpu.SemaphoreType.DMA,
            ],
        ),
        out_shape=[
            jax.ShapeDtypeStruct((vocab, width), FLOAT),
            jax.ShapeDtypeStruct((1, width), FLOAT),
        ],
        compiler_params=pltpu.CompilerParams(vmem_limit_bytes=VMEM_LIMIT),
    )(
        counts,
        places.reshape(chunks, 1, chunk),
        rows.reshape(chunks, 1, chunk),
        token_grads.reshape(chunks * chunk, width),
    )


def update_rule(weight, grad, moment, average, rate, clip_factor):
    clipped = clip_factor * grad
    new_moment = MOMENTUM * moment + clipped
    new_weight = weight - rate * (clipped + MOMENTUM * new_moment)
    new_average = DECAY * average + (1.0 - DECAY) * new_weight
    return (new_weight, new_moment, new_average)


def table_update(table, grad, moment_low, moment, average, rate, clip):
    vocab, width = table.shape
    sub = moment.shape[0]
    block = 512

    def whole_kernel(clip_ref, table_ref, grad_ref, moment_ref, new_ref):
        new_ref[...], _, _ = update_rule(
            table_ref[...],
            grad_ref[...],
            moment_ref[...].astype(FLOAT),
            table_ref[...],
            rate,
            clip_ref[0],
        )

    spec = pl.BlockSpec((block, width), lambda i: (i, 0))
    scalar = pl.BlockSpec(memory_space=pltpu.SMEM)
    new_table = pl.pallas_call(
        whole_kernel,
        grid=(-(-vocab // block),),
        in_specs=[scalar, spec, spec, spec],
        out_specs=spec,
        out_shape=jax.ShapeDtypeStruct((vocab, width), FLOAT),
        compiler_params=pltpu.CompilerParams(vmem_limit_bytes=VMEM_LIMIT),
    )(clip, table, grad, moment_low)

    window = max(-(-(sub + sub * r % 8) // 8) * 8 for r in range(vocab // sub))
    tile = 264
    tiles = -(-window // tile)

    def own_kernel(
        clip_ref, table_ref, grad_ref, moment_ref, average_ref, moment_out, average_out, *scratch
    ):
        table_win, grad_win, sems = scratch
        step = pl.program_id(0)
        begin = lax.axis_index("dp") * sub
        low = pl.multiple_of(begin // 8 * 8, 8)
        shift = begin - low

        def fetch(t):
            first = t * tile
            size = min(tile, window - first)
            return [
                pltpu.make_async_copy(
                    source.at[pl.ds(low + first, size), :],
                    win.at[pl.ds(first, size), :],
                    sems.at[i, t],
                )
                for i, (source, win) in enumerate(((table_ref, table_win), (grad_ref, grad_win)))
            ]

        for t in range(tiles):

            @pl.when(step == t)
            def _():
                if t == 0:
                    for other in range(tiles):
                        for copy in fetch(other):
                            copy.start()
                    for copy in fetch(0):
                        copy.wait()
                if t + 1 < tiles:
                    for copy in fetch(t + 1):
                        copy.wait()

        first = pl.multiple_of(step * tile, 8)
        amount = jnp.where(shift == 0, 0, tile + 8 - shift)
        own_table = pltpu.roll(table_win[pl.ds(first, tile + 8), :], amount, 0)[:tile]
        own_grad = pltpu.roll(grad_win[pl.ds(first, tile + 8), :], amount, 0)[:tile]
        _, moment_out[...], average_out[...] = update_rule(
            own_table, own_grad, moment_ref[...], average_ref[...], rate, clip_ref[0]
        )

    anywhere = pl.BlockSpec(memory_space=pl.ANY)
    state = jax.ShapeDtypeStruct((sub, width), FLOAT)
    piece = pl.BlockSpec((tile, width), lambda i: (i, 0))
    new_moment, new_average = pl.pallas_call(
        own_kernel,
        grid=(tiles,),
        in_specs=[scalar, anywhere, anywhere, piece, piece],
        out_specs=[piece, piece],
        out_shape=[state, state],
        scratch_shapes=[
            pltpu.VMEM((tiles * tile + 8, width), FLOAT),
            pltpu.VMEM((tiles * tile + 8, width), FLOAT),
            pltpu.SemaphoreType.DMA((2, tiles)),
        ],
        compiler_params=pltpu.CompilerParams(vmem_limit_bytes=VMEM_LIMIT),
    )(clip, table, grad, moment, average)
    return new_table, new_moment, new_average


def shards(
    token_ids,
    loss_mask,
    lengths,
    buffer_ids,
    embed_table,
    embed_moment,
    embed_average,
    head_table,
    head_moment,
    head_average,
    in_weights,
    in_moment,
    in_average,
    out_weights,
    out_moment,
    out_average,
    vectors,
    vector_moment,
    vector_average,
):
    groups = lax.axis_size("fsdp")
    replicas = lax.axis_size("dp")
    member = lax.axis_index("fsdp")
    replica = lax.axis_index("dp")
    batches, _, seq = token_ids.shape
    vocab_rows, width = embed_table.shape
    hidden = out_weights.shape[0] * groups - width
    head_size = width // HEADS
    rot = head_size // 4
    factor = 1.0 / math.sqrt(head_size)
    vocab_start = member * vocab_rows
    own_rows = batches * seq
    rows_all = groups * own_rows

    tokens, marks, buffers = token_ids[:, 0], loss_mask[:, 0], buffer_ids[:, 0]
    divisor, offset, counted = jax.vmap(functools.partial(slot_info, buffer_count=NSEG))(
        tokens, marks, lengths[:, 0], buffers
    )
    packed = jnp.concatenate(
        [
            tokens,
            divisor,
            jnp.broadcast_to(jnp.sum(counted), (8 - 2 * batches, seq)),
        ],
        axis=0,
    )
    amount = vectors.shape[0]
    line = jnp.pad(vectors, (0, -amount % 1024)).reshape(-1, 128)
    everyone, lines, in_full, out_full, resid = start_kernel(
        packed, line, in_weights, out_weights, embed_table, batches, groups, replicas
    )
    vector_full = lines.reshape(groups, -1)[:, :amount].reshape(-1).astype(NARROW)
    embed_moment, head_moment, everyone = lax.optimization_barrier(
        (embed_moment, head_moment, everyone)
    )
    embed_moment_low = lax.all_gather(embed_moment.astype(NARROW), "dp", axis=0, tiled=True)
    head_moment_low = lax.all_gather(head_moment.astype(NARROW), "dp", axis=0, tiled=True)
    tokens_all = everyone[:, :batches]
    count = jnp.maximum(jnp.sum(everyone[:, 2 * batches, 0]).astype(FLOAT), 1.0)
    divisor_all = everyone[:, batches : 2 * batches].astype(FLOAT)
    share_all = jnp.where(divisor_all > 0.5, 1.0 / jnp.maximum(divisor_all, 1.0), 0.0)
    weight_all = (share_all / count).reshape(-1)
    target_all = (
        jnp.concatenate([tokens_all[:, :, 1:], jnp.zeros_like(tokens_all[:, :, :1])], axis=2)
        .reshape(-1)
    ) - vocab_start
    tokens_flat = tokens_all.reshape(-1)
    local_all = tokens_flat - vocab_start
    inside_all = (local_all >= 0) & (local_all < vocab_rows)

    def group_part(values):
        return lax.dynamic_slice_in_dim(values, replica * rows_all, rows_all, 0)

    parts = vector_parts(vector_full.astype(FLOAT), width, hidden)
    places = jnp.arange(seq, dtype=jnp.int32)
    allowed = (buffers[:, :, None] == buffers[:, None, :]) & (
        places[None, None, :] <= places[None, :, None]
    )
    cosine, sine = rotary_tables(offset.reshape(-1), rot)
    layer_out, kept = layer_forward(resid, in_full, out_full, parts, allowed, cosine, sine, factor)
    unit_last, scale_last = norm_unit(layer_out)
    final = (unit_last * parts[4] + parts[5]).astype(NARROW)
    final_grad, logsum_all, loss_part, all_hidden = head_kernel(
        head_table, final, group_part(target_all), group_part(weight_all), groups, replicas
    )

    less_weight = logsum_all - jnp.log(jnp.maximum(weight_all, 1e-30))
    shifted = jnp.where(weight_all > 0.0, less_weight, 1e30)
    chunk = min(512, rows_all)
    lists = chunk_lists(local_all, inside_all, chunk)

    layer_grad = norm_back(final_grad * parts[4], unit_last, scale_last)
    resid_grad, in_grad, out_grad, small = layer_backward(
        layer_grad, in_full, out_full, parts, kept, allowed, cosine, sine, factor
    )
    vector_grad = jnp.concatenate(
        [
            small[0],
            small[1],
            small[2],
            small[3],
            jnp.sum(final_grad * unit_last, axis=0),
            jnp.sum(final_grad, axis=0),
            small[4],
            small[5],
            small[6],
            small[7],
        ]
    )
    token_grad, in_grad, out_grad, vector_grad, embed_moment_low, head_moment_low, lists = (
        lax.optimization_barrier(
            (
                resid_grad.astype(NARROW),
                in_grad,
                out_grad,
                vector_grad,
                embed_moment_low,
                head_moment_low,
                lists,
            )
        )
    )
    parts_low = [
        lax.psum_scatter(grad, "fsdp", scatter_dimension=0, tiled=True)
        for grad in (in_grad, out_grad)
    ]
    slices = jnp.pad(vector_grad.reshape(groups, amount), ((0, 0), (0, -amount % 1024)))
    head_grad, head_square, token_grads, vector_sum = head_table_grad(
        head_table,
        all_hidden,
        shifted,
        weight_all,
        target_all,
        token_grad,
        slices.reshape(groups, -1, 128),
        groups,
        replicas,
    )
    parts_low, token_grads = lax.optimization_barrier((parts_low, token_grads))
    layer_grads = list(lax.psum(parts_low, "dp")) + [vector_sum.reshape(-1)[:amount]]
    embed_grad, embed_square = embed_table_grad(token_grads, *lists, vocab_rows)
    square = jnp.sum(embed_square) + jnp.sum(head_square)
    for grad in layer_grads:
        square = square + jnp.sum(grad * grad)
    line = jnp.stack([loss_part, square / replicas])[:, None]
    line = jnp.pad(jnp.broadcast_to(line, (2, 128)), ((0, 6), (0, 0)))
    pair = jnp.sum(exchange_scalars(line, groups, replicas)[:, :2, 0], axis=0)
    loss = pair[0]
    grad_norm = jnp.sqrt(pair[1])
    clip_factor = CLIP_LEVEL / jnp.maximum(grad_norm, CLIP_LEVEL)
    clip = clip_factor.reshape(1)
    base = math.sqrt(NPARAM) / CLIP_LEVEL
    root = math.sqrt(width)
    embed = table_update(
        embed_table, embed_grad, embed_moment_low, embed_moment, embed_average, base, clip
    )
    head = table_update(
        head_table, head_grad, head_moment_low, head_moment, head_average, base / root, clip
    )
    inner = update_rule(
        in_weights, layer_grads[0], in_moment, in_average, base / root, clip_factor
    )
    outer = update_rule(
        out_weights, layer_grads[1], out_moment, out_average, base / root, clip_factor
    )
    vector = update_rule(
        vectors, layer_grads[2], vector_moment, vector_average, 0.3 * base, clip_factor
    )
    return (*embed, *head, *inner, *outer, *vector, loss, grad_norm)


def solution(mesh):
    placed = (
        P(None, ("dp", "fsdp"), None),
        P(None, ("dp", "fsdp"), None),
        P(None, ("dp", "fsdp")),
        P(None, ("dp", "fsdp"), None),
        P("fsdp", None),
        P(("fsdp", "dp"), None),
        P(("fsdp", "dp"), None),
        P("fsdp", None),
        P(("fsdp", "dp"), None),
        P(("fsdp", "dp"), None),
        P("fsdp", None),
        P("fsdp", None),
        P("fsdp", None),
        P("fsdp", None),
        P("fsdp", None),
        P("fsdp", None),
        P("fsdp"),
        P("fsdp"),
        P("fsdp"),
    )
    return jax.shard_map(
        shards,
        mesh=mesh,
        in_specs=placed,
        out_specs=(
            P("fsdp", None),
            P(("fsdp", "dp"), None),
            P(("fsdp", "dp"), None),
            P("fsdp", None),
            P(("fsdp", "dp"), None),
            P(("fsdp", "dp"), None),
            P("fsdp", None),
            P("fsdp", None),
            P("fsdp", None),
            P("fsdp", None),
            P("fsdp", None),
            P("fsdp", None),
            P("fsdp"),
            P("fsdp"),
            P("fsdp"),
            P(),
            P(),
        ),
        check_vma=False,
    )
```

```python
import functools
import math

import jax
import jax.numpy as jnp
from jax import lax
from jax.experimental import pallas as pl
from jax.experimental.pallas import tpu as pltpu
from jax.sharding import PartitionSpec as P

HEADS = 8
NPARAM = 54664704
NSEG = 3


EPSILON = 1e-05
CLIP_LEVEL = 0.002
MOMENTUM = 0.5
DECAY = 0.5
NARROW = jnp.bfloat16
FLOAT = jnp.float32
ROWS_CONTRACT = (((0,), (0,)), ((), ()))
LAST_CONTRACT = (((1,), (1,)), ((), ()))


VMEM_LIMIT = 60 * 2**20


def slot_info(tokens, marks, length, buffers, buffer_count):
    seq = tokens.shape[0]
    places = jnp.arange(seq, dtype=jnp.int32)
    same_buffer = jnp.concatenate([buffers[1:] == buffers[:-1], jnp.zeros((1,), dtype=bool)])
    valid = jnp.where((marks == 1) & (places + 1 < length) & same_buffer, 1.0, 0.0).astype(FLOAT)
    member = buffers[None, :] == jnp.arange(buffer_count, dtype=jnp.int32)[:, None]
    weights = jnp.where(member, 1.0, 0.0).astype(FLOAT)
    tally = jnp.sum(weights * valid[None, :], axis=1)
    divisor = valid * jnp.sum(weights * tally[:, None], axis=0)
    counted = jnp.sum(jnp.where(tally > 0.5, 1.0, 0.0).astype(FLOAT))
    first = jnp.min(jnp.where(member, places[None, :], seq), axis=1)
    offset = places - jnp.sum(jnp.where(member, first[:, None], 0), axis=0)
    return (divisor.astype(jnp.int32), offset, counted.astype(jnp.int32))


def rotary_tables(offset, head_size):
    rot = head_size // 4
    half = rot // 2
    lanes = 128
    freqs = jnp.power(10000.0, -2.0 * jnp.arange(half, dtype=FLOAT) / rot)
    angles = offset.astype(FLOAT)[:, None] * freqs[None, :]
    cosine, sine = jnp.cos(angles), jnp.sin(angles)
    rows = offset.shape[0]
    rest = head_size - rot
    ones, none = jnp.ones((rows, rest), FLOAT), jnp.zeros((rows, rest), FLOAT)
    blank = jnp.zeros((rows, half), FLOAT)
    stay = jnp.concatenate([cosine, cosine, ones], axis=1)
    ahead = jnp.concatenate([-sine, blank, none], axis=1)
    behind = jnp.concatenate([blank, sine, none], axis=1)
    return [
        jnp.concatenate([part] * (lanes // head_size), axis=1) for part in (stay, ahead, behind)
    ]


def wide_tables(refs, width):
    return [jnp.concatenate([ref[...]] * (width // ref.shape[1]), axis=1) for ref in refs]


def norm_unit(values):
    mean = jnp.mean(values, axis=-1, keepdims=True)
    centred = values - mean
    scale = lax.rsqrt(jnp.mean(centred * centred, axis=-1, keepdims=True) + EPSILON)
    return (centred * scale, scale)


def norm_back(scaled, unit, scale):
    return scale * (
        scaled
        - jnp.mean(scaled, axis=-1, keepdims=True)
        - unit * jnp.mean(scaled * unit, axis=-1, keepdims=True)
    )


def vector_spans(width, hidden):
    amounts = [width] * 6 + [3 * width, width, hidden, width]
    spans = []
    begin = 0
    for amount in amounts:
        spans.append(slice(begin, begin + amount))
        begin = begin + amount
    return spans


def masked_probs(queries, keys, mask, factor):
    scores = lax.dot_general(queries, keys, LAST_CONTRACT, preferred_element_type=FLOAT) * factor
    scores = jnp.where(mask, scores, -1e30)
    top = jnp.max(scores, axis=-1, keepdims=True)
    logsum = top + jnp.log(jnp.sum(jnp.exp(scores - top), axis=-1, keepdims=True))
    return jnp.exp(scores - logsum)


def slot_mask(line_ref, column_ref, b, seq):
    later = lax.broadcasted_iota(jnp.int32, (seq, seq), 1)
    place = lax.broadcasted_iota(jnp.int32, (seq, seq), 0)
    return (column_ref[b] == line_ref[b]) & (later <= place)


def layer_forward(resid, in_full, out_full, vector, tables, lines, columns):
    rows, width = resid.shape
    hidden = out_full.shape[0] - width
    batches, _, seq = lines.shape
    head_size = width // HEADS
    half = head_size // 8
    factor = 1.0 / math.sqrt(head_size)
    spans = vector_spans(width, hidden)

    def kernel(
        resid_ref,
        in_ref,
        out_ref,
        vector_ref,
        stay_ref,
        ahead_ref,
        behind_ref,
        line_ref,
        column_ref,
        final_ref,
        qkv_ref,
        pre_ref,
        joined_ref,
        last_ref,
    ):
        def part(i):
            return vector_ref[:, spans[i]]

        start = resid_ref[...]
        unit, _ = norm_unit(start)
        input_one = (unit * part(0) + part(1)).astype(NARROW)
        input_two = (unit * part(2) + part(3)).astype(NARROW)
        stay, ahead, behind = wide_tables((stay_ref, ahead_ref, behind_ref), width)
        bias = part(6)
        for i in range(3):
            span = slice(i * width, (i + 1) * width)
            values = jnp.dot(input_one, in_ref[:, span], preferred_element_type=FLOAT)
            values = values + bias[:, span]
            if i < 2:
                values = (
                    values * stay
                    + pltpu.roll(values, width - half, 1) * ahead
                    + pltpu.roll(values, half, 1) * behind
                )
            qkv_ref[:, span] = values.astype(NARROW)
        for b in range(batches):
            mask = slot_mask(line_ref, column_ref, b, seq)
            there = slice(b * seq, (b + 1) * seq)
            for head in range(HEADS):
                first = head * head_size
                queries, keys, values = [
                    qkv_ref[there, i * width + first : i * width + first + head_size]
                    for i in range(3)
                ]
                probs = masked_probs(queries, keys, mask, factor).astype(NARROW)
                joined_ref[there, first : first + head_size] = jnp.dot(
                    probs, values, preferred_element_type=FLOAT
                ).astype(NARROW)
        bias = part(8)
        for i in range(hidden // width):
            span = slice(i * width, (i + 1) * width)
            pre = (
                jnp.dot(
                    input_two,
                    in_ref[:, (3 + i) * width : (4 + i) * width],
                    preferred_element_type=FLOAT,
                )
                + bias[:, span]
            )
            pre_ref[:, span] = pre
            joined_ref[:, (1 + i) * width : (2 + i) * width] = (
                0.5 * pre * (1.0 + lax.erf(pre * 0.7071067811865476))
            ).astype(NARROW)
        last = (
            start
            + jnp.dot(joined_ref[...], out_ref[...], preferred_element_type=FLOAT)
            + part(7)
            + part(9)
        )
        last_ref[...] = last
        unit_last, _ = norm_unit(last)
        final_ref[...] = (unit_last * part(4) + part(5)).astype(NARROW)

    return pl.pallas_call(
        kernel,
        out_shape=[
            jax.ShapeDtypeStruct((rows, width), NARROW),
            jax.ShapeDtypeStruct((rows, 3 * width), NARROW),
            jax.ShapeDtypeStruct((rows, hidden), FLOAT),
            jax.ShapeDtypeStruct((rows, width + hidden), NARROW),
            jax.ShapeDtypeStruct((rows, width), FLOAT),
        ],
        compiler_params=pltpu.CompilerParams(vmem_limit_bytes=VMEM_LIMIT),
    )(resid, in_full, out_full, vector, *tables, lines, columns)


def layer_backward(
    final_grad, resid, in_full, out_full, vector, tables, lines, columns, kept, groups
):
    rows, width = resid.shape
    hidden = out_full.shape[0] - width
    batches, _, seq = lines.shape
    head_size = width // HEADS
    half = head_size // 8
    factor = 1.0 / math.sqrt(head_size)
    spans = vector_spans(width, hidden)
    blocks = in_full.shape[1] // width
    in_rows = width // groups
    out_rows = out_full.shape[0] // groups
    first_out = blocks * in_rows
    shard = first_out + out_rows

    def kernel(
        final_grad_ref,
        resid_ref,
        in_ref,
        out_ref,
        vector_ref,
        stay_ref,
        ahead_ref,
        behind_ref,
        line_ref,
        column_ref,
        qkv_ref,
        pre_ref,
        joined_ref,
        last_ref,
        token_ref,
        small_ref,
        owners_ref,
        owners,
        low,
        wide,
        sems,
    ):
        def part(i):
            return vector_ref[:, spans[i]]

        def column_sum(i, values):
            small_ref[:, spans[i]] = jnp.sum(values, axis=0, keepdims=True)

        final_grad_in = final_grad_ref[...]
        unit_last, scale_last = norm_unit(last_ref[...])
        column_sum(4, final_grad_in * unit_last)
        column_sum(5, final_grad_in)
        grad_out = norm_back(final_grad_in * part(4), unit_last, scale_last)
        column_sum(7, grad_out)
        column_sum(9, grad_out)
        grad_low = grad_out.astype(NARROW)
        for c in range((width + hidden) // width):
            there = slice(c * width, (c + 1) * width)
            piece = lax.dot_general(
                joined_ref[:, there], grad_low, ROWS_CONTRACT, preferred_element_type=FLOAT
            )
            at = c * width
            while at < (c + 1) * width:
                owner, row = at // out_rows, at % out_rows
                size = min(out_rows - row, (c + 1) * width - at)
                owners[owner, first_out + row : first_out + row + size, :] = piece[
                    at - c * width : at - c * width + size
                ]
                at = at + size
        out_copy = pltpu.make_async_copy(
            owners.at[:, pl.ds(first_out, out_rows), :],
            owners_ref.at[:, pl.ds(first_out, out_rows), :],
            sems.at[0],
        )
        out_copy.start()
        unit, scale = norm_unit(resid_ref[...])
        input_one = (unit * part(0) + part(1)).astype(NARROW)
        input_two = (unit * part(2) + part(3)).astype(NARROW)

        def in_piece(inputs, c, grads):
            piece = lax.dot_general(
                inputs, grads, ROWS_CONTRACT, preferred_element_type=FLOAT
            )
            for owner in range(groups):
                owners[owner, c * in_rows : (c + 1) * in_rows, :] = piece[
                    owner * in_rows : (owner + 1) * in_rows
                ]

        back_two = jnp.zeros((rows, width), FLOAT)
        bias_sums = []
        for i in range(hidden // width):
            grads = lax.dot_general(
                grad_low,
                out_ref[(1 + i) * width : (2 + i) * width, :],
                LAST_CONTRACT,
                preferred_element_type=FLOAT,
            )
            pre = pre_ref[:, i * width : (i + 1) * width]
            slope = (
                0.5 * (1.0 + lax.erf(pre * 0.7071067811865476))
                + pre * jnp.exp(-0.5 * pre * pre) * 0.3989422804014327
            )
            grads = grads * slope
            bias_sums.append(jnp.sum(grads, axis=0, keepdims=True))
            grads = grads.astype(NARROW)
            in_piece(input_two, 3 + i, grads)
            back_two = back_two + lax.dot_general(
                grads,
                in_ref[:, (3 + i) * width : (4 + i) * width],
                LAST_CONTRACT,
                preferred_element_type=FLOAT,
            )
        small_ref[:, spans[8]] = jnp.concatenate(bias_sums, axis=1)
        low[...] = lax.dot_general(
            grad_low, out_ref[:width, :], LAST_CONTRACT, preferred_element_type=FLOAT
        ).astype(NARROW)
        for b in range(batches):
            mask = slot_mask(line_ref, column_ref, b, seq)
            there = slice(b * seq, (b + 1) * seq)
            for head in range(HEADS):
                first = head * head_size
                at = [
                    slice(i * width + first, i * width + first + head_size) for i in range(3)
                ]
                queries, keys, values = [qkv_ref[there, at[i]] for i in range(3)]
                mixed = low[there, first : first + head_size]
                probs = masked_probs(queries, keys, mask, factor)
                back = lax.dot_general(
                    mixed, values, LAST_CONTRACT, preferred_element_type=FLOAT
                )
                wide[there, at[2]] = lax.dot_general(
                    probs.astype(NARROW), mixed, ROWS_CONTRACT, preferred_element_type=FLOAT
                )
                scores = (
                    probs
                    * (back - jnp.sum(probs * back, axis=-1, keepdims=True))
                    * factor
                ).astype(NARROW)
                wide[there, at[0]] = jnp.dot(scores, keys, preferred_element_type=FLOAT)
                wide[there, at[1]] = lax.dot_general(
                    scores, queries, ROWS_CONTRACT, preferred_element_type=FLOAT
                )
        stay, ahead, behind = wide_tables((stay_ref, ahead_ref, behind_ref), width)
        back_one = jnp.zeros((rows, width), FLOAT)
        bias_sums = []
        for i in range(3):
            span = slice(i * width, (i + 1) * width)
            grads = wide[:, span]
            if i < 2:
                grads = (
                    grads * stay
                    + pltpu.roll(grads * ahead, half, 1)
                    + pltpu.roll(grads * behind, width - half, 1)
                )
            bias_sums.append(jnp.sum(grads, axis=0, keepdims=True))
            grads = grads.astype(NARROW)
            in_piece(input_one, i, grads)
            back_one = back_one + lax.dot_general(
                grads, in_ref[:, span], LAST_CONTRACT, preferred_element_type=FLOAT
            )
        in_copy = pltpu.make_async_copy(
            owners.at[:, pl.ds(0, first_out), :],
            owners_ref.at[:, pl.ds(0, first_out), :],
            sems.at[1],
        )
        in_copy.start()
        small_ref[:, spans[6]] = jnp.concatenate(bias_sums, axis=1)
        column_sum(0, back_one * unit)
        column_sum(1, back_one)
        column_sum(2, back_two * unit)
        column_sum(3, back_two)
        token_ref[...] = (
            grad_out + norm_back(back_one * part(0) + back_two * part(2), unit, scale)
        ).astype(NARROW)
        out_copy.wait()
        in_copy.wait()

    whole = pl.BlockSpec(memory_space=pltpu.VMEM)
    return pl.pallas_call(
        kernel,
        in_specs=[whole] * 14,
        out_specs=[whole, whole, pl.BlockSpec(memory_space=pl.ANY)],
        out_shape=[
            jax.ShapeDtypeStruct((rows, width), NARROW),
            jax.ShapeDtypeStruct(vector.shape, FLOAT),
            jax.ShapeDtypeStruct((groups, shard, width), FLOAT),
        ],
        scratch_shapes=[
            pltpu.VMEM((groups, shard, width), FLOAT),
            pltpu.VMEM((rows, width), NARROW),
            pltpu.VMEM((rows, 3 * width), FLOAT),
            pltpu.SemaphoreType.DMA((2,)),
        ],
        compiler_params=pltpu.CompilerParams(vmem_limit_bytes=VMEM_LIMIT),
    )(final_grad, resid, in_full, out_full, vector, *tables, lines, columns, *kept)


def block_rows(rows, cap):
    best = rows
    for size in range(8, cap + 1, 8):
        if rows % size == 0:
            best = size
    return best


MESH = pl.DeviceIdType.MESH


def meet(peers):
    barrier = pltpu.get_barrier_semaphore()
    for peer in peers:
        pl.semaphore_signal(barrier, inc=1, device_id=peer, device_id_type=MESH)
    pl.semaphore_wait(barrier, len(peers))


class Place:
    def __init__(self, groups, replicas):
        self.groups = groups
        self.replicas = replicas
        self.chips = groups // 2
        self.replica = lax.axis_index("dp")
        self.member = lax.axis_index("fsdp")
        self.chip = self.member // 2
        self.core = self.member % 2
        self.sibling_member = self.chip * 2 + 1 - self.core

    def lane_chip(self, step):
        return lax.rem(self.chip + step, self.chips)

    def at(self, replica, member):
        return {"dp": replica, "fsdp": member}

    def lane(self, step):
        return self.at(self.replica, self.lane_chip(step) * 2 + self.core)

    def plane_replica(self, step):
        return lax.rem(self.replica + step, self.replicas)

    def plane(self, step):
        return self.at(self.plane_replica(step), self.member)

    def sibling(self):
        return self.at(self.replica, self.sibling_member)

    def lanes(self):
        return [self.lane(step) for step in range(1, self.chips)]

    def planes(self):
        return [self.plane(step) for step in range(1, self.replicas)]


def remote(source, target, send, recv, device):
    return pltpu.make_async_remote_copy(
        src_ref=source,
        dst_ref=target,
        send_sem=send,
        recv_sem=recv,
        device_id=device,
        device_id_type=MESH,
    )


def start_kernel(packed, line, in_shard, out_shard, table, batches, groups, replicas):
    vocab, width = table.shape
    seq = packed.shape[1]
    own = batches * seq
    chips = groups // 2
    amount = groups * replicas
    shards_in = (in_shard, out_shard)
    split = all(shard.shape[0] % (16 * replicas) == 0 for shard in shards_in)
    pieces = replicas if split else 1
    unroll = 8

    def kernel(
        packed_ref,
        line_ref,
        in_ref,
        out_ref,
        table_ref,
        every_ref,
        lines_ref,
        in_full,
        out_full,
        resid_ref,
        in_low,
        out_low,
        wide,
        looked,
        to_core,
        from_core,
        to_lane,
        from_lane,
        ids,
        table_sem,
        ids_sem,
        local_sem,
        meta_send,
        meta_recv,
        line_send,
        line_recv,
        lane_send,
        lane_recv,
        plane_send,
        plane_recv,
        core_send,
        core_recv,
        part_send,
        part_recv,
        sum_send,
        sum_recv,
    ):
        place = Place(groups, replicas)
        member = place.member
        core = place.core
        replica = place.replica
        me = replica * groups + member
        fulls = (in_full, out_full)
        lows = (in_low, out_low)

        def device(index):
            return place.at(index // groups, lax.rem(index, groups))

        def chip_at(j):
            return lax.rem(place.chip + j, chips)

        def chip_before(j):
            return lax.rem(place.chip + chips - j, chips)

        def replica_before(k):
            return lax.rem(replica + replicas - k, replicas)

        def lane_device(j):
            return place.at(replica, chip_at(j) * 2 + core)

        def plane_device(k):
            return place.at(lax.rem(replica + k, replicas), member)

        def meta_copy(k):
            return remote(
                packed_ref,
                every_ref.at[me],
                meta_send.at[k],
                meta_recv.at[k],
                device(lax.rem(me + k, amount)),
            )

        def line_copy(k):
            return remote(
                line_ref,
                lines_ref.at[member],
                line_send.at[k],
                line_recv.at[k],
                place.at(replica, lax.rem(member + k, groups)),
            )

        def piece(w, slot, from_replica):
            full = fulls[w]
            if not split:
                return full.at[slot]
            rows = full.shape[1] // pieces
            return full.at[slot, pl.ds(pl.multiple_of(from_replica * rows, 16), rows), :]

        def own_piece(w):
            low = lows[w]
            if not split:
                return low
            rows = low.shape[0] // pieces
            return low.at[pl.ds(pl.multiple_of(replica * rows, 16), rows), :]

        def lane_copy(w, j):
            return remote(
                own_piece(w),
                piece(w, member, replica),
                lane_send.at[w, j],
                lane_recv.at[w, j],
                lane_device(j),
            )

        def lane_wait(w, j):
            there = piece(w, chip_before(j) * 2 + core, replica)
            remote(
                there, there, lane_send.at[w, j], lane_recv.at[w, j], lane_device(j)
            ).wait_recv()

        def plane_copy(w, k, j):
            there = piece(w, chip_before(j) * 2 + core, replica)
            return remote(
                there, there, plane_send.at[w, k, j], plane_recv.at[w, k, j], plane_device(k)
            )

        def plane_wait(w, k, j):
            there = piece(w, chip_before(j) * 2 + core, replica_before(k))
            remote(
                there, there, plane_send.at[w, k, j], plane_recv.at[w, k, j], plane_device(k)
            ).wait_recv()

        def core_copy(w, j):
            here = fulls[w].at[chip_before(j) * 2 + core]
            return remote(here, here, core_send.at[w, j], core_recv.at[w, j], place.sibling())

        def own_core_copy(w):
            return remote(
                lows[w],
                fulls[w].at[member],
                core_send.at[w, 0],
                core_recv.at[w, 0],
                place.sibling(),
            )

        def core_wait(w, j):
            there = fulls[w].at[chip_before(j) * 2 + 1 - core]
            remote(
                there, there, core_send.at[w, j], core_recv.at[w, j], place.sibling()
            ).wait_recv()

        def part_copy(j):
            return remote(
                to_core.at[j], from_core.at[j], part_send.at[j], part_recv.at[j], place.sibling()
            )

        def sum_copy(j):
            return remote(
                to_lane.at[j], from_lane.at[j], sum_send.at[j], sum_recv.at[j], lane_device(j)
            )

        fetch = pltpu.make_async_copy(table_ref, wide, table_sem)
        fetch.start()
        barrier = pltpu.get_barrier_semaphore()

        def greet(k, carry):
            pl.semaphore_signal(
                barrier, inc=1, device_id=device(lax.rem(me + k, amount)), device_id_type=MESH
            )
            return carry

        lax.fori_loop(1, amount, greet, 0)
        in_low[...] = in_ref[...].astype(NARROW)
        out_low[...] = out_ref[...].astype(NARROW)
        every_ref[me] = packed_ref[...]
        lines_ref[member] = line_ref[...]
        pl.semaphore_wait(barrier, amount - 1)

        def tell(k, carry):
            meta_copy(k).start()
            return carry

        lax.fori_loop(1, amount, tell, 0)
        for k in range(1, groups):
            line_copy(k).start()
        for w in range(2):
            for j in range(1, chips):
                lane_copy(w, j).start()
            own_core_copy(w).start()
        kept = [
            pltpu.make_async_copy(lows[w], fulls[w].at[member], local_sem.at[w])
            for w in range(2)
        ]
        for copy in kept:
            copy.start()

        def hear(k, carry):
            there = every_ref.at[lax.rem(me + amount - k, amount)]
            remote(there, there, meta_send.at[k], meta_recv.at[k], device(me)).wait_recv()
            return carry

        lax.fori_loop(1, amount, hear, 0)
        load = pltpu.make_async_copy(
            every_ref.at[pl.ds(replica * groups, groups)], ids, ids_sem
        )
        load.start()
        load.wait()
        fetch.wait()
        start = member * vocab

        def look(slot):
            for b in range(batches):

                def lap(i, carry):
                    for u in range(unroll):
                        spot = i * unroll + u
                        row = ids[slot, b, spot] - start
                        inside = (row >= 0) & (row < vocab)
                        safe = jnp.where(inside, row, 0)
                        keep = jnp.where(inside, 1.0, 0.0)
                        looked[pl.ds(b * seq + spot, 1), :] = wide[pl.ds(safe, 1), :] * keep
                    return carry

                lax.fori_loop(0, seq // unroll, lap, 0)
            return looked[...].astype(NARROW)

        def lap(step, carry):
            j = lax.rem(step + 1, chips)
            there = chip_at(j) * 2

            @pl.when(step == chips // 2)
            def _():
                for w in range(2):
                    for c in range(1, chips):
                        lane_wait(w, c)
                        if split:
                            for k in range(1, replicas):
                                plane_copy(w, k, c).start()

            to_core[j] = look(there + 1 - core)
            part_copy(j).start()
            mine = look(there + core).astype(FLOAT)
            part_copy(j).wait_recv()
            mine = mine + from_core[j].astype(FLOAT)

            @pl.when(j > 0)
            def _():
                to_lane[j] = mine.astype(NARROW)
                sum_copy(j).start()

            @pl.when(j == 0)
            def _():
                resid_ref[...] = mine

            return carry

        lax.fori_loop(0, chips, lap, 0)
        for j in range(1, chips):
            sum_copy(j).wait_recv()
            resid_ref[...] += from_lane[j].astype(FLOAT)
        for w in range(2):
            for j in range(1, chips):
                if split:
                    for k in range(1, replicas):
                        plane_wait(w, k, j)
                core_copy(w, j).start()
        for w in range(2):
            kept[w].wait()
            for j in range(chips):
                core_wait(w, j)
                if j == 0:
                    own_core_copy(w).wait_send()
                else:
                    core_copy(w, j).wait_send()
                    lane_copy(w, j).wait_send()
                if split and j > 0:
                    for k in range(1, replicas):
                        plane_copy(w, k, j).wait_send()
        for k in range(1, groups):
            there = lines_ref.at[lax.rem(member + groups - k, groups)]
            remote(
                there, there, line_send.at[k], line_recv.at[k], place.at(replica, member)
            ).wait_recv()
            line_copy(k).wait_send()
        for j in range(chips):
            part_copy(j).wait_send()
            if j > 0:
                sum_copy(j).wait_send()

        def told(k, carry):
            meta_copy(k).wait_send()
            return carry

        lax.fori_loop(1, amount, told, 0)

    whole = pl.BlockSpec(memory_space=pltpu.VMEM)
    anywhere = pl.BlockSpec(memory_space=pl.ANY)
    dma = pltpu.SemaphoreType.DMA
    vmem = pltpu.VMEM
    every, lines, in_full, out_full, resid = pl.pallas_call(
        kernel,
        in_specs=[whole, whole, whole, whole, anywhere],
        out_specs=[whole, whole, anywhere, anywhere, whole],
        out_shape=[
            jax.ShapeDtypeStruct((amount,) + packed.shape, jnp.int32),
            jax.ShapeDtypeStruct((groups,) + line.shape, FLOAT),
            jax.ShapeDtypeStruct((groups,) + in_shard.shape, NARROW),
            jax.ShapeDtypeStruct((groups,) + out_shard.shape, NARROW),
            jax.ShapeDtypeStruct((own, width), FLOAT),
        ],
        scratch_shapes=[
            vmem(in_shard.shape, NARROW),
            vmem(out_shard.shape, NARROW),
            vmem((vocab, width), FLOAT),
            vmem((own, width), FLOAT),
            vmem((chips, own, width), NARROW),
            vmem((chips, own, width), NARROW),
            vmem((chips, own, width), NARROW),
            vmem((chips, own, width), NARROW),
            pltpu.SMEM((groups,) + packed.shape, jnp.int32),
            dma,
            dma,
            dma((2,)),
            dma((amount,)),
            dma((amount,)),
            dma((groups,)),
            dma((groups,)),
            dma((2, chips)),
            dma((2, chips)),
            dma((2, replicas, chips)),
            dma((2, replicas, chips)),
            dma((2, chips)),
            dma((2, chips)),
            dma((chips,)),
            dma((chips,)),
            dma((chips,)),
            dma((chips,)),
        ],
        compiler_params=pltpu.CompilerParams(
            vmem_limit_bytes=VMEM_LIMIT, collective_id=4, has_side_effects=True
        ),
        cost_estimate=pl.CostEstimate(
            flops=0, bytes_accessed=vocab * width * 4, transcendentals=0
        ),
    )(packed, line, in_shard, out_shard, table)
    return (
        every,
        lines,
        in_full.reshape(-1, in_shard.shape[1]),
        out_full.reshape(-1, out_shard.shape[1]),
        resid,
    )


def head_kernel(table, own_hidden, target, weight, groups, replicas):
    vocab, width = table.shape
    own = own_hidden.shape[0]
    block = block_rows(vocab, 1100)
    blocks = vocab // block
    chips = groups // 2
    lines = -(-blocks // 8) * 8

    def kernel(
        table_ref,
        own_ref,
        target_ref,
        weight_ref,
        grad_ref,
        logsum_ref,
        loss_ref,
        all_ref,
        wide,
        low,
        hid,
        exps,
        tops,
        totals,
        hits,
        shares,
        to_core,
        from_core,
        to_lane,
        from_lane,
        table_sem,
        local_sem,
        lane_send,
        lane_recv,
        core_send,
        core_recv,
        plane_send,
        plane_recv,
        pass_send,
        pass_recv,
        stat_send,
        stat_recv,
        line_send,
        line_recv,
        part_send,
        part_recv,
        sum_send,
        sum_recv,
    ):
        place = Place(groups, replicas)
        me = place.member
        core = place.core

        def table_copy(b):
            return pltpu.make_async_copy(
                table_ref.at[pl.ds(b * block, block), :], wide.at[b % 2], table_sem.at[b % 2]
            )

        def chip_at(j):
            return lax.rem(place.chip + j, chips)

        def chip_before(j):
            return lax.rem(place.chip + chips - j, chips)

        def lane_device(j):
            return place.at(place.replica, chip_at(j) * 2 + core)

        def plane_device(k):
            return place.at(lax.rem(place.replica + k, replicas), me)

        def replica_before(k):
            return lax.rem(place.replica + replicas - k, replicas)

        def lane_copy(j):
            return remote(own_ref, hid.at[me], lane_send.at[j], lane_recv.at[j], lane_device(j))

        def lane_slot(j):
            return chip_before(j) * 2 + core

        def lane_wait(j):
            there = hid.at[lane_slot(j)]
            remote(there, there, lane_send.at[j], lane_recv.at[j], lane_device(j)).wait_recv()

        def core_copy(j):
            here = hid.at[lane_slot(j)]
            return remote(here, here, core_send.at[j], core_recv.at[j], place.sibling())

        def core_wait(j):
            there = hid.at[chip_before(j) * 2 + 1 - core]
            remote(there, there, core_send.at[j], core_recv.at[j], place.sibling()).wait_recv()

        def plane_copy(k, j):
            slot = lane_slot(j)
            return remote(
                hid.at[slot],
                all_ref.at[place.replica * groups + slot],
                plane_send.at[k, j],
                plane_recv.at[k, j],
                plane_device(k),
            )

        def plane_wait(k, j):
            there = all_ref.at[replica_before(k) * groups + lane_slot(j)]
            remote(
                there, there, plane_send.at[k, j], plane_recv.at[k, j], plane_device(k)
            ).wait_recv()

        def pass_copy(k, j):
            here = all_ref.at[replica_before(k) * groups + lane_slot(j)]
            return remote(
                here, here, pass_send.at[k, j], pass_recv.at[k, j], place.sibling()
            )

        def pass_wait(k, j):
            there = all_ref.at[
                replica_before(k) * groups + chip_before(j) * 2 + 1 - core
            ]
            remote(
                there, there, pass_send.at[k, j], pass_recv.at[k, j], place.sibling()
            ).wait_recv()

        def member_at(k):
            return lax.rem(me + k, groups)

        def stat_copy(k):
            return remote(
                shares.at[me],
                shares.at[me],
                stat_send.at[k],
                stat_recv.at[k],
                place.at(place.replica, member_at(k)),
            )

        def stat_wait(k):
            there = shares.at[lax.rem(me + groups - k, groups)]
            remote(
                there, there, stat_send.at[k], stat_recv.at[k], place.at(place.replica, me)
            ).wait_recv()

        def line_copy(k):
            here = logsum_ref.at[place.replica]
            return remote(here, here, line_send.at[k], line_recv.at[k], plane_device(k))

        def line_wait(k):
            there = logsum_ref.at[replica_before(k)]
            remote(there, there, line_send.at[k], line_recv.at[k], plane_device(k)).wait_recv()

        def part_copy(j):
            return remote(
                to_core.at[j], from_core.at[j], part_send.at[j], part_recv.at[j], place.sibling()
            )

        def sum_copy(j):
            return remote(
                to_lane.at[j], from_lane.at[j], sum_send.at[j], sum_recv.at[j], lane_device(j)
            )

        table_copy(0).start()
        if blocks > 1:
            table_copy(1).start()
        meet(
            [place.at(place.replica, member_at(k)) for k in range(1, groups)] + place.planes()
        )
        own_core = remote(own_ref, hid.at[me], core_send.at[0], core_recv.at[0], place.sibling())
        own_core.start()
        for j in range(1, chips):
            lane_copy(j).start()
        hid[me] = own_ref[...]
        for k in range(1, replicas):
            plane_copy(k, 0).start()
        for b in range(blocks):
            table_copy(b).wait()
            low[b] = wide[b % 2].astype(NARROW)
            if b + 2 < blocks:
                table_copy(b + 2).start()

        spots = lax.broadcasted_iota(jnp.int32, (block, own), 0)

        def forward(step, carry):
            j = step // 2
            other = lax.rem(step, 2)

            @pl.when(step == 1)
            def _():
                there = hid.at[place.sibling_member]
                remote(
                    there, there, core_send.at[0], core_recv.at[0], place.sibling()
                ).wait_recv()

            @pl.when((step > 1) & (other == 0))
            def _():
                lane_wait(j)
                core_copy(j).start()

                def spread(k, carry):
                    plane_copy(k, j).start()
                    return carry

                lax.fori_loop(1, replicas, spread, 0)

            @pl.when((step > 1) & (other == 1))
            def _():
                core_wait(j)

            member = chip_before(j) * 2 + lax.rem(core + other, 2)
            here = hid[member]
            wanted = target_ref[member]
            hit = jnp.zeros((1, own), FLOAT)
            for b in range(blocks):
                logits = lax.dot_general(
                    low[b], here, LAST_CONTRACT, preferred_element_type=FLOAT
                )
                top = jnp.max(logits, axis=0, keepdims=True)
                values = jnp.exp(logits - top)
                tops[member, b : b + 1, :] = top
                totals[member, b : b + 1, :] = jnp.sum(values, axis=0, keepdims=True)
                hit = hit + jnp.sum(
                    jnp.where(spots == wanted - b * block, logits, 0.0), axis=0, keepdims=True
                )
                exps[b, member] = values.astype(NARROW)
            hits[pl.ds(member, 1), :] = hit
            block_tops = tops[member, :blocks, :]
            top = jnp.max(block_tops, axis=0, keepdims=True)
            total = jnp.sum(
                totals[member, :blocks, :] * jnp.exp(block_tops - top), axis=0, keepdims=True
            )
            shares[me, pl.ds(member, 1), :] = top + jnp.log(total)
            return carry

        lax.fori_loop(0, groups, forward, 0)
        local = pltpu.make_async_copy(
            hid, all_ref.at[pl.ds(place.replica * groups, groups)], local_sem
        )
        local.start()
        for k in range(1, groups):
            stat_copy(k).start()
        for k in range(1, groups):
            stat_wait(k)
        every = shares[...]
        top = jnp.max(every, axis=0)
        logsum_ref[place.replica] = top + jnp.log(jnp.sum(jnp.exp(every - top[None]), axis=0))
        for k in range(1, replicas):
            line_copy(k).start()

        def member_back(member):
            wanted = target_ref[member]
            weights = weight_ref[member]
            logsum = logsum_ref[place.replica, pl.ds(member, 1), :]
            total = jnp.zeros((own, width), FLOAT)
            for b in range(blocks):
                scale = weights * jnp.exp(tops[member, b : b + 1, :] - logsum)
                grads = exps[b, member].astype(FLOAT) * scale
                grads = jnp.where(spots == wanted - b * block, grads - weights, grads)
                total = total + lax.dot_general(
                    grads.astype(NARROW), low[b], ROWS_CONTRACT, preferred_element_type=FLOAT
                )
            return total

        def backward(step, carry):
            j = lax.rem(step + 1, chips)

            @pl.when(step == chips - 1)
            def _():
                for k in range(1, replicas):
                    for c in range(chips):
                        plane_wait(k, c)
                for k in range(1, replicas):
                    for c in range(chips):
                        pass_copy(k, c).start()

            there = chip_at(j) * 2
            to_core[j] = member_back(there + 1 - core)
            part_copy(j).start()
            mine = member_back(there + core)
            part_copy(j).wait_recv()
            mine = mine + from_core[j]

            @pl.when(j > 0)
            def _():
                to_lane[j] = mine
                sum_copy(j).start()

            @pl.when(j == 0)
            def _():
                grad_ref[...] = mine

            return carry

        lax.fori_loop(0, chips, backward, 0)
        held = lax.broadcasted_iota(jnp.int32, (groups, own), 0) == me
        amounts = jnp.concatenate([weight_ref[m] for m in range(groups)], axis=0)
        losses = amounts * (jnp.where(held, logsum_ref[place.replica], 0.0) - hits[...])
        loss_ref[...] = jnp.sum(losses, axis=0, keepdims=True)
        for j in range(1, chips):
            sum_copy(j).wait_recv()
            grad_ref[...] += from_lane[j]
        local.wait()
        own_core.wait_send()
        for k in range(1, groups):
            stat_copy(k).wait_send()
        for k in range(1, replicas):
            line_wait(k)
            line_copy(k).wait_send()
            for j in range(chips):
                pass_wait(k, j)
                plane_copy(k, j).wait_send()
                pass_copy(k, j).wait_send()
        for j in range(chips):
            part_copy(j).wait_send()
            if j > 0:
                lane_copy(j).wait_send()
                core_copy(j).wait_send()
                sum_copy(j).wait_send()

    whole = pl.BlockSpec(memory_space=pltpu.VMEM)
    anywhere = pl.BlockSpec(memory_space=pl.ANY)
    dma = pltpu.SemaphoreType.DMA
    vmem = pltpu.VMEM
    grad, logsum, loss, everyone = pl.pallas_call(
        kernel,
        in_specs=[anywhere, whole, whole, whole],
        out_specs=[whole, whole, whole, anywhere],
        out_shape=[
            jax.ShapeDtypeStruct((own, width), FLOAT),
            jax.ShapeDtypeStruct((replicas, groups, own), FLOAT),
            jax.ShapeDtypeStruct((1, own), FLOAT),
            jax.ShapeDtypeStruct((replicas * groups, own, width), NARROW),
        ],
        scratch_shapes=[
            vmem((2, block, width), FLOAT),
            vmem((blocks, block, width), NARROW),
            vmem((groups, own, width), NARROW),
            vmem((blocks, groups, block, own), NARROW),
            vmem((groups, lines, own), FLOAT),
            vmem((groups, lines, own), FLOAT),
            vmem((groups, own), FLOAT),
            vmem((groups, groups, own), FLOAT),
            vmem((chips, own, width), FLOAT),
            vmem((chips, own, width), FLOAT),
            vmem((chips, own, width), FLOAT),
            vmem((chips, own, width), FLOAT),
            dma((2,)),
            dma,
            dma((chips,)),
            dma((chips,)),
            dma((chips,)),
            dma((chips,)),
            dma((replicas, chips)),
            dma((replicas, chips)),
            dma((replicas, chips)),
            dma((replicas, chips)),
            dma((groups,)),
            dma((groups,)),
            dma((replicas,)),
            dma((replicas,)),
            dma((chips,)),
            dma((chips,)),
            dma((chips,)),
            dma((chips,)),
        ],
        compiler_params=pltpu.CompilerParams(
            vmem_limit_bytes=VMEM_LIMIT, collective_id=3, has_side_effects=True
        ),
        cost_estimate=pl.CostEstimate(
            flops=4 * vocab * groups * own * width,
            bytes_accessed=vocab * width * 4,
            transcendentals=vocab * groups * own,
        ),
    )(
        table,
        own_hidden,
        target.reshape(groups, 1, own),
        weight.reshape(groups, 1, own),
    )
    return grad, logsum.reshape(-1), jnp.sum(loss), everyone.reshape(-1, width)


def head_table_grad(
    table, hidden, logsum, weights, target, token_grad, slices, owner_grads, cut, groups, replicas
):
    vocab, width = table.shape
    amount = groups * replicas
    rows = hidden.shape[0]
    own = token_grad.shape[0]
    tile = math.gcd(rows, 2048)
    block = block_rows(vocab, 1100)
    tiles = rows // tile
    steps = vocab // block
    chips = groups // 2
    last = steps - 1
    shard = owner_grads.shape[1]
    regions = ((0, cut), (cut, shard - cut))
    firsts, seconds = (replicas, chips), (chips, replicas)
    reduce = all(count % (8 * replicas) == 0 for _, count in regions)
    laps = steps * tiles

    def when(part):
        return min(int(laps * part), laps - 1)

    def kernel(
        table_ref,
        hidden_ref,
        logsum_ref,
        weight_ref,
        target_ref,
        own_ref,
        slices_ref,
        owner_ref,
        grad_ref,
        square_ref,
        all_ref,
        summed_ref,
        owned_out,
        gathered,
        owned_ref,
        from_core,
        acc_in,
        acc_out,
        one_in,
        one_out,
        two_in,
        two_out,
        piece_sem,
        half_send,
        half_recv,
        one_send,
        one_recv,
        two_send,
        two_recv,
        end_send,
        end_recv,
        local_sem,
        slice_send,
        slice_recv,
        lane_send,
        lane_recv,
        plane_send,
        plane_recv,
        core_send,
        core_recv,
    ):
        step = pl.program_id(0)
        place = Place(groups, replicas)
        me = place.replica * groups + place.member

        def slot(replica, member):
            return all_ref.at[replica * groups + member]

        def lane_copy(k):
            here = all_ref.at[me]
            return remote(own_ref, here, lane_send.at[k], lane_recv.at[k], place.lane(k))

        def lane_wait(k):
            back = lax.rem(place.chip + chips - k, chips) * 2 + place.core
            there = slot(place.replica, back)
            remote(there, there, lane_send.at[k], lane_recv.at[k], place.lane(k)).wait_recv()

        def plane_copy(k, c):
            here = slot(place.replica, c * 2 + place.core)
            return remote(here, here, plane_send.at[k, c], plane_recv.at[k, c], place.plane(k))

        def plane_wait(k, c):
            back = lax.rem(place.replica + replicas - k, replicas)
            there = slot(back, c * 2 + place.core)
            remote(
                there, there, plane_send.at[k, c], plane_recv.at[k, c], place.plane(k)
            ).wait_recv()

        def core_copy(r, c):
            here = slot(r, c * 2 + place.core)
            return remote(here, here, core_send.at[r, c], core_recv.at[r, c], place.sibling())

        def core_wait(r, c):
            there = slot(r, c * 2 + 1 - place.core)
            remote(
                there, there, core_send.at[r, c], core_recv.at[r, c], place.sibling()
            ).wait_recv()

        def device(index):
            return place.at(index // groups, lax.rem(index, groups))

        def slice_copy(k):
            there = lax.rem(me + k, amount)
            return remote(
                slices_ref.at[lax.rem(there, groups)],
                gathered.at[me],
                slice_send.at[k],
                slice_recv.at[k],
                device(there),
            )

        local = pltpu.make_async_copy(own_ref, all_ref.at[me], local_sem)
        accs, ones, twos = (acc_in, acc_out), (one_in, one_out), (two_in, two_out)

        def chip_at(j):
            return lax.rem(place.chip + j, chips)

        def pieces(g):
            first, rows = regions[g]
            size = rows // replicas
            for k in range(firsts[g]):
                for i in range(seconds[g]):
                    if g == 0:
                        chip, replica = i, place.plane_replica(k)
                    else:
                        chip, replica = chip_at(k), i
                    yield k, i, chip, pl.multiple_of(first + replica * size, 8), size

        def piece_copy(g, k, i, chip, row, size):
            return pltpu.make_async_copy(
                owner_ref.at[chip * 2 + place.core, pl.ds(row, size), :],
                accs[g].at[k, i],
                piece_sem.at[g, k, i],
            )

        def half_copy(c):
            return remote(
                owner_ref.at[c * 2 + 1 - place.core],
                from_core.at[c],
                half_send.at[c],
                half_recv.at[c],
                place.sibling(),
            )

        def partner(over_dp, k):
            if over_dp:
                return place.plane(k)
            return place.lane(k)

        def one_copy(g, k):
            return remote(
                accs[g].at[k],
                ones[g].at[k],
                one_send.at[g, k],
                one_recv.at[g, k],
                partner(g == 0, k),
            )

        def mine(g):
            return place.chip if g == 0 else place.replica

        def two_copy(g, k):
            return remote(
                accs[g].at[0, lax.rem(mine(g) + k, seconds[g])],
                twos[g].at[k],
                two_send.at[g, k],
                two_recv.at[g, k],
                partner(g == 1, k),
            )

        def end_copy(g, k, there):
            first, rows = regions[g]
            size = rows // replicas
            span = owned_ref.at[pl.ds(pl.multiple_of(first + there * size, 8), size), :]
            return remote(span, span, end_send.at[g, k], end_recv.at[g, k], place.plane(k))

        def begin_sums():
            for c in range(chips):
                half_copy(c).start()
            for g in range(2):
                for item in pieces(g):
                    piece_copy(g, *item).start()

        def begin_one():
            for c in range(chips):
                half_copy(c).wait_recv()
            for g in range(2):
                for item in pieces(g):
                    piece_copy(g, *item).wait()
                    k, i, chip, row, size = item
                    accs[g][k, i] += from_core[chip, pl.ds(row, size), :]
                for k in range(1, firsts[g]):
                    one_copy(g, k).start()

        def begin_two(g):
            for k in range(1, firsts[g]):
                one_copy(g, k).wait_recv()
            for i in range(seconds[g]):
                total = accs[g][0, i]
                for k in range(1, firsts[g]):
                    total = total + ones[g][k, i]
                accs[g][0, i] = total
            for k in range(1, seconds[g]):
                two_copy(g, k).start()

        def begin_end(g):
            first, rows = regions[g]
            size = rows // replicas
            total = accs[g][0, mine(g)]
            for k in range(1, seconds[g]):
                two_copy(g, k).wait_recv()
                total = total + twos[g][k]
            row = pl.multiple_of(first + place.replica * size, 8)
            owned_ref[pl.ds(row, size), :] = total
            for k in range(1, replicas):
                end_copy(g, k, place.replica).start()

        def end_sums():
            for g in range(2):
                for k in range(1, replicas):
                    end_copy(g, k, lax.rem(place.replica + replicas - k, replicas)).wait_recv()
                    end_copy(g, k, place.replica).wait_send()
                for k in range(1, firsts[g]):
                    one_copy(g, k).wait_send()
                for k in range(1, seconds[g]):
                    two_copy(g, k).wait_send()
            for c in range(chips):
                half_copy(c).wait_send()

        def begin_all():
            barrier = pltpu.get_barrier_semaphore()

            def greet(k, carry):
                pl.semaphore_signal(
                    barrier,
                    inc=1,
                    device_id=device(lax.rem(me + k, amount)),
                    device_id_type=MESH,
                )
                return carry

            lax.fori_loop(1, amount, greet, 0)
            pl.semaphore_wait(barrier, amount - 1)
            local.start()
            if reduce:
                begin_sums()
            for k in range(1, chips):
                lane_copy(k).start()

            def give(k, carry):
                slice_copy(k).start()
                return carry

            lax.fori_loop(1, amount, give, 0)
            gathered[me] = slices_ref[place.member]

        def token_lane():
            local.wait()
            for k in range(1, chips):
                lane_wait(k)
            for c in range(chips):
                core_copy(place.replica, c).start()

        def token_plane():
            for c in range(chips):
                for k in range(1, replicas):
                    plane_copy(k, c).start()

        def token_core():
            for k in range(1, replicas):
                for c in range(chips):
                    plane_wait(k, c)
            for k in range(1, replicas):
                for c in range(chips):
                    core_copy(place.plane_replica(k), c).start()

        plan = [(0.0, begin_all)]
        if reduce:
            plan = plan + [
                (0.09, begin_one),
                (0.25, token_lane),
                (0.4, lambda: begin_two(0)),
                (0.4, token_plane),
                (0.65, lambda: begin_two(1)),
                (0.75, lambda: begin_end(0)),
                (0.8, lambda: begin_end(1)),
                (0.8, token_core),
            ]
        else:
            plan = plan + [(0.17, token_lane), (0.17, token_plane), (0.5, token_core)]

        start = step * block
        part = table_ref[...].astype(NARROW)
        places = lax.broadcasted_iota(jnp.int32, (block, tile), 0)

        def lap(k, carry):
            for part_of, act in plan:
                pl.when(step * tiles + k == when(part_of))(act)
            here = hidden_ref[pl.ds(pl.multiple_of(k * tile, tile), tile), :]
            logits = lax.dot_general(part, here, LAST_CONTRACT, preferred_element_type=FLOAT)
            probs = jnp.exp(logits - logsum_ref[k])
            grads = jnp.where(
                places == target_ref[k] - start, probs - weight_ref[k], probs
            ).astype(NARROW)
            piece = jnp.dot(grads, here, preferred_element_type=FLOAT)

            @pl.when(k == 0)
            def _():
                grad_ref[...] = piece

            @pl.when(k > 0)
            def _():
                grad_ref[...] += piece

            return carry

        lax.fori_loop(0, tiles, lap, 0)
        squares = jnp.sum(jnp.square(grad_ref[...]), axis=0, keepdims=True)

        @pl.when(step == 0)
        def _():
            square_ref[...] = squares

        @pl.when(step > 0)
        def _():
            square_ref[...] += squares

        @pl.when(step == last)
        def _():
            def take(k, carry):
                there = gathered.at[lax.rem(me + amount - k, amount)]
                remote(there, there, slice_send.at[k], slice_recv.at[k], device(me)).wait_recv()
                slice_copy(k).wait_send()
                return carry

            lax.fori_loop(1, amount, take, 0)
            if reduce:
                end_sums()
                owned_out[...] = owned_ref[...]
            summed_ref[...] = jnp.sum(gathered[...], axis=0)
            for r in range(replicas):
                for c in range(chips):
                    core_wait(r, c)
            for k in range(1, chips):
                lane_copy(k).wait_send()
            for c in range(chips):
                for k in range(1, replicas):
                    plane_copy(k, c).wait_send()
                for r in range(replicas):
                    core_copy(r, c).wait_send()

    whole = pl.BlockSpec(memory_space=pltpu.VMEM)
    anywhere = pl.BlockSpec(memory_space=pl.ANY)
    shape = (tiles, 1, tile)
    dma = pltpu.SemaphoreType.DMA
    return pl.pallas_call(
        kernel,
        grid=(steps,),
        in_specs=[pl.BlockSpec((block, width), lambda i: (i, 0))]
        + [whole] * 4
        + [anywhere, whole, anywhere],
        out_specs=[
            pl.BlockSpec((block, width), lambda i: (i, 0)),
            pl.BlockSpec((1, width), lambda i: (0, 0)),
            anywhere,
            whole,
            whole,
        ],
        out_shape=[
            jax.ShapeDtypeStruct((vocab, width), FLOAT),
            jax.ShapeDtypeStruct((1, width), FLOAT),
            jax.ShapeDtypeStruct((groups * replicas, own, width), NARROW),
            jax.ShapeDtypeStruct(slices.shape[1:], FLOAT),
            jax.ShapeDtypeStruct(owner_grads.shape[1:] if reduce else (8, 128), FLOAT),
        ],
        scratch_shapes=[
            pltpu.VMEM((amount,) + slices.shape[1:], FLOAT),
            pltpu.VMEM(owner_grads.shape[1:] if reduce else (8, 128), FLOAT),
            pltpu.VMEM((chips,) + owner_grads.shape[1:] if reduce else (8, 128), FLOAT),
        ]
        + [
            pltpu.VMEM(
                (counts[g], seconds[g], regions[g][1] // replicas, width)[skip:]
                if reduce
                else (8, 128),
                FLOAT,
            )
            for counts, skip in ((firsts, 0), (firsts, 0), (seconds, 1))
            for g in range(2)
        ]
        + [
            dma((2, max(firsts), max(seconds))),
            dma((chips,)),
            dma((chips,)),
            dma((2, max(firsts))),
            dma((2, max(firsts))),
            dma((2, max(seconds))),
            dma((2, max(seconds))),
            dma((2, replicas)),
            dma((2, replicas)),
            dma,
            dma((amount,)),
            dma((amount,)),
            dma((chips,)),
            dma((chips,)),
            dma((replicas, chips)),
            dma((replicas, chips)),
            dma((replicas, chips)),
            dma((replicas, chips)),
        ],
        compiler_params=pltpu.CompilerParams(
            vmem_limit_bytes=VMEM_LIMIT, collective_id=1, has_side_effects=True
        ),
        cost_estimate=pl.CostEstimate(
            flops=4 * vocab * rows * width,
            bytes_accessed=vocab * width * 8 + rows * width * 4,
            transcendentals=vocab * rows,
        ),
    )(
        table,
        hidden,
        logsum.reshape(shape),
        weights.reshape(shape),
        target.reshape(shape),
        token_grad,
        slices,
        owner_grads,
    )


def exchange_scalars(line, groups, replicas):
    amount = groups * replicas

    def kernel(own_ref, all_ref, local_sem, send_sem, recv_sem):
        place = Place(groups, replicas)
        me = place.replica * groups + place.member

        def device(index):
            return place.at(index // groups, lax.rem(index, groups))

        barrier = pltpu.get_barrier_semaphore()

        def greet(k, carry):
            pl.semaphore_signal(
                barrier, inc=1, device_id=device(lax.rem(me + k, amount)), device_id_type=MESH
            )
            return carry

        def copy(k):
            return remote(
                own_ref,
                all_ref.at[me],
                send_sem.at[k],
                recv_sem.at[k],
                device(lax.rem(me + k, amount)),
            )

        def begin(k, carry):
            copy(k).start()
            return carry

        def finish(k, carry):
            there = all_ref.at[lax.rem(me + amount - k, amount)]
            remote(there, there, send_sem.at[k], recv_sem.at[k], device(me)).wait_recv()
            copy(k).wait_send()
            return carry

        lax.fori_loop(1, amount, greet, 0)
        local = pltpu.make_async_copy(own_ref, all_ref.at[me], local_sem)
        local.start()
        pl.semaphore_wait(barrier, amount - 1)
        lax.fori_loop(1, amount, begin, 0)
        local.wait()
        lax.fori_loop(1, amount, finish, 0)

    whole = pl.BlockSpec(memory_space=pltpu.VMEM)
    dma = pltpu.SemaphoreType.DMA
    return pl.pallas_call(
        kernel,
        in_specs=[whole],
        out_specs=whole,
        out_shape=jax.ShapeDtypeStruct((amount,) + line.shape, line.dtype),
        scratch_shapes=[dma, dma((amount,)), dma((amount,))],
        compiler_params=pltpu.CompilerParams(collective_id=2, has_side_effects=True),
    )(line)


def chunk_lists(local, inside, chunk):
    chunks = local.shape[0] // chunk
    flags = inside.reshape(chunks, chunk)
    spots = jnp.arange(chunk, dtype=jnp.int32)
    ahead = (spots[:, None] < spots[None, :]).astype(NARROW)
    order = jnp.dot(flags.astype(NARROW), ahead, preferred_element_type=FLOAT).astype(jnp.int32)
    chosen = (order[:, None, :] == spots[None, :, None]) & flags[:, None, :]
    places = jnp.sum(jnp.where(chosen, spots[None, None, :], 0), axis=2)
    rows = jnp.sum(jnp.where(chosen, local.reshape(chunks, 1, chunk), 0), axis=2)
    return places, rows, jnp.sum(flags.astype(jnp.int32), axis=1)


def embed_table_grad(token_grads, places, rows, counts, vocab):
    chunks, chunk = places.shape
    width = token_grads.shape[-1]
    padded = vocab + 8
    unroll = 4

    def kernel(
        count_ref, place_ref, row_ref, tokens_ref, grad_ref, square_ref, wide_ref, total_ref, sem
    ):
        step = pl.program_id(0)

        @pl.when(step == 0)
        def _():
            total_ref[...] = jnp.zeros_like(total_ref)

        wide_ref[...] = tokens_ref[...].astype(FLOAT)
        amount = count_ref[step]

        def lap(j, carry):
            for u in range(unroll):
                spot = j * unroll + u
                row = jnp.where(spot < amount, row_ref[0, 0, spot], vocab)
                place = place_ref[0, 0, spot]
                total_ref[pl.ds(row, 1), :] += wide_ref[pl.ds(place, 1), :]
            return carry

        lax.fori_loop(0, (amount + unroll - 1) // unroll, lap, 0)

        @pl.when(step == chunks - 1)
        def _():
            out = pltpu.make_async_copy(total_ref.at[pl.ds(0, vocab), :], grad_ref, sem)
            out.start()
            square_ref[...] = jnp.sum(
                jnp.square(total_ref[pl.ds(0, vocab), :]), axis=0, keepdims=True
            )
            out.wait()

    line = pl.BlockSpec((1, 1, chunk), lambda i, c: (i, 0, 0), memory_space=pltpu.SMEM)
    return pl.pallas_call(
        kernel,
        grid_spec=pltpu.PrefetchScalarGridSpec(
            num_scalar_prefetch=1,
            grid=(chunks,),
            in_specs=[line, line, pl.BlockSpec((chunk, width), lambda i, c: (i, 0))],
            out_specs=[
                pl.BlockSpec(memory_space=pl.ANY),
                pl.BlockSpec((1, width), lambda i, c: (0, 0)),
            ],
            scratch_shapes=[
                pltpu.VMEM((chunk, width), FLOAT),
                pltpu.VMEM((padded, width), FLOAT),
                pltpu.SemaphoreType.DMA,
            ],
        ),
        out_shape=[
            jax.ShapeDtypeStruct((vocab, width), FLOAT),
            jax.ShapeDtypeStruct((1, width), FLOAT),
        ],
        compiler_params=pltpu.CompilerParams(vmem_limit_bytes=VMEM_LIMIT),
    )(
        counts,
        places.reshape(chunks, 1, chunk),
        rows.reshape(chunks, 1, chunk),
        token_grads.reshape(chunks * chunk, width),
    )


def update_rule(weight, grad, moment, average, rate, clip_factor):
    clipped = clip_factor * grad
    new_moment = MOMENTUM * moment + clipped
    new_weight = weight - rate * (clipped + MOMENTUM * new_moment)
    new_average = DECAY * average + (1.0 - DECAY) * new_weight
    return (new_weight, new_moment, new_average)


def update_all(scalars, tables, matrices, rates):
    vocab, width = tables[0][0].shape
    sub = tables[0][3].shape[0]
    block = block_rows(vocab, 1100)
    blocks = vocab // block
    window = max(-(-(sub + sub * r % 8) // 8) * 8 for r in range(vocab // sub))
    tile = 264
    tiles = -(-window // tile)
    steps = 2 * blocks + 2 * tiles
    count = len(matrices)

    def kernel(*refs):
        refs = list(refs)

        def take(amount):
            taken = refs[:amount]
            del refs[:amount]
            return taken

        (scalars_ref,) = take(1)
        whole_in = [take(3) for _ in range(2)]
        own_in = [take(4) for _ in range(2)]
        small_in = [take(4) for _ in range(count)]
        new_tables = take(2)
        own_out = [take(2) for _ in range(2)]
        small_out = [take(3) for _ in range(count)]
        (factor_ref,) = take(1)
        windows = take(2)
        (sems,) = take(1)
        step = pl.program_id(0)
        begin = lax.axis_index("dp") * sub
        low = pl.multiple_of(begin // 8 * 8, 8)
        shift = begin - low

        def fetch(w, t):
            first = t * tile
            size = min(tile, window - first)
            return [
                pltpu.make_async_copy(
                    own_in[w][i].at[pl.ds(low + first, size), :],
                    windows[i].at[pl.ds(first, size), :],
                    sems.at[w, i, t],
                )
                for i in range(2)
            ]

        @pl.when(step == 0)
        def _():
            total = jnp.sum(scalars_ref[...], axis=0)
            norm = jnp.sqrt(total)
            factor_ref[...] = CLIP_LEVEL / jnp.maximum(norm, CLIP_LEVEL)

        factor = factor_ref[1:2, 0:1]
        for w in range(2):

            @pl.when((step >= w * blocks) & (step < (w + 1) * blocks))
            def _():
                table_ref, grad_ref, moment_ref = whole_in[w]
                table = table_ref[...]
                new_tables[w][...], _, _ = update_rule(
                    table, grad_ref[...], moment_ref[...].astype(FLOAT), table, rates[w], factor
                )

        @pl.when(step == 1)
        def _():
            for i in range(count):
                weight, grad, moment, average = [ref[...] for ref in small_in[i]]
                results = update_rule(weight, grad, moment, average, rates[2 + i], factor)
                for ref, result in zip(small_out[i], results):
                    ref[...] = result

        for w in range(2):
            base = 2 * blocks + w * tiles
            for t in range(tiles):

                @pl.when(step == (base - tiles + t + 1 if w else blocks))
                def _():
                    for copy in fetch(w, t):
                        copy.start()

            for t in range(tiles):

                @pl.when(step == base + t)
                def _():
                    if t == 0:
                        for copy in fetch(w, 0):
                            copy.wait()
                    if t + 1 < tiles:
                        for copy in fetch(w, t + 1):
                            copy.wait()

            @pl.when((step >= base) & (step < base + tiles))
            def _():
                first = pl.multiple_of((step - base) * tile, 8)
                amount = jnp.where(shift == 0, 0, tile + 8 - shift)
                own_table, own_grad = [
                    pltpu.roll(win[pl.ds(first, tile + 8), :], amount, 0)[:tile]
                    for win in windows
                ]
                _, own_out[w][0][...], own_out[w][1][...] = update_rule(
                    own_table, own_grad, own_in[w][2][...], own_in[w][3][...], rates[w], factor
                )

    whole = pl.BlockSpec(memory_space=pltpu.VMEM)
    anywhere = pl.BlockSpec(memory_space=pl.ANY)

    def table_spec(w):
        return pl.BlockSpec(
            (block, width), lambda i: (jnp.clip(i - w * blocks, 0, blocks - 1), 0)
        )

    def own_spec(w):
        return pl.BlockSpec(
            (tile, width),
            lambda i: (jnp.clip(i - 2 * blocks - w * tiles, 0, tiles - 1), 0),
        )

    state = jax.ShapeDtypeStruct((sub, width), FLOAT)
    operands = [scalars]
    in_specs = [whole]
    for w in range(2):
        operands += list(tables[w][:3])
        in_specs += [table_spec(w)] * 3
    for w in range(2):
        operands += [tables[w][0], tables[w][1], tables[w][3], tables[w][4]]
        in_specs += [anywhere, anywhere, own_spec(w), own_spec(w)]
    for item in matrices:
        operands += list(item)
        in_specs += [whole] * 4
    out_specs = [table_spec(0), table_spec(1)]
    out_shape = [jax.ShapeDtypeStruct((vocab, width), FLOAT)] * 2
    for w in range(2):
        out_specs += [own_spec(w)] * 2
        out_shape += [state] * 2
    for item in matrices:
        out_specs += [whole] * 3
        out_shape += [jax.ShapeDtypeStruct(item[0].shape, FLOAT)] * 3
    results = pl.pallas_call(
        kernel,
        grid=(steps,),
        in_specs=in_specs,
        out_specs=out_specs,
        out_shape=out_shape,
        scratch_shapes=[pltpu.VMEM((8, 128), FLOAT)]
        + [pltpu.VMEM((tiles * tile + 8, width), FLOAT)] * 2
        + [pltpu.SemaphoreType.DMA((2, 2, tiles))],
        compiler_params=pltpu.CompilerParams(vmem_limit_bytes=VMEM_LIMIT),
    )(*operands)
    tables_out = [(results[w], *results[2 + 2 * w : 4 + 2 * w]) for w in range(2)]
    return tables_out, [results[6 + 3 * i : 9 + 3 * i] for i in range(count)]


def shards(
    token_ids,
    loss_mask,
    lengths,
    buffer_ids,
    embed_table,
    embed_moment,
    embed_average,
    head_table,
    head_moment,
    head_average,
    in_weights,
    in_moment,
    in_average,
    out_weights,
    out_moment,
    out_average,
    vectors,
    vector_moment,
    vector_average,
):
    groups = lax.axis_size("fsdp")
    replicas = lax.axis_size("dp")
    member = lax.axis_index("fsdp")
    replica = lax.axis_index("dp")
    batches, _, seq = token_ids.shape
    vocab_rows, width = embed_table.shape
    head_size = width // HEADS
    vocab_start = member * vocab_rows
    own_rows = batches * seq
    rows_all = groups * own_rows

    tokens, marks, buffers = token_ids[:, 0], loss_mask[:, 0], buffer_ids[:, 0]
    divisor, offset, counted = jax.vmap(functools.partial(slot_info, buffer_count=NSEG))(
        tokens, marks, lengths[:, 0], buffers
    )
    packed = jnp.concatenate(
        [
            tokens,
            divisor,
            jnp.broadcast_to(jnp.sum(counted), (8 - 2 * batches, seq)),
        ],
        axis=0,
    )
    amount = vectors.shape[0]
    line = jnp.pad(vectors, (0, -amount % 1024)).reshape(-1, 128)
    everyone, lines, in_full, out_full, resid = start_kernel(
        packed, line, in_weights, out_weights, embed_table, batches, groups, replicas
    )
    vector_full = lines.reshape(groups, -1)[:, :amount].reshape(-1).astype(NARROW)
    embed_moment_low = lax.all_gather(embed_moment.astype(NARROW), "dp", axis=0, tiled=True)
    head_moment_low = lax.all_gather(head_moment.astype(NARROW), "dp", axis=0, tiled=True)
    tokens_all = everyone[:, :batches]
    count = jnp.maximum(jnp.sum(everyone[:, 2 * batches, 0]).astype(FLOAT), 1.0)
    divisor_all = everyone[:, batches : 2 * batches].astype(FLOAT)
    share_all = jnp.where(divisor_all > 0.5, 1.0 / jnp.maximum(divisor_all, 1.0), 0.0)
    weight_all = (share_all / count).reshape(-1)
    target_all = (
        jnp.concatenate([tokens_all[:, :, 1:], jnp.zeros_like(tokens_all[:, :, :1])], axis=2)
        .reshape(-1)
    ) - vocab_start
    tokens_flat = tokens_all.reshape(-1)
    local_all = tokens_flat - vocab_start
    inside_all = (local_all >= 0) & (local_all < vocab_rows)

    def group_part(values):
        return lax.dynamic_slice_in_dim(values, replica * rows_all, rows_all, 0)

    vector = vector_full.astype(FLOAT).reshape(1, -1)
    tables = rotary_tables(offset.reshape(-1), head_size)
    lines_of, columns_of = buffers[:, None, :], buffers[:, :, None]
    final, *kept = layer_forward(resid, in_full, out_full, vector, tables, lines_of, columns_of)
    final_grad, logsum_all, loss_part, all_hidden = head_kernel(
        head_table, final, group_part(target_all), group_part(weight_all), groups, replicas
    )

    less_weight = logsum_all - jnp.log(jnp.maximum(weight_all, 1e-30))
    shifted = jnp.where(weight_all > 0.0, less_weight, 1e30)
    chunk = min(512, rows_all)
    lists = chunk_lists(local_all, inside_all, chunk)

    token_grad, vector_grad, owner_grads = layer_backward(
        final_grad,
        resid,
        in_full,
        out_full,
        vector,
        tables,
        lines_of,
        columns_of,
        kept,
        groups,
    )
    slices = jnp.pad(vector_grad.reshape(groups, amount), ((0, 0), (0, -amount % 1024)))
    in_rows = in_weights.shape[0]
    cut = owner_grads.shape[1] - out_weights.shape[0]
    head_grad, head_square, token_grads, vector_sum, owned = head_table_grad(
        head_table,
        all_hidden,
        shifted,
        weight_all,
        target_all,
        token_grad,
        slices.reshape(groups, -1, 128),
        owner_grads,
        cut,
        groups,
        replicas,
    )
    if owned.shape != owner_grads.shape[1:]:
        owned = lax.psum(lax.psum_scatter(owner_grads, "fsdp", scatter_dimension=0), "dp")
    layer_grads = [
        owned[:cut].reshape(-1, in_rows, width).transpose(1, 0, 2).reshape(in_rows, -1),
        owned[cut:],
        vector_sum.reshape(-1)[:amount],
    ]
    embed_grad, embed_square = embed_table_grad(token_grads, *lists, vocab_rows)
    square = jnp.sum(embed_square) + jnp.sum(head_square)
    for grad in layer_grads:
        square = square + jnp.sum(grad * grad)
    line = jnp.stack([loss_part, square / replicas])[:, None]
    line = jnp.pad(jnp.broadcast_to(line, (2, 128)), ((0, 6), (0, 0)))
    scalars = exchange_scalars(line, groups, replicas)
    pair = jnp.sum(scalars[:, :2, 0], axis=0)
    loss = pair[0]
    grad_norm = jnp.sqrt(pair[1])
    base = math.sqrt(NPARAM) / CLIP_LEVEL
    root = math.sqrt(width)

    def row(values):
        return values.reshape(1, -1)

    (embed, head), (inner, outer, vector) = update_all(
        scalars,
        [
            (embed_table, embed_grad, embed_moment_low, embed_moment, embed_average),
            (head_table, head_grad, head_moment_low, head_moment, head_average),
        ],
        [
            (in_weights, layer_grads[0], in_moment, in_average),
            (out_weights, layer_grads[1], out_moment, out_average),
            tuple(map(row, (vectors, layer_grads[2], vector_moment, vector_average))),
        ],
        (base, base / root, base / root, base / root, 0.3 * base),
    )
    vector = [values.reshape(-1) for values in vector]
    return (*embed, *head, *inner, *outer, *vector, loss, grad_norm)


def solution(mesh):
    placed = (
        P(None, ("dp", "fsdp"), None),
        P(None, ("dp", "fsdp"), None),
        P(None, ("dp", "fsdp")),
        P(None, ("dp", "fsdp"), None),
        P("fsdp", None),
        P(("fsdp", "dp"), None),
        P(("fsdp", "dp"), None),
        P("fsdp", None),
        P(("fsdp", "dp"), None),
        P(("fsdp", "dp"), None),
        P("fsdp", None),
        P("fsdp", None),
        P("fsdp", None),
        P("fsdp", None),
        P("fsdp", None),
        P("fsdp", None),
        P("fsdp"),
        P("fsdp"),
        P("fsdp"),
    )
    return jax.shard_map(
        shards,
        mesh=mesh,
        in_specs=placed,
        out_specs=(
            P("fsdp", None),
            P(("fsdp", "dp"), None),
            P(("fsdp", "dp"), None),
            P("fsdp", None),
            P(("fsdp", "dp"), None),
            P(("fsdp", "dp"), None),
            P("fsdp", None),
            P("fsdp", None),
            P("fsdp", None),
            P("fsdp", None),
            P("fsdp", None),
            P("fsdp", None),
            P("fsdp"),
            P("fsdp"),
            P("fsdp"),
            P(),
            P(),
        ),
        check_vma=False,
    )
```

```python
import functools
import math

import jax
import jax.numpy as jnp
from jax import lax
from jax.experimental import pallas as pl
from jax.experimental.pallas import tpu as pltpu
from jax.sharding import PartitionSpec as P

HEADS = 8
NPARAM = 54664704
NSEG = 3


EPSILON = 1e-05
CLIP_LEVEL = 0.002
MOMENTUM = 0.5
DECAY = 0.5
NARROW = jnp.bfloat16
FLOAT = jnp.float32
ROWS_CONTRACT = (((0,), (0,)), ((), ()))
LAST_CONTRACT = (((1,), (1,)), ((), ()))


VMEM_LIMIT = 60 * 2**20


def slot_info(tokens, marks, length, buffers, buffer_count):
    seq = tokens.shape[0]
    places = jnp.arange(seq, dtype=jnp.int32)
    same_buffer = jnp.concatenate([buffers[1:] == buffers[:-1], jnp.zeros((1,), dtype=bool)])
    valid = jnp.where((marks == 1) & (places + 1 < length) & same_buffer, 1.0, 0.0).astype(FLOAT)
    member = buffers[None, :] == jnp.arange(buffer_count, dtype=jnp.int32)[:, None]
    weights = jnp.where(member, 1.0, 0.0).astype(FLOAT)
    tally = jnp.sum(weights * valid[None, :], axis=1)
    divisor = valid * jnp.sum(weights * tally[:, None], axis=0)
    counted = jnp.sum(jnp.where(tally > 0.5, 1.0, 0.0).astype(FLOAT))
    first = jnp.min(jnp.where(member, places[None, :], seq), axis=1)
    offset = places - jnp.sum(jnp.where(member, first[:, None], 0), axis=0)
    return (divisor.astype(jnp.int32), offset, counted.astype(jnp.int32))


def rotary_tables(offset, head_size):
    rot = head_size // 4
    half = rot // 2
    lanes = 128
    freqs = jnp.power(10000.0, -2.0 * jnp.arange(half, dtype=FLOAT) / rot)
    angles = offset.astype(FLOAT)[:, None] * freqs[None, :]
    cosine, sine = jnp.cos(angles), jnp.sin(angles)
    rows = offset.shape[0]
    rest = head_size - rot
    ones, none = jnp.ones((rows, rest), FLOAT), jnp.zeros((rows, rest), FLOAT)
    blank = jnp.zeros((rows, half), FLOAT)
    stay = jnp.concatenate([cosine, cosine, ones], axis=1)
    ahead = jnp.concatenate([-sine, blank, none], axis=1)
    behind = jnp.concatenate([blank, sine, none], axis=1)
    return [
        jnp.concatenate([part] * (lanes // head_size), axis=1) for part in (stay, ahead, behind)
    ]


def wide_tables(refs, width):
    return [jnp.concatenate([ref[...]] * (width // ref.shape[1]), axis=1) for ref in refs]


def norm_unit(values):
    mean = jnp.mean(values, axis=-1, keepdims=True)
    centred = values - mean
    scale = lax.rsqrt(jnp.mean(centred * centred, axis=-1, keepdims=True) + EPSILON)
    return (centred * scale, scale)


def norm_back(scaled, unit, scale):
    return scale * (
        scaled
        - jnp.mean(scaled, axis=-1, keepdims=True)
        - unit * jnp.mean(scaled * unit, axis=-1, keepdims=True)
    )


def vector_spans(width, hidden):
    amounts = [width] * 6 + [3 * width, width, hidden, width]
    spans = []
    begin = 0
    for amount in amounts:
        spans.append(slice(begin, begin + amount))
        begin = begin + amount
    return spans


def masked_probs(queries, keys, mask, factor):
    scores = lax.dot_general(queries, keys, LAST_CONTRACT, preferred_element_type=FLOAT) * factor
    scores = jnp.where(mask, scores, -1e30)
    top = jnp.max(scores, axis=-1, keepdims=True)
    logsum = top + jnp.log(jnp.sum(jnp.exp(scores - top), axis=-1, keepdims=True))
    return jnp.exp(scores - logsum)


def slot_mask(line_ref, column_ref, b, seq):
    later = lax.broadcasted_iota(jnp.int32, (seq, seq), 1)
    place = lax.broadcasted_iota(jnp.int32, (seq, seq), 0)
    return (column_ref[b] == line_ref[b]) & (later <= place)


def layer_forward(resid, in_full, out_full, vector, tables, lines, columns):
    rows, width = resid.shape
    hidden = out_full.shape[0] - width
    batches, _, seq = lines.shape
    head_size = width // HEADS
    half = head_size // 8
    factor = 1.0 / math.sqrt(head_size)
    spans = vector_spans(width, hidden)

    def kernel(
        resid_ref,
        in_ref,
        out_ref,
        vector_ref,
        stay_ref,
        ahead_ref,
        behind_ref,
        line_ref,
        column_ref,
        final_ref,
        qkv_ref,
        pre_ref,
        joined_ref,
        last_ref,
    ):
        def part(i):
            return vector_ref[:, spans[i]]

        start = resid_ref[...]
        unit, _ = norm_unit(start)
        input_one = (unit * part(0) + part(1)).astype(NARROW)
        input_two = (unit * part(2) + part(3)).astype(NARROW)
        stay, ahead, behind = wide_tables((stay_ref, ahead_ref, behind_ref), width)
        bias = part(6)
        for i in range(3):
            span = slice(i * width, (i + 1) * width)
            values = jnp.dot(input_one, in_ref[:, span], preferred_element_type=FLOAT)
            values = values + bias[:, span]
            if i < 2:
                values = (
                    values * stay
                    + pltpu.roll(values, width - half, 1) * ahead
                    + pltpu.roll(values, half, 1) * behind
                )
            qkv_ref[:, span] = values.astype(NARROW)
        for b in range(batches):
            mask = slot_mask(line_ref, column_ref, b, seq)
            there = slice(b * seq, (b + 1) * seq)
            for head in range(HEADS):
                first = head * head_size
                queries, keys, values = [
                    qkv_ref[there, i * width + first : i * width + first + head_size]
                    for i in range(3)
                ]
                probs = masked_probs(queries, keys, mask, factor).astype(NARROW)
                joined_ref[there, first : first + head_size] = jnp.dot(
                    probs, values, preferred_element_type=FLOAT
                ).astype(NARROW)
        bias = part(8)
        for i in range(hidden // width):
            span = slice(i * width, (i + 1) * width)
            pre = (
                jnp.dot(
                    input_two,
                    in_ref[:, (3 + i) * width : (4 + i) * width],
                    preferred_element_type=FLOAT,
                )
                + bias[:, span]
            )
            pre_ref[:, span] = pre
            joined_ref[:, (1 + i) * width : (2 + i) * width] = (
                0.5 * pre * (1.0 + lax.erf(pre * 0.7071067811865476))
            ).astype(NARROW)
        last = (
            start
            + jnp.dot(joined_ref[...], out_ref[...], preferred_element_type=FLOAT)
            + part(7)
            + part(9)
        )
        last_ref[...] = last
        unit_last, _ = norm_unit(last)
        final_ref[...] = (unit_last * part(4) + part(5)).astype(NARROW)

    return pl.pallas_call(
        kernel,
        out_shape=[
            jax.ShapeDtypeStruct((rows, width), NARROW),
            jax.ShapeDtypeStruct((rows, 3 * width), NARROW),
            jax.ShapeDtypeStruct((rows, hidden), FLOAT),
            jax.ShapeDtypeStruct((rows, width + hidden), NARROW),
            jax.ShapeDtypeStruct((rows, width), FLOAT),
        ],
        compiler_params=pltpu.CompilerParams(vmem_limit_bytes=VMEM_LIMIT),
    )(resid, in_full, out_full, vector, *tables, lines, columns)


def layer_backward(
    final_grad, resid, in_full, out_full, vector, tables, lines, columns, kept, groups
):
    rows, width = resid.shape
    hidden = out_full.shape[0] - width
    batches, _, seq = lines.shape
    head_size = width // HEADS
    half = head_size // 8
    factor = 1.0 / math.sqrt(head_size)
    spans = vector_spans(width, hidden)
    blocks = in_full.shape[1] // width
    in_rows = width // groups
    out_rows = out_full.shape[0] // groups
    first_out = blocks * in_rows
    shard = first_out + out_rows

    def kernel(
        final_grad_ref,
        resid_ref,
        in_ref,
        out_ref,
        vector_ref,
        stay_ref,
        ahead_ref,
        behind_ref,
        line_ref,
        column_ref,
        qkv_ref,
        pre_ref,
        joined_ref,
        last_ref,
        token_ref,
        small_ref,
        owners_ref,
        owners,
        low,
        wide,
        sems,
    ):
        def part(i):
            return vector_ref[:, spans[i]]

        def column_sum(i, values):
            small_ref[:, spans[i]] = jnp.sum(values, axis=0, keepdims=True)

        final_grad_in = final_grad_ref[...]
        unit_last, scale_last = norm_unit(last_ref[...])
        column_sum(4, final_grad_in * unit_last)
        column_sum(5, final_grad_in)
        grad_out = norm_back(final_grad_in * part(4), unit_last, scale_last)
        column_sum(7, grad_out)
        column_sum(9, grad_out)
        grad_low = grad_out.astype(NARROW)
        for c in range((width + hidden) // width):
            there = slice(c * width, (c + 1) * width)
            piece = lax.dot_general(
                joined_ref[:, there], grad_low, ROWS_CONTRACT, preferred_element_type=FLOAT
            )
            at = c * width
            while at < (c + 1) * width:
                owner, row = at // out_rows, at % out_rows
                size = min(out_rows - row, (c + 1) * width - at)
                owners[owner, first_out + row : first_out + row + size, :] = piece[
                    at - c * width : at - c * width + size
                ]
                at = at + size
        out_copy = pltpu.make_async_copy(
            owners.at[:, pl.ds(first_out, out_rows), :],
            owners_ref.at[:, pl.ds(first_out, out_rows), :],
            sems.at[0],
        )
        out_copy.start()
        unit, scale = norm_unit(resid_ref[...])
        input_one = (unit * part(0) + part(1)).astype(NARROW)
        input_two = (unit * part(2) + part(3)).astype(NARROW)

        def in_piece(inputs, c, grads):
            piece = lax.dot_general(
                inputs, grads, ROWS_CONTRACT, preferred_element_type=FLOAT
            )
            for owner in range(groups):
                owners[owner, c * in_rows : (c + 1) * in_rows, :] = piece[
                    owner * in_rows : (owner + 1) * in_rows
                ]

        back_two = jnp.zeros((rows, width), FLOAT)
        bias_sums = []
        for i in range(hidden // width):
            grads = lax.dot_general(
                grad_low,
                out_ref[(1 + i) * width : (2 + i) * width, :],
                LAST_CONTRACT,
                preferred_element_type=FLOAT,
            )
            pre = pre_ref[:, i * width : (i + 1) * width]
            slope = (
                0.5 * (1.0 + lax.erf(pre * 0.7071067811865476))
                + pre * jnp.exp(-0.5 * pre * pre) * 0.3989422804014327
            )
            grads = grads * slope
            bias_sums.append(jnp.sum(grads, axis=0, keepdims=True))
            grads = grads.astype(NARROW)
            in_piece(input_two, 3 + i, grads)
            back_two = back_two + lax.dot_general(
                grads,
                in_ref[:, (3 + i) * width : (4 + i) * width],
                LAST_CONTRACT,
                preferred_element_type=FLOAT,
            )
        small_ref[:, spans[8]] = jnp.concatenate(bias_sums, axis=1)
        low[...] = lax.dot_general(
            grad_low, out_ref[:width, :], LAST_CONTRACT, preferred_element_type=FLOAT
        ).astype(NARROW)
        for b in range(batches):
            mask = slot_mask(line_ref, column_ref, b, seq)
            there = slice(b * seq, (b + 1) * seq)
            for head in range(HEADS):
                first = head * head_size
                at = [
                    slice(i * width + first, i * width + first + head_size) for i in range(3)
                ]
                queries, keys, values = [qkv_ref[there, at[i]] for i in range(3)]
                mixed = low[there, first : first + head_size]
                probs = masked_probs(queries, keys, mask, factor)
                back = lax.dot_general(
                    mixed, values, LAST_CONTRACT, preferred_element_type=FLOAT
                )
                wide[there, at[2]] = lax.dot_general(
                    probs.astype(NARROW), mixed, ROWS_CONTRACT, preferred_element_type=FLOAT
                )
                scores = (
                    probs
                    * (back - jnp.sum(probs * back, axis=-1, keepdims=True))
                    * factor
                ).astype(NARROW)
                wide[there, at[0]] = jnp.dot(scores, keys, preferred_element_type=FLOAT)
                wide[there, at[1]] = lax.dot_general(
                    scores, queries, ROWS_CONTRACT, preferred_element_type=FLOAT
                )
        stay, ahead, behind = wide_tables((stay_ref, ahead_ref, behind_ref), width)
        back_one = jnp.zeros((rows, width), FLOAT)
        bias_sums = []
        for i in range(3):
            span = slice(i * width, (i + 1) * width)
            grads = wide[:, span]
            if i < 2:
                grads = (
                    grads * stay
                    + pltpu.roll(grads * ahead, half, 1)
                    + pltpu.roll(grads * behind, width - half, 1)
                )
            bias_sums.append(jnp.sum(grads, axis=0, keepdims=True))
            grads = grads.astype(NARROW)
            in_piece(input_one, i, grads)
            back_one = back_one + lax.dot_general(
                grads, in_ref[:, span], LAST_CONTRACT, preferred_element_type=FLOAT
            )
        in_copy = pltpu.make_async_copy(
            owners.at[:, pl.ds(0, first_out), :],
            owners_ref.at[:, pl.ds(0, first_out), :],
            sems.at[1],
        )
        in_copy.start()
        small_ref[:, spans[6]] = jnp.concatenate(bias_sums, axis=1)
        column_sum(0, back_one * unit)
        column_sum(1, back_one)
        column_sum(2, back_two * unit)
        column_sum(3, back_two)
        token_ref[...] = (
            grad_out + norm_back(back_one * part(0) + back_two * part(2), unit, scale)
        ).astype(NARROW)
        out_copy.wait()
        in_copy.wait()

    whole = pl.BlockSpec(memory_space=pltpu.VMEM)
    return pl.pallas_call(
        kernel,
        in_specs=[whole] * 14,
        out_specs=[whole, whole, pl.BlockSpec(memory_space=pl.ANY)],
        out_shape=[
            jax.ShapeDtypeStruct((rows, width), NARROW),
            jax.ShapeDtypeStruct(vector.shape, FLOAT),
            jax.ShapeDtypeStruct((groups, shard, width), FLOAT),
        ],
        scratch_shapes=[
            pltpu.VMEM((groups, shard, width), FLOAT),
            pltpu.VMEM((rows, width), NARROW),
            pltpu.VMEM((rows, 3 * width), FLOAT),
            pltpu.SemaphoreType.DMA((2,)),
        ],
        compiler_params=pltpu.CompilerParams(vmem_limit_bytes=VMEM_LIMIT),
    )(final_grad, resid, in_full, out_full, vector, *tables, lines, columns, *kept)


def block_rows(rows, cap):
    best = rows
    for size in range(8, cap + 1, 8):
        if rows % size == 0:
            best = size
    return best


MESH = pl.DeviceIdType.MESH


def meet(peers):
    barrier = pltpu.get_barrier_semaphore()
    for peer in peers:
        pl.semaphore_signal(barrier, inc=1, device_id=peer, device_id_type=MESH)
    pl.semaphore_wait(barrier, len(peers))


class Place:
    def __init__(self, groups, replicas):
        self.groups = groups
        self.replicas = replicas
        self.chips = groups // 2
        self.replica = lax.axis_index("dp")
        self.member = lax.axis_index("fsdp")
        self.chip = self.member // 2
        self.core = self.member % 2
        self.sibling_member = self.chip * 2 + 1 - self.core

    def lane_chip(self, step):
        return lax.rem(self.chip + step, self.chips)

    def at(self, replica, member):
        return {"dp": replica, "fsdp": member}

    def lane(self, step):
        return self.at(self.replica, self.lane_chip(step) * 2 + self.core)

    def plane_replica(self, step):
        return lax.rem(self.replica + step, self.replicas)

    def plane(self, step):
        return self.at(self.plane_replica(step), self.member)

    def sibling(self):
        return self.at(self.replica, self.sibling_member)

    def lanes(self):
        return [self.lane(step) for step in range(1, self.chips)]

    def planes(self):
        return [self.plane(step) for step in range(1, self.replicas)]


def remote(source, target, send, recv, device):
    return pltpu.make_async_remote_copy(
        src_ref=source,
        dst_ref=target,
        send_sem=send,
        recv_sem=recv,
        device_id=device,
        device_id_type=MESH,
    )


def start_kernel(
    packed, line, in_shard, out_shard, table, head, batches, groups, replicas
):
    vocab, width = table.shape
    seq = packed.shape[1]
    own = batches * seq
    chips = groups // 2
    amount = groups * replicas
    shards_in = (in_shard, out_shard)
    split = all(shard.shape[0] % (16 * replicas) == 0 for shard in shards_in)
    pieces = replicas if split else 1
    unroll = 8

    def kernel(
        packed_ref,
        line_ref,
        in_ref,
        out_ref,
        table_ref,
        head_ref,
        every_ref,
        lines_ref,
        in_full,
        out_full,
        resid_ref,
        aims_ref,
        in_low,
        out_low,
        wide,
        looked,
        to_core,
        from_core,
        to_lane,
        from_lane,
        ids,
        table_sem,
        ids_sem,
        local_sem,
        meta_send,
        meta_recv,
        line_send,
        line_recv,
        lane_send,
        lane_recv,
        plane_send,
        plane_recv,
        core_send,
        core_recv,
        part_send,
        part_recv,
        sum_send,
        sum_recv,
    ):
        place = Place(groups, replicas)
        member = place.member
        core = place.core
        replica = place.replica
        me = replica * groups + member
        fulls = (in_full, out_full)
        lows = (in_low, out_low)

        def device(index):
            return place.at(index // groups, lax.rem(index, groups))

        def chip_at(j):
            return lax.rem(place.chip + j, chips)

        def chip_before(j):
            return lax.rem(place.chip + chips - j, chips)

        def replica_before(k):
            return lax.rem(replica + replicas - k, replicas)

        def lane_device(j):
            return place.at(replica, chip_at(j) * 2 + core)

        def plane_device(k):
            return place.at(lax.rem(replica + k, replicas), member)

        def meta_copy(k):
            return remote(
                packed_ref,
                every_ref.at[me],
                meta_send.at[k],
                meta_recv.at[k],
                device(lax.rem(me + k, amount)),
            )

        def line_copy(k):
            return remote(
                line_ref,
                lines_ref.at[member],
                line_send.at[k],
                line_recv.at[k],
                place.at(replica, lax.rem(member + k, groups)),
            )

        def piece(w, slot, from_replica):
            full = fulls[w]
            if not split:
                return full.at[slot]
            rows = full.shape[1] // pieces
            return full.at[slot, pl.ds(pl.multiple_of(from_replica * rows, 16), rows), :]

        def own_piece(w):
            low = lows[w]
            if not split:
                return low
            rows = low.shape[0] // pieces
            return low.at[pl.ds(pl.multiple_of(replica * rows, 16), rows), :]

        def lane_copy(w, j):
            return remote(
                own_piece(w),
                piece(w, member, replica),
                lane_send.at[w, j],
                lane_recv.at[w, j],
                lane_device(j),
            )

        def lane_wait(w, j):
            there = piece(w, chip_before(j) * 2 + core, replica)
            remote(
                there, there, lane_send.at[w, j], lane_recv.at[w, j], lane_device(j)
            ).wait_recv()

        def plane_copy(w, k, j):
            there = piece(w, chip_before(j) * 2 + core, replica)
            return remote(
                there, there, plane_send.at[w, k, j], plane_recv.at[w, k, j], plane_device(k)
            )

        def plane_wait(w, k, j):
            there = piece(w, chip_before(j) * 2 + core, replica_before(k))
            remote(
                there, there, plane_send.at[w, k, j], plane_recv.at[w, k, j], plane_device(k)
            ).wait_recv()

        def core_copy(w, j):
            here = fulls[w].at[chip_before(j) * 2 + core]
            return remote(here, here, core_send.at[w, j], core_recv.at[w, j], place.sibling())

        def own_core_copy(w):
            return remote(
                lows[w],
                fulls[w].at[member],
                core_send.at[w, 0],
                core_recv.at[w, 0],
                place.sibling(),
            )

        def core_wait(w, j):
            there = fulls[w].at[chip_before(j) * 2 + 1 - core]
            remote(
                there, there, core_send.at[w, j], core_recv.at[w, j], place.sibling()
            ).wait_recv()

        def part_copy(j):
            return remote(
                to_core.at[j], from_core.at[j], part_send.at[j], part_recv.at[j], place.sibling()
            )

        def sum_copy(j):
            return remote(
                to_lane.at[j], from_lane.at[j], sum_send.at[j], sum_recv.at[j], lane_device(j)
            )

        fetch = pltpu.make_async_copy(table_ref, wide, table_sem)
        fetch.start()
        barrier = pltpu.get_barrier_semaphore()

        def greet(k, carry):
            pl.semaphore_signal(
                barrier, inc=1, device_id=device(lax.rem(me + k, amount)), device_id_type=MESH
            )
            return carry

        lax.fori_loop(1, amount, greet, 0)
        in_low[...] = in_ref[...].astype(NARROW)
        out_low[...] = out_ref[...].astype(NARROW)
        every_ref[me] = packed_ref[...]
        lines_ref[member] = line_ref[...]
        pl.semaphore_wait(barrier, amount - 1)

        def tell(k, carry):
            meta_copy(k).start()
            return carry

        lax.fori_loop(1, amount, tell, 0)
        for k in range(1, groups):
            line_copy(k).start()
        for w in range(2):
            for j in range(1, chips):
                lane_copy(w, j).start()
            own_core_copy(w).start()
        kept = [
            pltpu.make_async_copy(lows[w], fulls[w].at[member], local_sem.at[w])
            for w in range(2)
        ]
        for copy in kept:
            copy.start()

        def hear(k, carry):
            there = every_ref.at[lax.rem(me + amount - k, amount)]
            remote(there, there, meta_send.at[k], meta_recv.at[k], device(me)).wait_recv()
            return carry

        lax.fori_loop(1, amount, hear, 0)
        load = pltpu.make_async_copy(
            every_ref.at[pl.ds(replica * groups, groups)], ids, ids_sem
        )
        load.start()
        load.wait()
        fetch.wait()
        start = member * vocab

        def look(slot, ahead):
            for b in range(batches):

                def lap(i, carry):
                    for u in range(unroll):
                        spot = i * unroll + u
                        token = ids[slot, b, jnp.minimum(spot + ahead, seq - 1)]
                        row = jnp.where(spot + ahead < seq, token, 0) - start
                        inside = (row >= 0) & (row < vocab)
                        safe = jnp.where(inside, row, 0)
                        keep = jnp.where(inside, 1.0, 0.0)
                        looked[pl.ds(b * seq + spot, 1), :] = wide[pl.ds(safe, 1), :] * keep
                    return carry

                lax.fori_loop(0, seq // unroll, lap, 0)
            return looked[...].astype(NARROW)

        def lap(step, carry):
            j = lax.rem(step + 1, chips)
            there = chip_at(j) * 2

            @pl.when(step == chips // 2)
            def _():
                for w in range(2):
                    for c in range(1, chips):
                        lane_wait(w, c)
                        if split:
                            for k in range(1, replicas):
                                plane_copy(w, k, c).start()

            to_core[j] = look(there + 1 - core, 0)
            part_copy(j).start()
            mine = look(there + core, 0).astype(FLOAT)
            part_copy(j).wait_recv()
            mine = mine + from_core[j].astype(FLOAT)

            @pl.when(j > 0)
            def _():
                to_lane[j] = mine.astype(NARROW)
                sum_copy(j).start()

            @pl.when(j == 0)
            def _():
                resid_ref[...] = mine

            return carry

        lax.fori_loop(0, chips, lap, 0)
        again = pltpu.make_async_copy(head_ref, wide, table_sem)
        again.start()
        again.wait()

        def aim(slot, carry):
            aims_ref[slot] = look(slot, 1)
            return carry

        lax.fori_loop(0, groups, aim, 0)
        for j in range(1, chips):
            sum_copy(j).wait_recv()
            resid_ref[...] += from_lane[j].astype(FLOAT)
        for w in range(2):
            for j in range(1, chips):
                if split:
                    for k in range(1, replicas):
                        plane_wait(w, k, j)
                core_copy(w, j).start()
        for w in range(2):
            kept[w].wait()
            for j in range(chips):
                core_wait(w, j)
                if j == 0:
                    own_core_copy(w).wait_send()
                else:
                    core_copy(w, j).wait_send()
                    lane_copy(w, j).wait_send()
                if split and j > 0:
                    for k in range(1, replicas):
                        plane_copy(w, k, j).wait_send()
        for k in range(1, groups):
            there = lines_ref.at[lax.rem(member + groups - k, groups)]
            remote(
                there, there, line_send.at[k], line_recv.at[k], place.at(replica, member)
            ).wait_recv()
            line_copy(k).wait_send()
        for j in range(chips):
            part_copy(j).wait_send()
            if j > 0:
                sum_copy(j).wait_send()

        def told(k, carry):
            meta_copy(k).wait_send()
            return carry

        lax.fori_loop(1, amount, told, 0)

    whole = pl.BlockSpec(memory_space=pltpu.VMEM)
    anywhere = pl.BlockSpec(memory_space=pl.ANY)
    dma = pltpu.SemaphoreType.DMA
    vmem = pltpu.VMEM
    every, lines, in_full, out_full, resid, aims = pl.pallas_call(
        kernel,
        in_specs=[whole, whole, whole, whole, anywhere, anywhere],
        out_specs=[whole, whole, anywhere, anywhere, whole, whole],
        out_shape=[
            jax.ShapeDtypeStruct((amount,) + packed.shape, jnp.int32),
            jax.ShapeDtypeStruct((groups,) + line.shape, FLOAT),
            jax.ShapeDtypeStruct((groups,) + in_shard.shape, NARROW),
            jax.ShapeDtypeStruct((groups,) + out_shard.shape, NARROW),
            jax.ShapeDtypeStruct((own, width), FLOAT),
            jax.ShapeDtypeStruct((groups, own, width), NARROW),
        ],
        scratch_shapes=[
            vmem(in_shard.shape, NARROW),
            vmem(out_shard.shape, NARROW),
            vmem((vocab, width), FLOAT),
            vmem((own, width), FLOAT),
            vmem((chips, own, width), NARROW),
            vmem((chips, own, width), NARROW),
            vmem((chips, own, width), NARROW),
            vmem((chips, own, width), NARROW),
            pltpu.SMEM((groups,) + packed.shape, jnp.int32),
            dma,
            dma,
            dma((2,)),
            dma((amount,)),
            dma((amount,)),
            dma((groups,)),
            dma((groups,)),
            dma((2, chips)),
            dma((2, chips)),
            dma((2, replicas, chips)),
            dma((2, replicas, chips)),
            dma((2, chips)),
            dma((2, chips)),
            dma((chips,)),
            dma((chips,)),
            dma((chips,)),
            dma((chips,)),
        ],
        compiler_params=pltpu.CompilerParams(
            vmem_limit_bytes=VMEM_LIMIT, collective_id=4, has_side_effects=True
        ),
        cost_estimate=pl.CostEstimate(
            flops=0, bytes_accessed=vocab * width * 4, transcendentals=0
        ),
    )(packed, line, in_shard, out_shard, table, head)
    return (
        every,
        lines,
        in_full.reshape(-1, in_shard.shape[1]),
        out_full.reshape(-1, out_shard.shape[1]),
        resid,
        aims,
    )


def head_kernel(table, own_hidden, aims, target, weight, groups, replicas):
    vocab, width = table.shape
    own = own_hidden.shape[0]
    block = block_rows(vocab, 1100)
    blocks = vocab // block
    chips = groups // 2
    lines = -(-blocks // 8) * 8

    def kernel(
        table_ref,
        own_ref,
        aims_ref,
        target_ref,
        weight_ref,
        grad_ref,
        logsum_ref,
        loss_ref,
        all_ref,
        wide,
        low,
        hid,
        exps,
        tops,
        totals,
        shares,
        to_core,
        from_core,
        to_lane,
        from_lane,
        aim_core,
        aim_lane,
        aim_from,
        table_sem,
        local_sem,
        lane_send,
        lane_recv,
        core_send,
        core_recv,
        plane_send,
        plane_recv,
        pass_send,
        pass_recv,
        stat_send,
        stat_recv,
        line_send,
        line_recv,
        part_send,
        part_recv,
        sum_send,
        sum_recv,
        aim_half_send,
        aim_half_recv,
        aim_send,
        aim_recv,
    ):
        place = Place(groups, replicas)
        me = place.member
        core = place.core

        def table_copy(b):
            return pltpu.make_async_copy(
                table_ref.at[pl.ds(b * block, block), :], wide.at[b % 2], table_sem.at[b % 2]
            )

        def chip_at(j):
            return lax.rem(place.chip + j, chips)

        def chip_before(j):
            return lax.rem(place.chip + chips - j, chips)

        def lane_device(j):
            return place.at(place.replica, chip_at(j) * 2 + core)

        def plane_device(k):
            return place.at(lax.rem(place.replica + k, replicas), me)

        def replica_before(k):
            return lax.rem(place.replica + replicas - k, replicas)

        def lane_copy(j):
            return remote(own_ref, hid.at[me], lane_send.at[j], lane_recv.at[j], lane_device(j))

        def lane_slot(j):
            return chip_before(j) * 2 + core

        def lane_wait(j):
            there = hid.at[lane_slot(j)]
            remote(there, there, lane_send.at[j], lane_recv.at[j], lane_device(j)).wait_recv()

        def core_copy(j):
            here = hid.at[lane_slot(j)]
            return remote(here, here, core_send.at[j], core_recv.at[j], place.sibling())

        def core_wait(j):
            there = hid.at[chip_before(j) * 2 + 1 - core]
            remote(there, there, core_send.at[j], core_recv.at[j], place.sibling()).wait_recv()

        def plane_copy(k, j):
            slot = lane_slot(j)
            return remote(
                hid.at[slot],
                all_ref.at[place.replica * groups + slot],
                plane_send.at[k, j],
                plane_recv.at[k, j],
                plane_device(k),
            )

        def plane_wait(k, j):
            there = all_ref.at[replica_before(k) * groups + lane_slot(j)]
            remote(
                there, there, plane_send.at[k, j], plane_recv.at[k, j], plane_device(k)
            ).wait_recv()

        def pass_copy(k, j):
            here = all_ref.at[replica_before(k) * groups + lane_slot(j)]
            return remote(
                here, here, pass_send.at[k, j], pass_recv.at[k, j], place.sibling()
            )

        def pass_wait(k, j):
            there = all_ref.at[
                replica_before(k) * groups + chip_before(j) * 2 + 1 - core
            ]
            remote(
                there, there, pass_send.at[k, j], pass_recv.at[k, j], place.sibling()
            ).wait_recv()

        def member_at(k):
            return lax.rem(me + k, groups)

        def stat_copy(k):
            return remote(
                shares.at[me],
                shares.at[me],
                stat_send.at[k],
                stat_recv.at[k],
                place.at(place.replica, member_at(k)),
            )

        def stat_wait(k):
            there = shares.at[lax.rem(me + groups - k, groups)]
            remote(
                there, there, stat_send.at[k], stat_recv.at[k], place.at(place.replica, me)
            ).wait_recv()

        def line_copy(k):
            here = logsum_ref.at[place.replica]
            return remote(here, here, line_send.at[k], line_recv.at[k], plane_device(k))

        def line_wait(k):
            there = logsum_ref.at[replica_before(k)]
            remote(there, there, line_send.at[k], line_recv.at[k], plane_device(k)).wait_recv()

        def part_copy(j):
            return remote(
                to_core.at[j], from_core.at[j], part_send.at[j], part_recv.at[j], place.sibling()
            )

        def sum_copy(j):
            return remote(
                to_lane.at[j], from_lane.at[j], sum_send.at[j], sum_recv.at[j], lane_device(j)
            )

        def aim_half(c):
            return remote(
                aims_ref.at[c * 2 + 1 - core],
                aim_core.at[c],
                aim_half_send.at[c],
                aim_half_recv.at[c],
                place.sibling(),
            )

        def aim_copy(j):
            return remote(
                aim_lane.at[j], aim_from.at[j], aim_send.at[j], aim_recv.at[j], lane_device(j)
            )

        table_copy(0).start()
        if blocks > 1:
            table_copy(1).start()
        meet(
            [place.at(place.replica, member_at(k)) for k in range(1, groups)] + place.planes()
        )
        own_core = remote(own_ref, hid.at[me], core_send.at[0], core_recv.at[0], place.sibling())
        own_core.start()
        for j in range(1, chips):
            lane_copy(j).start()
        hid[me] = own_ref[...]
        for k in range(1, replicas):
            plane_copy(k, 0).start()
        for c in range(chips):
            aim_half(c).start()
        for b in range(blocks):
            table_copy(b).wait()
            low[b] = wide[b % 2].astype(NARROW)
            if b + 2 < blocks:
                table_copy(b + 2).start()

        spots = lax.broadcasted_iota(jnp.int32, (block, own), 0)

        def forward(step, carry):
            j = step // 2
            other = lax.rem(step, 2)

            @pl.when(step == 1)
            def _():
                there = hid.at[place.sibling_member]
                remote(
                    there, there, core_send.at[0], core_recv.at[0], place.sibling()
                ).wait_recv()

            @pl.when((step > 1) & (other == 0))
            def _():
                lane_wait(j)
                core_copy(j).start()

                def spread(k, carry):
                    plane_copy(k, j).start()
                    return carry

                lax.fori_loop(1, replicas, spread, 0)

            @pl.when((step > 1) & (other == 1))
            def _():
                core_wait(j)

            @pl.when(step == groups // 2 + 1)
            def _():
                for c in range(chips):
                    aim_half(c).wait_recv()
                for i in range(chips):
                    chip = chip_at(i)
                    aim_lane[i] = (
                        aims_ref[chip * 2 + core].astype(FLOAT) + aim_core[chip].astype(FLOAT)
                    ).astype(NARROW)
                for i in range(1, chips):
                    aim_copy(i).start()

            member = chip_before(j) * 2 + lax.rem(core + other, 2)
            here = hid[member]
            for b in range(blocks):
                logits = lax.dot_general(
                    low[b], here, LAST_CONTRACT, preferred_element_type=FLOAT
                )
                top = jnp.max(logits, axis=0, keepdims=True)
                values = jnp.exp(logits - top)
                tops[member, b : b + 1, :] = top
                totals[member, b : b + 1, :] = jnp.sum(values, axis=0, keepdims=True)
                exps[b, member] = values.astype(NARROW)
            block_tops = tops[member, :blocks, :]
            top = jnp.max(block_tops, axis=0, keepdims=True)
            total = jnp.sum(
                totals[member, :blocks, :] * jnp.exp(block_tops - top), axis=0, keepdims=True
            )
            shares[me, pl.ds(member, 1), :] = top + jnp.log(total)
            return carry

        lax.fori_loop(0, groups, forward, 0)
        local = pltpu.make_async_copy(
            hid, all_ref.at[pl.ds(place.replica * groups, groups)], local_sem
        )
        local.start()
        for k in range(1, groups):
            stat_copy(k).start()
        for k in range(1, groups):
            stat_wait(k)
        every = shares[...]
        top = jnp.max(every, axis=0)
        logsum_ref[place.replica] = top + jnp.log(jnp.sum(jnp.exp(every - top[None]), axis=0))
        for k in range(1, replicas):
            line_copy(k).start()

        def member_back(member):
            wanted = target_ref[member]
            weights = weight_ref[member]
            logsum = logsum_ref[place.replica, pl.ds(member, 1), :]
            total = jnp.zeros((own, width), FLOAT)
            for b in range(blocks):
                scale = weights * jnp.exp(tops[member, b : b + 1, :] - logsum)
                grads = exps[b, member].astype(FLOAT) * scale
                grads = jnp.where(spots == wanted - b * block, 0.0, grads)
                total = total + lax.dot_general(
                    grads.astype(NARROW), low[b], ROWS_CONTRACT, preferred_element_type=FLOAT
                )
            return total

        def backward(step, carry):
            j = lax.rem(step + 1, chips)

            @pl.when(step == chips - 1)
            def _():
                for k in range(1, replicas):
                    for c in range(chips):
                        plane_wait(k, c)
                for k in range(1, replicas):
                    for c in range(chips):
                        pass_copy(k, c).start()

            there = chip_at(j) * 2
            to_core[j] = member_back(there + 1 - core).astype(NARROW)
            part_copy(j).start()
            mine = member_back(there + core)
            part_copy(j).wait_recv()
            mine = mine + from_core[j].astype(FLOAT)

            @pl.when(j > 0)
            def _():
                to_lane[j] = mine.astype(NARROW)
                sum_copy(j).start()

            @pl.when(j == 0)
            def _():
                grad_ref[...] = mine

            return carry

        lax.fori_loop(0, chips, backward, 0)
        held = lax.broadcasted_iota(jnp.int32, (groups, own), 0) == me
        amounts = jnp.concatenate([weight_ref[m] for m in range(groups)], axis=0)

        def own_column(values):
            return jnp.sum(jnp.where(held, values, 0.0).T, axis=1, keepdims=True)

        amount = own_column(amounts)
        logsum = own_column(logsum_ref[place.replica])
        aimed = aim_lane[0].astype(FLOAT)
        for j in range(1, chips):
            aim_copy(j).wait_recv()
            aimed = aimed + aim_from[j].astype(FLOAT)
        hit = jnp.sum(own_ref[...].astype(FLOAT) * aimed, axis=1, keepdims=True)
        loss_ref[...] = amount * (logsum - hit)
        part = (amount * (jnp.exp(hit - logsum) - 1.0)).astype(NARROW).astype(FLOAT)
        total = grad_ref[...] + part * aimed
        for j in range(1, chips):
            sum_copy(j).wait_recv()
            total = total + from_lane[j].astype(FLOAT)
        grad_ref[...] = total
        local.wait()
        own_core.wait_send()
        for k in range(1, groups):
            stat_copy(k).wait_send()
        for k in range(1, replicas):
            line_wait(k)
            line_copy(k).wait_send()
            for j in range(chips):
                pass_wait(k, j)
                plane_copy(k, j).wait_send()
                pass_copy(k, j).wait_send()
        for j in range(chips):
            part_copy(j).wait_send()
            aim_half(j).wait_send()
            if j > 0:
                lane_copy(j).wait_send()
                core_copy(j).wait_send()
                sum_copy(j).wait_send()
                aim_copy(j).wait_send()

    whole = pl.BlockSpec(memory_space=pltpu.VMEM)
    anywhere = pl.BlockSpec(memory_space=pl.ANY)
    dma = pltpu.SemaphoreType.DMA
    vmem = pltpu.VMEM
    grad, logsum, loss, everyone = pl.pallas_call(
        kernel,
        in_specs=[anywhere, whole, whole, whole, whole],
        out_specs=[whole, whole, whole, anywhere],
        out_shape=[
            jax.ShapeDtypeStruct((own, width), FLOAT),
            jax.ShapeDtypeStruct((replicas, groups, own), FLOAT),
            jax.ShapeDtypeStruct((own, 1), FLOAT),
            jax.ShapeDtypeStruct((replicas * groups, own, width), NARROW),
        ],
        scratch_shapes=[
            vmem((2, block, width), FLOAT),
            vmem((blocks, block, width), NARROW),
            vmem((groups, own, width), NARROW),
            vmem((blocks, groups, block, own), NARROW),
            vmem((groups, lines, own), FLOAT),
            vmem((groups, lines, own), FLOAT),
            vmem((groups, groups, own), FLOAT),
            vmem((chips, own, width), NARROW),
            vmem((chips, own, width), NARROW),
            vmem((chips, own, width), NARROW),
            vmem((chips, own, width), NARROW),
            vmem((chips, own, width), NARROW),
            vmem((chips, own, width), NARROW),
            vmem((chips, own, width), NARROW),
            dma((2,)),
            dma,
            dma((chips,)),
            dma((chips,)),
            dma((chips,)),
            dma((chips,)),
            dma((replicas, chips)),
            dma((replicas, chips)),
            dma((replicas, chips)),
            dma((replicas, chips)),
            dma((groups,)),
            dma((groups,)),
            dma((replicas,)),
            dma((replicas,)),
            dma((chips,)),
            dma((chips,)),
            dma((chips,)),
            dma((chips,)),
            dma((chips,)),
            dma((chips,)),
            dma((chips,)),
            dma((chips,)),
        ],
        compiler_params=pltpu.CompilerParams(
            vmem_limit_bytes=VMEM_LIMIT + 2**21, collective_id=3, has_side_effects=True
        ),
        cost_estimate=pl.CostEstimate(
            flops=4 * vocab * groups * own * width,
            bytes_accessed=vocab * width * 4,
            transcendentals=vocab * groups * own,
        ),
    )(
        table,
        own_hidden,
        aims,
        target.reshape(groups, 1, own),
        weight.reshape(groups, 1, own),
    )
    return grad, logsum.reshape(-1), jnp.sum(loss), everyone.reshape(-1, width)


def head_table_grad(
    table, hidden, logsum, weights, target, token_grad, slices, owner_grads, cut, groups, replicas
):
    vocab, width = table.shape
    amount = groups * replicas
    rows = hidden.shape[0]
    own = token_grad.shape[0]
    tile = math.gcd(rows, 2048)
    block = block_rows(vocab, 1100)
    tiles = rows // tile
    steps = vocab // block
    chips = groups // 2
    last = steps - 1
    shard = owner_grads.shape[1]
    regions = ((0, cut), (cut, shard - cut))
    firsts, seconds = (replicas, chips), (chips, replicas)
    reduce = all(count % (8 * replicas) == 0 for _, count in regions)
    laps = steps * tiles

    def when(part):
        return min(int(laps * part), laps - 1)

    def kernel(
        table_ref,
        hidden_ref,
        logsum_ref,
        weight_ref,
        target_ref,
        own_ref,
        slices_ref,
        owner_ref,
        grad_ref,
        square_ref,
        all_ref,
        summed_ref,
        owned_out,
        gathered,
        owned_ref,
        from_core,
        acc_in,
        acc_out,
        one_in,
        one_out,
        two_in,
        two_out,
        piece_sem,
        half_send,
        half_recv,
        one_send,
        one_recv,
        two_send,
        two_recv,
        end_send,
        end_recv,
        local_sem,
        slice_send,
        slice_recv,
        lane_send,
        lane_recv,
        plane_send,
        plane_recv,
        core_send,
        core_recv,
    ):
        step = pl.program_id(0)
        place = Place(groups, replicas)
        me = place.replica * groups + place.member

        def slot(replica, member):
            return all_ref.at[replica * groups + member]

        def lane_copy(k):
            here = all_ref.at[me]
            return remote(own_ref, here, lane_send.at[k], lane_recv.at[k], place.lane(k))

        def lane_wait(k):
            back = lax.rem(place.chip + chips - k, chips) * 2 + place.core
            there = slot(place.replica, back)
            remote(there, there, lane_send.at[k], lane_recv.at[k], place.lane(k)).wait_recv()

        def plane_copy(k, c):
            here = slot(place.replica, c * 2 + place.core)
            return remote(here, here, plane_send.at[k, c], plane_recv.at[k, c], place.plane(k))

        def plane_wait(k, c):
            back = lax.rem(place.replica + replicas - k, replicas)
            there = slot(back, c * 2 + place.core)
            remote(
                there, there, plane_send.at[k, c], plane_recv.at[k, c], place.plane(k)
            ).wait_recv()

        def core_copy(r, c):
            here = slot(r, c * 2 + place.core)
            return remote(here, here, core_send.at[r, c], core_recv.at[r, c], place.sibling())

        def core_wait(r, c):
            there = slot(r, c * 2 + 1 - place.core)
            remote(
                there, there, core_send.at[r, c], core_recv.at[r, c], place.sibling()
            ).wait_recv()

        def device(index):
            return place.at(index // groups, lax.rem(index, groups))

        def slice_copy(k):
            there = lax.rem(me + k, amount)
            return remote(
                slices_ref.at[lax.rem(there, groups)],
                gathered.at[me],
                slice_send.at[k],
                slice_recv.at[k],
                device(there),
            )

        local = pltpu.make_async_copy(own_ref, all_ref.at[me], local_sem)
        accs, ones, twos = (acc_in, acc_out), (one_in, one_out), (two_in, two_out)

        def chip_at(j):
            return lax.rem(place.chip + j, chips)

        def pieces(g):
            first, rows = regions[g]
            size = rows // replicas
            for k in range(firsts[g]):
                for i in range(seconds[g]):
                    if g == 0:
                        chip, replica = i, place.plane_replica(k)
                    else:
                        chip, replica = chip_at(k), i
                    yield k, i, chip, pl.multiple_of(first + replica * size, 8), size

        def piece_copy(g, k, i, chip, row, size):
            return pltpu.make_async_copy(
                owner_ref.at[chip * 2 + place.core, pl.ds(row, size), :],
                accs[g].at[k, i],
                piece_sem.at[g, k, i],
            )

        def half_copy(c):
            return remote(
                owner_ref.at[c * 2 + 1 - place.core],
                from_core.at[c],
                half_send.at[c],
                half_recv.at[c],
                place.sibling(),
            )

        def partner(over_dp, k):
            if over_dp:
                return place.plane(k)
            return place.lane(k)

        def one_copy(g, k):
            return remote(
                accs[g].at[k],
                ones[g].at[k],
                one_send.at[g, k],
                one_recv.at[g, k],
                partner(g == 0, k),
            )

        def mine(g):
            return place.chip if g == 0 else place.replica

        def two_copy(g, k):
            return remote(
                accs[g].at[0, lax.rem(mine(g) + k, seconds[g])],
                twos[g].at[k],
                two_send.at[g, k],
                two_recv.at[g, k],
                partner(g == 1, k),
            )

        def end_copy(g, k, there):
            first, rows = regions[g]
            size = rows // replicas
            span = owned_ref.at[pl.ds(pl.multiple_of(first + there * size, 8), size), :]
            return remote(span, span, end_send.at[g, k], end_recv.at[g, k], place.plane(k))

        def begin_sums():
            for c in range(chips):
                half_copy(c).start()
            for g in range(2):
                for item in pieces(g):
                    piece_copy(g, *item).start()

        def begin_one():
            for c in range(chips):
                half_copy(c).wait_recv()
            for g in range(2):
                for item in pieces(g):
                    piece_copy(g, *item).wait()
                    k, i, chip, row, size = item
                    accs[g][k, i] += from_core[chip, pl.ds(row, size), :]
                for k in range(1, firsts[g]):
                    one_copy(g, k).start()

        def begin_two(g):
            for k in range(1, firsts[g]):
                one_copy(g, k).wait_recv()
            for i in range(seconds[g]):
                total = accs[g][0, i]
                for k in range(1, firsts[g]):
                    total = total + ones[g][k, i]
                accs[g][0, i] = total
            for k in range(1, seconds[g]):
                two_copy(g, k).start()

        def begin_end(g):
            first, rows = regions[g]
            size = rows // replicas
            total = accs[g][0, mine(g)]
            for k in range(1, seconds[g]):
                two_copy(g, k).wait_recv()
                total = total + twos[g][k]
            row = pl.multiple_of(first + place.replica * size, 8)
            owned_ref[pl.ds(row, size), :] = total
            for k in range(1, replicas):
                end_copy(g, k, place.replica).start()

        def end_sums():
            for g in range(2):
                for k in range(1, replicas):
                    end_copy(g, k, lax.rem(place.replica + replicas - k, replicas)).wait_recv()
                    end_copy(g, k, place.replica).wait_send()
                for k in range(1, firsts[g]):
                    one_copy(g, k).wait_send()
                for k in range(1, seconds[g]):
                    two_copy(g, k).wait_send()
            for c in range(chips):
                half_copy(c).wait_send()

        def begin_all():
            barrier = pltpu.get_barrier_semaphore()

            def greet(k, carry):
                pl.semaphore_signal(
                    barrier,
                    inc=1,
                    device_id=device(lax.rem(me + k, amount)),
                    device_id_type=MESH,
                )
                return carry

            lax.fori_loop(1, amount, greet, 0)
            pl.semaphore_wait(barrier, amount - 1)
            local.start()
            if reduce:
                begin_sums()
            for k in range(1, chips):
                lane_copy(k).start()

            def give(k, carry):
                slice_copy(k).start()
                return carry

            lax.fori_loop(1, amount, give, 0)
            gathered[me] = slices_ref[place.member]

        def token_lane():
            local.wait()
            for k in range(1, chips):
                lane_wait(k)
            for c in range(chips):
                core_copy(place.replica, c).start()

        def token_plane():
            for c in range(chips):
                for k in range(1, replicas):
                    plane_copy(k, c).start()

        def token_core():
            for k in range(1, replicas):
                for c in range(chips):
                    plane_wait(k, c)
            for k in range(1, replicas):
                for c in range(chips):
                    core_copy(place.plane_replica(k), c).start()

        plan = [(0.0, begin_all)]
        if reduce:
            plan = plan + [
                (0.09, begin_one),
                (0.25, token_lane),
                (0.4, lambda: begin_two(0)),
                (0.4, token_plane),
                (0.65, lambda: begin_two(1)),
                (0.75, lambda: begin_end(0)),
                (0.8, lambda: begin_end(1)),
                (0.8, token_core),
            ]
        else:
            plan = plan + [(0.17, token_lane), (0.17, token_plane), (0.5, token_core)]

        start = step * block
        part = table_ref[...].astype(NARROW)
        places = lax.broadcasted_iota(jnp.int32, (block, tile), 0)

        def lap(k, carry):
            for part_of, act in plan:
                pl.when(step * tiles + k == when(part_of))(act)
            here = hidden_ref[pl.ds(pl.multiple_of(k * tile, tile), tile), :]
            logits = lax.dot_general(part, here, LAST_CONTRACT, preferred_element_type=FLOAT)
            probs = jnp.exp(logits - logsum_ref[k])
            grads = jnp.where(
                places == target_ref[k] - start, probs - weight_ref[k], probs
            ).astype(NARROW)
            piece = jnp.dot(grads, here, preferred_element_type=FLOAT)

            @pl.when(k == 0)
            def _():
                grad_ref[...] = piece

            @pl.when(k > 0)
            def _():
                grad_ref[...] += piece

            return carry

        lax.fori_loop(0, tiles, lap, 0)
        squares = jnp.sum(jnp.square(grad_ref[...]), axis=0, keepdims=True)

        @pl.when(step == 0)
        def _():
            square_ref[...] = squares

        @pl.when(step > 0)
        def _():
            square_ref[...] += squares

        @pl.when(step == last)
        def _():
            def take(k, carry):
                there = gathered.at[lax.rem(me + amount - k, amount)]
                remote(there, there, slice_send.at[k], slice_recv.at[k], device(me)).wait_recv()
                slice_copy(k).wait_send()
                return carry

            lax.fori_loop(1, amount, take, 0)
            if reduce:
                end_sums()
                owned_out[...] = owned_ref[...]
            summed_ref[...] = jnp.sum(gathered[...], axis=0)
            for r in range(replicas):
                for c in range(chips):
                    core_wait(r, c)
            for k in range(1, chips):
                lane_copy(k).wait_send()
            for c in range(chips):
                for k in range(1, replicas):
                    plane_copy(k, c).wait_send()
                for r in range(replicas):
                    core_copy(r, c).wait_send()

    whole = pl.BlockSpec(memory_space=pltpu.VMEM)
    anywhere = pl.BlockSpec(memory_space=pl.ANY)
    shape = (tiles, 1, tile)
    dma = pltpu.SemaphoreType.DMA
    return pl.pallas_call(
        kernel,
        grid=(steps,),
        in_specs=[pl.BlockSpec((block, width), lambda i: (i, 0))]
        + [whole] * 4
        + [anywhere, whole, anywhere],
        out_specs=[
            pl.BlockSpec((block, width), lambda i: (i, 0)),
            pl.BlockSpec((1, width), lambda i: (0, 0)),
            anywhere,
            whole,
            whole,
        ],
        out_shape=[
            jax.ShapeDtypeStruct((vocab, width), FLOAT),
            jax.ShapeDtypeStruct((1, width), FLOAT),
            jax.ShapeDtypeStruct((groups * replicas, own, width), NARROW),
            jax.ShapeDtypeStruct(slices.shape[1:], FLOAT),
            jax.ShapeDtypeStruct(owner_grads.shape[1:] if reduce else (8, 128), FLOAT),
        ],
        scratch_shapes=[
            pltpu.VMEM((amount,) + slices.shape[1:], FLOAT),
            pltpu.VMEM(owner_grads.shape[1:] if reduce else (8, 128), FLOAT),
            pltpu.VMEM((chips,) + owner_grads.shape[1:] if reduce else (8, 128), FLOAT),
        ]
        + [
            pltpu.VMEM(
                (counts[g], seconds[g], regions[g][1] // replicas, width)[skip:]
                if reduce
                else (8, 128),
                FLOAT,
            )
            for counts, skip in ((firsts, 0), (firsts, 0), (seconds, 1))
            for g in range(2)
        ]
        + [
            dma((2, max(firsts), max(seconds))),
            dma((chips,)),
            dma((chips,)),
            dma((2, max(firsts))),
            dma((2, max(firsts))),
            dma((2, max(seconds))),
            dma((2, max(seconds))),
            dma((2, replicas)),
            dma((2, replicas)),
            dma,
            dma((amount,)),
            dma((amount,)),
            dma((chips,)),
            dma((chips,)),
            dma((replicas, chips)),
            dma((replicas, chips)),
            dma((replicas, chips)),
            dma((replicas, chips)),
        ],
        compiler_params=pltpu.CompilerParams(
            vmem_limit_bytes=VMEM_LIMIT, collective_id=1, has_side_effects=True
        ),
        cost_estimate=pl.CostEstimate(
            flops=4 * vocab * rows * width,
            bytes_accessed=vocab * width * 8 + rows * width * 4,
            transcendentals=vocab * rows,
        ),
    )(
        table,
        hidden,
        logsum.reshape(shape),
        weights.reshape(shape),
        target.reshape(shape),
        token_grad,
        slices,
        owner_grads,
    )


def exchange_scalars(line, groups, replicas):
    amount = groups * replicas

    def kernel(own_ref, all_ref, local_sem, send_sem, recv_sem):
        place = Place(groups, replicas)
        me = place.replica * groups + place.member

        def device(index):
            return place.at(index // groups, lax.rem(index, groups))

        barrier = pltpu.get_barrier_semaphore()

        def greet(k, carry):
            pl.semaphore_signal(
                barrier, inc=1, device_id=device(lax.rem(me + k, amount)), device_id_type=MESH
            )
            return carry

        def copy(k):
            return remote(
                own_ref,
                all_ref.at[me],
                send_sem.at[k],
                recv_sem.at[k],
                device(lax.rem(me + k, amount)),
            )

        def begin(k, carry):
            copy(k).start()
            return carry

        def finish(k, carry):
            there = all_ref.at[lax.rem(me + amount - k, amount)]
            remote(there, there, send_sem.at[k], recv_sem.at[k], device(me)).wait_recv()
            copy(k).wait_send()
            return carry

        lax.fori_loop(1, amount, greet, 0)
        local = pltpu.make_async_copy(own_ref, all_ref.at[me], local_sem)
        local.start()
        pl.semaphore_wait(barrier, amount - 1)
        lax.fori_loop(1, amount, begin, 0)
        local.wait()
        lax.fori_loop(1, amount, finish, 0)

    whole = pl.BlockSpec(memory_space=pltpu.VMEM)
    dma = pltpu.SemaphoreType.DMA
    return pl.pallas_call(
        kernel,
        in_specs=[whole],
        out_specs=whole,
        out_shape=jax.ShapeDtypeStruct((amount,) + line.shape, line.dtype),
        scratch_shapes=[dma, dma((amount,)), dma((amount,))],
        compiler_params=pltpu.CompilerParams(collective_id=2, has_side_effects=True),
    )(line)


def chunk_lists(local, inside, chunk):
    chunks = local.shape[0] // chunk
    flags = inside.reshape(chunks, chunk)
    spots = jnp.arange(chunk, dtype=jnp.int32)
    ahead = (spots[:, None] < spots[None, :]).astype(NARROW)
    order = jnp.dot(flags.astype(NARROW), ahead, preferred_element_type=FLOAT).astype(jnp.int32)
    chosen = (order[:, None, :] == spots[None, :, None]) & flags[:, None, :]
    places = jnp.sum(jnp.where(chosen, spots[None, None, :], 0), axis=2)
    rows = jnp.sum(jnp.where(chosen, local.reshape(chunks, 1, chunk), 0), axis=2)
    return places, rows, jnp.sum(flags.astype(jnp.int32), axis=1)


def embed_table_grad(token_grads, places, rows, counts, vocab):
    chunks, chunk = places.shape
    width = token_grads.shape[-1]
    padded = vocab + 8
    unroll = 4

    def kernel(
        count_ref, place_ref, row_ref, tokens_ref, grad_ref, square_ref, wide_ref, total_ref, sem
    ):
        step = pl.program_id(0)

        @pl.when(step == 0)
        def _():
            total_ref[...] = jnp.zeros_like(total_ref)

        wide_ref[...] = tokens_ref[...].astype(FLOAT)
        amount = count_ref[step]

        def lap(j, carry):
            for u in range(unroll):
                spot = j * unroll + u
                row = jnp.where(spot < amount, row_ref[0, 0, spot], vocab)
                place = place_ref[0, 0, spot]
                total_ref[pl.ds(row, 1), :] += wide_ref[pl.ds(place, 1), :]
            return carry

        lax.fori_loop(0, (amount + unroll - 1) // unroll, lap, 0)

        @pl.when(step == chunks - 1)
        def _():
            out = pltpu.make_async_copy(total_ref.at[pl.ds(0, vocab), :], grad_ref, sem)
            out.start()
            square_ref[...] = jnp.sum(
                jnp.square(total_ref[pl.ds(0, vocab), :]), axis=0, keepdims=True
            )
            out.wait()

    line = pl.BlockSpec((1, 1, chunk), lambda i, c: (i, 0, 0), memory_space=pltpu.SMEM)
    return pl.pallas_call(
        kernel,
        grid_spec=pltpu.PrefetchScalarGridSpec(
            num_scalar_prefetch=1,
            grid=(chunks,),
            in_specs=[line, line, pl.BlockSpec((chunk, width), lambda i, c: (i, 0))],
            out_specs=[
                pl.BlockSpec(memory_space=pl.ANY),
                pl.BlockSpec((1, width), lambda i, c: (0, 0)),
            ],
            scratch_shapes=[
                pltpu.VMEM((chunk, width), FLOAT),
                pltpu.VMEM((padded, width), FLOAT),
                pltpu.SemaphoreType.DMA,
            ],
        ),
        out_shape=[
            jax.ShapeDtypeStruct((vocab, width), FLOAT),
            jax.ShapeDtypeStruct((1, width), FLOAT),
        ],
        compiler_params=pltpu.CompilerParams(vmem_limit_bytes=VMEM_LIMIT),
    )(
        counts,
        places.reshape(chunks, 1, chunk),
        rows.reshape(chunks, 1, chunk),
        token_grads.reshape(chunks * chunk, width),
    )


def update_rule(weight, grad, moment, average, rate, clip_factor):
    clipped = clip_factor * grad
    new_moment = MOMENTUM * moment + clipped
    new_weight = weight - rate * (clipped + MOMENTUM * new_moment)
    new_average = DECAY * average + (1.0 - DECAY) * new_weight
    return (new_weight, new_moment, new_average)


def update_all(scalars, tables, matrices, rates):
    vocab, width = tables[0][0].shape
    sub = tables[0][3].shape[0]
    block = block_rows(vocab, 1100)
    blocks = vocab // block
    window = max(-(-(sub + sub * r % 8) // 8) * 8 for r in range(vocab // sub))
    tile = 264
    tiles = -(-window // tile)
    steps = 2 * blocks + 2 * tiles
    count = len(matrices)

    def kernel(*refs):
        refs = list(refs)

        def take(amount):
            taken = refs[:amount]
            del refs[:amount]
            return taken

        (scalars_ref,) = take(1)
        whole_in = [take(3) for _ in range(2)]
        own_in = [take(4) for _ in range(2)]
        small_in = [take(4) for _ in range(count)]
        new_tables = take(2)
        own_out = [take(2) for _ in range(2)]
        small_out = [take(3) for _ in range(count)]
        (factor_ref,) = take(1)
        windows = take(2)
        (sems,) = take(1)
        step = pl.program_id(0)
        begin = lax.axis_index("dp") * sub
        low = pl.multiple_of(begin // 8 * 8, 8)
        shift = begin - low

        def fetch(w, t):
            first = t * tile
            size = min(tile, window - first)
            return [
                pltpu.make_async_copy(
                    own_in[w][i].at[pl.ds(low + first, size), :],
                    windows[i].at[pl.ds(first, size), :],
                    sems.at[w, i, t],
                )
                for i in range(2)
            ]

        @pl.when(step == 0)
        def _():
            total = jnp.sum(scalars_ref[...], axis=0)
            norm = jnp.sqrt(total)
            factor_ref[...] = CLIP_LEVEL / jnp.maximum(norm, CLIP_LEVEL)

        factor = factor_ref[1:2, 0:1]
        for w in range(2):

            @pl.when((step >= w * blocks) & (step < (w + 1) * blocks))
            def _():
                table_ref, grad_ref, moment_ref = whole_in[w]
                table = table_ref[...]
                new_tables[w][...], _, _ = update_rule(
                    table, grad_ref[...], moment_ref[...].astype(FLOAT), table, rates[w], factor
                )

        @pl.when(step == 1)
        def _():
            for i in range(count):
                weight, grad, moment, average = [ref[...] for ref in small_in[i]]
                results = update_rule(weight, grad, moment, average, rates[2 + i], factor)
                for ref, result in zip(small_out[i], results):
                    ref[...] = result

        for w in range(2):
            base = 2 * blocks + w * tiles
            for t in range(tiles):

                @pl.when(step == (base - tiles + t + 1 if w else blocks))
                def _():
                    for copy in fetch(w, t):
                        copy.start()

            for t in range(tiles):

                @pl.when(step == base + t)
                def _():
                    if t == 0:
                        for copy in fetch(w, 0):
                            copy.wait()
                    if t + 1 < tiles:
                        for copy in fetch(w, t + 1):
                            copy.wait()

            @pl.when((step >= base) & (step < base + tiles))
            def _():
                first = pl.multiple_of((step - base) * tile, 8)
                amount = jnp.where(shift == 0, 0, tile + 8 - shift)
                own_table, own_grad = [
                    pltpu.roll(win[pl.ds(first, tile + 8), :], amount, 0)[:tile]
                    for win in windows
                ]
                _, own_out[w][0][...], own_out[w][1][...] = update_rule(
                    own_table, own_grad, own_in[w][2][...], own_in[w][3][...], rates[w], factor
                )

    whole = pl.BlockSpec(memory_space=pltpu.VMEM)
    anywhere = pl.BlockSpec(memory_space=pl.ANY)

    def table_spec(w):
        return pl.BlockSpec(
            (block, width), lambda i: (jnp.clip(i - w * blocks, 0, blocks - 1), 0)
        )

    def own_spec(w):
        return pl.BlockSpec(
            (tile, width),
            lambda i: (jnp.clip(i - 2 * blocks - w * tiles, 0, tiles - 1), 0),
        )

    state = jax.ShapeDtypeStruct((sub, width), FLOAT)
    operands = [scalars]
    in_specs = [whole]
    for w in range(2):
        operands += list(tables[w][:3])
        in_specs += [table_spec(w)] * 3
    for w in range(2):
        operands += [tables[w][0], tables[w][1], tables[w][3], tables[w][4]]
        in_specs += [anywhere, anywhere, own_spec(w), own_spec(w)]
    for item in matrices:
        operands += list(item)
        in_specs += [whole] * 4
    out_specs = [table_spec(0), table_spec(1)]
    out_shape = [jax.ShapeDtypeStruct((vocab, width), FLOAT)] * 2
    for w in range(2):
        out_specs += [own_spec(w)] * 2
        out_shape += [state] * 2
    for item in matrices:
        out_specs += [whole] * 3
        out_shape += [jax.ShapeDtypeStruct(item[0].shape, FLOAT)] * 3
    results = pl.pallas_call(
        kernel,
        grid=(steps,),
        in_specs=in_specs,
        out_specs=out_specs,
        out_shape=out_shape,
        scratch_shapes=[pltpu.VMEM((8, 128), FLOAT)]
        + [pltpu.VMEM((tiles * tile + 8, width), FLOAT)] * 2
        + [pltpu.SemaphoreType.DMA((2, 2, tiles))],
        compiler_params=pltpu.CompilerParams(vmem_limit_bytes=VMEM_LIMIT),
    )(*operands)
    tables_out = [(results[w], *results[2 + 2 * w : 4 + 2 * w]) for w in range(2)]
    return tables_out, [results[6 + 3 * i : 9 + 3 * i] for i in range(count)]


def shards(
    token_ids,
    loss_mask,
    lengths,
    buffer_ids,
    embed_table,
    embed_moment,
    embed_average,
    head_table,
    head_moment,
    head_average,
    in_weights,
    in_moment,
    in_average,
    out_weights,
    out_moment,
    out_average,
    vectors,
    vector_moment,
    vector_average,
):
    groups = lax.axis_size("fsdp")
    replicas = lax.axis_size("dp")
    member = lax.axis_index("fsdp")
    replica = lax.axis_index("dp")
    batches, _, seq = token_ids.shape
    vocab_rows, width = embed_table.shape
    head_size = width // HEADS
    vocab_start = member * vocab_rows
    own_rows = batches * seq
    rows_all = groups * own_rows

    tokens, marks, buffers = token_ids[:, 0], loss_mask[:, 0], buffer_ids[:, 0]
    divisor, offset, counted = jax.vmap(functools.partial(slot_info, buffer_count=NSEG))(
        tokens, marks, lengths[:, 0], buffers
    )
    packed = jnp.concatenate(
        [
            tokens,
            divisor,
            jnp.broadcast_to(jnp.sum(counted), (8 - 2 * batches, seq)),
        ],
        axis=0,
    )
    amount = vectors.shape[0]
    line = jnp.pad(vectors, (0, -amount % 1024)).reshape(-1, 128)
    everyone, lines, in_full, out_full, resid, aims = start_kernel(
        packed,
        line,
        in_weights,
        out_weights,
        embed_table,
        head_table,
        batches,
        groups,
        replicas,
    )
    vector_full = lines.reshape(groups, -1)[:, :amount].reshape(-1).astype(NARROW)
    embed_moment_low = lax.all_gather(embed_moment.astype(NARROW), "dp", axis=0, tiled=True)
    head_moment_low = lax.all_gather(head_moment.astype(NARROW), "dp", axis=0, tiled=True)
    tokens_all = everyone[:, :batches]
    count = jnp.maximum(jnp.sum(everyone[:, 2 * batches, 0]).astype(FLOAT), 1.0)
    divisor_all = everyone[:, batches : 2 * batches].astype(FLOAT)
    share_all = jnp.where(divisor_all > 0.5, 1.0 / jnp.maximum(divisor_all, 1.0), 0.0)
    weight_all = (share_all / count).reshape(-1)
    target_all = (
        jnp.concatenate([tokens_all[:, :, 1:], jnp.zeros_like(tokens_all[:, :, :1])], axis=2)
        .reshape(-1)
    ) - vocab_start
    tokens_flat = tokens_all.reshape(-1)
    local_all = tokens_flat - vocab_start
    inside_all = (local_all >= 0) & (local_all < vocab_rows)

    def group_part(values):
        return lax.dynamic_slice_in_dim(values, replica * rows_all, rows_all, 0)

    vector = vector_full.astype(FLOAT).reshape(1, -1)
    tables = rotary_tables(offset.reshape(-1), head_size)
    lines_of, columns_of = buffers[:, None, :], buffers[:, :, None]
    final, *kept = layer_forward(resid, in_full, out_full, vector, tables, lines_of, columns_of)
    final_grad, logsum_all, loss_part, all_hidden = head_kernel(
        head_table, final, aims, group_part(target_all), group_part(weight_all), groups, replicas
    )

    less_weight = logsum_all - jnp.log(jnp.maximum(weight_all, 1e-30))
    shifted = jnp.where(weight_all > 0.0, less_weight, 1e30)
    chunk = min(512, rows_all)
    lists = chunk_lists(local_all, inside_all, chunk)

    token_grad, vector_grad, owner_grads = layer_backward(
        final_grad,
        resid,
        in_full,
        out_full,
        vector,
        tables,
        lines_of,
        columns_of,
        kept,
        groups,
    )
    slices = jnp.pad(vector_grad.reshape(groups, amount), ((0, 0), (0, -amount % 1024)))
    in_rows = in_weights.shape[0]
    cut = owner_grads.shape[1] - out_weights.shape[0]
    head_grad, head_square, token_grads, vector_sum, owned = head_table_grad(
        head_table,
        all_hidden,
        shifted,
        weight_all,
        target_all,
        token_grad,
        slices.reshape(groups, -1, 128),
        owner_grads,
        cut,
        groups,
        replicas,
    )
    if owned.shape != owner_grads.shape[1:]:
        owned = lax.psum(lax.psum_scatter(owner_grads, "fsdp", scatter_dimension=0), "dp")
    layer_grads = [
        owned[:cut].reshape(-1, in_rows, width).transpose(1, 0, 2).reshape(in_rows, -1),
        owned[cut:],
        vector_sum.reshape(-1)[:amount],
    ]
    embed_grad, embed_square = embed_table_grad(token_grads, *lists, vocab_rows)
    square = jnp.sum(embed_square) + jnp.sum(head_square)
    for grad in layer_grads:
        square = square + jnp.sum(grad * grad)
    line = jnp.stack([loss_part, square / replicas])[:, None]
    line = jnp.pad(jnp.broadcast_to(line, (2, 128)), ((0, 6), (0, 0)))
    scalars = exchange_scalars(line, groups, replicas)
    pair = jnp.sum(scalars[:, :2, 0], axis=0)
    loss = pair[0]
    grad_norm = jnp.sqrt(pair[1])
    base = math.sqrt(NPARAM) / CLIP_LEVEL
    root = math.sqrt(width)

    def row(values):
        return values.reshape(1, -1)

    (embed, head), (inner, outer, vector) = update_all(
        scalars,
        [
            (embed_table, embed_grad, embed_moment_low, embed_moment, embed_average),
            (head_table, head_grad, head_moment_low, head_moment, head_average),
        ],
        [
            (in_weights, layer_grads[0], in_moment, in_average),
            (out_weights, layer_grads[1], out_moment, out_average),
            tuple(map(row, (vectors, layer_grads[2], vector_moment, vector_average))),
        ],
        (base, base / root, base / root, base / root, 0.3 * base),
    )
    vector = [values.reshape(-1) for values in vector]
    return (*embed, *head, *inner, *outer, *vector, loss, grad_norm)


def solution(mesh):
    placed = (
        P(None, ("dp", "fsdp"), None),
        P(None, ("dp", "fsdp"), None),
        P(None, ("dp", "fsdp")),
        P(None, ("dp", "fsdp"), None),
        P("fsdp", None),
        P(("fsdp", "dp"), None),
        P(("fsdp", "dp"), None),
        P("fsdp", None),
        P(("fsdp", "dp"), None),
        P(("fsdp", "dp"), None),
        P("fsdp", None),
        P("fsdp", None),
        P("fsdp", None),
        P("fsdp", None),
        P("fsdp", None),
        P("fsdp", None),
        P("fsdp"),
        P("fsdp"),
        P("fsdp"),
    )
    return jax.shard_map(
        shards,
        mesh=mesh,
        in_specs=placed,
        out_specs=(
            P("fsdp", None),
            P(("fsdp", "dp"), None),
            P(("fsdp", "dp"), None),
            P("fsdp", None),
            P(("fsdp", "dp"), None),
            P(("fsdp", "dp"), None),
            P("fsdp", None),
            P("fsdp", None),
            P("fsdp", None),
            P("fsdp", None),
            P("fsdp", None),
            P("fsdp", None),
            P("fsdp"),
            P("fsdp"),
            P("fsdp"),
            P(),
            P(),
        ),
        check_vma=False,
    )
```

```python
import functools
import math

import jax
import jax.numpy as jnp
from jax import lax
from jax.experimental import pallas as pl
from jax.experimental.pallas import tpu as pltpu
from jax.sharding import PartitionSpec as P

HEADS = 8
NPARAM = 54664704
NSEG = 3


EPSILON = 1e-05
CLIP_LEVEL = 0.002
MOMENTUM = 0.5
DECAY = 0.5
NARROW = jnp.bfloat16
FLOAT = jnp.float32
ROWS_CONTRACT = (((0,), (0,)), ((), ()))
LAST_CONTRACT = (((1,), (1,)), ((), ()))


VMEM_LIMIT = 60 * 2**20


def slot_info(tokens, marks, length, buffers, buffer_count):
    seq = tokens.shape[0]
    places = jnp.arange(seq, dtype=jnp.int32)
    same_buffer = jnp.concatenate([buffers[1:] == buffers[:-1], jnp.zeros((1,), dtype=bool)])
    valid = jnp.where((marks == 1) & (places + 1 < length) & same_buffer, 1.0, 0.0).astype(FLOAT)
    member = buffers[None, :] == jnp.arange(buffer_count, dtype=jnp.int32)[:, None]
    weights = jnp.where(member, 1.0, 0.0).astype(FLOAT)
    tally = jnp.sum(weights * valid[None, :], axis=1)
    divisor = valid * jnp.sum(weights * tally[:, None], axis=0)
    counted = jnp.sum(jnp.where(tally > 0.5, 1.0, 0.0).astype(FLOAT))
    first = jnp.min(jnp.where(member, places[None, :], seq), axis=1)
    offset = places - jnp.sum(jnp.where(member, first[:, None], 0), axis=0)
    return (divisor.astype(jnp.int32), offset, counted.astype(jnp.int32))


def rotary_tables(offset, head_size):
    rot = head_size // 4
    half = rot // 2
    lanes = 128
    freqs = jnp.power(10000.0, -2.0 * jnp.arange(half, dtype=FLOAT) / rot)
    angles = offset.astype(FLOAT)[:, None] * freqs[None, :]
    cosine, sine = jnp.cos(angles), jnp.sin(angles)
    rows = offset.shape[0]
    rest = head_size - rot
    ones, none = jnp.ones((rows, rest), FLOAT), jnp.zeros((rows, rest), FLOAT)
    blank = jnp.zeros((rows, half), FLOAT)
    stay = jnp.concatenate([cosine, cosine, ones], axis=1)
    ahead = jnp.concatenate([-sine, blank, none], axis=1)
    behind = jnp.concatenate([blank, sine, none], axis=1)
    return [
        jnp.concatenate([part] * (lanes // head_size), axis=1) for part in (stay, ahead, behind)
    ]


def wide_tables(refs, width):
    return [jnp.concatenate([ref[...]] * (width // ref.shape[1]), axis=1) for ref in refs]


def norm_unit(values):
    mean = jnp.mean(values, axis=-1, keepdims=True)
    centred = values - mean
    scale = lax.rsqrt(jnp.mean(centred * centred, axis=-1, keepdims=True) + EPSILON)
    return (centred * scale, scale)


def norm_back(scaled, unit, scale):
    return scale * (
        scaled
        - jnp.mean(scaled, axis=-1, keepdims=True)
        - unit * jnp.mean(scaled * unit, axis=-1, keepdims=True)
    )


def vector_spans(width, hidden):
    amounts = [width] * 6 + [3 * width, width, hidden, width]
    spans = []
    begin = 0
    for amount in amounts:
        spans.append(slice(begin, begin + amount))
        begin = begin + amount
    return spans


def masked_probs(queries, keys, mask, factor):
    scores = lax.dot_general(queries, keys, LAST_CONTRACT, preferred_element_type=FLOAT) * factor
    scores = jnp.where(mask, scores, -1e30)
    top = jnp.max(scores, axis=-1, keepdims=True)
    logsum = top + jnp.log(jnp.sum(jnp.exp(scores - top), axis=-1, keepdims=True))
    return jnp.exp(scores - logsum)


def slot_mask(line_ref, column_ref, b, seq):
    later = lax.broadcasted_iota(jnp.int32, (seq, seq), 1)
    place = lax.broadcasted_iota(jnp.int32, (seq, seq), 0)
    return (column_ref[b] == line_ref[b]) & (later <= place)


def layer_forward(resid, in_full, out_full, vector, tables, lines, columns):
    rows, width = resid.shape
    hidden = out_full.shape[0] - width
    batches, _, seq = lines.shape
    head_size = width // HEADS
    half = head_size // 8
    factor = 1.0 / math.sqrt(head_size)
    spans = vector_spans(width, hidden)

    def kernel(
        resid_ref,
        in_ref,
        out_ref,
        vector_ref,
        stay_ref,
        ahead_ref,
        behind_ref,
        line_ref,
        column_ref,
        final_ref,
        qkv_ref,
        pre_ref,
        joined_ref,
        last_ref,
    ):
        def part(i):
            return vector_ref[:, spans[i]]

        start = resid_ref[...]
        unit, _ = norm_unit(start)
        input_one = (unit * part(0) + part(1)).astype(NARROW)
        input_two = (unit * part(2) + part(3)).astype(NARROW)
        stay, ahead, behind = wide_tables((stay_ref, ahead_ref, behind_ref), width)
        bias = part(6)
        for i in range(3):
            span = slice(i * width, (i + 1) * width)
            values = jnp.dot(input_one, in_ref[:, span], preferred_element_type=FLOAT)
            values = values + bias[:, span]
            if i < 2:
                values = (
                    values * stay
                    + pltpu.roll(values, width - half, 1) * ahead
                    + pltpu.roll(values, half, 1) * behind
                )
            qkv_ref[:, span] = values.astype(NARROW)
        for b in range(batches):
            mask = slot_mask(line_ref, column_ref, b, seq)
            there = slice(b * seq, (b + 1) * seq)
            for head in range(HEADS):
                first = head * head_size
                queries, keys, values = [
                    qkv_ref[there, i * width + first : i * width + first + head_size]
                    for i in range(3)
                ]
                probs = masked_probs(queries, keys, mask, factor).astype(NARROW)
                joined_ref[there, first : first + head_size] = jnp.dot(
                    probs, values, preferred_element_type=FLOAT
                ).astype(NARROW)
        bias = part(8)
        for i in range(hidden // width):
            span = slice(i * width, (i + 1) * width)
            pre = (
                jnp.dot(
                    input_two,
                    in_ref[:, (3 + i) * width : (4 + i) * width],
                    preferred_element_type=FLOAT,
                )
                + bias[:, span]
            )
            pre_ref[:, span] = pre
            joined_ref[:, (1 + i) * width : (2 + i) * width] = (
                0.5 * pre * (1.0 + lax.erf(pre * 0.7071067811865476))
            ).astype(NARROW)
        last = (
            start
            + jnp.dot(joined_ref[...], out_ref[...], preferred_element_type=FLOAT)
            + part(7)
            + part(9)
        )
        last_ref[...] = last
        unit_last, _ = norm_unit(last)
        final_ref[...] = (unit_last * part(4) + part(5)).astype(NARROW)

    return pl.pallas_call(
        kernel,
        out_shape=[
            jax.ShapeDtypeStruct((rows, width), NARROW),
            jax.ShapeDtypeStruct((rows, 3 * width), NARROW),
            jax.ShapeDtypeStruct((rows, hidden), FLOAT),
            jax.ShapeDtypeStruct((rows, width + hidden), NARROW),
            jax.ShapeDtypeStruct((rows, width), FLOAT),
        ],
        compiler_params=pltpu.CompilerParams(vmem_limit_bytes=VMEM_LIMIT),
    )(resid, in_full, out_full, vector, *tables, lines, columns)


def layer_backward(
    final_grad, resid, in_full, out_full, vector, tables, lines, columns, kept, groups
):
    rows, width = resid.shape
    hidden = out_full.shape[0] - width
    batches, _, seq = lines.shape
    head_size = width // HEADS
    half = head_size // 8
    factor = 1.0 / math.sqrt(head_size)
    spans = vector_spans(width, hidden)
    blocks = in_full.shape[1] // width
    in_rows = width // groups
    out_rows = out_full.shape[0] // groups
    first_out = blocks * in_rows
    shard = first_out + out_rows

    def kernel(
        final_grad_ref,
        resid_ref,
        in_ref,
        out_ref,
        vector_ref,
        stay_ref,
        ahead_ref,
        behind_ref,
        line_ref,
        column_ref,
        qkv_ref,
        pre_ref,
        joined_ref,
        last_ref,
        token_ref,
        small_ref,
        owners_ref,
        owners,
        low,
        wide,
        sems,
    ):
        def part(i):
            return vector_ref[:, spans[i]]

        def column_sum(i, values):
            small_ref[:, spans[i]] = jnp.sum(values, axis=0, keepdims=True)

        final_grad_in = final_grad_ref[...]
        unit_last, scale_last = norm_unit(last_ref[...])
        column_sum(4, final_grad_in * unit_last)
        column_sum(5, final_grad_in)
        grad_out = norm_back(final_grad_in * part(4), unit_last, scale_last)
        column_sum(7, grad_out)
        column_sum(9, grad_out)
        grad_low = grad_out.astype(NARROW)
        for c in range((width + hidden) // width):
            there = slice(c * width, (c + 1) * width)
            piece = lax.dot_general(
                joined_ref[:, there], grad_low, ROWS_CONTRACT, preferred_element_type=FLOAT
            )
            at = c * width
            while at < (c + 1) * width:
                owner, row = at // out_rows, at % out_rows
                size = min(out_rows - row, (c + 1) * width - at)
                owners[owner, first_out + row : first_out + row + size, :] = piece[
                    at - c * width : at - c * width + size
                ]
                at = at + size
        out_copy = pltpu.make_async_copy(
            owners.at[:, pl.ds(first_out, out_rows), :],
            owners_ref.at[:, pl.ds(first_out, out_rows), :],
            sems.at[0],
        )
        out_copy.start()
        unit, scale = norm_unit(resid_ref[...])
        input_one = (unit * part(0) + part(1)).astype(NARROW)
        input_two = (unit * part(2) + part(3)).astype(NARROW)

        def in_piece(inputs, c, grads):
            piece = lax.dot_general(
                inputs, grads, ROWS_CONTRACT, preferred_element_type=FLOAT
            )
            for owner in range(groups):
                owners[owner, c * in_rows : (c + 1) * in_rows, :] = piece[
                    owner * in_rows : (owner + 1) * in_rows
                ]

        back_two = jnp.zeros((rows, width), FLOAT)
        bias_sums = []
        for i in range(hidden // width):
            grads = lax.dot_general(
                grad_low,
                out_ref[(1 + i) * width : (2 + i) * width, :],
                LAST_CONTRACT,
                preferred_element_type=FLOAT,
            )
            pre = pre_ref[:, i * width : (i + 1) * width]
            slope = (
                0.5 * (1.0 + lax.erf(pre * 0.7071067811865476))
                + pre * jnp.exp(-0.5 * pre * pre) * 0.3989422804014327
            )
            grads = grads * slope
            bias_sums.append(jnp.sum(grads, axis=0, keepdims=True))
            grads = grads.astype(NARROW)
            in_piece(input_two, 3 + i, grads)
            back_two = back_two + lax.dot_general(
                grads,
                in_ref[:, (3 + i) * width : (4 + i) * width],
                LAST_CONTRACT,
                preferred_element_type=FLOAT,
            )
        small_ref[:, spans[8]] = jnp.concatenate(bias_sums, axis=1)
        low[...] = lax.dot_general(
            grad_low, out_ref[:width, :], LAST_CONTRACT, preferred_element_type=FLOAT
        ).astype(NARROW)
        for b in range(batches):
            mask = slot_mask(line_ref, column_ref, b, seq)
            there = slice(b * seq, (b + 1) * seq)
            for head in range(HEADS):
                first = head * head_size
                at = [
                    slice(i * width + first, i * width + first + head_size) for i in range(3)
                ]
                queries, keys, values = [qkv_ref[there, at[i]] for i in range(3)]
                mixed = low[there, first : first + head_size]
                probs = masked_probs(queries, keys, mask, factor)
                back = lax.dot_general(
                    mixed, values, LAST_CONTRACT, preferred_element_type=FLOAT
                )
                wide[there, at[2]] = lax.dot_general(
                    probs.astype(NARROW), mixed, ROWS_CONTRACT, preferred_element_type=FLOAT
                )
                scores = (
                    probs
                    * (back - jnp.sum(probs * back, axis=-1, keepdims=True))
                    * factor
                ).astype(NARROW)
                wide[there, at[0]] = jnp.dot(scores, keys, preferred_element_type=FLOAT)
                wide[there, at[1]] = lax.dot_general(
                    scores, queries, ROWS_CONTRACT, preferred_element_type=FLOAT
                )
        stay, ahead, behind = wide_tables((stay_ref, ahead_ref, behind_ref), width)
        back_one = jnp.zeros((rows, width), FLOAT)
        bias_sums = []
        for i in range(3):
            span = slice(i * width, (i + 1) * width)
            grads = wide[:, span]
            if i < 2:
                grads = (
                    grads * stay
                    + pltpu.roll(grads * ahead, half, 1)
                    + pltpu.roll(grads * behind, width - half, 1)
                )
            bias_sums.append(jnp.sum(grads, axis=0, keepdims=True))
            grads = grads.astype(NARROW)
            in_piece(input_one, i, grads)
            back_one = back_one + lax.dot_general(
                grads, in_ref[:, span], LAST_CONTRACT, preferred_element_type=FLOAT
            )
        in_copy = pltpu.make_async_copy(
            owners.at[:, pl.ds(0, first_out), :],
            owners_ref.at[:, pl.ds(0, first_out), :],
            sems.at[1],
        )
        in_copy.start()
        small_ref[:, spans[6]] = jnp.concatenate(bias_sums, axis=1)
        column_sum(0, back_one * unit)
        column_sum(1, back_one)
        column_sum(2, back_two * unit)
        column_sum(3, back_two)
        token_ref[...] = (
            grad_out + norm_back(back_one * part(0) + back_two * part(2), unit, scale)
        ).astype(NARROW)
        out_copy.wait()
        in_copy.wait()

    whole = pl.BlockSpec(memory_space=pltpu.VMEM)
    return pl.pallas_call(
        kernel,
        in_specs=[whole] * 14,
        out_specs=[whole, whole, pl.BlockSpec(memory_space=pl.ANY)],
        out_shape=[
            jax.ShapeDtypeStruct((rows, width), NARROW),
            jax.ShapeDtypeStruct(vector.shape, FLOAT),
            jax.ShapeDtypeStruct((groups, shard, width), FLOAT),
        ],
        scratch_shapes=[
            pltpu.VMEM((groups, shard, width), FLOAT),
            pltpu.VMEM((rows, width), NARROW),
            pltpu.VMEM((rows, 3 * width), FLOAT),
            pltpu.SemaphoreType.DMA((2,)),
        ],
        compiler_params=pltpu.CompilerParams(vmem_limit_bytes=VMEM_LIMIT),
    )(final_grad, resid, in_full, out_full, vector, *tables, lines, columns, *kept)


def block_rows(rows, cap):
    best = rows
    for size in range(8, cap + 1, 8):
        if rows % size == 0:
            best = size
    return best


MESH = pl.DeviceIdType.MESH


def meet(peers):
    barrier = pltpu.get_barrier_semaphore()
    for peer in peers:
        pl.semaphore_signal(barrier, inc=1, device_id=peer, device_id_type=MESH)
    pl.semaphore_wait(barrier, len(peers))


class Place:
    def __init__(self, groups, replicas):
        self.groups = groups
        self.replicas = replicas
        self.chips = groups // 2
        self.replica = lax.axis_index("dp")
        self.member = lax.axis_index("fsdp")
        self.chip = self.member // 2
        self.core = self.member % 2
        self.sibling_member = self.chip * 2 + 1 - self.core

    def lane_chip(self, step):
        return lax.rem(self.chip + step, self.chips)

    def at(self, replica, member):
        return {"dp": replica, "fsdp": member}

    def lane(self, step):
        return self.at(self.replica, self.lane_chip(step) * 2 + self.core)

    def plane_replica(self, step):
        return lax.rem(self.replica + step, self.replicas)

    def plane(self, step):
        return self.at(self.plane_replica(step), self.member)

    def sibling(self):
        return self.at(self.replica, self.sibling_member)

    def lanes(self):
        return [self.lane(step) for step in range(1, self.chips)]

    def planes(self):
        return [self.plane(step) for step in range(1, self.replicas)]


def remote(source, target, send, recv, device):
    return pltpu.make_async_remote_copy(
        src_ref=source,
        dst_ref=target,
        send_sem=send,
        recv_sem=recv,
        device_id=device,
        device_id_type=MESH,
    )


def start_kernel(
    packed, line, in_shard, out_shard, table, head, batches, groups, replicas
):
    vocab, width = table.shape
    seq = packed.shape[1]
    own = batches * seq
    chips = groups // 2
    amount = groups * replicas
    shards_in = (in_shard, out_shard)
    split = all(shard.shape[0] % (16 * replicas) == 0 for shard in shards_in)
    pieces = replicas if split else 1
    unroll = 8

    def kernel(
        packed_ref,
        line_ref,
        in_ref,
        out_ref,
        table_ref,
        head_ref,
        every_ref,
        lines_ref,
        in_full,
        out_full,
        resid_ref,
        aims_ref,
        in_low,
        out_low,
        wide,
        again,
        looked,
        to_core,
        from_core,
        to_lane,
        from_lane,
        ids,
        table_sem,
        ids_sem,
        local_sem,
        meta_send,
        meta_recv,
        line_send,
        line_recv,
        lane_send,
        lane_recv,
        plane_send,
        plane_recv,
        core_send,
        core_recv,
        part_send,
        part_recv,
        sum_send,
        sum_recv,
    ):
        place = Place(groups, replicas)
        member = place.member
        core = place.core
        replica = place.replica
        me = replica * groups + member
        fulls = (in_full, out_full)
        lows = (in_low, out_low)

        def device(index):
            return place.at(index // groups, lax.rem(index, groups))

        def chip_at(j):
            return lax.rem(place.chip + j, chips)

        def chip_before(j):
            return lax.rem(place.chip + chips - j, chips)

        def replica_before(k):
            return lax.rem(replica + replicas - k, replicas)

        def lane_device(j):
            return place.at(replica, chip_at(j) * 2 + core)

        def plane_device(k):
            return place.at(lax.rem(replica + k, replicas), member)

        def meta_copy(k):
            return remote(
                packed_ref,
                every_ref.at[me],
                meta_send.at[k],
                meta_recv.at[k],
                device(lax.rem(me + k, amount)),
            )

        def line_copy(k):
            return remote(
                line_ref,
                lines_ref.at[member],
                line_send.at[k],
                line_recv.at[k],
                place.at(replica, lax.rem(member + k, groups)),
            )

        def piece(w, slot, from_replica):
            full = fulls[w]
            if not split:
                return full.at[slot]
            rows = full.shape[1] // pieces
            return full.at[slot, pl.ds(pl.multiple_of(from_replica * rows, 16), rows), :]

        def own_piece(w):
            low = lows[w]
            if not split:
                return low
            rows = low.shape[0] // pieces
            return low.at[pl.ds(pl.multiple_of(replica * rows, 16), rows), :]

        def lane_copy(w, j):
            return remote(
                own_piece(w),
                piece(w, member, replica),
                lane_send.at[w, j],
                lane_recv.at[w, j],
                lane_device(j),
            )

        def lane_wait(w, j):
            there = piece(w, chip_before(j) * 2 + core, replica)
            remote(
                there, there, lane_send.at[w, j], lane_recv.at[w, j], lane_device(j)
            ).wait_recv()

        def plane_copy(w, k, j):
            there = piece(w, chip_before(j) * 2 + core, replica)
            return remote(
                there, there, plane_send.at[w, k, j], plane_recv.at[w, k, j], plane_device(k)
            )

        def plane_wait(w, k, j):
            there = piece(w, chip_before(j) * 2 + core, replica_before(k))
            remote(
                there, there, plane_send.at[w, k, j], plane_recv.at[w, k, j], plane_device(k)
            ).wait_recv()

        def core_copy(w, j):
            here = fulls[w].at[chip_before(j) * 2 + core]
            return remote(here, here, core_send.at[w, j], core_recv.at[w, j], place.sibling())

        def own_core_copy(w):
            return remote(
                lows[w],
                fulls[w].at[member],
                core_send.at[w, 0],
                core_recv.at[w, 0],
                place.sibling(),
            )

        def core_wait(w, j):
            there = fulls[w].at[chip_before(j) * 2 + 1 - core]
            remote(
                there, there, core_send.at[w, j], core_recv.at[w, j], place.sibling()
            ).wait_recv()

        def part_copy(j):
            return remote(
                to_core.at[j], from_core.at[j], part_send.at[j], part_recv.at[j], place.sibling()
            )

        def sum_copy(j):
            return remote(
                to_lane.at[j], from_lane.at[j], sum_send.at[j], sum_recv.at[j], lane_device(j)
            )

        fetch = pltpu.make_async_copy(
            table_ref, wide.at[pl.ds(0, vocab), :], table_sem.at[0]
        )
        refetch = pltpu.make_async_copy(
            head_ref, again.at[pl.ds(0, vocab), :], table_sem.at[1]
        )
        fetch.start()
        refetch.start()
        barrier = pltpu.get_barrier_semaphore()

        def greet(k, carry):
            pl.semaphore_signal(
                barrier, inc=1, device_id=device(lax.rem(me + k, amount)), device_id_type=MESH
            )
            return carry

        lax.fori_loop(1, amount, greet, 0)
        for held in (wide, again):
            held[vocab : vocab + 8, :] = jnp.zeros((8, width), FLOAT)
        in_low[...] = in_ref[...].astype(NARROW)
        out_low[...] = out_ref[...].astype(NARROW)
        every_ref[me] = packed_ref[...]
        lines_ref[member] = line_ref[...]
        pl.semaphore_wait(barrier, amount - 1)

        def tell(k, carry):
            meta_copy(k).start()
            return carry

        lax.fori_loop(1, amount, tell, 0)
        for k in range(1, groups):
            line_copy(k).start()
        for w in range(2):
            for j in range(1, chips):
                lane_copy(w, j).start()
            own_core_copy(w).start()
        kept = [
            pltpu.make_async_copy(lows[w], fulls[w].at[member], local_sem.at[w])
            for w in range(2)
        ]
        for copy in kept:
            copy.start()

        def hear(k, carry):
            there = every_ref.at[lax.rem(me + amount - k, amount)]
            remote(there, there, meta_send.at[k], meta_recv.at[k], device(me)).wait_recv()
            return carry

        lax.fori_loop(1, amount, hear, 0)
        load = pltpu.make_async_copy(
            every_ref.at[pl.ds(replica * groups, groups)], ids, ids_sem
        )
        load.start()
        load.wait()
        fetch.wait()
        start = member * vocab

        def look(slot, ahead, source):
            for b in range(batches):

                def lap(i, carry):
                    first = pl.multiple_of(i * unroll, unroll)
                    for u in range(unroll):
                        if ahead and u + ahead >= unroll:
                            spot = first + u + ahead
                            token = ids[slot, b, jnp.minimum(spot, seq - 1)]
                            token = jnp.where(spot < seq, token, 0)
                        else:
                            token = ids[slot, b, first + u + ahead]
                        row = token - start
                        row = jnp.where((row >= 0) & (row < vocab), row, vocab)
                        looked[pl.ds(b * seq + first + u, 1), :] = source[pl.ds(row, 1), :]
                    return carry

                lax.fori_loop(0, seq // unroll, lap, 0)
            return looked[...].astype(NARROW)

        def lap(step, carry):
            j = lax.rem(step + 1, chips)
            there = chip_at(j) * 2

            to_core[j] = look(there + 1 - core, 0, wide)
            part_copy(j).start()
            mine = look(there + core, 0, wide).astype(FLOAT)
            part_copy(j).wait_recv()
            mine = mine + from_core[j].astype(FLOAT)

            @pl.when(j > 0)
            def _():
                to_lane[j] = mine.astype(NARROW)
                sum_copy(j).start()

            @pl.when(j == 0)
            def _():
                resid_ref[...] = mine

            return carry

        lax.fori_loop(0, chips, lap, 0)
        refetch.wait()

        def aim(slot, carry):
            @pl.when(slot == 0)
            def _():
                for w in range(2):
                    for c in range(1, chips):
                        lane_wait(w, c)
                        if split:
                            for k in range(1, replicas):
                                plane_copy(w, k, c).start()

            aims_ref[slot] = look(slot, 1, again)
            return carry

        lax.fori_loop(0, groups, aim, 0)
        for j in range(1, chips):
            sum_copy(j).wait_recv()
            resid_ref[...] += from_lane[j].astype(FLOAT)
        for w in range(2):
            for j in range(1, chips):
                if split:
                    for k in range(1, replicas):
                        plane_wait(w, k, j)
                core_copy(w, j).start()
        for w in range(2):
            kept[w].wait()
            for j in range(chips):
                core_wait(w, j)
                if j == 0:
                    own_core_copy(w).wait_send()
                else:
                    core_copy(w, j).wait_send()
                    lane_copy(w, j).wait_send()
                if split and j > 0:
                    for k in range(1, replicas):
                        plane_copy(w, k, j).wait_send()
        for k in range(1, groups):
            there = lines_ref.at[lax.rem(member + groups - k, groups)]
            remote(
                there, there, line_send.at[k], line_recv.at[k], place.at(replica, member)
            ).wait_recv()
            line_copy(k).wait_send()
        for j in range(chips):
            part_copy(j).wait_send()
            if j > 0:
                sum_copy(j).wait_send()

        def told(k, carry):
            meta_copy(k).wait_send()
            return carry

        lax.fori_loop(1, amount, told, 0)

    whole = pl.BlockSpec(memory_space=pltpu.VMEM)
    anywhere = pl.BlockSpec(memory_space=pl.ANY)
    dma = pltpu.SemaphoreType.DMA
    vmem = pltpu.VMEM
    every, lines, in_full, out_full, resid, aims = pl.pallas_call(
        kernel,
        in_specs=[whole, whole, whole, whole, anywhere, anywhere],
        out_specs=[whole, whole, anywhere, anywhere, whole, whole],
        out_shape=[
            jax.ShapeDtypeStruct((amount,) + packed.shape, jnp.int32),
            jax.ShapeDtypeStruct((groups,) + line.shape, FLOAT),
            jax.ShapeDtypeStruct((groups,) + in_shard.shape, NARROW),
            jax.ShapeDtypeStruct((groups,) + out_shard.shape, NARROW),
            jax.ShapeDtypeStruct((own, width), FLOAT),
            jax.ShapeDtypeStruct((groups, own, width), NARROW),
        ],
        scratch_shapes=[
            vmem(in_shard.shape, NARROW),
            vmem(out_shard.shape, NARROW),
            vmem((vocab + 8, width), FLOAT),
            vmem((vocab + 8, width), FLOAT),
            vmem((own, width), FLOAT),
            vmem((chips, own, width), NARROW),
            vmem((chips, own, width), NARROW),
            vmem((chips, own, width), NARROW),
            vmem((chips, own, width), NARROW),
            pltpu.SMEM((groups,) + packed.shape, jnp.int32),
            dma((2,)),
            dma,
            dma((2,)),
            dma((amount,)),
            dma((amount,)),
            dma((groups,)),
            dma((groups,)),
            dma((2, chips)),
            dma((2, chips)),
            dma((2, replicas, chips)),
            dma((2, replicas, chips)),
            dma((2, chips)),
            dma((2, chips)),
            dma((chips,)),
            dma((chips,)),
            dma((chips,)),
            dma((chips,)),
        ],
        compiler_params=pltpu.CompilerParams(
            vmem_limit_bytes=VMEM_LIMIT, collective_id=4, has_side_effects=True
        ),
        cost_estimate=pl.CostEstimate(
            flops=0, bytes_accessed=vocab * width * 4, transcendentals=0
        ),
    )(packed, line, in_shard, out_shard, table, head)
    return (
        every,
        lines,
        in_full.reshape(-1, in_shard.shape[1]),
        out_full.reshape(-1, out_shard.shape[1]),
        resid,
        aims,
    )


def head_kernel(table, own_hidden, aims, target, weight, groups, replicas):
    vocab, width = table.shape
    own = own_hidden.shape[0]
    block = block_rows(vocab, 1100)
    blocks = vocab // block
    chips = groups // 2
    lines = -(-blocks // 8) * 8

    def kernel(
        table_ref,
        own_ref,
        aims_ref,
        target_ref,
        weight_ref,
        grad_ref,
        logsum_ref,
        loss_ref,
        all_ref,
        wide,
        low,
        hid,
        exps,
        tops,
        totals,
        shares,
        to_core,
        from_core,
        to_lane,
        from_lane,
        aim_core,
        aim_lane,
        aim_from,
        table_sem,
        local_sem,
        lane_send,
        lane_recv,
        core_send,
        core_recv,
        plane_send,
        plane_recv,
        pass_send,
        pass_recv,
        stat_send,
        stat_recv,
        line_send,
        line_recv,
        part_send,
        part_recv,
        sum_send,
        sum_recv,
        aim_half_send,
        aim_half_recv,
        aim_send,
        aim_recv,
    ):
        place = Place(groups, replicas)
        me = place.member
        core = place.core

        def table_copy(b):
            return pltpu.make_async_copy(
                table_ref.at[pl.ds(b * block, block), :], wide.at[b % 2], table_sem.at[b % 2]
            )

        def chip_at(j):
            return lax.rem(place.chip + j, chips)

        def chip_before(j):
            return lax.rem(place.chip + chips - j, chips)

        def lane_device(j):
            return place.at(place.replica, chip_at(j) * 2 + core)

        def plane_device(k):
            return place.at(lax.rem(place.replica + k, replicas), me)

        def replica_before(k):
            return lax.rem(place.replica + replicas - k, replicas)

        def turn(step):
            if isinstance(step, int):
                return (step + 1) // 2 if step % 2 else (chips - step // 2) % chips
            ahead = (step + 1) // 2
            behind = lax.rem(chips - step // 2, chips)
            return jnp.where(lax.rem(step, 2) == 1, ahead, behind)

        def lane_copy(j):
            return remote(own_ref, hid.at[me], lane_send.at[j], lane_recv.at[j], lane_device(j))

        def lane_slot(j):
            return chip_before(j) * 2 + core

        def lane_wait(j):
            there = hid.at[lane_slot(j)]
            remote(there, there, lane_send.at[j], lane_recv.at[j], lane_device(j)).wait_recv()

        def core_copy(j):
            here = hid.at[lane_slot(j)]
            return remote(here, here, core_send.at[j], core_recv.at[j], place.sibling())

        def core_wait(j):
            there = hid.at[chip_before(j) * 2 + 1 - core]
            remote(there, there, core_send.at[j], core_recv.at[j], place.sibling()).wait_recv()

        def plane_copy(k, j):
            slot = lane_slot(j)
            return remote(
                hid.at[slot],
                all_ref.at[place.replica * groups + slot],
                plane_send.at[k, j],
                plane_recv.at[k, j],
                plane_device(k),
            )

        def plane_wait(k, j):
            there = all_ref.at[replica_before(k) * groups + lane_slot(j)]
            remote(
                there, there, plane_send.at[k, j], plane_recv.at[k, j], plane_device(k)
            ).wait_recv()

        def pass_copy(k, j):
            here = all_ref.at[replica_before(k) * groups + lane_slot(j)]
            return remote(
                here, here, pass_send.at[k, j], pass_recv.at[k, j], place.sibling()
            )

        def pass_wait(k, j):
            there = all_ref.at[
                replica_before(k) * groups + chip_before(j) * 2 + 1 - core
            ]
            remote(
                there, there, pass_send.at[k, j], pass_recv.at[k, j], place.sibling()
            ).wait_recv()

        def member_at(k):
            return lax.rem(me + k, groups)

        def stat_copy(k):
            return remote(
                shares.at[me],
                shares.at[me],
                stat_send.at[k],
                stat_recv.at[k],
                place.at(place.replica, member_at(k)),
            )

        def stat_wait(k):
            there = shares.at[lax.rem(me + groups - k, groups)]
            remote(
                there, there, stat_send.at[k], stat_recv.at[k], place.at(place.replica, me)
            ).wait_recv()

        def line_copy(k):
            here = logsum_ref.at[place.replica]
            return remote(here, here, line_send.at[k], line_recv.at[k], plane_device(k))

        def line_wait(k):
            there = logsum_ref.at[replica_before(k)]
            remote(there, there, line_send.at[k], line_recv.at[k], plane_device(k)).wait_recv()

        def part_copy(j):
            return remote(
                to_core.at[j], from_core.at[j], part_send.at[j], part_recv.at[j], place.sibling()
            )

        def sum_copy(j):
            return remote(
                to_lane.at[j], from_lane.at[j], sum_send.at[j], sum_recv.at[j], lane_device(j)
            )

        def aim_half(c):
            return remote(
                aims_ref.at[c * 2 + 1 - core],
                aim_core.at[c],
                aim_half_send.at[c],
                aim_half_recv.at[c],
                place.sibling(),
            )

        def aim_copy(j):
            return remote(
                aim_lane.at[j], aim_from.at[j], aim_send.at[j], aim_recv.at[j], lane_device(j)
            )

        table_copy(0).start()
        if blocks > 1:
            table_copy(1).start()
        meet(
            [place.at(place.replica, member_at(k)) for k in range(1, groups)] + place.planes()
        )
        own_core = remote(own_ref, hid.at[me], core_send.at[0], core_recv.at[0], place.sibling())
        own_core.start()
        for step in range(1, min(3, chips)):
            lane_copy(turn(step)).start()
        hid[me] = own_ref[...]
        for k in range(1, replicas):
            plane_copy(k, 0).start()
        for c in range(chips):
            aim_half(c).start()
        for b in range(blocks):
            table_copy(b).wait()
            low[b] = wide[b % 2].astype(NARROW)
            if b + 2 < blocks:
                table_copy(b + 2).start()

        spots = lax.broadcasted_iota(jnp.int32, (block, own), 0)

        def forward(step, carry):
            j = turn(step // 2)
            other = lax.rem(step, 2)

            @pl.when(step == 1)
            def _():
                for later in range(3, chips):
                    lane_copy(turn(later)).start()
                there = hid.at[place.sibling_member]
                remote(
                    there, there, core_send.at[0], core_recv.at[0], place.sibling()
                ).wait_recv()

            @pl.when((step > 1) & (other == 0))
            def _():
                lane_wait(j)
                core_copy(j).start()

                def spread(k, carry):
                    plane_copy(k, j).start()
                    return carry

                lax.fori_loop(1, replicas, spread, 0)

            @pl.when((step > 1) & (other == 1))
            def _():
                core_wait(j)

            @pl.when(step == groups // 2 + 1)
            def _():
                for c in range(chips):
                    aim_half(c).wait_recv()
                for i in range(chips):
                    chip = chip_at(i)
                    aim_lane[i] = (
                        aims_ref[chip * 2 + core].astype(FLOAT) + aim_core[chip].astype(FLOAT)
                    ).astype(NARROW)
                for i in range(1, chips):
                    aim_copy(i).start()

            member = chip_before(j) * 2 + lax.rem(core + other, 2)
            here = hid[member]
            for b in range(blocks):
                logits = lax.dot_general(
                    low[b], here, LAST_CONTRACT, preferred_element_type=FLOAT
                )
                top = jnp.max(logits, axis=0, keepdims=True)
                values = jnp.exp(logits - top)
                tops[member, b : b + 1, :] = top
                totals[member, b : b + 1, :] = jnp.sum(values, axis=0, keepdims=True)
                exps[b, member] = values.astype(NARROW)
            block_tops = tops[member, :blocks, :]
            top = jnp.max(block_tops, axis=0, keepdims=True)
            total = jnp.sum(
                totals[member, :blocks, :] * jnp.exp(block_tops - top), axis=0, keepdims=True
            )
            shares[me, pl.ds(member, 1), :] = top + jnp.log(total)
            return carry

        lax.fori_loop(0, groups, forward, 0)
        local = pltpu.make_async_copy(
            hid, all_ref.at[pl.ds(place.replica * groups, groups)], local_sem
        )
        local.start()
        for k in range(1, groups):
            stat_copy(k).start()
        for k in range(1, groups):
            stat_wait(k)
        every = shares[...]
        top = jnp.max(every, axis=0)
        logsum_ref[place.replica] = top + jnp.log(jnp.sum(jnp.exp(every - top[None]), axis=0))
        for k in range(1, replicas):
            line_copy(k).start()

        def member_back(member):
            wanted = target_ref[member]
            weights = weight_ref[member]
            logsum = logsum_ref[place.replica, pl.ds(member, 1), :]
            total = jnp.zeros((own, width), FLOAT)
            for b in range(blocks):
                scale = weights * jnp.exp(tops[member, b : b + 1, :] - logsum)
                grads = exps[b, member].astype(FLOAT) * scale
                grads = jnp.where(spots == wanted - b * block, 0.0, grads)
                total = total + lax.dot_general(
                    grads.astype(NARROW), low[b], ROWS_CONTRACT, preferred_element_type=FLOAT
                )
            return total

        def backward(step, carry):
            j = turn(chips - 1 - step)

            @pl.when(step == chips - 1)
            def _():
                for k in range(1, replicas):
                    for c in range(chips):
                        plane_wait(k, c)
                for k in range(1, replicas):
                    for c in range(chips):
                        pass_copy(k, c).start()

            there = chip_at(j) * 2
            to_core[j] = member_back(there + 1 - core).astype(NARROW)
            part_copy(j).start()
            mine = member_back(there + core)
            part_copy(j).wait_recv()
            mine = mine + from_core[j].astype(FLOAT)

            @pl.when(j > 0)
            def _():
                to_lane[j] = mine.astype(NARROW)
                sum_copy(j).start()

            @pl.when(j == 0)
            def _():
                grad_ref[...] = mine

            return carry

        lax.fori_loop(0, chips, backward, 0)
        held = lax.broadcasted_iota(jnp.int32, (groups, own), 0) == me
        amounts = jnp.concatenate([weight_ref[m] for m in range(groups)], axis=0)

        def own_column(values):
            return jnp.sum(jnp.where(held, values, 0.0).T, axis=1, keepdims=True)

        amount = own_column(amounts)
        logsum = own_column(logsum_ref[place.replica])
        aimed = aim_lane[0].astype(FLOAT)
        for j in range(1, chips):
            aim_copy(j).wait_recv()
            aimed = aimed + aim_from[j].astype(FLOAT)
        hit = jnp.sum(own_ref[...].astype(FLOAT) * aimed, axis=1, keepdims=True)
        loss_ref[...] = amount * (logsum - hit)
        part = (amount * (jnp.exp(hit - logsum) - 1.0)).astype(NARROW).astype(FLOAT)
        total = grad_ref[...] + part * aimed
        for j in range(1, chips):
            sum_copy(j).wait_recv()
            total = total + from_lane[j].astype(FLOAT)
        grad_ref[...] = total
        local.wait()
        own_core.wait_send()
        for k in range(1, groups):
            stat_copy(k).wait_send()
        for k in range(1, replicas):
            line_wait(k)
            line_copy(k).wait_send()
            for j in range(chips):
                pass_wait(k, j)
                plane_copy(k, j).wait_send()
                pass_copy(k, j).wait_send()
        for j in range(chips):
            part_copy(j).wait_send()
            aim_half(j).wait_send()
            if j > 0:
                lane_copy(j).wait_send()
                core_copy(j).wait_send()
                sum_copy(j).wait_send()
                aim_copy(j).wait_send()

    whole = pl.BlockSpec(memory_space=pltpu.VMEM)
    anywhere = pl.BlockSpec(memory_space=pl.ANY)
    dma = pltpu.SemaphoreType.DMA
    vmem = pltpu.VMEM
    grad, logsum, loss, everyone = pl.pallas_call(
        kernel,
        in_specs=[anywhere, whole, whole, whole, whole],
        out_specs=[whole, whole, whole, anywhere],
        out_shape=[
            jax.ShapeDtypeStruct((own, width), FLOAT),
            jax.ShapeDtypeStruct((replicas, groups, own), FLOAT),
            jax.ShapeDtypeStruct((own, 1), FLOAT),
            jax.ShapeDtypeStruct((replicas * groups, own, width), NARROW),
        ],
        scratch_shapes=[
            vmem((2, block, width), FLOAT),
            vmem((blocks, block, width), NARROW),
            vmem((groups, own, width), NARROW),
            vmem((blocks, groups, block, own), NARROW),
            vmem((groups, lines, own), FLOAT),
            vmem((groups, lines, own), FLOAT),
            vmem((groups, groups, own), FLOAT),
            vmem((chips, own, width), NARROW),
            vmem((chips, own, width), NARROW),
            vmem((chips, own, width), NARROW),
            vmem((chips, own, width), NARROW),
            vmem((chips, own, width), NARROW),
            vmem((chips, own, width), NARROW),
            vmem((chips, own, width), NARROW),
            dma((2,)),
            dma,
            dma((chips,)),
            dma((chips,)),
            dma((chips,)),
            dma((chips,)),
            dma((replicas, chips)),
            dma((replicas, chips)),
            dma((replicas, chips)),
            dma((replicas, chips)),
            dma((groups,)),
            dma((groups,)),
            dma((replicas,)),
            dma((replicas,)),
            dma((chips,)),
            dma((chips,)),
            dma((chips,)),
            dma((chips,)),
            dma((chips,)),
            dma((chips,)),
            dma((chips,)),
            dma((chips,)),
        ],
        compiler_params=pltpu.CompilerParams(
            vmem_limit_bytes=VMEM_LIMIT + 2**21, collective_id=3, has_side_effects=True
        ),
        cost_estimate=pl.CostEstimate(
            flops=4 * vocab * groups * own * width,
            bytes_accessed=vocab * width * 4,
            transcendentals=vocab * groups * own,
        ),
    )(
        table,
        own_hidden,
        aims,
        target.reshape(groups, 1, own),
        weight.reshape(groups, 1, own),
    )
    return grad, logsum.reshape(-1), jnp.sum(loss), everyone.reshape(-1, width)


def head_table_grad(
    table, hidden, logsum, weights, target, token_grad, slices, owner_grads, cut, groups, replicas
):
    vocab, width = table.shape
    amount = groups * replicas
    rows = hidden.shape[0]
    own = token_grad.shape[0]
    tile = math.gcd(rows, 2048)
    block = block_rows(vocab, 1100)
    tiles = rows // tile
    steps = vocab // block
    chips = groups // 2
    last = steps - 1
    shard = owner_grads.shape[1]
    regions = ((0, cut), (cut, shard - cut))
    firsts, seconds = (replicas, chips), (chips, replicas)
    reduce = all(count % (8 * replicas) == 0 for _, count in regions)
    laps = steps * tiles

    def when(part):
        return min(int(laps * part), laps - 1)

    def kernel(
        table_ref,
        hidden_ref,
        logsum_ref,
        weight_ref,
        target_ref,
        own_ref,
        slices_ref,
        owner_ref,
        grad_ref,
        square_ref,
        all_ref,
        summed_ref,
        owned_out,
        gathered,
        owned_ref,
        from_core,
        acc_in,
        acc_out,
        one_in,
        one_out,
        two_in,
        two_out,
        piece_sem,
        half_send,
        half_recv,
        one_send,
        one_recv,
        two_send,
        two_recv,
        end_send,
        end_recv,
        local_sem,
        slice_send,
        slice_recv,
        lane_send,
        lane_recv,
        plane_send,
        plane_recv,
        core_send,
        core_recv,
    ):
        step = pl.program_id(0)
        place = Place(groups, replicas)
        me = place.replica * groups + place.member

        def slot(replica, member):
            return all_ref.at[replica * groups + member]

        def lane_copy(k):
            here = all_ref.at[me]
            return remote(own_ref, here, lane_send.at[k], lane_recv.at[k], place.lane(k))

        def lane_wait(k):
            back = lax.rem(place.chip + chips - k, chips) * 2 + place.core
            there = slot(place.replica, back)
            remote(there, there, lane_send.at[k], lane_recv.at[k], place.lane(k)).wait_recv()

        def plane_copy(k, c):
            here = slot(place.replica, c * 2 + place.core)
            return remote(here, here, plane_send.at[k, c], plane_recv.at[k, c], place.plane(k))

        def plane_wait(k, c):
            back = lax.rem(place.replica + replicas - k, replicas)
            there = slot(back, c * 2 + place.core)
            remote(
                there, there, plane_send.at[k, c], plane_recv.at[k, c], place.plane(k)
            ).wait_recv()

        def core_copy(r, c):
            here = slot(r, c * 2 + place.core)
            return remote(here, here, core_send.at[r, c], core_recv.at[r, c], place.sibling())

        def core_wait(r, c):
            there = slot(r, c * 2 + 1 - place.core)
            remote(
                there, there, core_send.at[r, c], core_recv.at[r, c], place.sibling()
            ).wait_recv()

        def device(index):
            return place.at(index // groups, lax.rem(index, groups))

        def slice_copy(k):
            there = lax.rem(me + k, amount)
            return remote(
                slices_ref.at[lax.rem(there, groups)],
                gathered.at[me],
                slice_send.at[k],
                slice_recv.at[k],
                device(there),
            )

        local = pltpu.make_async_copy(own_ref, all_ref.at[me], local_sem)
        accs, ones, twos = (acc_in, acc_out), (one_in, one_out), (two_in, two_out)

        def chip_at(j):
            return lax.rem(place.chip + j, chips)

        def pieces(g):
            first, rows = regions[g]
            size = rows // replicas
            for k in range(firsts[g]):
                for i in range(seconds[g]):
                    if g == 0:
                        chip, replica = i, place.plane_replica(k)
                    else:
                        chip, replica = chip_at(k), i
                    yield k, i, chip, pl.multiple_of(first + replica * size, 8), size

        def piece_copy(g, k, i, chip, row, size):
            return pltpu.make_async_copy(
                owner_ref.at[chip * 2 + place.core, pl.ds(row, size), :],
                accs[g].at[k, i],
                piece_sem.at[g, k, i],
            )

        def half_copy(c):
            return remote(
                owner_ref.at[c * 2 + 1 - place.core],
                from_core.at[c],
                half_send.at[c],
                half_recv.at[c],
                place.sibling(),
            )

        def partner(over_dp, k):
            if over_dp:
                return place.plane(k)
            return place.lane(k)

        def one_copy(g, k):
            return remote(
                accs[g].at[k],
                ones[g].at[k],
                one_send.at[g, k],
                one_recv.at[g, k],
                partner(g == 0, k),
            )

        def mine(g):
            return place.chip if g == 0 else place.replica

        def two_copy(g, k):
            return remote(
                accs[g].at[0, lax.rem(mine(g) + k, seconds[g])],
                twos[g].at[k],
                two_send.at[g, k],
                two_recv.at[g, k],
                partner(g == 1, k),
            )

        def end_copy(g, k, there):
            first, rows = regions[g]
            size = rows // replicas
            span = owned_ref.at[pl.ds(pl.multiple_of(first + there * size, 8), size), :]
            return remote(span, span, end_send.at[g, k], end_recv.at[g, k], place.plane(k))

        def begin_sums():
            for c in range(chips):
                half_copy(c).start()
            for g in range(2):
                for item in pieces(g):
                    piece_copy(g, *item).start()

        def begin_one():
            for c in range(chips):
                half_copy(c).wait_recv()
            for g in range(2):
                for item in pieces(g):
                    piece_copy(g, *item).wait()
                    k, i, chip, row, size = item
                    accs[g][k, i] += from_core[chip, pl.ds(row, size), :]
                for k in range(1, firsts[g]):
                    one_copy(g, k).start()

        def begin_two(g):
            for k in range(1, firsts[g]):
                one_copy(g, k).wait_recv()
            for i in range(seconds[g]):
                total = accs[g][0, i]
                for k in range(1, firsts[g]):
                    total = total + ones[g][k, i]
                accs[g][0, i] = total
            for k in range(1, seconds[g]):
                two_copy(g, k).start()

        def begin_end(g):
            first, rows = regions[g]
            size = rows // replicas
            total = accs[g][0, mine(g)]
            for k in range(1, seconds[g]):
                two_copy(g, k).wait_recv()
                total = total + twos[g][k]
            row = pl.multiple_of(first + place.replica * size, 8)
            owned_ref[pl.ds(row, size), :] = total
            for k in range(1, replicas):
                end_copy(g, k, place.replica).start()

        def end_sums():
            for g in range(2):
                for k in range(1, replicas):
                    end_copy(g, k, lax.rem(place.replica + replicas - k, replicas)).wait_recv()
                    end_copy(g, k, place.replica).wait_send()
                for k in range(1, firsts[g]):
                    one_copy(g, k).wait_send()
                for k in range(1, seconds[g]):
                    two_copy(g, k).wait_send()
            for c in range(chips):
                half_copy(c).wait_send()

        def begin_all():
            barrier = pltpu.get_barrier_semaphore()

            def greet(k, carry):
                pl.semaphore_signal(
                    barrier,
                    inc=1,
                    device_id=device(lax.rem(me + k, amount)),
                    device_id_type=MESH,
                )
                return carry

            lax.fori_loop(1, amount, greet, 0)
            pl.semaphore_wait(barrier, amount - 1)
            local.start()
            if reduce:
                begin_sums()
            for k in range(1, chips):
                lane_copy(k).start()

            def give(k, carry):
                slice_copy(k).start()
                return carry

            lax.fori_loop(1, amount, give, 0)
            gathered[me] = slices_ref[place.member]

        def token_lane():
            local.wait()
            for k in range(1, chips):
                lane_wait(k)
            for c in range(chips):
                core_copy(place.replica, c).start()

        def token_plane():
            for c in range(chips):
                for k in range(1, replicas):
                    plane_copy(k, c).start()

        def token_core():
            for k in range(1, replicas):
                for c in range(chips):
                    plane_wait(k, c)
            for k in range(1, replicas):
                for c in range(chips):
                    core_copy(place.plane_replica(k), c).start()

        plan = [(0.0, begin_all)]
        if reduce:
            plan = plan + [
                (0.09, begin_one),
                (0.25, token_lane),
                (0.4, lambda: begin_two(0)),
                (0.4, token_plane),
                (0.65, lambda: begin_two(1)),
                (0.75, lambda: begin_end(0)),
                (0.8, lambda: begin_end(1)),
                (0.8, token_core),
            ]
        else:
            plan = plan + [(0.17, token_lane), (0.17, token_plane), (0.5, token_core)]

        start = step * block
        part = table_ref[...].astype(NARROW)
        places = lax.broadcasted_iota(jnp.int32, (block, tile), 0)

        def lap(k, carry):
            for part_of, act in plan:
                pl.when(step * tiles + k == when(part_of))(act)
            here = hidden_ref[pl.ds(pl.multiple_of(k * tile, tile), tile), :]
            logits = lax.dot_general(part, here, LAST_CONTRACT, preferred_element_type=FLOAT)
            probs = jnp.exp(logits - logsum_ref[k])
            grads = jnp.where(
                places == target_ref[k] - start, probs - weight_ref[k], probs
            ).astype(NARROW)
            piece = jnp.dot(grads, here, preferred_element_type=FLOAT)

            @pl.when(k == 0)
            def _():
                grad_ref[...] = piece

            @pl.when(k > 0)
            def _():
                grad_ref[...] += piece

            return carry

        lax.fori_loop(0, tiles, lap, 0)
        squares = jnp.sum(jnp.square(grad_ref[...]), axis=0, keepdims=True)

        @pl.when(step == 0)
        def _():
            square_ref[...] = squares

        @pl.when(step > 0)
        def _():
            square_ref[...] += squares

        @pl.when(step == last)
        def _():
            def take(k, carry):
                there = gathered.at[lax.rem(me + amount - k, amount)]
                remote(there, there, slice_send.at[k], slice_recv.at[k], device(me)).wait_recv()
                slice_copy(k).wait_send()
                return carry

            lax.fori_loop(1, amount, take, 0)
            if reduce:
                end_sums()
                owned_out[...] = owned_ref[...]
            summed_ref[...] = jnp.sum(gathered[...], axis=0)
            for r in range(replicas):
                for c in range(chips):
                    core_wait(r, c)
            for k in range(1, chips):
                lane_copy(k).wait_send()
            for c in range(chips):
                for k in range(1, replicas):
                    plane_copy(k, c).wait_send()
                for r in range(replicas):
                    core_copy(r, c).wait_send()

    whole = pl.BlockSpec(memory_space=pltpu.VMEM)
    anywhere = pl.BlockSpec(memory_space=pl.ANY)
    shape = (tiles, 1, tile)
    dma = pltpu.SemaphoreType.DMA
    return pl.pallas_call(
        kernel,
        grid=(steps,),
        in_specs=[pl.BlockSpec((block, width), lambda i: (i, 0))]
        + [whole] * 4
        + [anywhere, whole, anywhere],
        out_specs=[
            pl.BlockSpec((block, width), lambda i: (i, 0)),
            pl.BlockSpec((1, width), lambda i: (0, 0)),
            anywhere,
            whole,
            whole,
        ],
        out_shape=[
            jax.ShapeDtypeStruct((vocab, width), FLOAT),
            jax.ShapeDtypeStruct((1, width), FLOAT),
            jax.ShapeDtypeStruct((groups * replicas, own, width), NARROW),
            jax.ShapeDtypeStruct(slices.shape[1:], FLOAT),
            jax.ShapeDtypeStruct(owner_grads.shape[1:] if reduce else (8, 128), FLOAT),
        ],
        scratch_shapes=[
            pltpu.VMEM((amount,) + slices.shape[1:], FLOAT),
            pltpu.VMEM(owner_grads.shape[1:] if reduce else (8, 128), FLOAT),
            pltpu.VMEM((chips,) + owner_grads.shape[1:] if reduce else (8, 128), FLOAT),
        ]
        + [
            pltpu.VMEM(
                (counts[g], seconds[g], regions[g][1] // replicas, width)[skip:]
                if reduce
                else (8, 128),
                FLOAT,
            )
            for counts, skip in ((firsts, 0), (firsts, 0), (seconds, 1))
            for g in range(2)
        ]
        + [
            dma((2, max(firsts), max(seconds))),
            dma((chips,)),
            dma((chips,)),
            dma((2, max(firsts))),
            dma((2, max(firsts))),
            dma((2, max(seconds))),
            dma((2, max(seconds))),
            dma((2, replicas)),
            dma((2, replicas)),
            dma,
            dma((amount,)),
            dma((amount,)),
            dma((chips,)),
            dma((chips,)),
            dma((replicas, chips)),
            dma((replicas, chips)),
            dma((replicas, chips)),
            dma((replicas, chips)),
        ],
        compiler_params=pltpu.CompilerParams(
            vmem_limit_bytes=VMEM_LIMIT, collective_id=1, has_side_effects=True
        ),
        cost_estimate=pl.CostEstimate(
            flops=4 * vocab * rows * width,
            bytes_accessed=vocab * width * 8 + rows * width * 4,
            transcendentals=vocab * rows,
        ),
    )(
        table,
        hidden,
        logsum.reshape(shape),
        weights.reshape(shape),
        target.reshape(shape),
        token_grad,
        slices,
        owner_grads,
    )


def exchange_scalars(line, groups, replicas):
    amount = groups * replicas

    def kernel(own_ref, all_ref, local_sem, send_sem, recv_sem):
        place = Place(groups, replicas)
        me = place.replica * groups + place.member

        def device(index):
            return place.at(index // groups, lax.rem(index, groups))

        barrier = pltpu.get_barrier_semaphore()

        def greet(k, carry):
            pl.semaphore_signal(
                barrier, inc=1, device_id=device(lax.rem(me + k, amount)), device_id_type=MESH
            )
            return carry

        def copy(k):
            return remote(
                own_ref,
                all_ref.at[me],
                send_sem.at[k],
                recv_sem.at[k],
                device(lax.rem(me + k, amount)),
            )

        def begin(k, carry):
            copy(k).start()
            return carry

        def finish(k, carry):
            there = all_ref.at[lax.rem(me + amount - k, amount)]
            remote(there, there, send_sem.at[k], recv_sem.at[k], device(me)).wait_recv()
            copy(k).wait_send()
            return carry

        lax.fori_loop(1, amount, greet, 0)
        local = pltpu.make_async_copy(own_ref, all_ref.at[me], local_sem)
        local.start()
        pl.semaphore_wait(barrier, amount - 1)
        lax.fori_loop(1, amount, begin, 0)
        local.wait()
        lax.fori_loop(1, amount, finish, 0)

    whole = pl.BlockSpec(memory_space=pltpu.VMEM)
    dma = pltpu.SemaphoreType.DMA
    return pl.pallas_call(
        kernel,
        in_specs=[whole],
        out_specs=whole,
        out_shape=jax.ShapeDtypeStruct((amount,) + line.shape, line.dtype),
        scratch_shapes=[dma, dma((amount,)), dma((amount,))],
        compiler_params=pltpu.CompilerParams(collective_id=2, has_side_effects=True),
    )(line)


def chunk_lists(local, inside, chunk):
    chunks = local.shape[0] // chunk
    flags = inside.reshape(chunks, chunk)
    spots = jnp.arange(chunk, dtype=jnp.int32)
    ahead = (spots[:, None] < spots[None, :]).astype(NARROW)
    order = jnp.dot(flags.astype(NARROW), ahead, preferred_element_type=FLOAT).astype(jnp.int32)
    chosen = (order[:, None, :] == spots[None, :, None]) & flags[:, None, :]
    places = jnp.sum(jnp.where(chosen, spots[None, None, :], 0), axis=2)
    rows = jnp.sum(jnp.where(chosen, local.reshape(chunks, 1, chunk), 0), axis=2)
    return places, rows, jnp.sum(flags.astype(jnp.int32), axis=1)


def embed_table_grad(token_grads, places, rows, counts, vocab):
    chunks, chunk = places.shape
    width = token_grads.shape[-1]
    padded = vocab + 8
    unroll = 4

    def kernel(
        count_ref, place_ref, row_ref, tokens_ref, grad_ref, square_ref, wide_ref, total_ref, sem
    ):
        step = pl.program_id(0)

        @pl.when(step == 0)
        def _():
            total_ref[...] = jnp.zeros_like(total_ref)

        wide_ref[...] = tokens_ref[...].astype(FLOAT)
        amount = count_ref[step]

        def lap(j, carry):
            for u in range(unroll):
                spot = j * unroll + u
                row = jnp.where(spot < amount, row_ref[0, 0, spot], vocab)
                place = place_ref[0, 0, spot]
                total_ref[pl.ds(row, 1), :] += wide_ref[pl.ds(place, 1), :]
            return carry

        lax.fori_loop(0, (amount + unroll - 1) // unroll, lap, 0)

        @pl.when(step == chunks - 1)
        def _():
            out = pltpu.make_async_copy(total_ref.at[pl.ds(0, vocab), :], grad_ref, sem)
            out.start()
            square_ref[...] = jnp.sum(
                jnp.square(total_ref[pl.ds(0, vocab), :]), axis=0, keepdims=True
            )
            out.wait()

    line = pl.BlockSpec((1, 1, chunk), lambda i, c: (i, 0, 0), memory_space=pltpu.SMEM)
    return pl.pallas_call(
        kernel,
        grid_spec=pltpu.PrefetchScalarGridSpec(
            num_scalar_prefetch=1,
            grid=(chunks,),
            in_specs=[line, line, pl.BlockSpec((chunk, width), lambda i, c: (i, 0))],
            out_specs=[
                pl.BlockSpec(memory_space=pl.ANY),
                pl.BlockSpec((1, width), lambda i, c: (0, 0)),
            ],
            scratch_shapes=[
                pltpu.VMEM((chunk, width), FLOAT),
                pltpu.VMEM((padded, width), FLOAT),
                pltpu.SemaphoreType.DMA,
            ],
        ),
        out_shape=[
            jax.ShapeDtypeStruct((vocab, width), FLOAT),
            jax.ShapeDtypeStruct((1, width), FLOAT),
        ],
        compiler_params=pltpu.CompilerParams(vmem_limit_bytes=VMEM_LIMIT),
    )(
        counts,
        places.reshape(chunks, 1, chunk),
        rows.reshape(chunks, 1, chunk),
        token_grads.reshape(chunks * chunk, width),
    )


def update_rule(weight, grad, moment, average, rate, clip_factor):
    clipped = clip_factor * grad
    new_moment = MOMENTUM * moment + clipped
    new_weight = weight - rate * (clipped + MOMENTUM * new_moment)
    new_average = DECAY * average + (1.0 - DECAY) * new_weight
    return (new_weight, new_moment, new_average)


def update_all(scalars, tables, matrices, rates):
    vocab, width = tables[0][0].shape
    sub = tables[0][3].shape[0]
    block = block_rows(vocab, 1100)
    blocks = vocab // block
    window = max(-(-(sub + sub * r % 8) // 8) * 8 for r in range(vocab // sub))
    tile = 264
    tiles = -(-window // tile)
    steps = 2 * blocks + 2 * tiles
    count = len(matrices)

    def kernel(*refs):
        refs = list(refs)

        def take(amount):
            taken = refs[:amount]
            del refs[:amount]
            return taken

        (scalars_ref,) = take(1)
        whole_in = [take(3) for _ in range(2)]
        own_in = [take(4) for _ in range(2)]
        small_in = [take(4) for _ in range(count)]
        new_tables = take(2)
        own_out = [take(2) for _ in range(2)]
        small_out = [take(3) for _ in range(count)]
        (factor_ref,) = take(1)
        windows = take(2)
        (sems,) = take(1)
        step = pl.program_id(0)
        begin = lax.axis_index("dp") * sub
        low = pl.multiple_of(begin // 8 * 8, 8)
        shift = begin - low

        def fetch(w, t):
            first = t * tile
            size = min(tile, window - first)
            return [
                pltpu.make_async_copy(
                    own_in[w][i].at[pl.ds(low + first, size), :],
                    windows[i].at[pl.ds(first, size), :],
                    sems.at[w, i, t],
                )
                for i in range(2)
            ]

        @pl.when(step == 0)
        def _():
            total = jnp.sum(scalars_ref[...], axis=0)
            norm = jnp.sqrt(total)
            factor_ref[...] = CLIP_LEVEL / jnp.maximum(norm, CLIP_LEVEL)

        factor = factor_ref[1:2, 0:1]
        for w in range(2):

            @pl.when((step >= w * blocks) & (step < (w + 1) * blocks))
            def _():
                table_ref, grad_ref, moment_ref = whole_in[w]
                table = table_ref[...]
                new_tables[w][...], _, _ = update_rule(
                    table, grad_ref[...], moment_ref[...].astype(FLOAT), table, rates[w], factor
                )

        @pl.when(step == 1)
        def _():
            for i in range(count):
                weight, grad, moment, average = [ref[...] for ref in small_in[i]]
                results = update_rule(weight, grad, moment, average, rates[2 + i], factor)
                for ref, result in zip(small_out[i], results):
                    ref[...] = result

        for w in range(2):
            base = 2 * blocks + w * tiles
            for t in range(tiles):

                @pl.when(step == (base - tiles + t + 1 if w else blocks))
                def _():
                    for copy in fetch(w, t):
                        copy.start()

            for t in range(tiles):

                @pl.when(step == base + t)
                def _():
                    if t == 0:
                        for copy in fetch(w, 0):
                            copy.wait()
                    if t + 1 < tiles:
                        for copy in fetch(w, t + 1):
                            copy.wait()

            @pl.when((step >= base) & (step < base + tiles))
            def _():
                first = pl.multiple_of((step - base) * tile, 8)
                amount = jnp.where(shift == 0, 0, tile + 8 - shift)
                own_table, own_grad = [
                    pltpu.roll(win[pl.ds(first, tile + 8), :], amount, 0)[:tile]
                    for win in windows
                ]
                _, own_out[w][0][...], own_out[w][1][...] = update_rule(
                    own_table, own_grad, own_in[w][2][...], own_in[w][3][...], rates[w], factor
                )

    whole = pl.BlockSpec(memory_space=pltpu.VMEM)
    anywhere = pl.BlockSpec(memory_space=pl.ANY)

    def table_spec(w):
        return pl.BlockSpec(
            (block, width), lambda i: (jnp.clip(i - w * blocks, 0, blocks - 1), 0)
        )

    def own_spec(w):
        return pl.BlockSpec(
            (tile, width),
            lambda i: (jnp.clip(i - 2 * blocks - w * tiles, 0, tiles - 1), 0),
        )

    state = jax.ShapeDtypeStruct((sub, width), FLOAT)
    operands = [scalars]
    in_specs = [whole]
    for w in range(2):
        operands += list(tables[w][:3])
        in_specs += [table_spec(w)] * 3
    for w in range(2):
        operands += [tables[w][0], tables[w][1], tables[w][3], tables[w][4]]
        in_specs += [anywhere, anywhere, own_spec(w), own_spec(w)]
    for item in matrices:
        operands += list(item)
        in_specs += [whole] * 4
    out_specs = [table_spec(0), table_spec(1)]
    out_shape = [jax.ShapeDtypeStruct((vocab, width), FLOAT)] * 2
    for w in range(2):
        out_specs += [own_spec(w)] * 2
        out_shape += [state] * 2
    for item in matrices:
        out_specs += [whole] * 3
        out_shape += [jax.ShapeDtypeStruct(item[0].shape, FLOAT)] * 3
    results = pl.pallas_call(
        kernel,
        grid=(steps,),
        in_specs=in_specs,
        out_specs=out_specs,
        out_shape=out_shape,
        scratch_shapes=[pltpu.VMEM((8, 128), FLOAT)]
        + [pltpu.VMEM((tiles * tile + 8, width), FLOAT)] * 2
        + [pltpu.SemaphoreType.DMA((2, 2, tiles))],
        compiler_params=pltpu.CompilerParams(vmem_limit_bytes=VMEM_LIMIT),
    )(*operands)
    tables_out = [(results[w], *results[2 + 2 * w : 4 + 2 * w]) for w in range(2)]
    return tables_out, [results[6 + 3 * i : 9 + 3 * i] for i in range(count)]


def shards(
    token_ids,
    loss_mask,
    lengths,
    buffer_ids,
    embed_table,
    embed_moment,
    embed_average,
    head_table,
    head_moment,
    head_average,
    in_weights,
    in_moment,
    in_average,
    out_weights,
    out_moment,
    out_average,
    vectors,
    vector_moment,
    vector_average,
):
    groups = lax.axis_size("fsdp")
    replicas = lax.axis_size("dp")
    member = lax.axis_index("fsdp")
    replica = lax.axis_index("dp")
    batches, _, seq = token_ids.shape
    vocab_rows, width = embed_table.shape
    head_size = width // HEADS
    vocab_start = member * vocab_rows
    own_rows = batches * seq
    rows_all = groups * own_rows

    tokens, marks, buffers = token_ids[:, 0], loss_mask[:, 0], buffer_ids[:, 0]
    divisor, offset, counted = jax.vmap(functools.partial(slot_info, buffer_count=NSEG))(
        tokens, marks, lengths[:, 0], buffers
    )
    packed = jnp.concatenate(
        [
            tokens,
            divisor,
            jnp.broadcast_to(jnp.sum(counted), (8 - 2 * batches, seq)),
        ],
        axis=0,
    )
    amount = vectors.shape[0]
    line = jnp.pad(vectors, (0, -amount % 1024)).reshape(-1, 128)
    everyone, lines, in_full, out_full, resid, aims = start_kernel(
        packed,
        line,
        in_weights,
        out_weights,
        embed_table,
        head_table,
        batches,
        groups,
        replicas,
    )
    vector_full = lines.reshape(groups, -1)[:, :amount].reshape(-1).astype(NARROW)
    embed_moment_low = lax.all_gather(embed_moment.astype(NARROW), "dp", axis=0, tiled=True)
    head_moment_low = lax.all_gather(head_moment.astype(NARROW), "dp", axis=0, tiled=True)
    tokens_all = everyone[:, :batches]
    count = jnp.maximum(jnp.sum(everyone[:, 2 * batches, 0]).astype(FLOAT), 1.0)
    divisor_all = everyone[:, batches : 2 * batches].astype(FLOAT)
    share_all = jnp.where(divisor_all > 0.5, 1.0 / jnp.maximum(divisor_all, 1.0), 0.0)
    weight_all = (share_all / count).reshape(-1)
    target_all = (
        jnp.concatenate([tokens_all[:, :, 1:], jnp.zeros_like(tokens_all[:, :, :1])], axis=2)
        .reshape(-1)
    ) - vocab_start
    tokens_flat = tokens_all.reshape(-1)
    local_all = tokens_flat - vocab_start
    inside_all = (local_all >= 0) & (local_all < vocab_rows)

    def group_part(values):
        return lax.dynamic_slice_in_dim(values, replica * rows_all, rows_all, 0)

    vector = vector_full.astype(FLOAT).reshape(1, -1)
    tables = rotary_tables(offset.reshape(-1), head_size)
    lines_of, columns_of = buffers[:, None, :], buffers[:, :, None]
    final, *kept = layer_forward(resid, in_full, out_full, vector, tables, lines_of, columns_of)
    final_grad, logsum_all, loss_part, all_hidden = head_kernel(
        head_table, final, aims, group_part(target_all), group_part(weight_all), groups, replicas
    )

    less_weight = logsum_all - jnp.log(jnp.maximum(weight_all, 1e-30))
    shifted = jnp.where(weight_all > 0.0, less_weight, 1e30)
    chunk = min(512, rows_all)
    lists = chunk_lists(local_all, inside_all, chunk)

    token_grad, vector_grad, owner_grads = layer_backward(
        final_grad,
        resid,
        in_full,
        out_full,
        vector,
        tables,
        lines_of,
        columns_of,
        kept,
        groups,
    )
    slices = jnp.pad(vector_grad.reshape(groups, amount), ((0, 0), (0, -amount % 1024)))
    in_rows = in_weights.shape[0]
    cut = owner_grads.shape[1] - out_weights.shape[0]
    head_grad, head_square, token_grads, vector_sum, owned = head_table_grad(
        head_table,
        all_hidden,
        shifted,
        weight_all,
        target_all,
        token_grad,
        slices.reshape(groups, -1, 128),
        owner_grads,
        cut,
        groups,
        replicas,
    )
    if owned.shape != owner_grads.shape[1:]:
        owned = lax.psum(lax.psum_scatter(owner_grads, "fsdp", scatter_dimension=0), "dp")
    layer_grads = [
        owned[:cut].reshape(-1, in_rows, width).transpose(1, 0, 2).reshape(in_rows, -1),
        owned[cut:],
        vector_sum.reshape(-1)[:amount],
    ]
    embed_grad, embed_square = embed_table_grad(token_grads, *lists, vocab_rows)
    square = jnp.sum(embed_square) + jnp.sum(head_square)
    for grad in layer_grads:
        square = square + jnp.sum(grad * grad)
    line = jnp.stack([loss_part, square / replicas])[:, None]
    line = jnp.pad(jnp.broadcast_to(line, (2, 128)), ((0, 6), (0, 0)))
    scalars = exchange_scalars(line, groups, replicas)
    pair = jnp.sum(scalars[:, :2, 0], axis=0)
    loss = pair[0]
    grad_norm = jnp.sqrt(pair[1])
    base = math.sqrt(NPARAM) / CLIP_LEVEL
    root = math.sqrt(width)

    def row(values):
        return values.reshape(1, -1)

    (embed, head), (inner, outer, vector) = update_all(
        scalars,
        [
            (embed_table, embed_grad, embed_moment_low, embed_moment, embed_average),
            (head_table, head_grad, head_moment_low, head_moment, head_average),
        ],
        [
            (in_weights, layer_grads[0], in_moment, in_average),
            (out_weights, layer_grads[1], out_moment, out_average),
            tuple(map(row, (vectors, layer_grads[2], vector_moment, vector_average))),
        ],
        (base, base / root, base / root, base / root, 0.3 * base),
    )
    vector = [values.reshape(-1) for values in vector]
    return (*embed, *head, *inner, *outer, *vector, loss, grad_norm)


def solution(mesh):
    placed = (
        P(None, ("dp", "fsdp"), None),
        P(None, ("dp", "fsdp"), None),
        P(None, ("dp", "fsdp")),
        P(None, ("dp", "fsdp"), None),
        P("fsdp", None),
        P(("fsdp", "dp"), None),
        P(("fsdp", "dp"), None),
        P("fsdp", None),
        P(("fsdp", "dp"), None),
        P(("fsdp", "dp"), None),
        P("fsdp", None),
        P("fsdp", None),
        P("fsdp", None),
        P("fsdp", None),
        P("fsdp", None),
        P("fsdp", None),
        P("fsdp"),
        P("fsdp"),
        P("fsdp"),
    )
    return jax.shard_map(
        shards,
        mesh=mesh,
        in_specs=placed,
        out_specs=(
            P("fsdp", None),
            P(("fsdp", "dp"), None),
            P(("fsdp", "dp"), None),
            P("fsdp", None),
            P(("fsdp", "dp"), None),
            P(("fsdp", "dp"), None),
            P("fsdp", None),
            P("fsdp", None),
            P("fsdp", None),
            P("fsdp", None),
            P("fsdp", None),
            P("fsdp", None),
            P("fsdp"),
            P("fsdp"),
            P("fsdp"),
            P(),
            P(),
        ),
        check_vma=False,
    )
```

```python
import functools
import math

import jax
import jax.numpy as jnp
from jax import lax
from jax.experimental import pallas as pl
from jax.experimental.pallas import tpu as pltpu
from jax.sharding import PartitionSpec as P

HEADS = 8
NPARAM = 54664704
NSEG = 3


EPSILON = 1e-05
CLIP_LEVEL = 0.002
MOMENTUM = 0.5
DECAY = 0.5
NARROW = jnp.bfloat16
FLOAT = jnp.float32
ROWS_CONTRACT = (((0,), (0,)), ((), ()))
LAST_CONTRACT = (((1,), (1,)), ((), ()))


VMEM_LIMIT = 60 * 2**20


def slot_info(tokens, marks, length, buffers, buffer_count):
    seq = tokens.shape[0]
    places = jnp.arange(seq, dtype=jnp.int32)
    same_buffer = jnp.concatenate([buffers[1:] == buffers[:-1], jnp.zeros((1,), dtype=bool)])
    valid = jnp.where((marks == 1) & (places + 1 < length) & same_buffer, 1.0, 0.0).astype(FLOAT)
    member = buffers[None, :] == jnp.arange(buffer_count, dtype=jnp.int32)[:, None]
    weights = jnp.where(member, 1.0, 0.0).astype(FLOAT)
    tally = jnp.sum(weights * valid[None, :], axis=1)
    divisor = valid * jnp.sum(weights * tally[:, None], axis=0)
    counted = jnp.sum(jnp.where(tally > 0.5, 1.0, 0.0).astype(FLOAT))
    first = jnp.min(jnp.where(member, places[None, :], seq), axis=1)
    offset = places - jnp.sum(jnp.where(member, first[:, None], 0), axis=0)
    return (divisor.astype(jnp.int32), offset, counted.astype(jnp.int32))


def rotary_tables(offset, head_size):
    rot = head_size // 4
    half = rot // 2
    lanes = 128
    freqs = jnp.power(10000.0, -2.0 * jnp.arange(half, dtype=FLOAT) / rot)
    angles = offset.astype(FLOAT)[:, None] * freqs[None, :]
    cosine, sine = jnp.cos(angles), jnp.sin(angles)
    rows = offset.shape[0]
    rest = head_size - rot
    ones, none = jnp.ones((rows, rest), FLOAT), jnp.zeros((rows, rest), FLOAT)
    blank = jnp.zeros((rows, half), FLOAT)
    stay = jnp.concatenate([cosine, cosine, ones], axis=1)
    ahead = jnp.concatenate([-sine, blank, none], axis=1)
    behind = jnp.concatenate([blank, sine, none], axis=1)
    return [
        jnp.concatenate([part] * (lanes // head_size), axis=1) for part in (stay, ahead, behind)
    ]


def wide_tables(refs, width):
    return [jnp.concatenate([ref[...]] * (width // ref.shape[1]), axis=1) for ref in refs]


def norm_unit(values):
    mean = jnp.mean(values, axis=-1, keepdims=True)
    centred = values - mean
    scale = lax.rsqrt(jnp.mean(centred * centred, axis=-1, keepdims=True) + EPSILON)
    return (centred * scale, scale)


def norm_back(scaled, unit, scale):
    return scale * (
        scaled
        - jnp.mean(scaled, axis=-1, keepdims=True)
        - unit * jnp.mean(scaled * unit, axis=-1, keepdims=True)
    )


def vector_spans(width, hidden):
    amounts = [width] * 6 + [3 * width, width, hidden, width]
    spans = []
    begin = 0
    for amount in amounts:
        spans.append(slice(begin, begin + amount))
        begin = begin + amount
    return spans


def masked_probs(queries, keys, mask, factor):
    scores = lax.dot_general(queries, keys, LAST_CONTRACT, preferred_element_type=FLOAT) * factor
    scores = jnp.where(mask, scores, -1e30)
    top = jnp.max(scores, axis=-1, keepdims=True)
    logsum = top + jnp.log(jnp.sum(jnp.exp(scores - top), axis=-1, keepdims=True))
    return jnp.exp(scores - logsum)


def slot_mask(line_ref, column_ref, b, seq):
    later = lax.broadcasted_iota(jnp.int32, (seq, seq), 1)
    place = lax.broadcasted_iota(jnp.int32, (seq, seq), 0)
    return (column_ref[b] == line_ref[b]) & (later <= place)


def layer_forward(resid, in_full, out_full, vector, tables, lines, columns):
    rows, width = resid.shape
    hidden = out_full.shape[0] - width
    batches, _, seq = lines.shape
    head_size = width // HEADS
    half = head_size // 8
    factor = 1.0 / math.sqrt(head_size)
    spans = vector_spans(width, hidden)

    def kernel(
        resid_ref,
        in_ref,
        out_ref,
        vector_ref,
        stay_ref,
        ahead_ref,
        behind_ref,
        line_ref,
        column_ref,
        final_ref,
        qkv_ref,
        pre_ref,
        joined_ref,
        last_ref,
    ):
        def part(i):
            return vector_ref[:, spans[i]]

        start = resid_ref[...]
        unit, _ = norm_unit(start)
        input_one = (unit * part(0) + part(1)).astype(NARROW)
        input_two = (unit * part(2) + part(3)).astype(NARROW)
        stay, ahead, behind = wide_tables((stay_ref, ahead_ref, behind_ref), width)
        bias = part(6)
        for i in range(3):
            span = slice(i * width, (i + 1) * width)
            values = jnp.dot(input_one, in_ref[:, span], preferred_element_type=FLOAT)
            values = values + bias[:, span]
            if i < 2:
                values = (
                    values * stay
                    + pltpu.roll(values, width - half, 1) * ahead
                    + pltpu.roll(values, half, 1) * behind
                )
            qkv_ref[:, span] = values.astype(NARROW)
        for b in range(batches):
            mask = slot_mask(line_ref, column_ref, b, seq)
            there = slice(b * seq, (b + 1) * seq)
            for head in range(HEADS):
                first = head * head_size
                queries, keys, values = [
                    qkv_ref[there, i * width + first : i * width + first + head_size]
                    for i in range(3)
                ]
                probs = masked_probs(queries, keys, mask, factor).astype(NARROW)
                joined_ref[there, first : first + head_size] = jnp.dot(
                    probs, values, preferred_element_type=FLOAT
                ).astype(NARROW)
        bias = part(8)
        for i in range(hidden // width):
            span = slice(i * width, (i + 1) * width)
            pre = (
                jnp.dot(
                    input_two,
                    in_ref[:, (3 + i) * width : (4 + i) * width],
                    preferred_element_type=FLOAT,
                )
                + bias[:, span]
            )
            pre_ref[:, span] = pre
            joined_ref[:, (1 + i) * width : (2 + i) * width] = (
                0.5 * pre * (1.0 + lax.erf(pre * 0.7071067811865476))
            ).astype(NARROW)
        last = (
            start
            + jnp.dot(joined_ref[...], out_ref[...], preferred_element_type=FLOAT)
            + part(7)
            + part(9)
        )
        last_ref[...] = last
        unit_last, _ = norm_unit(last)
        final_ref[...] = (unit_last * part(4) + part(5)).astype(NARROW)

    return pl.pallas_call(
        kernel,
        out_shape=[
            jax.ShapeDtypeStruct((rows, width), NARROW),
            jax.ShapeDtypeStruct((rows, 3 * width), NARROW),
            jax.ShapeDtypeStruct((rows, hidden), FLOAT),
            jax.ShapeDtypeStruct((rows, width + hidden), NARROW),
            jax.ShapeDtypeStruct((rows, width), FLOAT),
        ],
        compiler_params=pltpu.CompilerParams(vmem_limit_bytes=VMEM_LIMIT),
    )(resid, in_full, out_full, vector, *tables, lines, columns)


def layer_backward(
    final_grad, resid, in_full, out_full, vector, tables, lines, columns, kept, groups
):
    rows, width = resid.shape
    hidden = out_full.shape[0] - width
    batches, _, seq = lines.shape
    head_size = width // HEADS
    half = head_size // 8
    factor = 1.0 / math.sqrt(head_size)
    spans = vector_spans(width, hidden)
    blocks = in_full.shape[1] // width
    in_rows = width // groups
    out_rows = out_full.shape[0] // groups
    first_out = blocks * in_rows
    shard = first_out + out_rows

    def kernel(
        final_grad_ref,
        resid_ref,
        in_ref,
        out_ref,
        vector_ref,
        stay_ref,
        ahead_ref,
        behind_ref,
        line_ref,
        column_ref,
        qkv_ref,
        pre_ref,
        joined_ref,
        last_ref,
        token_ref,
        small_ref,
        owners_ref,
        owners,
        low,
        wide,
        sems,
    ):
        def part(i):
            return vector_ref[:, spans[i]]

        def column_sum(i, values):
            small_ref[:, spans[i]] = jnp.sum(values, axis=0, keepdims=True)

        final_grad_in = final_grad_ref[...]
        unit_last, scale_last = norm_unit(last_ref[...])
        column_sum(4, final_grad_in * unit_last)
        column_sum(5, final_grad_in)
        grad_out = norm_back(final_grad_in * part(4), unit_last, scale_last)
        column_sum(7, grad_out)
        column_sum(9, grad_out)
        grad_low = grad_out.astype(NARROW)
        for c in range((width + hidden) // width):
            there = slice(c * width, (c + 1) * width)
            piece = lax.dot_general(
                joined_ref[:, there], grad_low, ROWS_CONTRACT, preferred_element_type=FLOAT
            )
            at = c * width
            while at < (c + 1) * width:
                owner, row = at // out_rows, at % out_rows
                size = min(out_rows - row, (c + 1) * width - at)
                owners[owner, first_out + row : first_out + row + size, :] = piece[
                    at - c * width : at - c * width + size
                ]
                at = at + size
        out_copy = pltpu.make_async_copy(
            owners.at[:, pl.ds(first_out, out_rows), :],
            owners_ref.at[:, pl.ds(first_out, out_rows), :],
            sems.at[0],
        )
        out_copy.start()
        unit, scale = norm_unit(resid_ref[...])
        input_one = (unit * part(0) + part(1)).astype(NARROW)
        input_two = (unit * part(2) + part(3)).astype(NARROW)

        def in_piece(inputs, c, grads):
            piece = lax.dot_general(
                inputs, grads, ROWS_CONTRACT, preferred_element_type=FLOAT
            )
            for owner in range(groups):
                owners[owner, c * in_rows : (c + 1) * in_rows, :] = piece[
                    owner * in_rows : (owner + 1) * in_rows
                ]

        back_two = jnp.zeros((rows, width), FLOAT)
        bias_sums = []
        for i in range(hidden // width):
            grads = lax.dot_general(
                grad_low,
                out_ref[(1 + i) * width : (2 + i) * width, :],
                LAST_CONTRACT,
                preferred_element_type=FLOAT,
            )
            pre = pre_ref[:, i * width : (i + 1) * width]
            slope = (
                0.5 * (1.0 + lax.erf(pre * 0.7071067811865476))
                + pre * jnp.exp(-0.5 * pre * pre) * 0.3989422804014327
            )
            grads = grads * slope
            bias_sums.append(jnp.sum(grads, axis=0, keepdims=True))
            grads = grads.astype(NARROW)
            in_piece(input_two, 3 + i, grads)
            back_two = back_two + lax.dot_general(
                grads,
                in_ref[:, (3 + i) * width : (4 + i) * width],
                LAST_CONTRACT,
                preferred_element_type=FLOAT,
            )
        small_ref[:, spans[8]] = jnp.concatenate(bias_sums, axis=1)
        low[...] = lax.dot_general(
            grad_low, out_ref[:width, :], LAST_CONTRACT, preferred_element_type=FLOAT
        ).astype(NARROW)
        for b in range(batches):
            mask = slot_mask(line_ref, column_ref, b, seq)
            there = slice(b * seq, (b + 1) * seq)
            for head in range(HEADS):
                first = head * head_size
                at = [
                    slice(i * width + first, i * width + first + head_size) for i in range(3)
                ]
                queries, keys, values = [qkv_ref[there, at[i]] for i in range(3)]
                mixed = low[there, first : first + head_size]
                probs = masked_probs(queries, keys, mask, factor)
                back = lax.dot_general(
                    mixed, values, LAST_CONTRACT, preferred_element_type=FLOAT
                )
                wide[there, at[2]] = lax.dot_general(
                    probs.astype(NARROW), mixed, ROWS_CONTRACT, preferred_element_type=FLOAT
                )
                scores = (
                    probs
                    * (back - jnp.sum(probs * back, axis=-1, keepdims=True))
                    * factor
                ).astype(NARROW)
                wide[there, at[0]] = jnp.dot(scores, keys, preferred_element_type=FLOAT)
                wide[there, at[1]] = lax.dot_general(
                    scores, queries, ROWS_CONTRACT, preferred_element_type=FLOAT
                )
        stay, ahead, behind = wide_tables((stay_ref, ahead_ref, behind_ref), width)
        back_one = jnp.zeros((rows, width), FLOAT)
        bias_sums = []
        for i in range(3):
            span = slice(i * width, (i + 1) * width)
            grads = wide[:, span]
            if i < 2:
                grads = (
                    grads * stay
                    + pltpu.roll(grads * ahead, half, 1)
                    + pltpu.roll(grads * behind, width - half, 1)
                )
            bias_sums.append(jnp.sum(grads, axis=0, keepdims=True))
            grads = grads.astype(NARROW)
            in_piece(input_one, i, grads)
            back_one = back_one + lax.dot_general(
                grads, in_ref[:, span], LAST_CONTRACT, preferred_element_type=FLOAT
            )
        in_copy = pltpu.make_async_copy(
            owners.at[:, pl.ds(0, first_out), :],
            owners_ref.at[:, pl.ds(0, first_out), :],
            sems.at[1],
        )
        in_copy.start()
        small_ref[:, spans[6]] = jnp.concatenate(bias_sums, axis=1)
        column_sum(0, back_one * unit)
        column_sum(1, back_one)
        column_sum(2, back_two * unit)
        column_sum(3, back_two)
        token_ref[...] = (
            grad_out + norm_back(back_one * part(0) + back_two * part(2), unit, scale)
        ).astype(NARROW)
        out_copy.wait()
        in_copy.wait()

    whole = pl.BlockSpec(memory_space=pltpu.VMEM)
    return pl.pallas_call(
        kernel,
        in_specs=[whole] * 14,
        out_specs=[whole, whole, pl.BlockSpec(memory_space=pl.ANY)],
        out_shape=[
            jax.ShapeDtypeStruct((rows, width), NARROW),
            jax.ShapeDtypeStruct(vector.shape, FLOAT),
            jax.ShapeDtypeStruct((groups, shard, width), FLOAT),
        ],
        scratch_shapes=[
            pltpu.VMEM((groups, shard, width), FLOAT),
            pltpu.VMEM((rows, width), NARROW),
            pltpu.VMEM((rows, 3 * width), FLOAT),
            pltpu.SemaphoreType.DMA((2,)),
        ],
        compiler_params=pltpu.CompilerParams(vmem_limit_bytes=VMEM_LIMIT),
    )(final_grad, resid, in_full, out_full, vector, *tables, lines, columns, *kept)


def block_rows(rows, cap):
    best = rows
    for size in range(8, cap + 1, 8):
        if rows % size == 0:
            best = size
    return best


MESH = pl.DeviceIdType.MESH


def meet(peers):
    barrier = pltpu.get_barrier_semaphore()
    for peer in peers:
        pl.semaphore_signal(barrier, inc=1, device_id=peer, device_id_type=MESH)
    pl.semaphore_wait(barrier, len(peers))


class Place:
    def __init__(self, groups, replicas):
        self.groups = groups
        self.replicas = replicas
        self.chips = groups // 2
        self.replica = lax.axis_index("dp")
        self.member = lax.axis_index("fsdp")
        self.chip = self.member // 2
        self.core = self.member % 2
        self.sibling_member = self.chip * 2 + 1 - self.core

    def lane_chip(self, step):
        return lax.rem(self.chip + step, self.chips)

    def at(self, replica, member):
        return {"dp": replica, "fsdp": member}

    def lane(self, step):
        return self.at(self.replica, self.lane_chip(step) * 2 + self.core)

    def plane_replica(self, step):
        return lax.rem(self.replica + step, self.replicas)

    def plane(self, step):
        return self.at(self.plane_replica(step), self.member)

    def sibling(self):
        return self.at(self.replica, self.sibling_member)

    def lanes(self):
        return [self.lane(step) for step in range(1, self.chips)]

    def planes(self):
        return [self.plane(step) for step in range(1, self.replicas)]


def remote(source, target, send, recv, device):
    return pltpu.make_async_remote_copy(
        src_ref=source,
        dst_ref=target,
        send_sem=send,
        recv_sem=recv,
        device_id=device,
        device_id_type=MESH,
    )


def start_kernel(
    packed, line, in_shard, out_shard, table, head, batches, groups, replicas
):
    vocab, width = table.shape
    seq = packed.shape[1]
    own = batches * seq
    chips = groups // 2
    amount = groups * replicas
    shards_in = (in_shard, out_shard)
    split = all(shard.shape[0] % (16 * replicas) == 0 for shard in shards_in)
    pieces = replicas if split else 1
    unroll = 8

    def kernel(
        packed_ref,
        line_ref,
        in_ref,
        out_ref,
        table_ref,
        head_ref,
        every_ref,
        lines_ref,
        in_full,
        out_full,
        resid_ref,
        aims_ref,
        in_low,
        out_low,
        wide,
        again,
        looked,
        to_core,
        from_core,
        to_lane,
        from_lane,
        ids,
        table_sem,
        ids_sem,
        local_sem,
        meta_send,
        meta_recv,
        line_send,
        line_recv,
        lane_send,
        lane_recv,
        plane_send,
        plane_recv,
        core_send,
        core_recv,
        part_send,
        part_recv,
        sum_send,
        sum_recv,
    ):
        place = Place(groups, replicas)
        member = place.member
        core = place.core
        replica = place.replica
        me = replica * groups + member
        fulls = (in_full, out_full)
        lows = (in_low, out_low)

        def device(index):
            return place.at(index // groups, lax.rem(index, groups))

        def chip_at(j):
            return lax.rem(place.chip + j, chips)

        def chip_before(j):
            return lax.rem(place.chip + chips - j, chips)

        def replica_before(k):
            return lax.rem(replica + replicas - k, replicas)

        def lane_device(j):
            return place.at(replica, chip_at(j) * 2 + core)

        def plane_device(k):
            return place.at(lax.rem(replica + k, replicas), member)

        def meta_copy(k):
            return remote(
                packed_ref,
                every_ref.at[me],
                meta_send.at[k],
                meta_recv.at[k],
                device(lax.rem(me + k, amount)),
            )

        def line_copy(k):
            return remote(
                line_ref,
                lines_ref.at[member],
                line_send.at[k],
                line_recv.at[k],
                place.at(replica, lax.rem(member + k, groups)),
            )

        def piece(w, slot, from_replica):
            full = fulls[w]
            if not split:
                return full.at[slot]
            rows = full.shape[1] // pieces
            return full.at[slot, pl.ds(pl.multiple_of(from_replica * rows, 16), rows), :]

        def own_piece(w):
            low = lows[w]
            if not split:
                return low
            rows = low.shape[0] // pieces
            return low.at[pl.ds(pl.multiple_of(replica * rows, 16), rows), :]

        def lane_copy(w, j):
            return remote(
                own_piece(w),
                piece(w, member, replica),
                lane_send.at[w, j],
                lane_recv.at[w, j],
                lane_device(j),
            )

        def lane_wait(w, j):
            there = piece(w, chip_before(j) * 2 + core, replica)
            remote(
                there, there, lane_send.at[w, j], lane_recv.at[w, j], lane_device(j)
            ).wait_recv()

        def plane_copy(w, k, j):
            there = piece(w, chip_before(j) * 2 + core, replica)
            return remote(
                there, there, plane_send.at[w, k, j], plane_recv.at[w, k, j], plane_device(k)
            )

        def plane_wait(w, k, j):
            there = piece(w, chip_before(j) * 2 + core, replica_before(k))
            remote(
                there, there, plane_send.at[w, k, j], plane_recv.at[w, k, j], plane_device(k)
            ).wait_recv()

        def core_copy(w, j):
            here = fulls[w].at[chip_before(j) * 2 + core]
            return remote(here, here, core_send.at[w, j], core_recv.at[w, j], place.sibling())

        def own_core_copy(w):
            return remote(
                lows[w],
                fulls[w].at[member],
                core_send.at[w, 0],
                core_recv.at[w, 0],
                place.sibling(),
            )

        def core_wait(w, j):
            there = fulls[w].at[chip_before(j) * 2 + 1 - core]
            remote(
                there, there, core_send.at[w, j], core_recv.at[w, j], place.sibling()
            ).wait_recv()

        def part_copy(j):
            return remote(
                to_core.at[j], from_core.at[j], part_send.at[j], part_recv.at[j], place.sibling()
            )

        def sum_copy(j):
            return remote(
                to_lane.at[j], from_lane.at[j], sum_send.at[j], sum_recv.at[j], lane_device(j)
            )

        fetch = pltpu.make_async_copy(
            table_ref, wide.at[pl.ds(0, vocab), :], table_sem.at[0]
        )
        refetch = pltpu.make_async_copy(
            head_ref, again.at[pl.ds(0, vocab), :], table_sem.at[1]
        )
        fetch.start()
        refetch.start()
        barrier = pltpu.get_barrier_semaphore()

        def greet(k, carry):
            pl.semaphore_signal(
                barrier, inc=1, device_id=device(lax.rem(me + k, amount)), device_id_type=MESH
            )
            return carry

        lax.fori_loop(1, amount, greet, 0)
        for held in (wide, again):
            held[vocab : vocab + 8, :] = jnp.zeros((8, width), FLOAT)
        in_low[...] = in_ref[...].astype(NARROW)
        out_low[...] = out_ref[...].astype(NARROW)
        every_ref[me] = packed_ref[...]
        lines_ref[member] = line_ref[...]
        pl.semaphore_wait(barrier, amount - 1)

        def tell(k, carry):
            meta_copy(k).start()
            return carry

        lax.fori_loop(1, amount, tell, 0)
        for k in range(1, groups):
            line_copy(k).start()
        for w in range(2):
            for j in range(1, chips):
                lane_copy(w, j).start()
            own_core_copy(w).start()
        kept = [
            pltpu.make_async_copy(lows[w], fulls[w].at[member], local_sem.at[w])
            for w in range(2)
        ]
        for copy in kept:
            copy.start()

        def hear(k, carry):
            there = every_ref.at[lax.rem(me + amount - k, amount)]
            remote(there, there, meta_send.at[k], meta_recv.at[k], device(me)).wait_recv()
            return carry

        lax.fori_loop(1, amount, hear, 0)
        load = pltpu.make_async_copy(
            every_ref.at[pl.ds(replica * groups, groups)], ids, ids_sem
        )
        load.start()
        load.wait()
        fetch.wait()
        start = member * vocab

        def look(slot, ahead, source):
            for b in range(batches):

                def lap(i, carry):
                    first = pl.multiple_of(i * unroll, unroll)
                    for u in range(unroll):
                        if ahead and u + ahead >= unroll:
                            spot = first + u + ahead
                            token = ids[slot, b, jnp.minimum(spot, seq - 1)]
                            token = jnp.where(spot < seq, token, 0)
                        else:
                            token = ids[slot, b, first + u + ahead]
                        row = token - start
                        row = jnp.where((row >= 0) & (row < vocab), row, vocab)
                        looked[pl.ds(b * seq + first + u, 1), :] = source[pl.ds(row, 1), :]
                    return carry

                lax.fori_loop(0, seq // unroll, lap, 0)
            return looked[...].astype(NARROW)

        def lap(step, carry):
            j = lax.rem(step + 1, chips)
            there = chip_at(j) * 2

            to_core[j] = look(there + 1 - core, 0, wide)
            part_copy(j).start()
            mine = look(there + core, 0, wide).astype(FLOAT)
            part_copy(j).wait_recv()
            mine = mine + from_core[j].astype(FLOAT)

            @pl.when(j > 0)
            def _():
                to_lane[j] = mine.astype(NARROW)
                sum_copy(j).start()

            @pl.when(j == 0)
            def _():
                resid_ref[...] = mine

            return carry

        lax.fori_loop(0, chips, lap, 0)
        refetch.wait()

        def aim(slot, carry):
            @pl.when(slot == 0)
            def _():
                for w in range(2):
                    for c in range(1, chips):
                        lane_wait(w, c)
                        if split:
                            for k in range(1, replicas):
                                plane_copy(w, k, c).start()

            aims_ref[slot] = look(slot, 1, again)
            return carry

        lax.fori_loop(0, groups, aim, 0)
        for j in range(1, chips):
            sum_copy(j).wait_recv()
            resid_ref[...] += from_lane[j].astype(FLOAT)
        for w in range(2):
            for j in range(1, chips):
                if split:
                    for k in range(1, replicas):
                        plane_wait(w, k, j)
                core_copy(w, j).start()
        for w in range(2):
            kept[w].wait()
            for j in range(chips):
                core_wait(w, j)
                if j == 0:
                    own_core_copy(w).wait_send()
                else:
                    core_copy(w, j).wait_send()
                    lane_copy(w, j).wait_send()
                if split and j > 0:
                    for k in range(1, replicas):
                        plane_copy(w, k, j).wait_send()
        for k in range(1, groups):
            there = lines_ref.at[lax.rem(member + groups - k, groups)]
            remote(
                there, there, line_send.at[k], line_recv.at[k], place.at(replica, member)
            ).wait_recv()
            line_copy(k).wait_send()
        for j in range(chips):
            part_copy(j).wait_send()
            if j > 0:
                sum_copy(j).wait_send()

        def told(k, carry):
            meta_copy(k).wait_send()
            return carry

        lax.fori_loop(1, amount, told, 0)

    whole = pl.BlockSpec(memory_space=pltpu.VMEM)
    anywhere = pl.BlockSpec(memory_space=pl.ANY)
    dma = pltpu.SemaphoreType.DMA
    vmem = pltpu.VMEM
    every, lines, in_full, out_full, resid, aims = pl.pallas_call(
        kernel,
        in_specs=[whole, whole, whole, whole, anywhere, anywhere],
        out_specs=[whole, whole, anywhere, anywhere, whole, whole],
        out_shape=[
            jax.ShapeDtypeStruct((amount,) + packed.shape, jnp.int32),
            jax.ShapeDtypeStruct((groups,) + line.shape, FLOAT),
            jax.ShapeDtypeStruct((groups,) + in_shard.shape, NARROW),
            jax.ShapeDtypeStruct((groups,) + out_shard.shape, NARROW),
            jax.ShapeDtypeStruct((own, width), FLOAT),
            jax.ShapeDtypeStruct((groups, own, width), NARROW),
        ],
        scratch_shapes=[
            vmem(in_shard.shape, NARROW),
            vmem(out_shard.shape, NARROW),
            vmem((vocab + 8, width), FLOAT),
            vmem((vocab + 8, width), FLOAT),
            vmem((own, width), FLOAT),
            vmem((chips, own, width), NARROW),
            vmem((chips, own, width), NARROW),
            vmem((chips, own, width), NARROW),
            vmem((chips, own, width), NARROW),
            pltpu.SMEM((groups,) + packed.shape, jnp.int32),
            dma((2,)),
            dma,
            dma((2,)),
            dma((amount,)),
            dma((amount,)),
            dma((groups,)),
            dma((groups,)),
            dma((2, chips)),
            dma((2, chips)),
            dma((2, replicas, chips)),
            dma((2, replicas, chips)),
            dma((2, chips)),
            dma((2, chips)),
            dma((chips,)),
            dma((chips,)),
            dma((chips,)),
            dma((chips,)),
        ],
        compiler_params=pltpu.CompilerParams(
            vmem_limit_bytes=VMEM_LIMIT, collective_id=4, has_side_effects=True
        ),
        cost_estimate=pl.CostEstimate(
            flops=0, bytes_accessed=vocab * width * 4, transcendentals=0
        ),
    )(packed, line, in_shard, out_shard, table, head)
    return (
        every,
        lines,
        in_full.reshape(-1, in_shard.shape[1]),
        out_full.reshape(-1, out_shard.shape[1]),
        resid,
        aims,
    )


def head_kernel(table, own_hidden, aims, target, weight, groups, replicas):
    vocab, width = table.shape
    own = own_hidden.shape[0]
    block = block_rows(vocab, 1100)
    blocks = vocab // block
    chips = groups // 2
    lines = -(-blocks // 8) * 8

    def kernel(
        table_ref,
        own_ref,
        aims_ref,
        target_ref,
        weight_ref,
        grad_ref,
        logsum_ref,
        loss_ref,
        all_ref,
        wide,
        low,
        hid,
        exps,
        tops,
        totals,
        shares,
        to_core,
        from_core,
        to_lane,
        from_lane,
        aim_core,
        aim_lane,
        aim_from,
        table_sem,
        local_sem,
        lane_send,
        lane_recv,
        core_send,
        core_recv,
        plane_send,
        plane_recv,
        pass_send,
        pass_recv,
        stat_send,
        stat_recv,
        line_send,
        line_recv,
        part_send,
        part_recv,
        sum_send,
        sum_recv,
        aim_half_send,
        aim_half_recv,
        aim_send,
        aim_recv,
    ):
        place = Place(groups, replicas)
        me = place.member
        core = place.core

        def table_copy(b):
            return pltpu.make_async_copy(
                table_ref.at[pl.ds(b * block, block), :], wide.at[b % 2], table_sem.at[b % 2]
            )

        def chip_at(j):
            return lax.rem(place.chip + j, chips)

        def chip_before(j):
            return lax.rem(place.chip + chips - j, chips)

        def lane_device(j):
            return place.at(place.replica, chip_at(j) * 2 + core)

        def plane_device(k):
            return place.at(lax.rem(place.replica + k, replicas), me)

        def replica_before(k):
            return lax.rem(place.replica + replicas - k, replicas)

        def turn(step):
            if isinstance(step, int):
                return (step + 1) // 2 if step % 2 else (chips - step // 2) % chips
            ahead = (step + 1) // 2
            behind = lax.rem(chips - step // 2, chips)
            return jnp.where(lax.rem(step, 2) == 1, ahead, behind)

        def lane_copy(j):
            return remote(own_ref, hid.at[me], lane_send.at[j], lane_recv.at[j], lane_device(j))

        def lane_slot(j):
            return chip_before(j) * 2 + core

        def lane_wait(j):
            there = hid.at[lane_slot(j)]
            remote(there, there, lane_send.at[j], lane_recv.at[j], lane_device(j)).wait_recv()

        def core_copy(j):
            here = hid.at[lane_slot(j)]
            return remote(here, here, core_send.at[j], core_recv.at[j], place.sibling())

        def core_wait(j):
            there = hid.at[chip_before(j) * 2 + 1 - core]
            remote(there, there, core_send.at[j], core_recv.at[j], place.sibling()).wait_recv()

        def plane_copy(k, j):
            slot = lane_slot(j)
            return remote(
                hid.at[slot],
                all_ref.at[place.replica * groups + slot],
                plane_send.at[k, j],
                plane_recv.at[k, j],
                plane_device(k),
            )

        def plane_wait(k, j):
            there = all_ref.at[replica_before(k) * groups + lane_slot(j)]
            remote(
                there, there, plane_send.at[k, j], plane_recv.at[k, j], plane_device(k)
            ).wait_recv()

        def pass_copy(k, j):
            here = all_ref.at[replica_before(k) * groups + lane_slot(j)]
            return remote(
                here, here, pass_send.at[k, j], pass_recv.at[k, j], place.sibling()
            )

        def pass_wait(k, j):
            there = all_ref.at[
                replica_before(k) * groups + chip_before(j) * 2 + 1 - core
            ]
            remote(
                there, there, pass_send.at[k, j], pass_recv.at[k, j], place.sibling()
            ).wait_recv()

        def member_at(k):
            return lax.rem(me + k, groups)

        def stat_copy(k):
            return remote(
                shares.at[me],
                shares.at[me],
                stat_send.at[k],
                stat_recv.at[k],
                place.at(place.replica, member_at(k)),
            )

        def stat_wait(k):
            there = shares.at[lax.rem(me + groups - k, groups)]
            remote(
                there, there, stat_send.at[k], stat_recv.at[k], place.at(place.replica, me)
            ).wait_recv()

        def line_copy(k):
            here = logsum_ref.at[place.replica]
            return remote(here, here, line_send.at[k], line_recv.at[k], plane_device(k))

        def line_wait(k):
            there = logsum_ref.at[replica_before(k)]
            remote(there, there, line_send.at[k], line_recv.at[k], plane_device(k)).wait_recv()

        def part_copy(j):
            return remote(
                to_core.at[j], from_core.at[j], part_send.at[j], part_recv.at[j], place.sibling()
            )

        def sum_copy(j):
            return remote(
                to_lane.at[j], from_lane.at[j], sum_send.at[j], sum_recv.at[j], lane_device(j)
            )

        def aim_half(c):
            return remote(
                aims_ref.at[c * 2 + 1 - core],
                aim_core.at[c],
                aim_half_send.at[c],
                aim_half_recv.at[c],
                place.sibling(),
            )

        def aim_copy(j):
            return remote(
                aim_lane.at[j], aim_from.at[j], aim_send.at[j], aim_recv.at[j], lane_device(j)
            )

        table_copy(0).start()
        if blocks > 1:
            table_copy(1).start()
        meet(
            [place.at(place.replica, member_at(k)) for k in range(1, groups)] + place.planes()
        )
        own_core = remote(own_ref, hid.at[me], core_send.at[0], core_recv.at[0], place.sibling())
        own_core.start()
        for step in range(1, min(3, chips)):
            lane_copy(turn(step)).start()
        hid[me] = own_ref[...]
        for k in range(1, replicas):
            plane_copy(k, 0).start()
        for c in range(chips):
            aim_half(c).start()
        for b in range(blocks):
            table_copy(b).wait()
            low[b] = wide[b % 2].astype(NARROW)
            if b + 2 < blocks:
                table_copy(b + 2).start()

        spots = lax.broadcasted_iota(jnp.int32, (block, own), 0)

        def forward(step, carry):
            j = turn(step // 2)
            other = lax.rem(step, 2)

            @pl.when(step == 1)
            def _():
                for later in range(3, chips):
                    lane_copy(turn(later)).start()
                there = hid.at[place.sibling_member]
                remote(
                    there, there, core_send.at[0], core_recv.at[0], place.sibling()
                ).wait_recv()

            @pl.when((step > 1) & (other == 0))
            def _():
                lane_wait(j)
                core_copy(j).start()

                def spread(k, carry):
                    plane_copy(k, j).start()
                    return carry

                lax.fori_loop(1, replicas, spread, 0)

            @pl.when((step > 1) & (other == 1))
            def _():
                core_wait(j)

            @pl.when(step == groups // 2 + 1)
            def _():
                for c in range(chips):
                    aim_half(c).wait_recv()
                for i in range(chips):
                    chip = chip_at(i)
                    aim_lane[i] = (
                        aims_ref[chip * 2 + core].astype(FLOAT) + aim_core[chip].astype(FLOAT)
                    ).astype(NARROW)
                for i in range(1, chips):
                    aim_copy(i).start()

            member = chip_before(j) * 2 + lax.rem(core + other, 2)
            here = hid[member]
            for b in range(blocks):
                logits = lax.dot_general(
                    low[b], here, LAST_CONTRACT, preferred_element_type=FLOAT
                )
                top = jnp.max(logits, axis=0, keepdims=True)
                values = jnp.exp(logits - top)
                tops[member, b : b + 1, :] = top
                totals[member, b : b + 1, :] = jnp.sum(values, axis=0, keepdims=True)
                exps[b, member] = values.astype(NARROW)
            block_tops = tops[member, :blocks, :]
            top = jnp.max(block_tops, axis=0, keepdims=True)
            total = jnp.sum(
                totals[member, :blocks, :] * jnp.exp(block_tops - top), axis=0, keepdims=True
            )
            shares[me, pl.ds(member, 1), :] = top + jnp.log(total)
            return carry

        lax.fori_loop(0, groups, forward, 0)
        local = pltpu.make_async_copy(
            hid, all_ref.at[pl.ds(place.replica * groups, groups)], local_sem
        )
        local.start()
        for k in range(1, groups):
            stat_copy(k).start()
        for k in range(1, groups):
            stat_wait(k)
        every = shares[...]
        top = jnp.max(every, axis=0)
        logsum_ref[place.replica] = top + jnp.log(jnp.sum(jnp.exp(every - top[None]), axis=0))
        for k in range(1, replicas):
            line_copy(k).start()

        def member_back(member):
            wanted = target_ref[member]
            weights = weight_ref[member]
            logsum = logsum_ref[place.replica, pl.ds(member, 1), :]
            total = jnp.zeros((own, width), FLOAT)
            for b in range(blocks):
                scale = weights * jnp.exp(tops[member, b : b + 1, :] - logsum)
                grads = exps[b, member].astype(FLOAT) * scale
                grads = jnp.where(spots == wanted - b * block, 0.0, grads)
                total = total + lax.dot_general(
                    grads.astype(NARROW), low[b], ROWS_CONTRACT, preferred_element_type=FLOAT
                )
            return total

        def backward(step, carry):
            j = turn(chips - 1 - step)

            @pl.when(step == chips - 1)
            def _():
                for k in range(1, replicas):
                    for c in range(chips):
                        plane_wait(k, c)
                for k in range(1, replicas):
                    for c in range(chips):
                        pass_copy(k, c).start()

            there = chip_at(j) * 2
            to_core[j] = member_back(there + 1 - core).astype(NARROW)
            part_copy(j).start()
            mine = member_back(there + core)
            part_copy(j).wait_recv()
            mine = mine + from_core[j].astype(FLOAT)

            @pl.when(j > 0)
            def _():
                to_lane[j] = mine.astype(NARROW)
                sum_copy(j).start()

            @pl.when(j == 0)
            def _():
                grad_ref[...] = mine

            return carry

        lax.fori_loop(0, chips, backward, 0)
        held = lax.broadcasted_iota(jnp.int32, (groups, own), 0) == me
        amounts = jnp.concatenate([weight_ref[m] for m in range(groups)], axis=0)

        def own_column(values):
            return jnp.sum(jnp.where(held, values, 0.0).T, axis=1, keepdims=True)

        amount = own_column(amounts)
        logsum = own_column(logsum_ref[place.replica])
        aimed = aim_lane[0].astype(FLOAT)
        for j in range(1, chips):
            aim_copy(j).wait_recv()
            aimed = aimed + aim_from[j].astype(FLOAT)
        hit = jnp.sum(own_ref[...].astype(FLOAT) * aimed, axis=1, keepdims=True)
        loss_ref[...] = amount * (logsum - hit)
        part = (amount * (jnp.exp(hit - logsum) - 1.0)).astype(NARROW).astype(FLOAT)
        total = grad_ref[...] + part * aimed
        for j in range(1, chips):
            sum_copy(j).wait_recv()
            total = total + from_lane[j].astype(FLOAT)
        grad_ref[...] = total
        local.wait()
        own_core.wait_send()
        for k in range(1, groups):
            stat_copy(k).wait_send()
        for k in range(1, replicas):
            line_wait(k)
            line_copy(k).wait_send()
            for j in range(chips):
                pass_wait(k, j)
                plane_copy(k, j).wait_send()
                pass_copy(k, j).wait_send()
        for j in range(chips):
            part_copy(j).wait_send()
            aim_half(j).wait_send()
            if j > 0:
                lane_copy(j).wait_send()
                core_copy(j).wait_send()
                sum_copy(j).wait_send()
                aim_copy(j).wait_send()

    whole = pl.BlockSpec(memory_space=pltpu.VMEM)
    anywhere = pl.BlockSpec(memory_space=pl.ANY)
    dma = pltpu.SemaphoreType.DMA
    vmem = pltpu.VMEM
    grad, logsum, loss, everyone = pl.pallas_call(
        kernel,
        in_specs=[anywhere, whole, whole, whole, whole],
        out_specs=[whole, whole, whole, anywhere],
        out_shape=[
            jax.ShapeDtypeStruct((own, width), FLOAT),
            jax.ShapeDtypeStruct((replicas, groups, own), FLOAT),
            jax.ShapeDtypeStruct((own, 1), FLOAT),
            jax.ShapeDtypeStruct((replicas * groups, own, width), NARROW),
        ],
        scratch_shapes=[
            vmem((2, block, width), FLOAT),
            vmem((blocks, block, width), NARROW),
            vmem((groups, own, width), NARROW),
            vmem((blocks, groups, block, own), NARROW),
            vmem((groups, lines, own), FLOAT),
            vmem((groups, lines, own), FLOAT),
            vmem((groups, groups, own), FLOAT),
            vmem((chips, own, width), NARROW),
            vmem((chips, own, width), NARROW),
            vmem((chips, own, width), NARROW),
            vmem((chips, own, width), NARROW),
            vmem((chips, own, width), NARROW),
            vmem((chips, own, width), NARROW),
            vmem((chips, own, width), NARROW),
            dma((2,)),
            dma,
            dma((chips,)),
            dma((chips,)),
            dma((chips,)),
            dma((chips,)),
            dma((replicas, chips)),
            dma((replicas, chips)),
            dma((replicas, chips)),
            dma((replicas, chips)),
            dma((groups,)),
            dma((groups,)),
            dma((replicas,)),
            dma((replicas,)),
            dma((chips,)),
            dma((chips,)),
            dma((chips,)),
            dma((chips,)),
            dma((chips,)),
            dma((chips,)),
            dma((chips,)),
            dma((chips,)),
        ],
        compiler_params=pltpu.CompilerParams(
            vmem_limit_bytes=VMEM_LIMIT + 2**21, collective_id=3, has_side_effects=True
        ),
        cost_estimate=pl.CostEstimate(
            flops=4 * vocab * groups * own * width,
            bytes_accessed=vocab * width * 4,
            transcendentals=vocab * groups * own,
        ),
    )(
        table,
        own_hidden,
        aims,
        target.reshape(groups, 1, own),
        weight.reshape(groups, 1, own),
    )
    return grad, logsum.reshape(-1), jnp.sum(loss), everyone.reshape(-1, width)


def head_table_grad(
    table, hidden, logsum, weights, target, token_grad, slices, owner_grads, cut, groups, replicas
):
    vocab, width = table.shape
    amount = groups * replicas
    rows = hidden.shape[0]
    own = token_grad.shape[0]
    tile = math.gcd(rows, 2048)
    block = block_rows(vocab, 1100)
    tiles = rows // tile
    steps = vocab // block
    chips = groups // 2
    last = steps - 1
    shard = owner_grads.shape[1]
    regions = ((0, cut), (cut, shard - cut))
    firsts, seconds = (replicas, chips), (chips, replicas)
    reduce = all(count % (8 * replicas) == 0 for _, count in regions)
    laps = steps * tiles

    def when(part):
        return min(int(laps * part), laps - 1)

    def kernel(
        table_ref,
        hidden_ref,
        logsum_ref,
        weight_ref,
        target_ref,
        own_ref,
        slices_ref,
        owner_ref,
        grad_ref,
        square_ref,
        all_ref,
        summed_ref,
        owned_out,
        gathered,
        owned_ref,
        from_core,
        acc_in,
        acc_out,
        one_in,
        one_out,
        two_in,
        two_out,
        piece_sem,
        half_send,
        half_recv,
        one_send,
        one_recv,
        two_send,
        two_recv,
        end_send,
        end_recv,
        local_sem,
        slice_send,
        slice_recv,
        lane_send,
        lane_recv,
        plane_send,
        plane_recv,
        core_send,
        core_recv,
    ):
        step = pl.program_id(0)
        place = Place(groups, replicas)
        me = place.replica * groups + place.member

        def slot(replica, member):
            return all_ref.at[replica * groups + member]

        def lane_copy(k):
            here = all_ref.at[me]
            return remote(own_ref, here, lane_send.at[k], lane_recv.at[k], place.lane(k))

        def lane_wait(k):
            back = lax.rem(place.chip + chips - k, chips) * 2 + place.core
            there = slot(place.replica, back)
            remote(there, there, lane_send.at[k], lane_recv.at[k], place.lane(k)).wait_recv()

        def plane_copy(k, c):
            here = slot(place.replica, c * 2 + place.core)
            return remote(here, here, plane_send.at[k, c], plane_recv.at[k, c], place.plane(k))

        def plane_wait(k, c):
            back = lax.rem(place.replica + replicas - k, replicas)
            there = slot(back, c * 2 + place.core)
            remote(
                there, there, plane_send.at[k, c], plane_recv.at[k, c], place.plane(k)
            ).wait_recv()

        def core_copy(r, c):
            here = slot(r, c * 2 + place.core)
            return remote(here, here, core_send.at[r, c], core_recv.at[r, c], place.sibling())

        def core_wait(r, c):
            there = slot(r, c * 2 + 1 - place.core)
            remote(
                there, there, core_send.at[r, c], core_recv.at[r, c], place.sibling()
            ).wait_recv()

        def device(index):
            return place.at(index // groups, lax.rem(index, groups))

        def slice_copy(k):
            there = lax.rem(me + k, amount)
            return remote(
                slices_ref.at[lax.rem(there, groups)],
                gathered.at[me],
                slice_send.at[k],
                slice_recv.at[k],
                device(there),
            )

        local = pltpu.make_async_copy(own_ref, all_ref.at[me], local_sem)
        accs, ones, twos = (acc_in, acc_out), (one_in, one_out), (two_in, two_out)

        def chip_at(j):
            return lax.rem(place.chip + j, chips)

        def pieces(g):
            first, rows = regions[g]
            size = rows // replicas
            for k in range(firsts[g]):
                for i in range(seconds[g]):
                    if g == 0:
                        chip, replica = i, place.plane_replica(k)
                    else:
                        chip, replica = chip_at(k), i
                    yield k, i, chip, pl.multiple_of(first + replica * size, 8), size

        def piece_copy(g, k, i, chip, row, size):
            return pltpu.make_async_copy(
                owner_ref.at[chip * 2 + place.core, pl.ds(row, size), :],
                accs[g].at[k, i],
                piece_sem.at[g, k, i],
            )

        def half_copy(c):
            return remote(
                owner_ref.at[c * 2 + 1 - place.core],
                from_core.at[c],
                half_send.at[c],
                half_recv.at[c],
                place.sibling(),
            )

        def partner(over_dp, k):
            if over_dp:
                return place.plane(k)
            return place.lane(k)

        def one_copy(g, k):
            return remote(
                accs[g].at[k],
                ones[g].at[k],
                one_send.at[g, k],
                one_recv.at[g, k],
                partner(g == 0, k),
            )

        def mine(g):
            return place.chip if g == 0 else place.replica

        def two_copy(g, k):
            return remote(
                accs[g].at[0, lax.rem(mine(g) + k, seconds[g])],
                twos[g].at[k],
                two_send.at[g, k],
                two_recv.at[g, k],
                partner(g == 1, k),
            )

        def end_copy(g, k, there):
            first, rows = regions[g]
            size = rows // replicas
            span = owned_ref.at[pl.ds(pl.multiple_of(first + there * size, 8), size), :]
            return remote(span, span, end_send.at[g, k], end_recv.at[g, k], place.plane(k))

        def begin_sums():
            for c in range(chips):
                half_copy(c).start()
            for g in range(2):
                for item in pieces(g):
                    piece_copy(g, *item).start()

        def begin_one():
            for c in range(chips):
                half_copy(c).wait_recv()
            for g in range(2):
                for item in pieces(g):
                    piece_copy(g, *item).wait()
                    k, i, chip, row, size = item
                    accs[g][k, i] += from_core[chip, pl.ds(row, size), :]
                for k in range(1, firsts[g]):
                    one_copy(g, k).start()

        def begin_two(g):
            for k in range(1, firsts[g]):
                one_copy(g, k).wait_recv()
            for i in range(seconds[g]):
                total = accs[g][0, i]
                for k in range(1, firsts[g]):
                    total = total + ones[g][k, i]
                accs[g][0, i] = total
            for k in range(1, seconds[g]):
                two_copy(g, k).start()

        def begin_end(g):
            first, rows = regions[g]
            size = rows // replicas
            total = accs[g][0, mine(g)]
            for k in range(1, seconds[g]):
                two_copy(g, k).wait_recv()
                total = total + twos[g][k]
            row = pl.multiple_of(first + place.replica * size, 8)
            owned_ref[pl.ds(row, size), :] = total
            for k in range(1, replicas):
                end_copy(g, k, place.replica).start()

        def end_sums():
            for g in range(2):
                for k in range(1, replicas):
                    end_copy(g, k, lax.rem(place.replica + replicas - k, replicas)).wait_recv()
                    end_copy(g, k, place.replica).wait_send()
                for k in range(1, firsts[g]):
                    one_copy(g, k).wait_send()
                for k in range(1, seconds[g]):
                    two_copy(g, k).wait_send()
            for c in range(chips):
                half_copy(c).wait_send()

        def begin_all():
            barrier = pltpu.get_barrier_semaphore()

            def greet(k, carry):
                pl.semaphore_signal(
                    barrier,
                    inc=1,
                    device_id=device(lax.rem(me + k, amount)),
                    device_id_type=MESH,
                )
                return carry

            lax.fori_loop(1, amount, greet, 0)
            pl.semaphore_wait(barrier, amount - 1)
            local.start()
            if reduce:
                begin_sums()
            for k in range(1, chips):
                lane_copy(k).start()

            def give(k, carry):
                slice_copy(k).start()
                return carry

            lax.fori_loop(1, amount, give, 0)
            gathered[me] = slices_ref[place.member]

        def token_lane():
            local.wait()
            for k in range(1, chips):
                lane_wait(k)
            for c in range(chips):
                core_copy(place.replica, c).start()

        def token_plane():
            for c in range(chips):
                for k in range(1, replicas):
                    plane_copy(k, c).start()

        def token_core():
            for k in range(1, replicas):
                for c in range(chips):
                    plane_wait(k, c)
            for k in range(1, replicas):
                for c in range(chips):
                    core_copy(place.plane_replica(k), c).start()

        plan = [(0.0, begin_all)]
        if reduce:
            plan = plan + [
                (0.09, begin_one),
                (0.25, token_lane),
                (0.4, lambda: begin_two(0)),
                (0.4, token_plane),
                (0.65, lambda: begin_two(1)),
                (0.75, lambda: begin_end(0)),
                (0.8, lambda: begin_end(1)),
                (0.8, token_core),
            ]
        else:
            plan = plan + [(0.17, token_lane), (0.17, token_plane), (0.5, token_core)]

        start = step * block
        part = table_ref[...].astype(NARROW)
        places = lax.broadcasted_iota(jnp.int32, (block, tile), 0)

        def lap(k, carry):
            for part_of, act in plan:
                pl.when(step * tiles + k == when(part_of))(act)
            here = hidden_ref[pl.ds(pl.multiple_of(k * tile, tile), tile), :]
            logits = lax.dot_general(part, here, LAST_CONTRACT, preferred_element_type=FLOAT)
            probs = jnp.exp(logits - logsum_ref[k])
            grads = jnp.where(
                places == target_ref[k] - start, probs - weight_ref[k], probs
            ).astype(NARROW)
            piece = jnp.dot(grads, here, preferred_element_type=FLOAT)

            @pl.when(k == 0)
            def _():
                grad_ref[...] = piece

            @pl.when(k > 0)
            def _():
                grad_ref[...] += piece

            return carry

        lax.fori_loop(0, tiles, lap, 0)
        squares = jnp.sum(jnp.square(grad_ref[...]), axis=0, keepdims=True)

        @pl.when(step == 0)
        def _():
            square_ref[...] = squares

        @pl.when(step > 0)
        def _():
            square_ref[...] += squares

        @pl.when(step == last)
        def _():
            def take(k, carry):
                there = gathered.at[lax.rem(me + amount - k, amount)]
                remote(there, there, slice_send.at[k], slice_recv.at[k], device(me)).wait_recv()
                slice_copy(k).wait_send()
                return carry

            lax.fori_loop(1, amount, take, 0)
            if reduce:
                end_sums()
                owned_out[...] = owned_ref[...]
            summed_ref[...] = jnp.sum(gathered[...], axis=0)
            for r in range(replicas):
                for c in range(chips):
                    core_wait(r, c)
            for k in range(1, chips):
                lane_copy(k).wait_send()
            for c in range(chips):
                for k in range(1, replicas):
                    plane_copy(k, c).wait_send()
                for r in range(replicas):
                    core_copy(r, c).wait_send()

    whole = pl.BlockSpec(memory_space=pltpu.VMEM)
    anywhere = pl.BlockSpec(memory_space=pl.ANY)
    shape = (tiles, 1, tile)
    dma = pltpu.SemaphoreType.DMA
    return pl.pallas_call(
        kernel,
        grid=(steps,),
        in_specs=[pl.BlockSpec((block, width), lambda i: (i, 0))]
        + [whole] * 4
        + [anywhere, whole, anywhere],
        out_specs=[
            pl.BlockSpec((block, width), lambda i: (i, 0)),
            pl.BlockSpec((1, width), lambda i: (0, 0)),
            anywhere,
            whole,
            whole,
        ],
        out_shape=[
            jax.ShapeDtypeStruct((vocab, width), FLOAT),
            jax.ShapeDtypeStruct((1, width), FLOAT),
            jax.ShapeDtypeStruct((groups * replicas, own, width), NARROW),
            jax.ShapeDtypeStruct(slices.shape[1:], FLOAT),
            jax.ShapeDtypeStruct(owner_grads.shape[1:] if reduce else (8, 128), FLOAT),
        ],
        scratch_shapes=[
            pltpu.VMEM((amount,) + slices.shape[1:], FLOAT),
            pltpu.VMEM(owner_grads.shape[1:] if reduce else (8, 128), FLOAT),
            pltpu.VMEM((chips,) + owner_grads.shape[1:] if reduce else (8, 128), FLOAT),
        ]
        + [
            pltpu.VMEM(
                (counts[g], seconds[g], regions[g][1] // replicas, width)[skip:]
                if reduce
                else (8, 128),
                FLOAT,
            )
            for counts, skip in ((firsts, 0), (firsts, 0), (seconds, 1))
            for g in range(2)
        ]
        + [
            dma((2, max(firsts), max(seconds))),
            dma((chips,)),
            dma((chips,)),
            dma((2, max(firsts))),
            dma((2, max(firsts))),
            dma((2, max(seconds))),
            dma((2, max(seconds))),
            dma((2, replicas)),
            dma((2, replicas)),
            dma,
            dma((amount,)),
            dma((amount,)),
            dma((chips,)),
            dma((chips,)),
            dma((replicas, chips)),
            dma((replicas, chips)),
            dma((replicas, chips)),
            dma((replicas, chips)),
        ],
        compiler_params=pltpu.CompilerParams(
            vmem_limit_bytes=VMEM_LIMIT, collective_id=1, has_side_effects=True
        ),
        cost_estimate=pl.CostEstimate(
            flops=4 * vocab * rows * width,
            bytes_accessed=vocab * width * 8 + rows * width * 4,
            transcendentals=vocab * rows,
        ),
    )(
        table,
        hidden,
        logsum.reshape(shape),
        weights.reshape(shape),
        target.reshape(shape),
        token_grad,
        slices,
        owner_grads,
    )


def exchange_scalars(line, groups, replicas):
    amount = groups * replicas

    def kernel(own_ref, all_ref, local_sem, send_sem, recv_sem):
        place = Place(groups, replicas)
        me = place.replica * groups + place.member

        def device(index):
            return place.at(index // groups, lax.rem(index, groups))

        barrier = pltpu.get_barrier_semaphore()

        def greet(k, carry):
            pl.semaphore_signal(
                barrier, inc=1, device_id=device(lax.rem(me + k, amount)), device_id_type=MESH
            )
            return carry

        def copy(k):
            return remote(
                own_ref,
                all_ref.at[me],
                send_sem.at[k],
                recv_sem.at[k],
                device(lax.rem(me + k, amount)),
            )

        def begin(k, carry):
            copy(k).start()
            return carry

        def finish(k, carry):
            there = all_ref.at[lax.rem(me + amount - k, amount)]
            remote(there, there, send_sem.at[k], recv_sem.at[k], device(me)).wait_recv()
            copy(k).wait_send()
            return carry

        lax.fori_loop(1, amount, greet, 0)
        local = pltpu.make_async_copy(own_ref, all_ref.at[me], local_sem)
        local.start()
        pl.semaphore_wait(barrier, amount - 1)
        lax.fori_loop(1, amount, begin, 0)
        local.wait()
        lax.fori_loop(1, amount, finish, 0)

    whole = pl.BlockSpec(memory_space=pltpu.VMEM)
    dma = pltpu.SemaphoreType.DMA
    return pl.pallas_call(
        kernel,
        in_specs=[whole],
        out_specs=whole,
        out_shape=jax.ShapeDtypeStruct((amount,) + line.shape, line.dtype),
        scratch_shapes=[dma, dma((amount,)), dma((amount,))],
        compiler_params=pltpu.CompilerParams(collective_id=2, has_side_effects=True),
    )(line)


def chunk_lists(local, inside, chunk):
    chunks = local.shape[0] // chunk
    flags = inside.reshape(chunks, chunk)
    spots = jnp.arange(chunk, dtype=jnp.int32)
    ahead = (spots[:, None] < spots[None, :]).astype(NARROW)
    order = jnp.dot(flags.astype(NARROW), ahead, preferred_element_type=FLOAT).astype(jnp.int32)
    chosen = (order[:, None, :] == spots[None, :, None]) & flags[:, None, :]
    places = jnp.sum(jnp.where(chosen, spots[None, None, :], 0), axis=2)
    rows = jnp.sum(jnp.where(chosen, local.reshape(chunks, 1, chunk), 0), axis=2)
    return places, rows, jnp.sum(flags.astype(jnp.int32), axis=1)


def embed_table_grad(token_grads, places, rows, counts, vocab):
    chunks, chunk = places.shape
    width = token_grads.shape[-1]
    padded = vocab + 8
    unroll = 4

    def kernel(
        count_ref, place_ref, row_ref, tokens_ref, grad_ref, square_ref, wide_ref, total_ref, sem
    ):
        step = pl.program_id(0)

        @pl.when(step == 0)
        def _():
            total_ref[...] = jnp.zeros_like(total_ref)

        wide_ref[...] = tokens_ref[...].astype(FLOAT)
        amount = count_ref[step]

        def lap(j, carry):
            for u in range(unroll):
                spot = j * unroll + u
                row = jnp.where(spot < amount, row_ref[0, 0, spot], vocab)
                place = place_ref[0, 0, spot]
                total_ref[pl.ds(row, 1), :] += wide_ref[pl.ds(place, 1), :]
            return carry

        lax.fori_loop(0, (amount + unroll - 1) // unroll, lap, 0)

        @pl.when(step == chunks - 1)
        def _():
            out = pltpu.make_async_copy(total_ref.at[pl.ds(0, vocab), :], grad_ref, sem)
            out.start()
            square_ref[...] = jnp.sum(
                jnp.square(total_ref[pl.ds(0, vocab), :]), axis=0, keepdims=True
            )
            out.wait()

    line = pl.BlockSpec((1, 1, chunk), lambda i, c: (i, 0, 0), memory_space=pltpu.SMEM)
    return pl.pallas_call(
        kernel,
        grid_spec=pltpu.PrefetchScalarGridSpec(
            num_scalar_prefetch=1,
            grid=(chunks,),
            in_specs=[line, line, pl.BlockSpec((chunk, width), lambda i, c: (i, 0))],
            out_specs=[
                pl.BlockSpec(memory_space=pl.ANY),
                pl.BlockSpec((1, width), lambda i, c: (0, 0)),
            ],
            scratch_shapes=[
                pltpu.VMEM((chunk, width), FLOAT),
                pltpu.VMEM((padded, width), FLOAT),
                pltpu.SemaphoreType.DMA,
            ],
        ),
        out_shape=[
            jax.ShapeDtypeStruct((vocab, width), FLOAT),
            jax.ShapeDtypeStruct((1, width), FLOAT),
        ],
        compiler_params=pltpu.CompilerParams(vmem_limit_bytes=VMEM_LIMIT),
    )(
        counts,
        places.reshape(chunks, 1, chunk),
        rows.reshape(chunks, 1, chunk),
        token_grads.reshape(chunks * chunk, width),
    )


def update_rule(weight, grad, moment, average, rate, clip_factor):
    clipped = clip_factor * grad
    new_moment = MOMENTUM * moment + clipped
    new_weight = weight - rate * (clipped + MOMENTUM * new_moment)
    new_average = DECAY * average + (1.0 - DECAY) * new_weight
    return (new_weight, new_moment, new_average)


def update_all(scalars, tables, matrices, rates):
    vocab, width = tables[0][0].shape
    sub = tables[0][3].shape[0]
    block = block_rows(vocab, 1100)
    blocks = vocab // block
    window = max(-(-(sub + sub * r % 8) // 8) * 8 for r in range(vocab // sub))
    tile = 264
    tiles = -(-window // tile)
    steps = 2 * blocks + 2 * tiles
    count = len(matrices)

    def kernel(*refs):
        refs = list(refs)

        def take(amount):
            taken = refs[:amount]
            del refs[:amount]
            return taken

        (scalars_ref,) = take(1)
        whole_in = [take(3) for _ in range(2)]
        own_in = [take(4) for _ in range(2)]
        small_in = [take(4) for _ in range(count)]
        new_tables = take(2)
        own_out = [take(2) for _ in range(2)]
        small_out = [take(3) for _ in range(count)]
        (factor_ref,) = take(1)
        windows = take(2)
        (sems,) = take(1)
        step = pl.program_id(0)
        begin = lax.axis_index("dp") * sub
        low = pl.multiple_of(begin // 8 * 8, 8)
        shift = begin - low

        def fetch(w, t):
            first = t * tile
            size = min(tile, window - first)
            return [
                pltpu.make_async_copy(
                    own_in[w][i].at[pl.ds(low + first, size), :],
                    windows[i].at[pl.ds(first, size), :],
                    sems.at[w, i, t],
                )
                for i in range(2)
            ]

        @pl.when(step == 0)
        def _():
            total = jnp.sum(scalars_ref[...], axis=0)
            norm = jnp.sqrt(total)
            factor_ref[...] = CLIP_LEVEL / jnp.maximum(norm, CLIP_LEVEL)

        factor = factor_ref[1:2, 0:1]
        for w in range(2):

            @pl.when((step >= w * blocks) & (step < (w + 1) * blocks))
            def _():
                table_ref, grad_ref, moment_ref = whole_in[w]
                table = table_ref[...]
                new_tables[w][...], _, _ = update_rule(
                    table, grad_ref[...], moment_ref[...].astype(FLOAT), table, rates[w], factor
                )

        @pl.when(step == 1)
        def _():
            for i in range(count):
                weight, grad, moment, average = [ref[...] for ref in small_in[i]]
                results = update_rule(weight, grad, moment, average, rates[2 + i], factor)
                for ref, result in zip(small_out[i], results):
                    ref[...] = result

        for w in range(2):
            base = 2 * blocks + w * tiles
            for t in range(tiles):

                @pl.when(step == (base - tiles + t + 1 if w else blocks))
                def _():
                    for copy in fetch(w, t):
                        copy.start()

            for t in range(tiles):

                @pl.when(step == base + t)
                def _():
                    if t == 0:
                        for copy in fetch(w, 0):
                            copy.wait()
                    if t + 1 < tiles:
                        for copy in fetch(w, t + 1):
                            copy.wait()

            @pl.when((step >= base) & (step < base + tiles))
            def _():
                first = pl.multiple_of((step - base) * tile, 8)
                amount = jnp.where(shift == 0, 0, tile + 8 - shift)
                own_table, own_grad = [
                    pltpu.roll(win[pl.ds(first, tile + 8), :], amount, 0)[:tile]
                    for win in windows
                ]
                _, own_out[w][0][...], own_out[w][1][...] = update_rule(
                    own_table, own_grad, own_in[w][2][...], own_in[w][3][...], rates[w], factor
                )

    whole = pl.BlockSpec(memory_space=pltpu.VMEM)
    anywhere = pl.BlockSpec(memory_space=pl.ANY)

    def table_spec(w):
        return pl.BlockSpec(
            (block, width), lambda i: (jnp.clip(i - w * blocks, 0, blocks - 1), 0)
        )

    def own_spec(w):
        return pl.BlockSpec(
            (tile, width),
            lambda i: (jnp.clip(i - 2 * blocks - w * tiles, 0, tiles - 1), 0),
        )

    state = jax.ShapeDtypeStruct((sub, width), FLOAT)
    operands = [scalars]
    in_specs = [whole]
    for w in range(2):
        operands += list(tables[w][:3])
        in_specs += [table_spec(w)] * 3
    for w in range(2):
        operands += [tables[w][0], tables[w][1], tables[w][3], tables[w][4]]
        in_specs += [anywhere, anywhere, own_spec(w), own_spec(w)]
    for item in matrices:
        operands += list(item)
        in_specs += [whole] * 4
    out_specs = [table_spec(0), table_spec(1)]
    out_shape = [jax.ShapeDtypeStruct((vocab, width), FLOAT)] * 2
    for w in range(2):
        out_specs += [own_spec(w)] * 2
        out_shape += [state] * 2
    for item in matrices:
        out_specs += [whole] * 3
        out_shape += [jax.ShapeDtypeStruct(item[0].shape, FLOAT)] * 3
    results = pl.pallas_call(
        kernel,
        grid=(steps,),
        in_specs=in_specs,
        out_specs=out_specs,
        out_shape=out_shape,
        scratch_shapes=[pltpu.VMEM((8, 128), FLOAT)]
        + [pltpu.VMEM((tiles * tile + 8, width), FLOAT)] * 2
        + [pltpu.SemaphoreType.DMA((2, 2, tiles))],
        compiler_params=pltpu.CompilerParams(vmem_limit_bytes=VMEM_LIMIT),
    )(*operands)
    tables_out = [(results[w], *results[2 + 2 * w : 4 + 2 * w]) for w in range(2)]
    return tables_out, [results[6 + 3 * i : 9 + 3 * i] for i in range(count)]


def shards(
    token_ids,
    loss_mask,
    lengths,
    buffer_ids,
    embed_table,
    embed_moment,
    embed_average,
    head_table,
    head_moment,
    head_average,
    in_weights,
    in_moment,
    in_average,
    out_weights,
    out_moment,
    out_average,
    vectors,
    vector_moment,
    vector_average,
):
    groups = lax.axis_size("fsdp")
    replicas = lax.axis_size("dp")
    member = lax.axis_index("fsdp")
    replica = lax.axis_index("dp")
    batches, _, seq = token_ids.shape
    vocab_rows, width = embed_table.shape
    head_size = width // HEADS
    vocab_start = member * vocab_rows
    own_rows = batches * seq
    rows_all = groups * own_rows

    tokens, marks, buffers = token_ids[:, 0], loss_mask[:, 0], buffer_ids[:, 0]
    divisor, offset, counted = jax.vmap(functools.partial(slot_info, buffer_count=NSEG))(
        tokens, marks, lengths[:, 0], buffers
    )
    packed = jnp.concatenate(
        [
            tokens,
            divisor,
            jnp.broadcast_to(jnp.sum(counted), (8 - 2 * batches, seq)),
        ],
        axis=0,
    )
    amount = vectors.shape[0]
    line = jnp.pad(vectors, (0, -amount % 1024)).reshape(-1, 128)
    everyone, lines, in_full, out_full, resid, aims = start_kernel(
        packed,
        line,
        in_weights,
        out_weights,
        embed_table,
        head_table,
        batches,
        groups,
        replicas,
    )
    vector_full = lines.reshape(groups, -1)[:, :amount].reshape(-1).astype(NARROW)
    early_moment, resid = lax.optimization_barrier((head_moment, resid))
    head_moment_low = lax.all_gather(early_moment.astype(NARROW), "dp", axis=0, tiled=True)
    tokens_all = everyone[:, :batches]
    count = jnp.maximum(jnp.sum(everyone[:, 2 * batches, 0]).astype(FLOAT), 1.0)
    divisor_all = everyone[:, batches : 2 * batches].astype(FLOAT)
    share_all = jnp.where(divisor_all > 0.5, 1.0 / jnp.maximum(divisor_all, 1.0), 0.0)
    weight_all = (share_all / count).reshape(-1)
    target_all = (
        jnp.concatenate([tokens_all[:, :, 1:], jnp.zeros_like(tokens_all[:, :, :1])], axis=2)
        .reshape(-1)
    ) - vocab_start
    tokens_flat = tokens_all.reshape(-1)
    local_all = tokens_flat - vocab_start
    inside_all = (local_all >= 0) & (local_all < vocab_rows)

    def group_part(values):
        return lax.dynamic_slice_in_dim(values, replica * rows_all, rows_all, 0)

    vector = vector_full.astype(FLOAT).reshape(1, -1)
    tables = rotary_tables(offset.reshape(-1), head_size)
    lines_of, columns_of = buffers[:, None, :], buffers[:, :, None]
    final, *kept = layer_forward(resid, in_full, out_full, vector, tables, lines_of, columns_of)
    final_grad, logsum_all, loss_part, all_hidden = head_kernel(
        head_table, final, aims, group_part(target_all), group_part(weight_all), groups, replicas
    )

    less_weight = logsum_all - jnp.log(jnp.maximum(weight_all, 1e-30))
    shifted = jnp.where(weight_all > 0.0, less_weight, 1e30)
    chunk = min(512, rows_all)
    lists = chunk_lists(local_all, inside_all, chunk)

    token_grad, vector_grad, owner_grads = layer_backward(
        final_grad,
        resid,
        in_full,
        out_full,
        vector,
        tables,
        lines_of,
        columns_of,
        kept,
        groups,
    )
    token_grad, head_moment_low = lax.optimization_barrier((token_grad, head_moment_low))
    slices = jnp.pad(vector_grad.reshape(groups, amount), ((0, 0), (0, -amount % 1024)))
    in_rows = in_weights.shape[0]
    cut = owner_grads.shape[1] - out_weights.shape[0]
    head_grad, head_square, token_grads, vector_sum, owned = head_table_grad(
        head_table,
        all_hidden,
        shifted,
        weight_all,
        target_all,
        token_grad,
        slices.reshape(groups, -1, 128),
        owner_grads,
        cut,
        groups,
        replicas,
    )
    if owned.shape != owner_grads.shape[1:]:
        owned = lax.psum(lax.psum_scatter(owner_grads, "fsdp", scatter_dimension=0), "dp")
    layer_grads = [
        owned[:cut].reshape(-1, in_rows, width).transpose(1, 0, 2).reshape(in_rows, -1),
        owned[cut:],
        vector_sum.reshape(-1)[:amount],
    ]
    late_moment, token_grads = lax.optimization_barrier((embed_moment, token_grads))
    embed_moment_low = lax.all_gather(late_moment.astype(NARROW), "dp", axis=0, tiled=True)
    embed_grad, embed_square = embed_table_grad(token_grads, *lists, vocab_rows)
    square = jnp.sum(embed_square) + jnp.sum(head_square)
    for grad in layer_grads:
        square = square + jnp.sum(grad * grad)
    line = jnp.stack([loss_part, square / replicas])[:, None]
    line = jnp.pad(jnp.broadcast_to(line, (2, 128)), ((0, 6), (0, 0)))
    scalars = exchange_scalars(line, groups, replicas)
    pair = jnp.sum(scalars[:, :2, 0], axis=0)
    loss = pair[0]
    grad_norm = jnp.sqrt(pair[1])
    base = math.sqrt(NPARAM) / CLIP_LEVEL
    root = math.sqrt(width)

    def row(values):
        return values.reshape(1, -1)

    (embed, head), (inner, outer, vector) = update_all(
        scalars,
        [
            (embed_table, embed_grad, embed_moment_low, embed_moment, embed_average),
            (head_table, head_grad, head_moment_low, head_moment, head_average),
        ],
        [
            (in_weights, layer_grads[0], in_moment, in_average),
            (out_weights, layer_grads[1], out_moment, out_average),
            tuple(map(row, (vectors, layer_grads[2], vector_moment, vector_average))),
        ],
        (base, base / root, base / root, base / root, 0.3 * base),
    )
    vector = [values.reshape(-1) for values in vector]
    return (*embed, *head, *inner, *outer, *vector, loss, grad_norm)


def solution(mesh):
    placed = (
        P(None, ("dp", "fsdp"), None),
        P(None, ("dp", "fsdp"), None),
        P(None, ("dp", "fsdp")),
        P(None, ("dp", "fsdp"), None),
        P("fsdp", None),
        P(("fsdp", "dp"), None),
        P(("fsdp", "dp"), None),
        P("fsdp", None),
        P(("fsdp", "dp"), None),
        P(("fsdp", "dp"), None),
        P("fsdp", None),
        P("fsdp", None),
        P("fsdp", None),
        P("fsdp", None),
        P("fsdp", None),
        P("fsdp", None),
        P("fsdp"),
        P("fsdp"),
        P("fsdp"),
    )
    return jax.shard_map(
        shards,
        mesh=mesh,
        in_specs=placed,
        out_specs=(
            P("fsdp", None),
            P(("fsdp", "dp"), None),
            P(("fsdp", "dp"), None),
            P("fsdp", None),
            P(("fsdp", "dp"), None),
            P(("fsdp", "dp"), None),
            P("fsdp", None),
            P("fsdp", None),
            P("fsdp", None),
            P("fsdp", None),
            P("fsdp", None),
            P("fsdp", None),
            P("fsdp"),
            P("fsdp"),
            P("fsdp"),
            P(),
            P(),
        ),
        check_vma=False,
    )
```

```python
import functools
import math

import jax
import jax.numpy as jnp
from jax import lax
from jax.experimental import pallas as pl
from jax.experimental.pallas import tpu as pltpu
from jax.sharding import PartitionSpec as P

HEADS = 8
NPARAM = 54664704
NSEG = 3


EPSILON = 1e-05
CLIP_LEVEL = 0.002
MOMENTUM = 0.5
DECAY = 0.5
NARROW = jnp.bfloat16
FLOAT = jnp.float32
ROWS_CONTRACT = (((0,), (0,)), ((), ()))
LAST_CONTRACT = (((1,), (1,)), ((), ()))


VMEM_LIMIT = 60 * 2**20


def slot_info(tokens, marks, length, buffers, buffer_count):
    seq = tokens.shape[0]
    places = jnp.arange(seq, dtype=jnp.int32)
    same_buffer = jnp.concatenate([buffers[1:] == buffers[:-1], jnp.zeros((1,), dtype=bool)])
    valid = jnp.where((marks == 1) & (places + 1 < length) & same_buffer, 1.0, 0.0).astype(FLOAT)
    member = buffers[None, :] == jnp.arange(buffer_count, dtype=jnp.int32)[:, None]
    weights = jnp.where(member, 1.0, 0.0).astype(FLOAT)
    tally = jnp.sum(weights * valid[None, :], axis=1)
    divisor = valid * jnp.sum(weights * tally[:, None], axis=0)
    counted = jnp.sum(jnp.where(tally > 0.5, 1.0, 0.0).astype(FLOAT))
    first = jnp.min(jnp.where(member, places[None, :], seq), axis=1)
    offset = places - jnp.sum(jnp.where(member, first[:, None], 0), axis=0)
    return (divisor.astype(jnp.int32), offset, counted.astype(jnp.int32))


def rotary_tables(offset, head_size):
    rot = head_size // 4
    half = rot // 2
    lanes = 128
    freqs = jnp.power(10000.0, -2.0 * jnp.arange(half, dtype=FLOAT) / rot)
    angles = offset.astype(FLOAT)[:, None] * freqs[None, :]
    cosine, sine = jnp.cos(angles), jnp.sin(angles)
    rows = offset.shape[0]
    rest = head_size - rot
    ones, none = jnp.ones((rows, rest), FLOAT), jnp.zeros((rows, rest), FLOAT)
    blank = jnp.zeros((rows, half), FLOAT)
    stay = jnp.concatenate([cosine, cosine, ones], axis=1)
    ahead = jnp.concatenate([-sine, blank, none], axis=1)
    behind = jnp.concatenate([blank, sine, none], axis=1)
    return [
        jnp.concatenate([part] * (lanes // head_size), axis=1) for part in (stay, ahead, behind)
    ]


def wide_tables(refs, width):
    return [jnp.concatenate([ref[...]] * (width // ref.shape[1]), axis=1) for ref in refs]


def norm_unit(values):
    mean = jnp.mean(values, axis=-1, keepdims=True)
    centred = values - mean
    scale = lax.rsqrt(jnp.mean(centred * centred, axis=-1, keepdims=True) + EPSILON)
    return (centred * scale, scale)


def norm_back(scaled, unit, scale):
    return scale * (
        scaled
        - jnp.mean(scaled, axis=-1, keepdims=True)
        - unit * jnp.mean(scaled * unit, axis=-1, keepdims=True)
    )


def vector_spans(width, hidden):
    amounts = [width] * 6 + [3 * width, width, hidden, width]
    spans = []
    begin = 0
    for amount in amounts:
        spans.append(slice(begin, begin + amount))
        begin = begin + amount
    return spans


def masked_probs(queries, keys, mask, factor):
    scores = lax.dot_general(queries, keys, LAST_CONTRACT, preferred_element_type=FLOAT) * factor
    scores = jnp.where(mask, scores, -1e30)
    top = jnp.max(scores, axis=-1, keepdims=True)
    logsum = top + jnp.log(jnp.sum(jnp.exp(scores - top), axis=-1, keepdims=True))
    return jnp.exp(scores - logsum)


def slot_mask(line_ref, column_ref, b, seq):
    later = lax.broadcasted_iota(jnp.int32, (seq, seq), 1)
    place = lax.broadcasted_iota(jnp.int32, (seq, seq), 0)
    return (column_ref[b] == line_ref[b]) & (later <= place)


def layer_forward(resid, in_full, out_full, vector, tables, lines, columns):
    rows, width = resid.shape
    hidden = out_full.shape[0] - width
    batches, _, seq = lines.shape
    head_size = width // HEADS
    half = head_size // 8
    factor = 1.0 / math.sqrt(head_size)
    spans = vector_spans(width, hidden)

    def kernel(
        resid_ref,
        in_ref,
        out_ref,
        vector_ref,
        stay_ref,
        ahead_ref,
        behind_ref,
        line_ref,
        column_ref,
        final_ref,
        qkv_ref,
        pre_ref,
        joined_ref,
        last_ref,
    ):
        def part(i):
            return vector_ref[:, spans[i]]

        start = resid_ref[...]
        unit, _ = norm_unit(start)
        input_one = (unit * part(0) + part(1)).astype(NARROW)
        input_two = (unit * part(2) + part(3)).astype(NARROW)
        stay, ahead, behind = wide_tables((stay_ref, ahead_ref, behind_ref), width)
        bias = part(6)
        for i in range(3):
            span = slice(i * width, (i + 1) * width)
            values = jnp.dot(input_one, in_ref[:, span], preferred_element_type=FLOAT)
            values = values + bias[:, span]
            if i < 2:
                values = (
                    values * stay
                    + pltpu.roll(values, width - half, 1) * ahead
                    + pltpu.roll(values, half, 1) * behind
                )
            qkv_ref[:, span] = values.astype(NARROW)
        for b in range(batches):
            mask = slot_mask(line_ref, column_ref, b, seq)
            there = slice(b * seq, (b + 1) * seq)
            for head in range(HEADS):
                first = head * head_size
                queries, keys, values = [
                    qkv_ref[there, i * width + first : i * width + first + head_size]
                    for i in range(3)
                ]
                probs = masked_probs(queries, keys, mask, factor).astype(NARROW)
                joined_ref[there, first : first + head_size] = jnp.dot(
                    probs, values, preferred_element_type=FLOAT
                ).astype(NARROW)
        bias = part(8)
        for i in range(hidden // width):
            span = slice(i * width, (i + 1) * width)
            pre = (
                jnp.dot(
                    input_two,
                    in_ref[:, (3 + i) * width : (4 + i) * width],
                    preferred_element_type=FLOAT,
                )
                + bias[:, span]
            )
            pre_ref[:, span] = pre
            joined_ref[:, (1 + i) * width : (2 + i) * width] = (
                0.5 * pre * (1.0 + lax.erf(pre * 0.7071067811865476))
            ).astype(NARROW)
        last = (
            start
            + jnp.dot(joined_ref[...], out_ref[...], preferred_element_type=FLOAT)
            + part(7)
            + part(9)
        )
        last_ref[...] = last
        unit_last, _ = norm_unit(last)
        final_ref[...] = (unit_last * part(4) + part(5)).astype(NARROW)

    return pl.pallas_call(
        kernel,
        out_shape=[
            jax.ShapeDtypeStruct((rows, width), NARROW),
            jax.ShapeDtypeStruct((rows, 3 * width), NARROW),
            jax.ShapeDtypeStruct((rows, hidden), FLOAT),
            jax.ShapeDtypeStruct((rows, width + hidden), NARROW),
            jax.ShapeDtypeStruct((rows, width), FLOAT),
        ],
        compiler_params=pltpu.CompilerParams(vmem_limit_bytes=VMEM_LIMIT),
    )(resid, in_full, out_full, vector, *tables, lines, columns)


def layer_backward(
    final_grad, resid, in_full, out_full, vector, tables, lines, columns, kept, groups
):
    rows, width = resid.shape
    hidden = out_full.shape[0] - width
    batches, _, seq = lines.shape
    head_size = width // HEADS
    half = head_size // 8
    factor = 1.0 / math.sqrt(head_size)
    spans = vector_spans(width, hidden)
    blocks = in_full.shape[1] // width
    in_rows = width // groups
    out_rows = out_full.shape[0] // groups
    first_out = blocks * in_rows
    shard = first_out + out_rows

    def kernel(
        final_grad_ref,
        resid_ref,
        in_ref,
        out_ref,
        vector_ref,
        stay_ref,
        ahead_ref,
        behind_ref,
        line_ref,
        column_ref,
        qkv_ref,
        pre_ref,
        joined_ref,
        last_ref,
        token_ref,
        small_ref,
        owners_ref,
        owners,
        low,
        wide,
        sems,
    ):
        def part(i):
            return vector_ref[:, spans[i]]

        def column_sum(i, values):
            small_ref[:, spans[i]] = jnp.sum(values, axis=0, keepdims=True)

        final_grad_in = final_grad_ref[...]
        unit_last, scale_last = norm_unit(last_ref[...])
        column_sum(4, final_grad_in * unit_last)
        column_sum(5, final_grad_in)
        grad_out = norm_back(final_grad_in * part(4), unit_last, scale_last)
        column_sum(7, grad_out)
        column_sum(9, grad_out)
        grad_low = grad_out.astype(NARROW)
        for c in range((width + hidden) // width):
            there = slice(c * width, (c + 1) * width)
            piece = lax.dot_general(
                joined_ref[:, there], grad_low, ROWS_CONTRACT, preferred_element_type=FLOAT
            )
            at = c * width
            while at < (c + 1) * width:
                owner, row = at // out_rows, at % out_rows
                size = min(out_rows - row, (c + 1) * width - at)
                owners[owner, first_out + row : first_out + row + size, :] = piece[
                    at - c * width : at - c * width + size
                ]
                at = at + size
        out_copy = pltpu.make_async_copy(
            owners.at[:, pl.ds(first_out, out_rows), :],
            owners_ref.at[:, pl.ds(first_out, out_rows), :],
            sems.at[0],
        )
        out_copy.start()
        unit, scale = norm_unit(resid_ref[...])
        input_one = (unit * part(0) + part(1)).astype(NARROW)
        input_two = (unit * part(2) + part(3)).astype(NARROW)

        def in_piece(inputs, c, grads):
            piece = lax.dot_general(
                inputs, grads, ROWS_CONTRACT, preferred_element_type=FLOAT
            )
            for owner in range(groups):
                owners[owner, c * in_rows : (c + 1) * in_rows, :] = piece[
                    owner * in_rows : (owner + 1) * in_rows
                ]

        back_two = jnp.zeros((rows, width), FLOAT)
        bias_sums = []
        for i in range(hidden // width):
            grads = lax.dot_general(
                grad_low,
                out_ref[(1 + i) * width : (2 + i) * width, :],
                LAST_CONTRACT,
                preferred_element_type=FLOAT,
            )
            pre = pre_ref[:, i * width : (i + 1) * width]
            slope = (
                0.5 * (1.0 + lax.erf(pre * 0.7071067811865476))
                + pre * jnp.exp(-0.5 * pre * pre) * 0.3989422804014327
            )
            grads = grads * slope
            bias_sums.append(jnp.sum(grads, axis=0, keepdims=True))
            grads = grads.astype(NARROW)
            in_piece(input_two, 3 + i, grads)
            back_two = back_two + lax.dot_general(
                grads,
                in_ref[:, (3 + i) * width : (4 + i) * width],
                LAST_CONTRACT,
                preferred_element_type=FLOAT,
            )
        small_ref[:, spans[8]] = jnp.concatenate(bias_sums, axis=1)
        low[...] = lax.dot_general(
            grad_low, out_ref[:width, :], LAST_CONTRACT, preferred_element_type=FLOAT
        ).astype(NARROW)
        for b in range(batches):
            mask = slot_mask(line_ref, column_ref, b, seq)
            there = slice(b * seq, (b + 1) * seq)
            for head in range(HEADS):
                first = head * head_size
                at = [
                    slice(i * width + first, i * width + first + head_size) for i in range(3)
                ]
                queries, keys, values = [qkv_ref[there, at[i]] for i in range(3)]
                mixed = low[there, first : first + head_size]
                probs = masked_probs(queries, keys, mask, factor)
                back = lax.dot_general(
                    mixed, values, LAST_CONTRACT, preferred_element_type=FLOAT
                )
                wide[there, at[2]] = lax.dot_general(
                    probs.astype(NARROW), mixed, ROWS_CONTRACT, preferred_element_type=FLOAT
                )
                scores = (
                    probs
                    * (back - jnp.sum(probs * back, axis=-1, keepdims=True))
                    * factor
                ).astype(NARROW)
                wide[there, at[0]] = jnp.dot(scores, keys, preferred_element_type=FLOAT)
                wide[there, at[1]] = lax.dot_general(
                    scores, queries, ROWS_CONTRACT, preferred_element_type=FLOAT
                )
        stay, ahead, behind = wide_tables((stay_ref, ahead_ref, behind_ref), width)
        back_one = jnp.zeros((rows, width), FLOAT)
        bias_sums = []
        for i in range(3):
            span = slice(i * width, (i + 1) * width)
            grads = wide[:, span]
            if i < 2:
                grads = (
                    grads * stay
                    + pltpu.roll(grads * ahead, half, 1)
                    + pltpu.roll(grads * behind, width - half, 1)
                )
            bias_sums.append(jnp.sum(grads, axis=0, keepdims=True))
            grads = grads.astype(NARROW)
            in_piece(input_one, i, grads)
            back_one = back_one + lax.dot_general(
                grads, in_ref[:, span], LAST_CONTRACT, preferred_element_type=FLOAT
            )
        in_copy = pltpu.make_async_copy(
            owners.at[:, pl.ds(0, first_out), :],
            owners_ref.at[:, pl.ds(0, first_out), :],
            sems.at[1],
        )
        in_copy.start()
        small_ref[:, spans[6]] = jnp.concatenate(bias_sums, axis=1)
        column_sum(0, back_one * unit)
        column_sum(1, back_one)
        column_sum(2, back_two * unit)
        column_sum(3, back_two)
        token_ref[...] = (
            grad_out + norm_back(back_one * part(0) + back_two * part(2), unit, scale)
        ).astype(NARROW)
        out_copy.wait()
        in_copy.wait()

    whole = pl.BlockSpec(memory_space=pltpu.VMEM)
    return pl.pallas_call(
        kernel,
        in_specs=[whole] * 14,
        out_specs=[whole, whole, pl.BlockSpec(memory_space=pl.ANY)],
        out_shape=[
            jax.ShapeDtypeStruct((rows, width), NARROW),
            jax.ShapeDtypeStruct(vector.shape, FLOAT),
            jax.ShapeDtypeStruct((groups, shard, width), FLOAT),
        ],
        scratch_shapes=[
            pltpu.VMEM((groups, shard, width), FLOAT),
            pltpu.VMEM((rows, width), NARROW),
            pltpu.VMEM((rows, 3 * width), FLOAT),
            pltpu.SemaphoreType.DMA((2,)),
        ],
        compiler_params=pltpu.CompilerParams(vmem_limit_bytes=VMEM_LIMIT),
    )(final_grad, resid, in_full, out_full, vector, *tables, lines, columns, *kept)


def block_rows(rows, cap):
    best = rows
    for size in range(8, cap + 1, 8):
        if rows % size == 0:
            best = size
    return best


MESH = pl.DeviceIdType.MESH


def meet(peers):
    barrier = pltpu.get_barrier_semaphore()
    for peer in peers:
        pl.semaphore_signal(barrier, inc=1, device_id=peer, device_id_type=MESH)
    pl.semaphore_wait(barrier, len(peers))


class Place:
    def __init__(self, groups, replicas):
        self.groups = groups
        self.replicas = replicas
        self.chips = groups // 2
        self.replica = lax.axis_index("dp")
        self.member = lax.axis_index("fsdp")
        self.chip = self.member // 2
        self.core = self.member % 2
        self.sibling_member = self.chip * 2 + 1 - self.core

    def lane_chip(self, step):
        return lax.rem(self.chip + step, self.chips)

    def at(self, replica, member):
        return {"dp": replica, "fsdp": member}

    def lane(self, step):
        return self.at(self.replica, self.lane_chip(step) * 2 + self.core)

    def plane_replica(self, step):
        return lax.rem(self.replica + step, self.replicas)

    def plane(self, step):
        return self.at(self.plane_replica(step), self.member)

    def sibling(self):
        return self.at(self.replica, self.sibling_member)

    def lanes(self):
        return [self.lane(step) for step in range(1, self.chips)]

    def planes(self):
        return [self.plane(step) for step in range(1, self.replicas)]


def remote(source, target, send, recv, device):
    return pltpu.make_async_remote_copy(
        src_ref=source,
        dst_ref=target,
        send_sem=send,
        recv_sem=recv,
        device_id=device,
        device_id_type=MESH,
    )


def start_kernel(
    packed, line, in_shard, out_shard, table, head, batches, groups, replicas
):
    vocab, width = table.shape
    seq = packed.shape[1]
    own = batches * seq
    chips = groups // 2
    amount = groups * replicas
    shards_in = (in_shard, out_shard)
    split = all(shard.shape[0] % (16 * replicas) == 0 for shard in shards_in)
    pieces = replicas if split else 1
    unroll = 8

    def kernel(
        packed_ref,
        line_ref,
        in_ref,
        out_ref,
        table_ref,
        head_ref,
        every_ref,
        lines_ref,
        in_full,
        out_full,
        resid_ref,
        aims_ref,
        in_low,
        out_low,
        wide,
        again,
        looked,
        to_core,
        from_core,
        to_lane,
        from_lane,
        ids,
        table_sem,
        ids_sem,
        local_sem,
        meta_send,
        meta_recv,
        line_send,
        line_recv,
        lane_send,
        lane_recv,
        plane_send,
        plane_recv,
        core_send,
        core_recv,
        part_send,
        part_recv,
        sum_send,
        sum_recv,
    ):
        place = Place(groups, replicas)
        member = place.member
        core = place.core
        replica = place.replica
        me = replica * groups + member
        fulls = (in_full, out_full)
        lows = (in_low, out_low)

        def device(index):
            return place.at(index // groups, lax.rem(index, groups))

        def chip_at(j):
            return lax.rem(place.chip + j, chips)

        def chip_before(j):
            return lax.rem(place.chip + chips - j, chips)

        def replica_before(k):
            return lax.rem(replica + replicas - k, replicas)

        def lane_device(j):
            return place.at(replica, chip_at(j) * 2 + core)

        def plane_device(k):
            return place.at(lax.rem(replica + k, replicas), member)

        def meta_copy(k):
            return remote(
                packed_ref,
                every_ref.at[me],
                meta_send.at[k],
                meta_recv.at[k],
                device(lax.rem(me + k, amount)),
            )

        def line_copy(k):
            return remote(
                line_ref,
                lines_ref.at[member],
                line_send.at[k],
                line_recv.at[k],
                place.at(replica, lax.rem(member + k, groups)),
            )

        def piece(w, slot, from_replica):
            full = fulls[w]
            if not split:
                return full.at[slot]
            rows = full.shape[1] // pieces
            return full.at[slot, pl.ds(pl.multiple_of(from_replica * rows, 16), rows), :]

        def own_piece(w):
            low = lows[w]
            if not split:
                return low
            rows = low.shape[0] // pieces
            return low.at[pl.ds(pl.multiple_of(replica * rows, 16), rows), :]

        def lane_copy(w, j):
            return remote(
                own_piece(w),
                piece(w, member, replica),
                lane_send.at[w, j],
                lane_recv.at[w, j],
                lane_device(j),
            )

        def lane_wait(w, j):
            there = piece(w, chip_before(j) * 2 + core, replica)
            remote(
                there, there, lane_send.at[w, j], lane_recv.at[w, j], lane_device(j)
            ).wait_recv()

        def plane_copy(w, k, j):
            there = piece(w, chip_before(j) * 2 + core, replica)
            return remote(
                there, there, plane_send.at[w, k, j], plane_recv.at[w, k, j], plane_device(k)
            )

        def plane_wait(w, k, j):
            there = piece(w, chip_before(j) * 2 + core, replica_before(k))
            remote(
                there, there, plane_send.at[w, k, j], plane_recv.at[w, k, j], plane_device(k)
            ).wait_recv()

        def core_copy(w, j):
            here = fulls[w].at[chip_before(j) * 2 + core]
            return remote(here, here, core_send.at[w, j], core_recv.at[w, j], place.sibling())

        def own_core_copy(w):
            return remote(
                lows[w],
                fulls[w].at[member],
                core_send.at[w, 0],
                core_recv.at[w, 0],
                place.sibling(),
            )

        def core_wait(w, j):
            there = fulls[w].at[chip_before(j) * 2 + 1 - core]
            remote(
                there, there, core_send.at[w, j], core_recv.at[w, j], place.sibling()
            ).wait_recv()

        def part_copy(j):
            return remote(
                to_core.at[j], from_core.at[j], part_send.at[j], part_recv.at[j], place.sibling()
            )

        def sum_copy(j):
            return remote(
                to_lane.at[j], from_lane.at[j], sum_send.at[j], sum_recv.at[j], lane_device(j)
            )

        fetch = pltpu.make_async_copy(
            table_ref, wide.at[pl.ds(0, vocab), :], table_sem.at[0]
        )
        refetch = pltpu.make_async_copy(
            head_ref, again.at[pl.ds(0, vocab), :], table_sem.at[1]
        )
        fetch.start()
        refetch.start()
        barrier = pltpu.get_barrier_semaphore()

        def greet(k, carry):
            pl.semaphore_signal(
                barrier, inc=1, device_id=device(lax.rem(me + k, amount)), device_id_type=MESH
            )
            return carry

        lax.fori_loop(1, amount, greet, 0)
        for held in (wide, again):
            held[vocab : vocab + 8, :] = jnp.zeros((8, width), FLOAT)
        in_low[...] = in_ref[...].astype(NARROW)
        out_low[...] = out_ref[...].astype(NARROW)
        every_ref[me] = packed_ref[...]
        lines_ref[member] = line_ref[...]
        pl.semaphore_wait(barrier, amount - 1)

        def tell(k, carry):
            meta_copy(k).start()
            return carry

        lax.fori_loop(1, amount, tell, 0)
        for k in range(1, groups):
            line_copy(k).start()
        for w in range(2):
            for j in range(1, chips):
                lane_copy(w, j).start()
            own_core_copy(w).start()
        kept = [
            pltpu.make_async_copy(lows[w], fulls[w].at[member], local_sem.at[w])
            for w in range(2)
        ]
        for copy in kept:
            copy.start()

        def hear(k, carry):
            there = every_ref.at[lax.rem(me + amount - k, amount)]
            remote(there, there, meta_send.at[k], meta_recv.at[k], device(me)).wait_recv()
            return carry

        lax.fori_loop(1, amount, hear, 0)
        load = pltpu.make_async_copy(
            every_ref.at[pl.ds(replica * groups, groups)], ids, ids_sem
        )
        load.start()
        load.wait()
        fetch.wait()
        start = member * vocab

        def look(slot, ahead, source):
            for b in range(batches):

                def lap(i, carry):
                    first = pl.multiple_of(i * unroll, unroll)
                    for u in range(unroll):
                        if ahead and u + ahead >= unroll:
                            spot = first + u + ahead
                            token = ids[slot, b, jnp.minimum(spot, seq - 1)]
                            token = jnp.where(spot < seq, token, 0)
                        else:
                            token = ids[slot, b, first + u + ahead]
                        row = token - start
                        row = jnp.where((row >= 0) & (row < vocab), row, vocab)
                        looked[pl.ds(b * seq + first + u, 1), :] = source[pl.ds(row, 1), :]
                    return carry

                lax.fori_loop(0, seq // unroll, lap, 0)
            return looked[...].astype(NARROW)

        def lap(step, carry):
            j = lax.rem(step + 1, chips)
            there = chip_at(j) * 2

            to_core[j] = look(there + 1 - core, 0, wide)
            part_copy(j).start()
            mine = look(there + core, 0, wide).astype(FLOAT)
            part_copy(j).wait_recv()
            mine = mine + from_core[j].astype(FLOAT)

            @pl.when(j > 0)
            def _():
                to_lane[j] = mine.astype(NARROW)
                sum_copy(j).start()

            @pl.when(j == 0)
            def _():
                resid_ref[...] = mine

            return carry

        lax.fori_loop(0, chips, lap, 0)
        refetch.wait()

        def aim(slot, carry):
            @pl.when(slot == 0)
            def _():
                for w in range(2):
                    for c in range(1, chips):
                        lane_wait(w, c)
                        if split:
                            for k in range(1, replicas):
                                plane_copy(w, k, c).start()

            aims_ref[slot] = look(slot, 1, again)
            return carry

        lax.fori_loop(0, groups, aim, 0)
        for j in range(1, chips):
            sum_copy(j).wait_recv()
            resid_ref[...] += from_lane[j].astype(FLOAT)
        for w in range(2):
            for j in range(1, chips):
                if split:
                    for k in range(1, replicas):
                        plane_wait(w, k, j)
                core_copy(w, j).start()
        for w in range(2):
            kept[w].wait()
            for j in range(chips):
                core_wait(w, j)
                if j == 0:
                    own_core_copy(w).wait_send()
                else:
                    core_copy(w, j).wait_send()
                    lane_copy(w, j).wait_send()
                if split and j > 0:
                    for k in range(1, replicas):
                        plane_copy(w, k, j).wait_send()
        for k in range(1, groups):
            there = lines_ref.at[lax.rem(member + groups - k, groups)]
            remote(
                there, there, line_send.at[k], line_recv.at[k], place.at(replica, member)
            ).wait_recv()
            line_copy(k).wait_send()
        for j in range(chips):
            part_copy(j).wait_send()
            if j > 0:
                sum_copy(j).wait_send()

        def told(k, carry):
            meta_copy(k).wait_send()
            return carry

        lax.fori_loop(1, amount, told, 0)

    whole = pl.BlockSpec(memory_space=pltpu.VMEM)
    anywhere = pl.BlockSpec(memory_space=pl.ANY)
    dma = pltpu.SemaphoreType.DMA
    vmem = pltpu.VMEM
    every, lines, in_full, out_full, resid, aims = pl.pallas_call(
        kernel,
        in_specs=[whole, whole, whole, whole, anywhere, anywhere],
        out_specs=[whole, whole, anywhere, anywhere, whole, whole],
        out_shape=[
            jax.ShapeDtypeStruct((amount,) + packed.shape, jnp.int32),
            jax.ShapeDtypeStruct((groups,) + line.shape, FLOAT),
            jax.ShapeDtypeStruct((groups,) + in_shard.shape, NARROW),
            jax.ShapeDtypeStruct((groups,) + out_shard.shape, NARROW),
            jax.ShapeDtypeStruct((own, width), FLOAT),
            jax.ShapeDtypeStruct((groups, own, width), NARROW),
        ],
        scratch_shapes=[
            vmem(in_shard.shape, NARROW),
            vmem(out_shard.shape, NARROW),
            vmem((vocab + 8, width), FLOAT),
            vmem((vocab + 8, width), FLOAT),
            vmem((own, width), FLOAT),
            vmem((chips, own, width), NARROW),
            vmem((chips, own, width), NARROW),
            vmem((chips, own, width), NARROW),
            vmem((chips, own, width), NARROW),
            pltpu.SMEM((groups,) + packed.shape, jnp.int32),
            dma((2,)),
            dma,
            dma((2,)),
            dma((amount,)),
            dma((amount,)),
            dma((groups,)),
            dma((groups,)),
            dma((2, chips)),
            dma((2, chips)),
            dma((2, replicas, chips)),
            dma((2, replicas, chips)),
            dma((2, chips)),
            dma((2, chips)),
            dma((chips,)),
            dma((chips,)),
            dma((chips,)),
            dma((chips,)),
        ],
        compiler_params=pltpu.CompilerParams(
            vmem_limit_bytes=VMEM_LIMIT, collective_id=4, has_side_effects=True
        ),
        cost_estimate=pl.CostEstimate(
            flops=0, bytes_accessed=vocab * width * 4, transcendentals=0
        ),
    )(packed, line, in_shard, out_shard, table, head)
    return (
        every,
        lines,
        in_full.reshape(-1, in_shard.shape[1]),
        out_full.reshape(-1, out_shard.shape[1]),
        resid,
        aims,
    )


def head_kernel(table, own_hidden, aims, target, weight, groups, replicas):
    vocab, width = table.shape
    own = own_hidden.shape[0]
    block = block_rows(vocab, 1100)
    blocks = vocab // block
    chips = groups // 2
    lines = -(-blocks // 8) * 8

    def kernel(
        table_ref,
        own_ref,
        aims_ref,
        target_ref,
        weight_ref,
        grad_ref,
        logsum_ref,
        loss_ref,
        all_ref,
        wide,
        low,
        hid,
        exps,
        tops,
        totals,
        shares,
        to_core,
        from_core,
        to_lane,
        from_lane,
        aim_core,
        aim_lane,
        aim_from,
        table_sem,
        local_sem,
        lane_send,
        lane_recv,
        core_send,
        core_recv,
        plane_send,
        plane_recv,
        pass_send,
        pass_recv,
        stat_send,
        stat_recv,
        line_send,
        line_recv,
        part_send,
        part_recv,
        sum_send,
        sum_recv,
        aim_half_send,
        aim_half_recv,
        aim_send,
        aim_recv,
    ):
        place = Place(groups, replicas)
        me = place.member
        core = place.core

        def table_copy(b):
            return pltpu.make_async_copy(
                table_ref.at[pl.ds(b * block, block), :], wide.at[b % 2], table_sem.at[b % 2]
            )

        def chip_at(j):
            return lax.rem(place.chip + j, chips)

        def chip_before(j):
            return lax.rem(place.chip + chips - j, chips)

        def lane_device(j):
            return place.at(place.replica, chip_at(j) * 2 + core)

        def plane_device(k):
            return place.at(lax.rem(place.replica + k, replicas), me)

        def replica_before(k):
            return lax.rem(place.replica + replicas - k, replicas)

        def lane_copy(j):
            return remote(own_ref, hid.at[me], lane_send.at[j], lane_recv.at[j], lane_device(j))

        def lane_slot(j):
            return chip_before(j) * 2 + core

        def lane_wait(j):
            there = hid.at[lane_slot(j)]
            remote(there, there, lane_send.at[j], lane_recv.at[j], lane_device(j)).wait_recv()

        def core_copy(j):
            here = hid.at[lane_slot(j)]
            return remote(here, here, core_send.at[j], core_recv.at[j], place.sibling())

        def core_wait(j):
            there = hid.at[chip_before(j) * 2 + 1 - core]
            remote(there, there, core_send.at[j], core_recv.at[j], place.sibling()).wait_recv()

        def plane_copy(k, j):
            slot = lane_slot(j)
            return remote(
                hid.at[slot],
                all_ref.at[place.replica * groups + slot],
                plane_send.at[k, j],
                plane_recv.at[k, j],
                plane_device(k),
            )

        def plane_wait(k, j):
            there = all_ref.at[replica_before(k) * groups + lane_slot(j)]
            remote(
                there, there, plane_send.at[k, j], plane_recv.at[k, j], plane_device(k)
            ).wait_recv()

        def pass_copy(k, j):
            here = all_ref.at[replica_before(k) * groups + lane_slot(j)]
            return remote(
                here, here, pass_send.at[k, j], pass_recv.at[k, j], place.sibling()
            )

        def pass_wait(k, j):
            there = all_ref.at[
                replica_before(k) * groups + chip_before(j) * 2 + 1 - core
            ]
            remote(
                there, there, pass_send.at[k, j], pass_recv.at[k, j], place.sibling()
            ).wait_recv()

        def member_at(k):
            return lax.rem(me + k, groups)

        def stat_copy(k):
            return remote(
                shares.at[me],
                shares.at[me],
                stat_send.at[k],
                stat_recv.at[k],
                place.at(place.replica, member_at(k)),
            )

        def stat_wait(k):
            there = shares.at[lax.rem(me + groups - k, groups)]
            remote(
                there, there, stat_send.at[k], stat_recv.at[k], place.at(place.replica, me)
            ).wait_recv()

        def line_copy(k):
            here = logsum_ref.at[place.replica]
            return remote(here, here, line_send.at[k], line_recv.at[k], plane_device(k))

        def line_wait(k):
            there = logsum_ref.at[replica_before(k)]
            remote(there, there, line_send.at[k], line_recv.at[k], plane_device(k)).wait_recv()

        def part_copy(j):
            return remote(
                to_core.at[j], from_core.at[j], part_send.at[j], part_recv.at[j], place.sibling()
            )

        def sum_copy(j):
            return remote(
                to_lane.at[j], from_lane.at[j], sum_send.at[j], sum_recv.at[j], lane_device(j)
            )

        def aim_half(c):
            return remote(
                aims_ref.at[c * 2 + 1 - core],
                aim_core.at[c],
                aim_half_send.at[c],
                aim_half_recv.at[c],
                place.sibling(),
            )

        def aim_copy(j):
            return remote(
                aim_lane.at[j], aim_from.at[j], aim_send.at[j], aim_recv.at[j], lane_device(j)
            )

        table_copy(0).start()
        if blocks > 1:
            table_copy(1).start()
        meet(
            [place.at(place.replica, member_at(k)) for k in range(1, groups)] + place.planes()
        )
        own_core = remote(own_ref, hid.at[me], core_send.at[0], core_recv.at[0], place.sibling())
        own_core.start()
        for j in range(1, chips):
            lane_copy(j).start()
        hid[me] = own_ref[...]
        for k in range(1, replicas):
            plane_copy(k, 0).start()
        for c in range(chips):
            aim_half(c).start()
        for b in range(blocks):
            table_copy(b).wait()
            low[b] = wide[b % 2].astype(NARROW)
            if b + 2 < blocks:
                table_copy(b + 2).start()

        spots = lax.broadcasted_iota(jnp.int32, (block, own), 0)

        def forward(step, carry):
            j = step // 2
            other = lax.rem(step, 2)

            @pl.when(step == 1)
            def _():
                there = hid.at[place.sibling_member]
                remote(
                    there, there, core_send.at[0], core_recv.at[0], place.sibling()
                ).wait_recv()

            @pl.when((step > 1) & (other == 0))
            def _():
                lane_wait(j)
                core_copy(j).start()

                def spread(k, carry):
                    plane_copy(k, j).start()
                    return carry

                lax.fori_loop(1, replicas, spread, 0)

            @pl.when((step > 1) & (other == 1))
            def _():
                core_wait(j)

            @pl.when(step == groups // 2 + 1)
            def _():
                for c in range(chips):
                    aim_half(c).wait_recv()
                for i in range(chips):
                    chip = chip_at(i)
                    aim_lane[i] = (
                        aims_ref[chip * 2 + core].astype(FLOAT) + aim_core[chip].astype(FLOAT)
                    ).astype(NARROW)
                for i in range(1, chips):
                    aim_copy(i).start()

            member = chip_before(j) * 2 + lax.rem(core + other, 2)
            here = hid[member]
            for b in range(blocks):
                logits = lax.dot_general(
                    low[b], here, LAST_CONTRACT, preferred_element_type=FLOAT
                )
                top = jnp.max(logits, axis=0, keepdims=True)
                values = jnp.exp(logits - top)
                tops[member, b : b + 1, :] = top
                totals[member, b : b + 1, :] = jnp.sum(values, axis=0, keepdims=True)
                exps[b, member] = values.astype(NARROW)
            block_tops = tops[member, :blocks, :]
            top = jnp.max(block_tops, axis=0, keepdims=True)
            total = jnp.sum(
                totals[member, :blocks, :] * jnp.exp(block_tops - top), axis=0, keepdims=True
            )
            shares[me, pl.ds(member, 1), :] = top + jnp.log(total)
            return carry

        lax.fori_loop(0, groups, forward, 0)
        local = pltpu.make_async_copy(
            hid, all_ref.at[pl.ds(place.replica * groups, groups)], local_sem
        )
        local.start()
        for k in range(1, groups):
            stat_copy(k).start()
        for k in range(1, groups):
            stat_wait(k)
        every = shares[...]
        top = jnp.max(every, axis=0)
        logsum_ref[place.replica] = top + jnp.log(jnp.sum(jnp.exp(every - top[None]), axis=0))
        for k in range(1, replicas):
            line_copy(k).start()

        def member_back(member):
            wanted = target_ref[member]
            weights = weight_ref[member]
            logsum = logsum_ref[place.replica, pl.ds(member, 1), :]
            total = jnp.zeros((own, width), FLOAT)
            for b in range(blocks):
                scale = weights * jnp.exp(tops[member, b : b + 1, :] - logsum)
                grads = exps[b, member].astype(FLOAT) * scale
                grads = jnp.where(spots == wanted - b * block, 0.0, grads)
                total = total + lax.dot_general(
                    grads.astype(NARROW), low[b], ROWS_CONTRACT, preferred_element_type=FLOAT
                )
            return total

        def backward(step, carry):
            j = lax.rem(step + 1, chips)

            @pl.when(step == chips - 1)
            def _():
                for k in range(1, replicas):
                    for c in range(chips):
                        plane_wait(k, c)
                for k in range(1, replicas):
                    for c in range(chips):
                        pass_copy(k, c).start()

            there = chip_at(j) * 2
            to_core[j] = member_back(there + 1 - core).astype(NARROW)
            part_copy(j).start()
            mine = member_back(there + core)
            part_copy(j).wait_recv()
            mine = mine + from_core[j].astype(FLOAT)

            @pl.when(j > 0)
            def _():
                to_lane[j] = mine.astype(NARROW)
                sum_copy(j).start()

            @pl.when(j == 0)
            def _():
                grad_ref[...] = mine

            return carry

        lax.fori_loop(0, chips, backward, 0)
        held = lax.broadcasted_iota(jnp.int32, (groups, own), 0) == me
        amounts = jnp.concatenate([weight_ref[m] for m in range(groups)], axis=0)

        def own_column(values):
            return jnp.sum(jnp.where(held, values, 0.0).T, axis=1, keepdims=True)

        amount = own_column(amounts)
        logsum = own_column(logsum_ref[place.replica])
        aimed = aim_lane[0].astype(FLOAT)
        for j in range(1, chips):
            aim_copy(j).wait_recv()
            aimed = aimed + aim_from[j].astype(FLOAT)
        hit = jnp.sum(own_ref[...].astype(FLOAT) * aimed, axis=1, keepdims=True)
        loss_ref[...] = amount * (logsum - hit)
        part = (amount * (jnp.exp(hit - logsum) - 1.0)).astype(NARROW).astype(FLOAT)
        total = grad_ref[...] + part * aimed
        for j in range(1, chips):
            sum_copy(j).wait_recv()
            total = total + from_lane[j].astype(FLOAT)
        grad_ref[...] = total
        local.wait()
        own_core.wait_send()
        for k in range(1, groups):
            stat_copy(k).wait_send()
        for k in range(1, replicas):
            line_wait(k)
            line_copy(k).wait_send()
            for j in range(chips):
                pass_wait(k, j)
                plane_copy(k, j).wait_send()
                pass_copy(k, j).wait_send()
        for j in range(chips):
            part_copy(j).wait_send()
            aim_half(j).wait_send()
            if j > 0:
                lane_copy(j).wait_send()
                core_copy(j).wait_send()
                sum_copy(j).wait_send()
                aim_copy(j).wait_send()

    whole = pl.BlockSpec(memory_space=pltpu.VMEM)
    anywhere = pl.BlockSpec(memory_space=pl.ANY)
    dma = pltpu.SemaphoreType.DMA
    vmem = pltpu.VMEM
    grad, logsum, loss, everyone = pl.pallas_call(
        kernel,
        in_specs=[anywhere, whole, whole, whole, whole],
        out_specs=[whole, whole, whole, anywhere],
        out_shape=[
            jax.ShapeDtypeStruct((own, width), FLOAT),
            jax.ShapeDtypeStruct((replicas, groups, own), FLOAT),
            jax.ShapeDtypeStruct((own, 1), FLOAT),
            jax.ShapeDtypeStruct((replicas * groups, own, width), NARROW),
        ],
        scratch_shapes=[
            vmem((2, block, width), FLOAT),
            vmem((blocks, block, width), NARROW),
            vmem((groups, own, width), NARROW),
            vmem((blocks, groups, block, own), NARROW),
            vmem((groups, lines, own), FLOAT),
            vmem((groups, lines, own), FLOAT),
            vmem((groups, groups, own), FLOAT),
            vmem((chips, own, width), NARROW),
            vmem((chips, own, width), NARROW),
            vmem((chips, own, width), NARROW),
            vmem((chips, own, width), NARROW),
            vmem((chips, own, width), NARROW),
            vmem((chips, own, width), NARROW),
            vmem((chips, own, width), NARROW),
            dma((2,)),
            dma,
            dma((chips,)),
            dma((chips,)),
            dma((chips,)),
            dma((chips,)),
            dma((replicas, chips)),
            dma((replicas, chips)),
            dma((replicas, chips)),
            dma((replicas, chips)),
            dma((groups,)),
            dma((groups,)),
            dma((replicas,)),
            dma((replicas,)),
            dma((chips,)),
            dma((chips,)),
            dma((chips,)),
            dma((chips,)),
            dma((chips,)),
            dma((chips,)),
            dma((chips,)),
            dma((chips,)),
        ],
        compiler_params=pltpu.CompilerParams(
            vmem_limit_bytes=VMEM_LIMIT + 2**21, collective_id=3, has_side_effects=True
        ),
        cost_estimate=pl.CostEstimate(
            flops=4 * vocab * groups * own * width,
            bytes_accessed=vocab * width * 4,
            transcendentals=vocab * groups * own,
        ),
    )(
        table,
        own_hidden,
        aims,
        target.reshape(groups, 1, own),
        weight.reshape(groups, 1, own),
    )
    return grad, logsum.reshape(-1), jnp.sum(loss), everyone.reshape(-1, width)


def head_table_grad(
    table, hidden, logsum, weights, target, token_grad, slices, owner_grads, cut, groups, replicas
):
    vocab, width = table.shape
    amount = groups * replicas
    rows = hidden.shape[0]
    own = token_grad.shape[0]
    tile = math.gcd(rows, 2048)
    block = block_rows(vocab, 1100)
    tiles = rows // tile
    steps = vocab // block
    chips = groups // 2
    last = steps - 1
    shard = owner_grads.shape[1]
    regions = ((0, cut), (cut, shard - cut))
    firsts, seconds = (replicas, chips), (chips, replicas)
    reduce = all(count % (8 * replicas) == 0 for _, count in regions)
    laps = steps * tiles

    def when(part):
        return min(int(laps * part), laps - 1)

    def kernel(
        table_ref,
        hidden_ref,
        logsum_ref,
        weight_ref,
        target_ref,
        own_ref,
        slices_ref,
        owner_ref,
        grad_ref,
        square_ref,
        all_ref,
        summed_ref,
        owned_out,
        gathered,
        owned_ref,
        from_core,
        acc_in,
        acc_out,
        one_in,
        one_out,
        two_in,
        two_out,
        piece_sem,
        half_send,
        half_recv,
        one_send,
        one_recv,
        two_send,
        two_recv,
        end_send,
        end_recv,
        local_sem,
        slice_send,
        slice_recv,
        lane_send,
        lane_recv,
        plane_send,
        plane_recv,
        core_send,
        core_recv,
    ):
        step = pl.program_id(0)
        place = Place(groups, replicas)
        me = place.replica * groups + place.member

        def slot(replica, member):
            return all_ref.at[replica * groups + member]

        def lane_copy(k):
            here = all_ref.at[me]
            return remote(own_ref, here, lane_send.at[k], lane_recv.at[k], place.lane(k))

        def lane_wait(k):
            back = lax.rem(place.chip + chips - k, chips) * 2 + place.core
            there = slot(place.replica, back)
            remote(there, there, lane_send.at[k], lane_recv.at[k], place.lane(k)).wait_recv()

        def plane_copy(k, c):
            here = slot(place.replica, c * 2 + place.core)
            return remote(here, here, plane_send.at[k, c], plane_recv.at[k, c], place.plane(k))

        def plane_wait(k, c):
            back = lax.rem(place.replica + replicas - k, replicas)
            there = slot(back, c * 2 + place.core)
            remote(
                there, there, plane_send.at[k, c], plane_recv.at[k, c], place.plane(k)
            ).wait_recv()

        def core_copy(r, c):
            here = slot(r, c * 2 + place.core)
            return remote(here, here, core_send.at[r, c], core_recv.at[r, c], place.sibling())

        def core_wait(r, c):
            there = slot(r, c * 2 + 1 - place.core)
            remote(
                there, there, core_send.at[r, c], core_recv.at[r, c], place.sibling()
            ).wait_recv()

        def device(index):
            return place.at(index // groups, lax.rem(index, groups))

        def slice_copy(k):
            there = lax.rem(me + k, amount)
            return remote(
                slices_ref.at[lax.rem(there, groups)],
                gathered.at[me],
                slice_send.at[k],
                slice_recv.at[k],
                device(there),
            )

        local = pltpu.make_async_copy(own_ref, all_ref.at[me], local_sem)
        accs, ones, twos = (acc_in, acc_out), (one_in, one_out), (two_in, two_out)

        def chip_at(j):
            return lax.rem(place.chip + j, chips)

        def pieces(g):
            first, rows = regions[g]
            size = rows // replicas
            for k in range(firsts[g]):
                for i in range(seconds[g]):
                    if g == 0:
                        chip, replica = i, place.plane_replica(k)
                    else:
                        chip, replica = chip_at(k), i
                    yield k, i, chip, pl.multiple_of(first + replica * size, 8), size

        def piece_copy(g, k, i, chip, row, size):
            return pltpu.make_async_copy(
                owner_ref.at[chip * 2 + place.core, pl.ds(row, size), :],
                accs[g].at[k, i],
                piece_sem.at[g, k, i],
            )

        def half_copy(c):
            return remote(
                owner_ref.at[c * 2 + 1 - place.core],
                from_core.at[c],
                half_send.at[c],
                half_recv.at[c],
                place.sibling(),
            )

        def partner(over_dp, k):
            if over_dp:
                return place.plane(k)
            return place.lane(k)

        def one_copy(g, k):
            return remote(
                accs[g].at[k],
                ones[g].at[k],
                one_send.at[g, k],
                one_recv.at[g, k],
                partner(g == 0, k),
            )

        def mine(g):
            return place.chip if g == 0 else place.replica

        def two_copy(g, k):
            return remote(
                accs[g].at[0, lax.rem(mine(g) + k, seconds[g])],
                twos[g].at[k],
                two_send.at[g, k],
                two_recv.at[g, k],
                partner(g == 1, k),
            )

        def end_copy(g, k, there):
            first, rows = regions[g]
            size = rows // replicas
            span = owned_ref.at[pl.ds(pl.multiple_of(first + there * size, 8), size), :]
            return remote(span, span, end_send.at[g, k], end_recv.at[g, k], place.plane(k))

        def begin_sums():
            for c in range(chips):
                half_copy(c).start()
            for g in range(2):
                for item in pieces(g):
                    piece_copy(g, *item).start()

        def begin_one():
            for c in range(chips):
                half_copy(c).wait_recv()
            for g in range(2):
                for item in pieces(g):
                    piece_copy(g, *item).wait()
                    k, i, chip, row, size = item
                    accs[g][k, i] += from_core[chip, pl.ds(row, size), :]
                for k in range(1, firsts[g]):
                    one_copy(g, k).start()

        def begin_two(g):
            for k in range(1, firsts[g]):
                one_copy(g, k).wait_recv()
            for i in range(seconds[g]):
                total = accs[g][0, i]
                for k in range(1, firsts[g]):
                    total = total + ones[g][k, i]
                accs[g][0, i] = total
            for k in range(1, seconds[g]):
                two_copy(g, k).start()

        def begin_end(g):
            first, rows = regions[g]
            size = rows // replicas
            total = accs[g][0, mine(g)]
            for k in range(1, seconds[g]):
                two_copy(g, k).wait_recv()
                total = total + twos[g][k]
            row = pl.multiple_of(first + place.replica * size, 8)
            owned_ref[pl.ds(row, size), :] = total
            for k in range(1, replicas):
                end_copy(g, k, place.replica).start()

        def end_sums():
            for g in range(2):
                for k in range(1, replicas):
                    end_copy(g, k, lax.rem(place.replica + replicas - k, replicas)).wait_recv()
                    end_copy(g, k, place.replica).wait_send()
                for k in range(1, firsts[g]):
                    one_copy(g, k).wait_send()
                for k in range(1, seconds[g]):
                    two_copy(g, k).wait_send()
            for c in range(chips):
                half_copy(c).wait_send()

        def begin_all():
            barrier = pltpu.get_barrier_semaphore()

            def greet(k, carry):
                pl.semaphore_signal(
                    barrier,
                    inc=1,
                    device_id=device(lax.rem(me + k, amount)),
                    device_id_type=MESH,
                )
                return carry

            lax.fori_loop(1, amount, greet, 0)
            pl.semaphore_wait(barrier, amount - 1)
            local.start()
            if reduce:
                begin_sums()
            for k in range(1, chips):
                lane_copy(k).start()

            def give(k, carry):
                slice_copy(k).start()
                return carry

            lax.fori_loop(1, amount, give, 0)
            gathered[me] = slices_ref[place.member]

        def token_lane():
            local.wait()
            for k in range(1, chips):
                lane_wait(k)
            for c in range(chips):
                core_copy(place.replica, c).start()

        def token_plane():
            for c in range(chips):
                for k in range(1, replicas):
                    plane_copy(k, c).start()

        def token_core():
            for k in range(1, replicas):
                for c in range(chips):
                    plane_wait(k, c)
            for k in range(1, replicas):
                for c in range(chips):
                    core_copy(place.plane_replica(k), c).start()

        plan = [(0.0, begin_all)]
        if reduce:
            plan = plan + [
                (0.09, begin_one),
                (0.25, token_lane),
                (0.4, lambda: begin_two(0)),
                (0.4, token_plane),
                (0.65, lambda: begin_two(1)),
                (0.75, lambda: begin_end(0)),
                (0.8, lambda: begin_end(1)),
                (0.8, token_core),
            ]
        else:
            plan = plan + [(0.17, token_lane), (0.17, token_plane), (0.5, token_core)]

        start = step * block
        part = table_ref[...].astype(NARROW)
        places = lax.broadcasted_iota(jnp.int32, (block, tile), 0)

        def lap(k, carry):
            for part_of, act in plan:
                pl.when(step * tiles + k == when(part_of))(act)
            here = hidden_ref[pl.ds(pl.multiple_of(k * tile, tile), tile), :]
            logits = lax.dot_general(part, here, LAST_CONTRACT, preferred_element_type=FLOAT)
            probs = jnp.exp(logits - logsum_ref[k])
            grads = jnp.where(
                places == target_ref[k] - start, probs - weight_ref[k], probs
            ).astype(NARROW)
            piece = jnp.dot(grads, here, preferred_element_type=FLOAT)

            @pl.when(k == 0)
            def _():
                grad_ref[...] = piece

            @pl.when(k > 0)
            def _():
                grad_ref[...] += piece

            return carry

        lax.fori_loop(0, tiles, lap, 0)
        squares = jnp.sum(jnp.square(grad_ref[...]), axis=0, keepdims=True)

        @pl.when(step == 0)
        def _():
            square_ref[...] = squares

        @pl.when(step > 0)
        def _():
            square_ref[...] += squares

        @pl.when(step == last)
        def _():
            def take(k, carry):
                there = gathered.at[lax.rem(me + amount - k, amount)]
                remote(there, there, slice_send.at[k], slice_recv.at[k], device(me)).wait_recv()
                slice_copy(k).wait_send()
                return carry

            lax.fori_loop(1, amount, take, 0)
            if reduce:
                end_sums()
                owned_out[...] = owned_ref[...]
            summed_ref[...] = jnp.sum(gathered[...], axis=0)
            for r in range(replicas):
                for c in range(chips):
                    core_wait(r, c)
            for k in range(1, chips):
                lane_copy(k).wait_send()
            for c in range(chips):
                for k in range(1, replicas):
                    plane_copy(k, c).wait_send()
                for r in range(replicas):
                    core_copy(r, c).wait_send()

    whole = pl.BlockSpec(memory_space=pltpu.VMEM)
    anywhere = pl.BlockSpec(memory_space=pl.ANY)
    shape = (tiles, 1, tile)
    dma = pltpu.SemaphoreType.DMA
    return pl.pallas_call(
        kernel,
        grid=(steps,),
        in_specs=[pl.BlockSpec((block, width), lambda i: (i, 0))]
        + [whole] * 4
        + [anywhere, whole, anywhere],
        out_specs=[
            pl.BlockSpec((block, width), lambda i: (i, 0)),
            pl.BlockSpec((1, width), lambda i: (0, 0)),
            anywhere,
            whole,
            whole,
        ],
        out_shape=[
            jax.ShapeDtypeStruct((vocab, width), FLOAT),
            jax.ShapeDtypeStruct((1, width), FLOAT),
            jax.ShapeDtypeStruct((groups * replicas, own, width), NARROW),
            jax.ShapeDtypeStruct(slices.shape[1:], FLOAT),
            jax.ShapeDtypeStruct(owner_grads.shape[1:] if reduce else (8, 128), FLOAT),
        ],
        scratch_shapes=[
            pltpu.VMEM((amount,) + slices.shape[1:], FLOAT),
            pltpu.VMEM(owner_grads.shape[1:] if reduce else (8, 128), FLOAT),
            pltpu.VMEM((chips,) + owner_grads.shape[1:] if reduce else (8, 128), FLOAT),
        ]
        + [
            pltpu.VMEM(
                (counts[g], seconds[g], regions[g][1] // replicas, width)[skip:]
                if reduce
                else (8, 128),
                FLOAT,
            )
            for counts, skip in ((firsts, 0), (firsts, 0), (seconds, 1))
            for g in range(2)
        ]
        + [
            dma((2, max(firsts), max(seconds))),
            dma((chips,)),
            dma((chips,)),
            dma((2, max(firsts))),
            dma((2, max(firsts))),
            dma((2, max(seconds))),
            dma((2, max(seconds))),
            dma((2, replicas)),
            dma((2, replicas)),
            dma,
            dma((amount,)),
            dma((amount,)),
            dma((chips,)),
            dma((chips,)),
            dma((replicas, chips)),
            dma((replicas, chips)),
            dma((replicas, chips)),
            dma((replicas, chips)),
        ],
        compiler_params=pltpu.CompilerParams(
            vmem_limit_bytes=VMEM_LIMIT, collective_id=1, has_side_effects=True
        ),
        cost_estimate=pl.CostEstimate(
            flops=4 * vocab * rows * width,
            bytes_accessed=vocab * width * 8 + rows * width * 4,
            transcendentals=vocab * rows,
        ),
    )(
        table,
        hidden,
        logsum.reshape(shape),
        weights.reshape(shape),
        target.reshape(shape),
        token_grad,
        slices,
        owner_grads,
    )


def exchange_scalars(line, groups, replicas):
    amount = groups * replicas

    def kernel(own_ref, all_ref, local_sem, send_sem, recv_sem):
        place = Place(groups, replicas)
        me = place.replica * groups + place.member

        def device(index):
            return place.at(index // groups, lax.rem(index, groups))

        barrier = pltpu.get_barrier_semaphore()

        def greet(k, carry):
            pl.semaphore_signal(
                barrier, inc=1, device_id=device(lax.rem(me + k, amount)), device_id_type=MESH
            )
            return carry

        def copy(k):
            return remote(
                own_ref,
                all_ref.at[me],
                send_sem.at[k],
                recv_sem.at[k],
                device(lax.rem(me + k, amount)),
            )

        def begin(k, carry):
            copy(k).start()
            return carry

        def finish(k, carry):
            there = all_ref.at[lax.rem(me + amount - k, amount)]
            remote(there, there, send_sem.at[k], recv_sem.at[k], device(me)).wait_recv()
            copy(k).wait_send()
            return carry

        lax.fori_loop(1, amount, greet, 0)
        local = pltpu.make_async_copy(own_ref, all_ref.at[me], local_sem)
        local.start()
        pl.semaphore_wait(barrier, amount - 1)
        lax.fori_loop(1, amount, begin, 0)
        local.wait()
        lax.fori_loop(1, amount, finish, 0)

    whole = pl.BlockSpec(memory_space=pltpu.VMEM)
    dma = pltpu.SemaphoreType.DMA
    return pl.pallas_call(
        kernel,
        in_specs=[whole],
        out_specs=whole,
        out_shape=jax.ShapeDtypeStruct((amount,) + line.shape, line.dtype),
        scratch_shapes=[dma, dma((amount,)), dma((amount,))],
        compiler_params=pltpu.CompilerParams(collective_id=2, has_side_effects=True),
    )(line)


def chunk_lists(local, inside, chunk):
    chunks = local.shape[0] // chunk
    flags = inside.reshape(chunks, chunk)
    spots = jnp.arange(chunk, dtype=jnp.int32)
    ahead = (spots[:, None] < spots[None, :]).astype(NARROW)
    order = jnp.dot(flags.astype(NARROW), ahead, preferred_element_type=FLOAT).astype(jnp.int32)
    chosen = (order[:, None, :] == spots[None, :, None]) & flags[:, None, :]
    places = jnp.sum(jnp.where(chosen, spots[None, None, :], 0), axis=2)
    rows = jnp.sum(jnp.where(chosen, local.reshape(chunks, 1, chunk), 0), axis=2)
    return places, rows, jnp.sum(flags.astype(jnp.int32), axis=1)


def embed_table_grad(token_grads, places, rows, counts, vocab):
    chunks, chunk = places.shape
    width = token_grads.shape[-1]
    padded = vocab + 8
    unroll = 4

    def kernel(
        count_ref, place_ref, row_ref, tokens_ref, grad_ref, square_ref, wide_ref, total_ref, sem
    ):
        step = pl.program_id(0)

        @pl.when(step == 0)
        def _():
            total_ref[...] = jnp.zeros_like(total_ref)

        wide_ref[...] = tokens_ref[...].astype(FLOAT)
        amount = count_ref[step]

        def lap(j, carry):
            for u in range(unroll):
                spot = j * unroll + u
                row = jnp.where(spot < amount, row_ref[0, 0, spot], vocab)
                place = place_ref[0, 0, spot]
                total_ref[pl.ds(row, 1), :] += wide_ref[pl.ds(place, 1), :]
            return carry

        lax.fori_loop(0, (amount + unroll - 1) // unroll, lap, 0)

        @pl.when(step == chunks - 1)
        def _():
            out = pltpu.make_async_copy(total_ref.at[pl.ds(0, vocab), :], grad_ref, sem)
            out.start()
            square_ref[...] = jnp.sum(
                jnp.square(total_ref[pl.ds(0, vocab), :]), axis=0, keepdims=True
            )
            out.wait()

    line = pl.BlockSpec((1, 1, chunk), lambda i, c: (i, 0, 0), memory_space=pltpu.SMEM)
    return pl.pallas_call(
        kernel,
        grid_spec=pltpu.PrefetchScalarGridSpec(
            num_scalar_prefetch=1,
            grid=(chunks,),
            in_specs=[line, line, pl.BlockSpec((chunk, width), lambda i, c: (i, 0))],
            out_specs=[
                pl.BlockSpec(memory_space=pl.ANY),
                pl.BlockSpec((1, width), lambda i, c: (0, 0)),
            ],
            scratch_shapes=[
                pltpu.VMEM((chunk, width), FLOAT),
                pltpu.VMEM((padded, width), FLOAT),
                pltpu.SemaphoreType.DMA,
            ],
        ),
        out_shape=[
            jax.ShapeDtypeStruct((vocab, width), FLOAT),
            jax.ShapeDtypeStruct((1, width), FLOAT),
        ],
        compiler_params=pltpu.CompilerParams(vmem_limit_bytes=VMEM_LIMIT),
    )(
        counts,
        places.reshape(chunks, 1, chunk),
        rows.reshape(chunks, 1, chunk),
        token_grads.reshape(chunks * chunk, width),
    )


def update_rule(weight, grad, moment, average, rate, clip_factor):
    clipped = clip_factor * grad
    new_moment = MOMENTUM * moment + clipped
    new_weight = weight - rate * (clipped + MOMENTUM * new_moment)
    new_average = DECAY * average + (1.0 - DECAY) * new_weight
    return (new_weight, new_moment, new_average)


def update_all(scalars, tables, matrices, rates):
    vocab, width = tables[0][0].shape
    sub = tables[0][3].shape[0]
    block = block_rows(vocab, 1100)
    blocks = vocab // block
    window = max(-(-(sub + sub * r % 8) // 8) * 8 for r in range(vocab // sub))
    tile = 264
    tiles = -(-window // tile)
    kinds = len(tables)
    steps = kinds * (blocks + tiles)
    count = len(matrices)

    def kernel(*refs):
        refs = list(refs)

        def take(amount):
            taken = refs[:amount]
            del refs[:amount]
            return taken

        (scalars_ref,) = take(1)
        whole_in = [take(3) for _ in range(kinds)]
        own_in = [take(4) for _ in range(kinds)]
        small_in = [take(4) for _ in range(count)]
        new_tables = take(kinds)
        own_out = [take(2) for _ in range(kinds)]
        small_out = [take(3) for _ in range(count)]
        (factor_ref,) = take(1)
        windows = take(2)
        (sems,) = take(1)
        step = pl.program_id(0)
        begin = lax.axis_index("dp") * sub
        low = pl.multiple_of(begin // 8 * 8, 8)
        shift = begin - low

        def fetch(w, t):
            first = t * tile
            size = min(tile, window - first)
            return [
                pltpu.make_async_copy(
                    own_in[w][i].at[pl.ds(low + first, size), :],
                    windows[i].at[pl.ds(first, size), :],
                    sems.at[w, i, t],
                )
                for i in range(2)
            ]

        @pl.when(step == 0)
        def _():
            total = jnp.sum(scalars_ref[...], axis=0)
            norm = jnp.sqrt(total)
            factor_ref[...] = CLIP_LEVEL / jnp.maximum(norm, CLIP_LEVEL)

        factor = factor_ref[1:2, 0:1]
        for w in range(kinds):

            @pl.when((step >= w * blocks) & (step < (w + 1) * blocks))
            def _():
                table_ref, grad_ref, moment_ref = whole_in[w]
                table = table_ref[...]
                new_tables[w][...], _, _ = update_rule(
                    table, grad_ref[...], moment_ref[...].astype(FLOAT), table, rates[w], factor
                )

        @pl.when(step == 1)
        def _():
            for i in range(count):
                weight, grad, moment, average = [ref[...] for ref in small_in[i]]
                results = update_rule(weight, grad, moment, average, rates[kinds + i], factor)
                for ref, result in zip(small_out[i], results):
                    ref[...] = result

        for w in range(kinds):
            base = kinds * blocks + w * tiles
            for t in range(tiles):

                @pl.when(step == (base - tiles + t + 1 if w else 1))
                def _():
                    for copy in fetch(w, t):
                        copy.start()

            for t in range(tiles):

                @pl.when(step == base + t)
                def _():
                    if t == 0:
                        for copy in fetch(w, 0):
                            copy.wait()
                    if t + 1 < tiles:
                        for copy in fetch(w, t + 1):
                            copy.wait()

            @pl.when((step >= base) & (step < base + tiles))
            def _():
                first = pl.multiple_of((step - base) * tile, 8)
                amount = jnp.where(shift == 0, 0, tile + 8 - shift)
                own_table, own_grad = [
                    pltpu.roll(win[pl.ds(first, tile + 8), :], amount, 0)[:tile]
                    for win in windows
                ]
                _, own_out[w][0][...], own_out[w][1][...] = update_rule(
                    own_table, own_grad, own_in[w][2][...], own_in[w][3][...], rates[w], factor
                )

    whole = pl.BlockSpec(memory_space=pltpu.VMEM)
    anywhere = pl.BlockSpec(memory_space=pl.ANY)

    def table_spec(w):
        return pl.BlockSpec(
            (block, width), lambda i: (jnp.clip(i - w * blocks, 0, blocks - 1), 0)
        )

    def own_spec(w):
        return pl.BlockSpec(
            (tile, width),
            lambda i: (jnp.clip(i - kinds * blocks - w * tiles, 0, tiles - 1), 0),
        )

    state = jax.ShapeDtypeStruct((sub, width), FLOAT)
    operands = [scalars]
    in_specs = [whole]
    for w in range(kinds):
        operands += list(tables[w][:3])
        in_specs += [table_spec(w)] * 3
    for w in range(kinds):
        operands += [tables[w][0], tables[w][1], tables[w][3], tables[w][4]]
        in_specs += [anywhere, anywhere, own_spec(w), own_spec(w)]
    for item in matrices:
        operands += list(item)
        in_specs += [whole] * 4
    out_specs = [table_spec(w) for w in range(kinds)]
    out_shape = [jax.ShapeDtypeStruct((vocab, width), FLOAT)] * kinds
    for w in range(kinds):
        out_specs += [own_spec(w)] * 2
        out_shape += [state] * 2
    for item in matrices:
        out_specs += [whole] * 3
        out_shape += [jax.ShapeDtypeStruct(item[0].shape, FLOAT)] * 3
    results = pl.pallas_call(
        kernel,
        grid=(steps,),
        in_specs=in_specs,
        out_specs=out_specs,
        out_shape=out_shape,
        scratch_shapes=[pltpu.VMEM((8, 128), FLOAT)]
        + [pltpu.VMEM((tiles * tile + 8, width), FLOAT)] * 2
        + [pltpu.SemaphoreType.DMA((kinds, 2, tiles))],
        compiler_params=pltpu.CompilerParams(vmem_limit_bytes=VMEM_LIMIT),
    )(*operands)
    tables_out = [
        (results[w], *results[kinds + 2 * w : kinds + 2 + 2 * w]) for w in range(kinds)
    ]
    return tables_out, [results[3 * (kinds + i) : 3 * (kinds + i + 1)] for i in range(count)]


def shards(
    token_ids,
    loss_mask,
    lengths,
    buffer_ids,
    embed_table,
    embed_moment,
    embed_average,
    head_table,
    head_moment,
    head_average,
    in_weights,
    in_moment,
    in_average,
    out_weights,
    out_moment,
    out_average,
    vectors,
    vector_moment,
    vector_average,
):
    groups = lax.axis_size("fsdp")
    replicas = lax.axis_size("dp")
    member = lax.axis_index("fsdp")
    replica = lax.axis_index("dp")
    batches, _, seq = token_ids.shape
    vocab_rows, width = embed_table.shape
    head_size = width // HEADS
    vocab_start = member * vocab_rows
    own_rows = batches * seq
    rows_all = groups * own_rows

    tokens, marks, buffers = token_ids[:, 0], loss_mask[:, 0], buffer_ids[:, 0]
    divisor, offset, counted = jax.vmap(functools.partial(slot_info, buffer_count=NSEG))(
        tokens, marks, lengths[:, 0], buffers
    )
    packed = jnp.concatenate(
        [
            tokens,
            divisor,
            jnp.broadcast_to(jnp.sum(counted), (8 - 2 * batches, seq)),
        ],
        axis=0,
    )
    amount = vectors.shape[0]
    line = jnp.pad(vectors, (0, -amount % 1024)).reshape(-1, 128)
    everyone, lines, in_full, out_full, resid, aims = start_kernel(
        packed,
        line,
        in_weights,
        out_weights,
        embed_table,
        head_table,
        batches,
        groups,
        replicas,
    )
    vector_full = lines.reshape(groups, -1)[:, :amount].reshape(-1).astype(NARROW)
    early_moment, resid = lax.optimization_barrier((head_moment, resid))
    head_moment_low = lax.all_gather(early_moment.astype(NARROW), "dp", axis=0, tiled=True)
    tokens_all = everyone[:, :batches]
    count = jnp.maximum(jnp.sum(everyone[:, 2 * batches, 0]).astype(FLOAT), 1.0)
    divisor_all = everyone[:, batches : 2 * batches].astype(FLOAT)
    share_all = jnp.where(divisor_all > 0.5, 1.0 / jnp.maximum(divisor_all, 1.0), 0.0)
    weight_all = (share_all / count).reshape(-1)
    target_all = (
        jnp.concatenate([tokens_all[:, :, 1:], jnp.zeros_like(tokens_all[:, :, :1])], axis=2)
        .reshape(-1)
    ) - vocab_start
    tokens_flat = tokens_all.reshape(-1)
    local_all = tokens_flat - vocab_start
    inside_all = (local_all >= 0) & (local_all < vocab_rows)

    def group_part(values):
        return lax.dynamic_slice_in_dim(values, replica * rows_all, rows_all, 0)

    vector = vector_full.astype(FLOAT).reshape(1, -1)
    tables = rotary_tables(offset.reshape(-1), head_size)
    lines_of, columns_of = buffers[:, None, :], buffers[:, :, None]
    final, *kept = layer_forward(resid, in_full, out_full, vector, tables, lines_of, columns_of)
    final_grad, logsum_all, loss_part, all_hidden = head_kernel(
        head_table, final, aims, group_part(target_all), group_part(weight_all), groups, replicas
    )

    less_weight = logsum_all - jnp.log(jnp.maximum(weight_all, 1e-30))
    shifted = jnp.where(weight_all > 0.0, less_weight, 1e30)
    chunk = min(512, rows_all)
    lists = chunk_lists(local_all, inside_all, chunk)

    token_grad, vector_grad, owner_grads = layer_backward(
        final_grad,
        resid,
        in_full,
        out_full,
        vector,
        tables,
        lines_of,
        columns_of,
        kept,
        groups,
    )
    token_grad, head_moment_low = lax.optimization_barrier((token_grad, head_moment_low))
    slices = jnp.pad(vector_grad.reshape(groups, amount), ((0, 0), (0, -amount % 1024)))
    in_rows = in_weights.shape[0]
    cut = owner_grads.shape[1] - out_weights.shape[0]
    head_grad, head_square, token_grads, vector_sum, owned = head_table_grad(
        head_table,
        all_hidden,
        shifted,
        weight_all,
        target_all,
        token_grad,
        slices.reshape(groups, -1, 128),
        owner_grads,
        cut,
        groups,
        replicas,
    )
    if owned.shape != owner_grads.shape[1:]:
        owned = lax.psum(lax.psum_scatter(owner_grads, "fsdp", scatter_dimension=0), "dp")
    layer_grads = [
        owned[:cut].reshape(-1, in_rows, width).transpose(1, 0, 2).reshape(in_rows, -1),
        owned[cut:],
        vector_sum.reshape(-1)[:amount],
    ]
    late_moment, token_grads = lax.optimization_barrier((embed_moment, token_grads))
    embed_moment_low = lax.all_gather(late_moment.astype(NARROW), "dp", axis=0, tiled=True)
    embed_grad, embed_square = embed_table_grad(token_grads, *lists, vocab_rows)
    square = jnp.sum(embed_square) + jnp.sum(head_square)
    for grad in layer_grads:
        square = square + jnp.sum(grad * grad)
    line = jnp.stack([loss_part, square / replicas])[:, None]
    line = jnp.pad(jnp.broadcast_to(line, (2, 128)), ((0, 6), (0, 0)))
    scalars = exchange_scalars(line, groups, replicas)
    pair = jnp.sum(scalars[:, :2, 0], axis=0)
    loss = pair[0]
    grad_norm = jnp.sqrt(pair[1])
    base = math.sqrt(NPARAM) / CLIP_LEVEL
    root = math.sqrt(width)

    def row(values):
        return values.reshape(1, -1)

    (head,), (inner, outer, vector) = update_all(
        scalars,
        [(head_table, head_grad, head_moment_low, head_moment, head_average)],
        [
            (in_weights, layer_grads[0], in_moment, in_average),
            (out_weights, layer_grads[1], out_moment, out_average),
            tuple(map(row, (vectors, layer_grads[2], vector_moment, vector_average))),
        ],
        (base / root, base / root, base / root, 0.3 * base),
    )
    scalars, new_head = lax.optimization_barrier((scalars, head[0]))
    head = (new_head, *head[1:])
    (embed,), _ = update_all(
        scalars,
        [(embed_table, embed_grad, embed_moment_low, embed_moment, embed_average)],
        [],
        (base,),
    )
    vector = [values.reshape(-1) for values in vector]
    return (*embed, *head, *inner, *outer, *vector, loss, grad_norm)


def solution(mesh):
    placed = (
        P(None, ("dp", "fsdp"), None),
        P(None, ("dp", "fsdp"), None),
        P(None, ("dp", "fsdp")),
        P(None, ("dp", "fsdp"), None),
        P("fsdp", None),
        P(("fsdp", "dp"), None),
        P(("fsdp", "dp"), None),
        P("fsdp", None),
        P(("fsdp", "dp"), None),
        P(("fsdp", "dp"), None),
        P("fsdp", None),
        P("fsdp", None),
        P("fsdp", None),
        P("fsdp", None),
        P("fsdp", None),
        P("fsdp", None),
        P("fsdp"),
        P("fsdp"),
        P("fsdp"),
    )
    return jax.shard_map(
        shards,
        mesh=mesh,
        in_specs=placed,
        out_specs=(
            P("fsdp", None),
            P(("fsdp", "dp"), None),
            P(("fsdp", "dp"), None),
            P("fsdp", None),
            P(("fsdp", "dp"), None),
            P(("fsdp", "dp"), None),
            P("fsdp", None),
            P("fsdp", None),
            P("fsdp", None),
            P("fsdp", None),
            P("fsdp", None),
            P("fsdp", None),
            P("fsdp"),
            P("fsdp"),
            P("fsdp"),
            P(),
            P(),
        ),
        check_vma=False,
    )
```
